32 devices in a mesh: rep: 2 (over x), sec: 8 (over z, y), term: 2 (over core).
Axes of the slice: x: 2, y: 2, z: 4, core: 2. Of those that a mesh axis runs over, the one named last changes fastest.
Arguments:
- wavefunction: bfloat16 [512, 128, 128], P(('rep', 'sec')), parts along dimension 0, may hold values from -6 to 6
- left_operator: bfloat16 [4, 512, 128, 128], P('term', ('rep', 'sec')), parts along dimension 1, may hold values from -3 to 3
- right_operator: bfloat16 [4, 512, 128, 128], P('term', ('rep', 'sec')), parts along dimension 1, may hold values from -3 to 3
- target_owner: int32 [4, 512, 1], P('term', ('rep', 'sec')), parts along dimension 1, may hold values from 0 to 7; in each aligned block of 32 rows (0 to 31, 32 to 63, ..., all dimensions but the last counted through in order) at most 8 rows name the same one
- target_local: int32 [4, 512], P('term', ('rep', 'sec')), parts along dimension 1, may hold values from 0 to 31
Outputs:
- sigma_two: bfloat16 [512, 128, 128], P(('rep', 'sec'), 'term'), parts along dimension 0
- rayleigh: float32 [2], P('rep'), parts along dimension 0
The draws below stay inside these ranges and needn't reach their ends.
There are 2 independent parts, one for each index of `rep`. The reference program is written for one: setup_inputs(seed, part) draws one part's arguments, and reference() takes and returns one part's arrays. A program takes and returns all parts, laid end to end along the dimension named above; each array names one. Nothing has to cross between parts.
Inputs may be any that keep to these rules, and one draw needn't show every extreme that they name: `target_owner`: among the 32 source blocks of one term on one owner no owner is named more than 8 times, and one is named exactly 8 times.
All inputs are finite; a program needn't handle non-finite values.
Results may differ from the reference program's by a relative error of at most 0.006.
Values may be sent and summed in bfloat16 or wider, within the bound.
No kernel may reach another device: no remote copies, remote signals or barrier semaphores. Data moves between devices by JAX's collectives and lax.ppermute only.
A program may use at most 64 MiB of HBM per device.

```python
import math
import jax
import jax.numpy as jnp
import numpy as np

BL = 128
BR = 128
BLK_DEV = 32
OWNERS = 8
CAP = 8
NBLK = 256
NTERM = 4


def draw_wavefunction(key, part):
    key = jax.random.fold_in(key, 11)
    first, second = jax.random.split(key, 2)
    common = jax.random.normal(first, (BL, BR), jnp.float32)
    noise = jax.random.normal(second, (NBLK, BL, BR), jnp.float32)
    values = 0.8 * common[None] + 0.6 * noise
    return jnp.clip(values, -6.0, 6.0).astype(jnp.bfloat16)


def operator_blocks(key, width):
    identity = jnp.eye(width, dtype=jnp.float32)
    noise = jax.random.normal(key, (NTERM, NBLK, width, width), jnp.float32)
    values = identity + noise / jnp.sqrt(jnp.float32(width))
    return jnp.clip(values, -3.0, 3.0).astype(jnp.bfloat16)


def draw_left_operator(key, part):
    key = jax.random.fold_in(key, 23)
    return operator_blocks(key, BL)


def draw_right_operator(key, part):
    key = jax.random.fold_in(key, 37)
    return operator_blocks(key, BR)


def plant(array, rng, least, top_value):
    extent = array.shape
    index_at = [jax.random.randint(jax.random.fold_in(rng, axis), (), 0, extent[axis]) for axis in range(len(extent))]
    array = array.at[tuple(index_at)].set(least)
    longest = extent.index(max(extent))
    index_at[longest] = (index_at[longest] + 1) % extent[longest]
    return array.at[tuple(index_at)].set(top_value)


def assign_block(stream_key, own, number, rows, amount, top, bound, slope):
    ranking = jax.random.permutation(stream_key, amount)
    heavy_load, usual = portions_of(amount, rows * top, bound, slope, True), portions_of(amount, rows * top, bound, slope, False)
    places = jnp.arange(amount)

    def named(tallies, offset_by):
        used = int((tallies > 0).sum())
        fixed = max(1, used // 4)
        passed = fixed + (places - fixed + offset_by * (used - fixed)) % max(1, amount - fixed)
        return jnp.zeros((amount,), jnp.int32).at[ranking[jnp.where(places < fixed, places, passed)]].set(jnp.asarray(tallies, jnp.int32))

    tallies = jnp.where(number % 4 == 0, named(heavy_load, number // 4), named(usual, number - number // 4 - 1))
    mixed = jax.random.permutation(jax.random.fold_in(own, 3), amount)
    source_of, taker = mixed[0:amount // 2 * 2:2], mixed[1:amount // 2 * 2:2]
    margin = jnp.minimum(tallies[source_of] - 1, bound - tallies[taker]) // 2
    margin = jnp.where((source_of == ranking[0]) | (taker == ranking[0]) | (tallies[taker] == 0), 0, jnp.maximum(margin, 0))
    passed = jax.random.randint(jax.random.fold_in(own, 4), (amount // 2,), 0, 1 << 20) % (margin + 1)
    tallies = tallies.at[source_of].add(-passed).at[taker].add(passed)
    items = jnp.searchsorted(jnp.cumsum(tallies), jnp.arange(rows * top), side="right").astype(jnp.int32)
    listing = items.reshape(top, rows).T
    listing = listing[jax.random.permutation(jax.random.fold_in(own, 1), rows)]
    offset_by = jax.random.randint(jax.random.fold_in(own, 2), (rows, 1), 0, top)
    return jnp.take_along_axis(listing, (jnp.arange(top)[None, :] + offset_by) % top, axis=1)


def portions_of(number_of, total, reach, lean, full):
    weights = [(1 << 20) // math.isqrt(rank ** lean) + 1 for rank in range(1, number_of + 1)]
    largest = reach if full else min(reach, max(-(-total // number_of), total * weights[0] // sum(weights)))
    least = 1 if total - largest >= number_of - 1 else 0
    holding, surplus = [largest] + [least] * (number_of - 1), total - largest - least * (number_of - 1)
    while surplus > 0:
        candidates = [i for i in range(1, number_of) if holding[i] < largest] or [i for i in range(1, number_of) if holding[i] < reach]
        whole, remaining = sum([weights[i] for i in candidates]), surplus
        for i in candidates:
            addition = min(reach - holding[i], max(1, remaining * weights[i] // whole), surplus)
            holding[i] = holding[i] + addition
            surplus = surplus - addition
    return np.array(holding)


def setup_inputs(seed: int = 0, part: int = 0) -> dict:
    seeds = jax.random.split(jax.random.key(seed), 6)
    part_splits = jax.random.split(jax.random.fold_in(seeds[5], part), 6)
    wavefunction = draw_wavefunction(jax.random.fold_in(jax.random.fold_in(seeds[5], part), 71), part)
    left_operator = draw_left_operator(jax.random.fold_in(jax.random.fold_in(seeds[5], part), 71), part)
    right_operator = draw_right_operator(jax.random.fold_in(jax.random.fold_in(seeds[5], part), 71), part)
    target_owner_keys = jax.random.split(jax.random.fold_in(part_splits[3], 1), NTERM * NBLK // BLK_DEV)
    target_owner_turns = jax.random.permutation(jax.random.fold_in(part_splits[3], 3), NTERM * NBLK // BLK_DEV)
    target_owner = jax.vmap(lambda own, number: assign_block(jax.random.fold_in(part_splits[3], 2), own, number, BLK_DEV, OWNERS, 1, CAP, 2))(target_owner_keys, target_owner_turns).reshape((NTERM, NBLK, 1))
    target_local = plant(jax.random.randint(part_splits[4], (NTERM, NBLK), 0, BLK_DEV), jax.random.fold_in(part_splits[4], 1), 0, BLK_DEV - 1).astype(jnp.int32)
    return {"wavefunction": wavefunction, "left_operator": left_operator, "right_operator": right_operator, "target_owner": target_owner, "target_local": target_local}


def apply_ham(vector, left_operator, right_operator, target):
    totals = jnp.zeros(vector.shape, jnp.float32)
    for term_index in range(NTERM):
        moved = jnp.einsum('bij,bjr->bir', left_operator[term_index].astype(jnp.float32), vector.astype(jnp.float32)).astype(jnp.bfloat16)
        picked = right_operator[term_index][target[term_index]]
        product = jnp.einsum('bir,brq->biq', moved.astype(jnp.float32), picked.astype(jnp.float32))
        totals = totals + jax.ops.segment_sum(product, target[term_index], num_segments=NBLK)
    return totals

def reference(wavefunction, left_operator, right_operator, target_owner, target_local):
    target = (target_owner[:, :, 0] * BLK_DEV + target_local).astype(jnp.int32)
    sigma_one = apply_ham(wavefunction, left_operator, right_operator, target)
    wave_float = wavefunction.astype(jnp.float32)
    rayleigh = jnp.sum(wave_float * sigma_one) / jnp.sum(wave_float * wave_float)
    residual = sigma_one - rayleigh * wave_float
    entries = NBLK * BL * BR
    direction = (residual * jax.lax.rsqrt(jnp.sum(residual * residual) / entries + 1e-06)).astype(jnp.bfloat16)
    sigma_two = apply_ham(direction, left_operator, right_operator, target).astype(jnp.bfloat16)
    return (sigma_two, jnp.reshape(rayleigh, (1,)))
```

```python
import functools

import jax
import jax.numpy as jnp
from jax import lax
from jax.experimental import pallas as pl
from jax.experimental.pallas import tpu as pltpu
from jax.sharding import PartitionSpec as P

BOTH = ("sec", "term")


def slot_codes(target_owner, target_local, owners, capacity):
    terms, blocks = target_local.shape
    owner = target_owner[:, :, 0]
    place = jnp.arange(blocks, dtype=jnp.int32)
    same = (owner[:, :, None] == owner[:, None, :]) & (place[None, :] < place[:, None])[None]
    position = jnp.sum(same.astype(jnp.int32), axis=2)
    hit = (
        owner[:, None, None, :] == jnp.arange(owners, dtype=jnp.int32)[None, :, None, None]
    ) & (position[:, None, None, :] == jnp.arange(capacity, dtype=jnp.int32)[None, None, :, None])
    code = place[None, :] * (2 * blocks) + target_local - blocks
    return blocks + jnp.sum(jnp.where(hit, code[:, None, None, :], 0), axis=3)


def apply_kernel(first, capacity, blocks, code_ref, left_ref, vector_ref, right_ref, *rest):
    total_in, total = (None, rest[0]) if first else rest
    step = pl.program_id(0)
    rows, width = left_ref.shape[2:]

    @pl.when(step == 0)
    def _():
        total[...] = jnp.zeros_like(total) if first else total_in[...]

    for term in range(2):
        moved, where = [], []
        for slot in range(capacity):
            code = code_ref[2 * step + term, slot]
            source, target = lax.div(code, 2 * blocks), lax.rem(code, 2 * blocks)
            block = vector_ref[0, :, source].reshape(2 * rows, width)
            product = jnp.dot(left_ref[term, slot], block, preferred_element_type=jnp.float32)
            moved.append(product.astype(jnp.bfloat16))
            where.append(target)
        for slot in range(capacity):
            target = where[slot]
            total[target] += jnp.dot(
                moved[slot],
                right_ref[term, jnp.minimum(target, blocks - 1)],
                preferred_element_type=jnp.float32,
            )


def apply_chunk(total, codes, left, vector, right):
    owners, _, blocks, rows, width = vector.shape
    capacity = left.shape[1]
    first = total is None
    spec_total = pl.BlockSpec((blocks + 1, rows, width), lambda s, c: (0, 0, 0))
    return pl.pallas_call(
        functools.partial(apply_kernel, first, capacity, blocks),
        out_shape=jax.ShapeDtypeStruct((blocks + 1, rows, width), jnp.float32),
        grid_spec=pltpu.PrefetchScalarGridSpec(
            num_scalar_prefetch=1,
            grid=(owners,),
            in_specs=[
                pl.BlockSpec((2, capacity, rows, width), lambda s, c: (s, 0, 0, 0)),
                pl.BlockSpec((1, 2, blocks, rows, width), lambda s, c: (s, 0, 0, 0, 0)),
                pl.BlockSpec((2, blocks, width, width), lambda s, c: (0, 0, 0, 0)),
            ]
            + ([] if first else [spec_total]),
            out_specs=spec_total,
        ),
        compiler_params=pltpu.CompilerParams(vmem_limit_bytes=32 * 2**20),
        cost_estimate=pl.CostEstimate(
            flops=owners * 2 * capacity * 2 * 2 * rows * width * width,
            bytes_accessed=left.size * 2 + vector.size * 2 + right.size * 2,
            transcendentals=0,
        ),
    )(codes, left, vector, right, *([] if first else [total]))


def per_device(wavefunction, left_operator, right_operator, target_owner, target_local):
    owners = lax.axis_size("sec")
    halves = lax.axis_size("term")
    me, half = lax.axis_index("sec"), lax.axis_index("term")
    terms, blocks, height, width = left_operator.shape
    rows = height // halves
    capacity = 2 * blocks // owners

    own_rows = lax.dynamic_slice_in_dim(wavefunction, half * rows, rows, 1)
    codes = slot_codes(target_owner, target_local, owners, capacity)
    sources = codes // (2 * blocks)

    moved_left = []
    for k in range(terms):
        pick = sources[k][:, None, :] * halves + jnp.arange(halves, dtype=jnp.int32)[None, :, None]
        pieces = left_operator[k].reshape(blocks * halves, rows, width)[pick.reshape(-1)]
        pieces = pieces.reshape(owners * halves, capacity, rows, width)
        moved_left.append(lax.all_to_all(pieces, BOTH, split_axis=0, concat_axis=0, tiled=True))
    all_codes = lax.all_gather(codes, BOTH, axis=0)
    my_codes = lax.dynamic_index_in_dim(all_codes, me, axis=3 - 1, keepdims=False)
    gathered = lax.all_gather(own_rows, BOTH, axis=0).reshape(owners, halves, blocks, rows, width)
    right = lax.all_gather(right_operator, "term", axis=1)

    def apply(vector):
        total = None
        for k in range(terms):
            total = apply_chunk(total, my_codes[:, k], moved_left[k], vector, right[k])
        return total[:blocks]

    sigma_rows = apply(gathered)
    wave = own_rows.astype(jnp.float32)
    cross, own = jnp.sum(wave * sigma_rows), jnp.sum(wave * wave)
    local = jnp.where(own > 0, cross / own, 0.0)
    about = jnp.sum(jnp.square(sigma_rows - local * wave))
    stats = lax.all_gather(jnp.stack([about, cross, own, local]), BOTH, axis=0)
    rayleigh = jnp.sum(stats[:, 1]) / jnp.sum(stats[:, 2])
    residual_sq = jnp.sum(stats[:, 0] + jnp.square(stats[:, 3] - rayleigh) * stats[:, 2])
    entries = blocks * owners * height * width
    factor = lax.rsqrt(residual_sq / entries + 1e-06)
    direction = ((sigma_rows - rayleigh * wave) * factor).astype(jnp.bfloat16)
    direction = lax.all_gather(direction, BOTH, axis=0).reshape(gathered.shape)
    sigma_two = apply(direction).astype(jnp.bfloat16)
    return (sigma_two, jnp.reshape(rayleigh, (1,)))


def solution(mesh):
    placed = (
        P(("rep", "sec"), None, None),
        P("term", ("rep", "sec"), None, None),
        P("term", ("rep", "sec"), None, None),
        P("term", ("rep", "sec"), None),
        P("term", ("rep", "sec")),
    )
    return jax.shard_map(
        per_device,
        mesh=mesh,
        in_specs=placed,
        out_specs=(P(("rep", "sec"), "term", None), P("rep")),
        check_vma=False,
    )
```

```python
import functools

import jax
import jax.numpy as jnp
from jax import lax
from jax.experimental import pallas as pl
from jax.experimental.pallas import tpu as pltpu
from jax.sharding import PartitionSpec as P

BOTH = ("sec", "term")
VMEM_LIMIT = 32 * 2**20
RING_BYTES = 24 * 2**20


def ring_order(owners):
    if owners % 2:
        return list(range(owners))
    return list(range(0, owners, 2)) + list(range(owners - 1, 0, -2))


def ring_place(owner, owners):
    if owners % 2:
        return owner
    return jnp.where(owner % 2 == 0, owner // 2, owners - 1 - owner // 2)


def ring_owner(place, owners):
    place = place % owners
    if owners % 2:
        return place
    return jnp.where(place < owners // 2, 2 * place, 2 * (owners - 1 - place) + 1)


def send(value, owners, halves, shifts, flip=0):
    ring = ring_order(owners)
    pairs = []
    for place in range(owners):
        for half in range(halves):
            to = ring[(place + shifts[half]) % owners]
            pairs.append((ring[place] * halves + half, to * halves + (half ^ flip)))
    return lax.ppermute(value, BOTH, pairs)


def swap(value, owners, halves):
    return send(value, owners, halves, (0,) * halves, 1)


def ring_gather(unit, owners, halves, half):
    units = {0: unit}
    reach = (owners - 1) // 2
    for step in range(1, reach + 1):
        units[step] = send(units[step - 1], owners, halves, (1,) * halves)
        units[-step] = send(units[1 - step], owners, halves, (-1,) * halves)
    if owners % 2 == 0:
        last = jnp.where(half == 0, units[reach], units[-reach])
        units[owners // 2] = send(last, owners, halves, (1, -1))
    return units


def spread(value, devices, me):
    if devices & (devices - 1):
        return lax.psum(value, BOTH)
    step = 1
    while step < devices:
        value = value + lax.ppermute(value, BOTH, [(d, d ^ step) for d in range(devices)])
        step *= 2
    return value


def slot_codes(target_owner, target_local, owners, capacity):
    terms, blocks = target_local.shape
    owner = target_owner[:, :, 0]
    place = jnp.arange(blocks, dtype=jnp.int32)
    same = (owner[:, :, None] == owner[:, None, :]) & (place[None, :] < place[:, None])[None]
    position = jnp.sum(same.astype(jnp.int32), axis=2)
    hit = (
        owner[:, None, None, :] == jnp.arange(owners, dtype=jnp.int32)[None, :, None, None]
    ) & (position[:, None, None, :] == jnp.arange(capacity, dtype=jnp.int32)[None, None, :, None])
    code = place[None, :] * (2 * blocks) + target_local - blocks
    return blocks + jnp.sum(jnp.where(hit, code[:, None, None, :], 0), axis=3)


def apply_kernel(
    sources, second, first, last, capacity, blocks, terms, half_ref, codes_ref, scale_ref, *refs
):
    refs = list(refs)
    pieces = [[refs.pop(0) for _ in range(6 if second else 4)] for _ in range(sources)]
    rights = [refs.pop(0), refs.pop(0)]
    total_in = None if first else refs.pop(0)
    if last:
        out, total = refs
    else:
        (total,) = refs
    upper = half_ref[0] == 0
    rows, width = pieces[0][0].shape[2:]

    total[...] = jnp.zeros_like(total) if first else total_in[...]

    for index, piece in enumerate(pieces):
        for flip in range(2):

            @pl.loop(0, terms)
            def _(term):
                moved, where = [], []
                for slot in range(capacity):
                    code = codes_ref[((index * 2 + flip) * terms + term) * capacity + slot]
                    source, target = lax.div(code, 2 * blocks), lax.rem(code, 2 * blocks)
                    near, far = piece[2][source], piece[3][source]
                    if second:
                        factor = scale_ref[0]
                        shift = scale_ref[1 + 2 * index], scale_ref[2 + 2 * index]
                        near = near.astype(jnp.float32) + shift[0] * piece[4][source].astype(
                            jnp.float32
                        )
                        far = far.astype(jnp.float32) + shift[1] * piece[5][source].astype(
                            jnp.float32
                        )
                        near = (near * factor).astype(jnp.bfloat16)
                        far = (far * factor).astype(jnp.bfloat16)
                    block = jnp.concatenate(
                        [jnp.where(upper, near, far), jnp.where(upper, far, near)], axis=0
                    )
                    product = jnp.dot(
                        piece[flip][term, slot], block, preferred_element_type=jnp.float32
                    )
                    moved.append(product.astype(jnp.bfloat16))
                    where.append(target)
                for slot in range(capacity):
                    target = where[slot]
                    total[target] += jnp.dot(
                        moved[slot],
                        rights[flip][term, jnp.minimum(target, blocks - 1)],
                        preferred_element_type=jnp.float32,
                    )

    if last:
        out[...] = total[:blocks].astype(out.dtype)


def apply_group(half, codes, scale, pieces, rights, total, last):
    terms, capacity, rows, width = pieces[0][0].shape
    blocks = rights[0].shape[1]
    first, second = total is None, len(pieces[0]) == 6
    arrays = [array for piece in pieces for array in piece] + list(rights)
    if not first:
        arrays.append(total)
    scalars = pl.BlockSpec(memory_space=pltpu.SMEM)
    whole = pl.BlockSpec(memory_space=pltpu.VMEM)
    total_shape = (blocks + 1, rows, width)
    if last:
        out_shape = jax.ShapeDtypeStruct((blocks, rows, width), jnp.bfloat16)
        scratch = [pltpu.VMEM(total_shape, jnp.float32)]
    else:
        out_shape = jax.ShapeDtypeStruct(total_shape, jnp.float32)
        scratch = []
    return pl.pallas_call(
        functools.partial(
            apply_kernel, len(pieces), second, first, last, capacity, blocks, terms
        ),
        out_shape=out_shape,
        in_specs=[scalars] * 3 + [whole] * len(arrays),
        out_specs=whole,
        scratch_shapes=scratch,
        compiler_params=pltpu.CompilerParams(vmem_limit_bytes=VMEM_LIMIT),
        cost_estimate=pl.CostEstimate(
            flops=len(pieces) * 2 * terms * capacity * 2 * 2 * rows * width * width,
            bytes_accessed=sum(array.size * array.dtype.itemsize for array in arrays),
            transcendentals=0,
        ),
    )(half, codes, scale, *arrays)


def residual_kernel(me_ref, total_ref, wave_ref, rest_ref, stats_ref):
    blocks = wave_ref.shape[0]

    def sums(block, carry):
        cross, own = carry
        wave = wave_ref[block].astype(jnp.float32)
        return cross + wave * total_ref[block], own + wave * wave

    zero = jnp.zeros(wave_ref.shape[1:], jnp.float32)
    cross, own = lax.fori_loop(0, blocks, sums, (zero, zero), unroll=4)
    cross, own = jnp.sum(cross, keepdims=True), jnp.sum(own, keepdims=True)
    local = jnp.where(own > 0, cross / own, 0.0)

    def rest(block, carry):
        value = total_ref[block] - local * wave_ref[block].astype(jnp.float32)
        rest_ref[block] = value.astype(jnp.bfloat16)
        return carry + value * value

    about = jnp.sum(lax.fori_loop(0, blocks, rest, zero, unroll=4), keepdims=True)
    lane = lax.broadcasted_iota(jnp.int32, stats_ref.shape, 1)
    row = lax.broadcasted_iota(jnp.int32, stats_ref.shape, 0)
    values = jnp.where(lane == 0, about, jnp.where(lane == 1, cross, jnp.where(lane == 2, own, local)))
    stats_ref[...] = jnp.where((row == me_ref[0]) & (lane < 4), values, 0.0)


def local_residual(me, devices, total, wave):
    scalars = pl.BlockSpec(memory_space=pltpu.SMEM)
    whole = pl.BlockSpec(memory_space=pltpu.VMEM)
    return pl.pallas_call(
        residual_kernel,
        out_shape=(
            jax.ShapeDtypeStruct(wave.shape, jnp.bfloat16),
            jax.ShapeDtypeStruct((devices, 128), jnp.float32),
        ),
        in_specs=[scalars, whole, whole],
        out_specs=(whole, whole),
        compiler_params=pltpu.CompilerParams(vmem_limit_bytes=VMEM_LIMIT),
    )(me, total, wave)


def per_device_ring(wavefunction, left_operator, right_operator, target_owner, target_local):
    owners, halves = lax.axis_size("sec"), lax.axis_size("term")
    devices = owners * halves
    me, half = lax.axis_index("sec"), lax.axis_index("term")
    terms, blocks, height, width = left_operator.shape
    rows = height // halves
    capacity = 2 * blocks // owners
    place = ring_place(me, owners)
    device = jnp.reshape(me * halves + half, (1,)).astype(jnp.int32)
    half_scalar = jnp.reshape(half, (1,)).astype(jnp.int32)

    own_rows = lax.dynamic_slice_in_dim(wavefunction, half * rows, rows, 1)
    other_rows = lax.dynamic_slice_in_dim(wavefunction, (1 - half) * rows, rows, 1)
    reach = (owners - 1) // 2
    distances = [0] + [s for step in range(1, reach + 1) for s in (step, -step)]
    if owners % 2 == 0:
        distances.append(owners // 2)

    codes = slot_codes(target_owner, target_local, owners, capacity)
    sources = codes // (2 * blocks)
    term_ids = jnp.arange(terms, dtype=jnp.int32)[:, None]
    flat_left = left_operator.reshape(terms * blocks * halves, rows, width)
    lefts = {}
    for s in reversed(distances):
        to = ring_owner(place + s, owners)
        picked = lax.dynamic_index_in_dim(sources, to, axis=1, keepdims=False)
        for flip in range(2):
            pick = (term_ids * blocks + picked) * halves + (half ^ flip)
            piece = flat_left[pick.reshape(-1)].reshape(terms, capacity, rows, width)
            if s or flip:
                piece = send(piece, owners, halves, (s,) * halves, flip)
            lefts[s, flip] = piece

    mine = jnp.arange(devices, dtype=jnp.int32) == device[0]
    table = jnp.where(mine[:, None], codes.reshape(1, -1), 0)
    table = spread(table, devices, device).reshape(devices, terms, owners, capacity)
    table = lax.dynamic_index_in_dim(table, me, axis=2, keepdims=False)
    rights = (right_operator, swap(right_operator, owners, halves))

    near = ring_gather(own_rows, owners, halves, half)
    far = {s: swap(unit, owners, halves) if s else other_rows for s, unit in near.items()}

    groups = [[0]] + [[step, -step] for step in range(1, reach + 1)]
    if owners % 2 == 0:
        groups.append([owners // 2])

    def origin(s, flip):
        return ring_owner(place - s, owners) * halves + (half ^ flip)

    group_codes = [
        jnp.concatenate(
            [
                lax.dynamic_index_in_dim(table, origin(s, flip), 0, keepdims=False).reshape(-1)
                for s in group
                for flip in range(2)
            ]
        )
        for group in groups
    ]

    total = None
    no_scale = jnp.zeros((1,), jnp.float32)
    for group, code in zip(groups, group_codes):
        pieces = [(lefts[s, 0], lefts[s, 1], near[s], far[s]) for s in group]
        total = apply_group(half_scalar, code, no_scale, pieces, rights, total, False)

    rest, stats = local_residual(device, devices, total, own_rows)
    near_rest = ring_gather(rest, owners, halves, half)
    far_rest = {s: swap(unit, owners, halves) for s, unit in near_rest.items()}

    stats = spread(stats, devices, device)
    rayleigh = jnp.sum(stats[:, 1]) / jnp.sum(stats[:, 2])
    offset = stats[:, 3] - rayleigh
    residual_sq = jnp.sum(stats[:, 0] + jnp.square(offset) * stats[:, 2])
    entries = blocks * owners * height * width
    factor = lax.rsqrt(residual_sq / entries + 1e-06)

    total = None
    for group, code in zip(groups, group_codes):
        pieces = [
            (lefts[s, 0], lefts[s, 1], near_rest[s], far_rest[s], near[s], far[s]) for s in group
        ]
        scale = jnp.stack([factor] + [offset[origin(s, flip)] for s in group for flip in range(2)])
        total = apply_group(
            half_scalar, code, scale, pieces, rights, total, group is groups[-1]
        )
    return (total, jnp.reshape(rayleigh, (1,)))


def stream_kernel(first, capacity, blocks, code_ref, left_ref, vector_ref, right_ref, *rest):
    total_in, total = (None, rest[0]) if first else rest
    step = pl.program_id(0)
    rows, width = left_ref.shape[2:]

    @pl.when(step == 0)
    def _():
        total[...] = jnp.zeros_like(total) if first else total_in[...]

    for term in range(2):
        moved, where = [], []
        for slot in range(capacity):
            code = code_ref[2 * step + term, slot]
            source, target = lax.div(code, 2 * blocks), lax.rem(code, 2 * blocks)
            block = vector_ref[0, :, source].reshape(2 * rows, width)
            product = jnp.dot(left_ref[term, slot], block, preferred_element_type=jnp.float32)
            moved.append(product.astype(jnp.bfloat16))
            where.append(target)
        for slot in range(capacity):
            target = where[slot]
            total[target] += jnp.dot(
                moved[slot],
                right_ref[term, jnp.minimum(target, blocks - 1)],
                preferred_element_type=jnp.float32,
            )


def stream_chunk(total, codes, left, vector, right):
    owners, _, blocks, rows, width = vector.shape
    capacity = left.shape[1]
    first = total is None
    spec_total = pl.BlockSpec((blocks + 1, rows, width), lambda s, c: (0, 0, 0))
    return pl.pallas_call(
        functools.partial(stream_kernel, first, capacity, blocks),
        out_shape=jax.ShapeDtypeStruct((blocks + 1, rows, width), jnp.float32),
        grid_spec=pltpu.PrefetchScalarGridSpec(
            num_scalar_prefetch=1,
            grid=(owners,),
            in_specs=[
                pl.BlockSpec((2, capacity, rows, width), lambda s, c: (s, 0, 0, 0)),
                pl.BlockSpec((1, 2, blocks, rows, width), lambda s, c: (s, 0, 0, 0, 0)),
                pl.BlockSpec((2, blocks, width, width), lambda s, c: (0, 0, 0, 0)),
            ]
            + ([] if first else [spec_total]),
            out_specs=spec_total,
        ),
        compiler_params=pltpu.CompilerParams(vmem_limit_bytes=32 * 2**20),
        cost_estimate=pl.CostEstimate(
            flops=owners * 2 * capacity * 2 * 2 * rows * width * width,
            bytes_accessed=left.size * 2 + vector.size * 2 + right.size * 2,
            transcendentals=0,
        ),
    )(codes, left, vector, right, *([] if first else [total]))


def per_device_streamed(wavefunction, left_operator, right_operator, target_owner, target_local):
    owners = lax.axis_size("sec")
    halves = lax.axis_size("term")
    me, half = lax.axis_index("sec"), lax.axis_index("term")
    terms, blocks, height, width = left_operator.shape
    rows = height // halves
    capacity = 2 * blocks // owners

    own_rows = lax.dynamic_slice_in_dim(wavefunction, half * rows, rows, 1)
    codes = slot_codes(target_owner, target_local, owners, capacity)
    sources = codes // (2 * blocks)

    moved_left = []
    for k in range(terms):
        pick = sources[k][:, None, :] * halves + jnp.arange(halves, dtype=jnp.int32)[None, :, None]
        pieces = left_operator[k].reshape(blocks * halves, rows, width)[pick.reshape(-1)]
        pieces = pieces.reshape(owners * halves, capacity, rows, width)
        moved_left.append(lax.all_to_all(pieces, BOTH, split_axis=0, concat_axis=0, tiled=True))
    all_codes = lax.all_gather(codes, BOTH, axis=0)
    my_codes = lax.dynamic_index_in_dim(all_codes, me, axis=3 - 1, keepdims=False)
    gathered = lax.all_gather(own_rows, BOTH, axis=0).reshape(owners, halves, blocks, rows, width)
    right = lax.all_gather(right_operator, "term", axis=1)

    def apply(vector):
        total = None
        for k in range(terms):
            total = stream_chunk(total, my_codes[:, k], moved_left[k], vector, right[k])
        return total[:blocks]

    sigma_rows = apply(gathered)
    wave = own_rows.astype(jnp.float32)
    cross, own = jnp.sum(wave * sigma_rows), jnp.sum(wave * wave)
    local = jnp.where(own > 0, cross / own, 0.0)
    about = jnp.sum(jnp.square(sigma_rows - local * wave))
    stats = lax.all_gather(jnp.stack([about, cross, own, local]), BOTH, axis=0)
    rayleigh = jnp.sum(stats[:, 1]) / jnp.sum(stats[:, 2])
    residual_sq = jnp.sum(stats[:, 0] + jnp.square(stats[:, 3] - rayleigh) * stats[:, 2])
    entries = blocks * owners * height * width
    factor = lax.rsqrt(residual_sq / entries + 1e-06)
    direction = ((sigma_rows - rayleigh * wave) * factor).astype(jnp.bfloat16)
    direction = lax.all_gather(direction, BOTH, axis=0).reshape(gathered.shape)
    sigma_two = apply(direction).astype(jnp.bfloat16)
    return (sigma_two, jnp.reshape(rayleigh, (1,)))


def per_device(wavefunction, *operands):
    gathered_bytes = lax.axis_size("sec") * wavefunction.size * wavefunction.dtype.itemsize
    if 2 * gathered_bytes > RING_BYTES:
        return per_device_streamed(wavefunction, *operands)
    return per_device_ring(wavefunction, *operands)


def solution(mesh):
    placed = (
        P(("rep", "sec"), None, None),
        P("term", ("rep", "sec"), None, None),
        P("term", ("rep", "sec"), None, None),
        P("term", ("rep", "sec"), None),
        P("term", ("rep", "sec")),
    )
    return jax.shard_map(
        per_device,
        mesh=mesh,
        in_specs=placed,
        out_specs=(P(("rep", "sec"), "term", None), P("rep")),
        check_vma=False,
    )
```

```python
import functools

import jax
import jax.numpy as jnp
from jax import lax
from jax.experimental import pallas as pl
from jax.experimental.pallas import tpu as pltpu
from jax.sharding import PartitionSpec as P

BOTH = ("sec", "term")
VMEM_LIMIT = 32 * 2**20
RING_BYTES = 24 * 2**20


def ring_order(owners):
    if owners % 2:
        return list(range(owners))
    return list(range(0, owners, 2)) + list(range(owners - 1, 0, -2))


def ring_place(owner, owners):
    if owners % 2:
        return owner
    return jnp.where(owner % 2 == 0, owner // 2, owners - 1 - owner // 2)


def ring_owner(place, owners):
    place = place % owners
    if owners % 2:
        return place
    return jnp.where(place < owners // 2, 2 * place, 2 * (owners - 1 - place) + 1)


def permute(value, owners, halves, target, flip=0):
    pairs = [
        (chip * halves + half, target(chip, half) * halves + (half ^ flip))
        for chip in range(owners)
        for half in range(halves)
    ]
    return lax.ppermute(value, BOTH, pairs)


def swap(value, owners, halves):
    return permute(value, owners, halves, lambda chip, half: chip, 1)


def exchange(value, owners, halves, mask):
    return permute(value, owners, halves, lambda chip, half: chip ^ mask)


def ring_send(value, owners, halves, shifts):
    ring = ring_order(owners)
    place = {chip: index for index, chip in enumerate(ring)}
    return permute(
        value, owners, halves, lambda chip, half: ring[(place[chip] + shifts[half]) % owners]
    )


def ring_gather(unit, owners, halves, half):
    units = {0: unit}
    reach = (owners - 1) // 2
    for step in range(1, reach + 1):
        units[step] = ring_send(units[step - 1], owners, halves, (1,) * halves)
        units[-step] = ring_send(units[1 - step], owners, halves, (-1,) * halves)
    if owners % 2 == 0:
        last = jnp.where(half == 0, units[reach], units[-reach])
        units[owners // 2] = ring_send(last, owners, halves, (1, -1))
    return units


def mask_gather(unit, owners, halves):
    units = {0: unit}
    step = owners // 2
    while step:
        for mask in list(units):
            units[mask | step] = exchange(units[mask], owners, halves, step)
        step //= 2
    return units


def doubled(value, count, axes, stride):
    step = 1
    total = lax.axis_size("sec") * lax.axis_size("term")
    while step < count:
        value = value + lax.ppermute(
            value, axes, [(d, d ^ (step * stride)) for d in range(total)]
        )
        step *= 2
    return value


def pack_kernel(capacity, blocks, terms, ids_ref, plan_ref, left_ref, other_ref, *refs):
    pieces, codes, seen = refs[:-2], refs[-2], refs[-1]
    owners = len(pieces)
    me, half = ids_ref[0], ids_ref[1]
    rows = other_ref.shape[2]
    start = pl.multiple_of(half * rows, rows)

    @pl.loop(0, owners)
    def _(owner):
        for index in range(2 * terms * capacity):
            codes[owner, index] = blocks

    for stream in range(2 * terms):

        @pl.loop(0, owners)
        def _(owner):
            seen[owner] = 0

        @pl.loop(0, blocks)
        def _(block):
            plan = plan_ref[stream, block]
            owner, target = lax.div(plan, blocks), lax.rem(plan, blocks)
            slot = seen[owner]
            seen[owner] = slot + 1
            codes[owner, stream * capacity + slot] = block * (2 * blocks) + target

    for mask, piece in enumerate(pieces):
        owner = me ^ mask
        for stream in range(2 * terms):

            @pl.loop(0, capacity, unroll=True)
            def _(slot):
                block = lax.div(codes[owner, stream * capacity + slot], 2 * blocks)
                if stream < terms:
                    value = left_ref[stream, block, pl.ds(start, rows), :]
                else:
                    value = other_ref[stream - terms, block]
                value = pltpu.roll(value.astype(jnp.float32), half * rows, 1)
                piece[stream, slot] = value.astype(jnp.bfloat16)


def pack(ids, plan, left, other, owners, capacity):
    terms, blocks, rows, width = other.shape
    scalars = pl.BlockSpec(memory_space=pltpu.SMEM)
    whole = pl.BlockSpec(memory_space=pltpu.VMEM)
    piece = jax.ShapeDtypeStruct((2 * terms, capacity, rows, width), jnp.bfloat16)
    *pieces, codes = pl.pallas_call(
        functools.partial(pack_kernel, capacity, blocks, terms),
        out_shape=[piece] * owners
        + [jax.ShapeDtypeStruct((owners, 2 * terms * capacity), jnp.int32)],
        in_specs=[scalars, scalars, whole, whole],
        out_specs=[whole] * owners + [scalars],
        scratch_shapes=[pltpu.SMEM((owners,), jnp.int32)],
        compiler_params=pltpu.CompilerParams(vmem_limit_bytes=VMEM_LIMIT),
    )(ids, plan, left, other)
    return pieces, codes


def add_products(piece, near, far, rights, total, code_of, blocks):
    streams, capacity = piece.shape[:2]
    terms = streams // 2
    for side in range(2):
        moved, where = [], []
        for stream in range(terms * side, terms * side + terms):
            for slot in range(capacity):
                code = code_of(stream * capacity + slot)
                source, target = lax.div(code, 2 * blocks), lax.rem(code, 2 * blocks)
                block = jnp.concatenate([near[source], far[source]], axis=0)
                product = jnp.dot(piece[stream, slot], block, preferred_element_type=jnp.float32)
                moved.append(product.astype(jnp.bfloat16))
                where.append((stream - terms * side, target))
        for value, (term, target) in zip(moved, where):
            total[target] += jnp.dot(
                value,
                rights[side][term, jnp.minimum(target, blocks - 1)],
                preferred_element_type=jnp.float32,
            )


def apply_kernel(sources, first, choices, last, blocks, ids_ref, codes_ref, *refs):
    refs = list(refs)
    lefts = [refs.pop(0) for _ in range(choices or sources)]
    vectors = [(refs.pop(0), refs.pop(0)) for _ in range(sources)]
    rights = refs.pop(0), refs.pop(0)
    total_in = None if first else refs.pop(0)
    out = refs.pop(0) if last else None
    total = refs.pop(0)
    chosen = refs.pop(0) if choices else None

    total[...] = jnp.zeros_like(total) if first else total_in[...]
    for index, (near, far) in enumerate(vectors):
        chip = ids_ref[2 * index]
        if choices:
            for choice, left in enumerate(lefts):

                @pl.when(ids_ref[2 * index + 1] == choice)
                def _():
                    chosen[...] = left[...]

            piece = chosen
        else:
            piece = lefts[index]
        add_products(piece, near, far, rights, total, lambda at: codes_ref[chip, at], blocks)
    if last:
        out[...] = total[:blocks].astype(out.dtype)


def apply_group(ids, codes, lefts, vectors, rights, total, choices, last):
    streams, capacity, rows, width = lefts[0].shape
    blocks = rights[0].shape[1]
    first = total is None
    arrays = list(lefts) + [unit for pair in vectors for unit in pair] + list(rights)
    if not first:
        arrays.append(total)
    scalars = pl.BlockSpec(memory_space=pltpu.SMEM)
    whole = pl.BlockSpec(memory_space=pltpu.VMEM)
    total_shape = (blocks + 1, rows, width)
    scratch = [pltpu.VMEM(lefts[0].shape, lefts[0].dtype)] if choices else []
    aliases = {}
    if last:
        out_shape = jax.ShapeDtypeStruct((blocks, rows, width), jnp.bfloat16)
        scratch = [pltpu.VMEM(total_shape, jnp.float32)] + scratch
    else:
        out_shape = jax.ShapeDtypeStruct(total_shape, jnp.float32)
        if not first:
            aliases = {len(arrays) + 1: 0}
    return pl.pallas_call(
        functools.partial(
            apply_kernel, len(vectors), first, len(lefts) if choices else 0, last, blocks
        ),
        out_shape=out_shape,
        in_specs=[scalars] * 2 + [whole] * len(arrays),
        out_specs=whole,
        scratch_shapes=scratch,
        input_output_aliases=aliases,
        compiler_params=pltpu.CompilerParams(vmem_limit_bytes=VMEM_LIMIT),
        cost_estimate=pl.CostEstimate(
            flops=len(vectors) * streams * capacity * 2 * 2 * rows * width * width,
            bytes_accessed=2 * len(vectors) * (streams * capacity + 2 * blocks) * rows * width,
            transcendentals=0,
        ),
    )(ids, codes, *arrays)


def stats_kernel(ids_ref, total_ref, wave_ref, stats_ref):
    blocks = wave_ref.shape[0]
    zero = jnp.zeros(wave_ref.shape[1:], jnp.float32)

    def sums(block, carry):
        cross, own = carry
        wave = wave_ref[block].astype(jnp.float32)
        return cross + wave * total_ref[block], own + wave * wave

    cross, own = lax.fori_loop(0, blocks, sums, (zero, zero), unroll=4)
    cross, own = jnp.sum(cross, keepdims=True), jnp.sum(own, keepdims=True)
    local = jnp.where(own > 0, cross / own, 0.0)

    def squares(block, carry):
        rest = total_ref[block] - local * wave_ref[block].astype(jnp.float32)
        return carry + rest * rest

    about = jnp.sum(lax.fori_loop(0, blocks, squares, zero, unroll=4), keepdims=True)
    lane = lax.broadcasted_iota(jnp.int32, stats_ref.shape, 1)
    row = lax.broadcasted_iota(jnp.int32, stats_ref.shape, 0)
    values = jnp.where(lane == 0, about, jnp.where(lane == 1, cross, jnp.where(lane == 2, own, local)))
    stats_ref[...] = jnp.where((row == ids_ref[2]) & (lane < 4), values, 0.0)


def direction_kernel(entries, total_ref, wave_ref, stats_ref, out_ref, rayleigh_ref):
    blocks = wave_ref.shape[0]
    stats = stats_ref[...]
    about, cross, own, local = (stats[:, lane : lane + 1] for lane in range(4))
    rayleigh = jnp.sum(cross, keepdims=True) / jnp.sum(own, keepdims=True)
    offset = local - rayleigh
    residual_sq = jnp.sum(about + offset * offset * own, keepdims=True)
    factor = lax.rsqrt(residual_sq / entries + 1e-06)
    rayleigh_ref[...] = rayleigh

    @pl.loop(0, blocks, unroll=4)
    def _(block):
        rest = total_ref[block] - rayleigh * wave_ref[block].astype(jnp.float32)
        out_ref[block] = (rest * factor).astype(jnp.bfloat16)


def new_direction(ids, total, wave, owners, halves, entries):
    devices = owners * halves
    scalars = pl.BlockSpec(memory_space=pltpu.SMEM)
    whole = pl.BlockSpec(memory_space=pltpu.VMEM)
    params = pltpu.CompilerParams(vmem_limit_bytes=VMEM_LIMIT)
    stats = pl.pallas_call(
        stats_kernel,
        out_shape=jax.ShapeDtypeStruct((devices, 128), jnp.float32),
        in_specs=[scalars, whole, whole],
        out_specs=whole,
        compiler_params=params,
    )(ids, total, wave)
    stats = doubled(stats, devices, BOTH, 1)
    return pl.pallas_call(
        functools.partial(direction_kernel, entries),
        out_shape=(
            jax.ShapeDtypeStruct(wave.shape, jnp.bfloat16),
            jax.ShapeDtypeStruct((1, 1), jnp.float32),
        ),
        in_specs=[whole] * 3,
        out_specs=(whole, whole),
        compiler_params=params,
    )(total, wave, stats)


def per_device_ring(wavefunction, left_operator, right_operator, target_owner, target_local):
    owners, halves = lax.axis_size("sec"), lax.axis_size("term")
    me, half = lax.axis_index("sec"), lax.axis_index("term")
    terms, blocks, height, width = left_operator.shape
    rows = height // halves
    capacity = 2 * blocks // owners
    place = ring_place(me, owners)
    ids = jnp.stack([me, half, me * halves + half]).astype(jnp.int32)

    own_rows = lax.dynamic_slice_in_dim(wavefunction, half * rows, rows, 1)
    other_rows = lax.dynamic_slice_in_dim(wavefunction, (1 - half) * rows, rows, 1)
    near = mask_gather(own_rows, owners, halves)
    far = {m: swap(unit, owners, halves) if m else other_rows for m, unit in near.items()}

    plan = target_owner[:, :, 0] * blocks + target_local
    plan = jnp.concatenate([plan, swap(plan, owners, halves)], axis=0)
    other_left = swap(
        lax.dynamic_slice_in_dim(left_operator, (1 - half) * rows, rows, 2), owners, halves
    )
    pieces, codes = pack(ids, plan, left_operator, other_left, owners, capacity)
    lefts = [exchange(piece, owners, halves, m) if m else piece for m, piece in enumerate(pieces)]
    codes = jnp.where(jnp.arange(owners)[:, None] == me, codes.reshape(1, -1), 0)
    codes = doubled(codes, owners, BOTH, halves).reshape(owners, owners, -1)
    codes = lax.dynamic_index_in_dim(codes, me, axis=1, keepdims=False)
    rights = (right_operator, swap(right_operator, owners, halves))

    order = [m for pair in zip(range(owners // 2), range(owners // 2, owners)) for m in pair]
    total = None
    for m in order:
        total = apply_group(
            jnp.stack([me ^ m, 0]).astype(jnp.int32),
            codes,
            [lefts[m]],
            [(near[m], far[m])],
            rights,
            total,
            False,
            False,
        )

    entries = blocks * owners * height * width
    direction, rayleigh = new_direction(ids, total, own_rows, owners, halves, entries)
    near = ring_gather(direction, owners, halves, half)
    far = {s: swap(unit, owners, halves) for s, unit in near.items()}
    reach = (owners - 1) // 2
    groups = [[0]] + [[step, -step] for step in range(1, reach + 1)]
    if owners % 2 == 0:
        groups.append([owners // 2])
    total = None
    for group in groups:
        chips = [ring_owner(place - s, owners) for s in group]
        total = apply_group(
            jnp.stack([value for chip in chips for value in (chip, chip ^ me)]).astype(jnp.int32),
            codes,
            lefts,
            [(near[s], far[s]) for s in group],
            rights,
            total,
            True,
            group is groups[-1],
        )
    return (total, rayleigh[0])


def slot_codes(target_owner, target_local, owners, capacity):
    terms, blocks = target_local.shape
    owner = target_owner[:, :, 0]
    place = jnp.arange(blocks, dtype=jnp.int32)
    same = (owner[:, :, None] == owner[:, None, :]) & (place[None, :] < place[:, None])[None]
    position = jnp.sum(same.astype(jnp.int32), axis=2)
    hit = (
        owner[:, None, None, :] == jnp.arange(owners, dtype=jnp.int32)[None, :, None, None]
    ) & (position[:, None, None, :] == jnp.arange(capacity, dtype=jnp.int32)[None, None, :, None])
    code = place[None, :] * (2 * blocks) + target_local - blocks
    return blocks + jnp.sum(jnp.where(hit, code[:, None, None, :], 0), axis=3)


def stream_kernel(first, capacity, blocks, code_ref, left_ref, vector_ref, right_ref, *rest):
    total_in, total = (None, rest[0]) if first else rest
    step = pl.program_id(0)
    rows, width = left_ref.shape[2:]

    @pl.when(step == 0)
    def _():
        total[...] = jnp.zeros_like(total) if first else total_in[...]

    for term in range(2):
        moved, where = [], []
        for slot in range(capacity):
            code = code_ref[2 * step + term, slot]
            source, target = lax.div(code, 2 * blocks), lax.rem(code, 2 * blocks)
            block = vector_ref[0, :, source].reshape(2 * rows, width)
            product = jnp.dot(left_ref[term, slot], block, preferred_element_type=jnp.float32)
            moved.append(product.astype(jnp.bfloat16))
            where.append(target)
        for slot in range(capacity):
            target = where[slot]
            total[target] += jnp.dot(
                moved[slot],
                right_ref[term, jnp.minimum(target, blocks - 1)],
                preferred_element_type=jnp.float32,
            )


def stream_chunk(total, codes, left, vector, right):
    owners, _, blocks, rows, width = vector.shape
    capacity = left.shape[1]
    first = total is None
    spec_total = pl.BlockSpec((blocks + 1, rows, width), lambda s, c: (0, 0, 0))
    return pl.pallas_call(
        functools.partial(stream_kernel, first, capacity, blocks),
        out_shape=jax.ShapeDtypeStruct((blocks + 1, rows, width), jnp.float32),
        grid_spec=pltpu.PrefetchScalarGridSpec(
            num_scalar_prefetch=1,
            grid=(owners,),
            in_specs=[
                pl.BlockSpec((2, capacity, rows, width), lambda s, c: (s, 0, 0, 0)),
                pl.BlockSpec((1, 2, blocks, rows, width), lambda s, c: (s, 0, 0, 0, 0)),
                pl.BlockSpec((2, blocks, width, width), lambda s, c: (0, 0, 0, 0)),
            ]
            + ([] if first else [spec_total]),
            out_specs=spec_total,
        ),
        compiler_params=pltpu.CompilerParams(vmem_limit_bytes=32 * 2**20),
        cost_estimate=pl.CostEstimate(
            flops=owners * 2 * capacity * 2 * 2 * rows * width * width,
            bytes_accessed=left.size * 2 + vector.size * 2 + right.size * 2,
            transcendentals=0,
        ),
    )(codes, left, vector, right, *([] if first else [total]))


def per_device_streamed(wavefunction, left_operator, right_operator, target_owner, target_local):
    owners = lax.axis_size("sec")
    halves = lax.axis_size("term")
    me, half = lax.axis_index("sec"), lax.axis_index("term")
    terms, blocks, height, width = left_operator.shape
    rows = height // halves
    capacity = 2 * blocks // owners

    own_rows = lax.dynamic_slice_in_dim(wavefunction, half * rows, rows, 1)
    codes = slot_codes(target_owner, target_local, owners, capacity)
    sources = codes // (2 * blocks)

    moved_left = []
    for k in range(terms):
        pick = sources[k][:, None, :] * halves + jnp.arange(halves, dtype=jnp.int32)[None, :, None]
        pieces = left_operator[k].reshape(blocks * halves, rows, width)[pick.reshape(-1)]
        pieces = pieces.reshape(owners * halves, capacity, rows, width)
        moved_left.append(lax.all_to_all(pieces, BOTH, split_axis=0, concat_axis=0, tiled=True))
    all_codes = lax.all_gather(codes, BOTH, axis=0)
    my_codes = lax.dynamic_index_in_dim(all_codes, me, axis=3 - 1, keepdims=False)
    gathered = lax.all_gather(own_rows, BOTH, axis=0).reshape(owners, halves, blocks, rows, width)
    right = lax.all_gather(right_operator, "term", axis=1)

    def apply(vector):
        total = None
        for k in range(terms):
            total = stream_chunk(total, my_codes[:, k], moved_left[k], vector, right[k])
        return total[:blocks]

    sigma_rows = apply(gathered)
    wave = own_rows.astype(jnp.float32)
    cross, own = jnp.sum(wave * sigma_rows), jnp.sum(wave * wave)
    local = jnp.where(own > 0, cross / own, 0.0)
    about = jnp.sum(jnp.square(sigma_rows - local * wave))
    stats = lax.all_gather(jnp.stack([about, cross, own, local]), BOTH, axis=0)
    rayleigh = jnp.sum(stats[:, 1]) / jnp.sum(stats[:, 2])
    residual_sq = jnp.sum(stats[:, 0] + jnp.square(stats[:, 3] - rayleigh) * stats[:, 2])
    entries = blocks * owners * height * width
    factor = lax.rsqrt(residual_sq / entries + 1e-06)
    direction = ((sigma_rows - rayleigh * wave) * factor).astype(jnp.bfloat16)
    direction = lax.all_gather(direction, BOTH, axis=0).reshape(gathered.shape)
    sigma_two = apply(direction).astype(jnp.bfloat16)
    return (sigma_two, jnp.reshape(rayleigh, (1,)))


def per_device(wavefunction, *operands):
    gathered_bytes = lax.axis_size("sec") * wavefunction.size * wavefunction.dtype.itemsize
    if 2 * gathered_bytes > RING_BYTES:
        return per_device_streamed(wavefunction, *operands)
    return per_device_ring(wavefunction, *operands)


def solution(mesh):
    placed = (
        P(("rep", "sec"), None, None),
        P("term", ("rep", "sec"), None, None),
        P("term", ("rep", "sec"), None, None),
        P("term", ("rep", "sec"), None),
        P("term", ("rep", "sec")),
    )
    return jax.shard_map(
        per_device,
        mesh=mesh,
        in_specs=placed,
        out_specs=(P(("rep", "sec"), "term", None), P("rep")),
        check_vma=False,
    )
```

```python
import functools

import jax
import jax.numpy as jnp
from jax import lax
from jax.experimental import pallas as pl
from jax.experimental.pallas import tpu as pltpu
from jax.sharding import PartitionSpec as P

BOTH = ("sec", "term")
VMEM_LIMIT = 20 * 2**20
PART = 16
RING_BYTES = 24 * 2**20


def ring_order(owners):
    if owners % 2:
        return list(range(owners))
    return list(range(0, owners, 2)) + list(range(owners - 1, 0, -2))


def ring_place(owner, owners):
    if owners % 2:
        return owner
    return jnp.where(owner % 2 == 0, owner // 2, owners - 1 - owner // 2)


def ring_owner(place, owners):
    place = place % owners
    if owners % 2:
        return place
    return jnp.where(place < owners // 2, 2 * place, 2 * (owners - 1 - place) + 1)


def permute(value, owners, halves, target, flip=0):
    pairs = [
        (chip * halves + half, target(chip, half) * halves + (half ^ flip))
        for chip in range(owners)
        for half in range(halves)
    ]
    return lax.ppermute(value, BOTH, pairs)


def swap(value, owners, halves):
    return permute(value, owners, halves, lambda chip, half: chip, 1)


def exchange(value, owners, halves, mask):
    return permute(value, owners, halves, lambda chip, half: chip ^ mask)


def ring_send(value, owners, halves, shifts):
    ring = ring_order(owners)
    place = {chip: index for index, chip in enumerate(ring)}
    return permute(
        value, owners, halves, lambda chip, half: ring[(place[chip] + shifts[half]) % owners]
    )


def select_kernel(half_ref, lower_ref, upper_ref, out_ref, sem):
    for half, source in enumerate((lower_ref, upper_ref)):

        @pl.when(half_ref[0] == half)
        def _():
            copy = pltpu.make_async_copy(source, out_ref, sem)
            copy.start()
            copy.wait()


def select_half(half, lower, upper):
    anywhere = pl.BlockSpec(memory_space=pl.ANY)
    return pl.pallas_call(
        select_kernel,
        out_shape=jax.ShapeDtypeStruct(lower.shape, lower.dtype),
        in_specs=[pl.BlockSpec(memory_space=pltpu.SMEM), anywhere, anywhere],
        out_specs=anywhere,
        scratch_shapes=[pltpu.SemaphoreType.DMA],
        cost_estimate=busy(0.8),
    )(jnp.reshape(half, (1,)).astype(jnp.int32), lower, upper)


def ring_gather(unit, owners, halves, half):
    units = {0: unit}
    reach = (owners - 1) // 2
    for step in range(1, reach + 1):
        units[step] = ring_send(units[step - 1], owners, halves, (1,) * halves)
        units[-step] = ring_send(units[1 - step], owners, halves, (-1,) * halves)
    if owners % 2 == 0:
        last = select_half(half, units[reach], units[-reach])
        units[owners // 2] = ring_send(last, owners, halves, (1, -1))
    return units


def after_kernel(*refs):
    del refs


def after(value, *others):
    anywhere = pl.BlockSpec(memory_space=pl.ANY)
    return pl.pallas_call(
        after_kernel,
        out_shape=jax.ShapeDtypeStruct(value.shape, value.dtype),
        in_specs=[anywhere] * (1 + len(others)),
        out_specs=anywhere,
        input_output_aliases={0: 0},
        cost_estimate=busy(0.3),
    )(value, *others)


def mask_gather(unit, lefts, owners, halves):
    units = {0: unit}
    step = owners // 2
    masks = []
    while step:
        masks.append(step)
        units[step] = exchange(unit, owners, halves, step)
        step //= 2
    for mask in masks[:-1]:
        units[mask] = after(units[mask], lefts[mask])
    for step in masks[1:]:
        for mask in [m for m in units if m >= 2 * step and m % (2 * step) == 0]:
            units[mask | step] = exchange(units[mask], owners, halves, step)
    return units


def doubled(value, count, axes, stride):
    step = 1
    total = lax.axis_size("sec") * lax.axis_size("term")
    while step < count:
        value = value + lax.ppermute(
            value, axes, [(d, d ^ (step * stride)) for d in range(total)]
        )
        step *= 2
    return value


def pack_kernel(order, capacity, blocks, terms, ids_ref, plan_ref, other_plan_ref, *refs):
    left_ref, other_ref, *pieces, codes, seen, built, sems = refs
    owners = len(order)
    me, half = ids_ref[0], ids_ref[1]
    rows, width = other_ref.shape[2:]
    start = pl.multiple_of(half * rows, rows)
    parts = rows // PART

    @pl.loop(0, owners)
    def _(owner):
        for index in range(2 * terms * capacity):
            codes[0, owner, index] = 0
            codes[1, owner, index] = blocks

    for stream in range(2 * terms):
        plan = plan_ref if stream < terms else other_plan_ref

        @pl.loop(0, owners)
        def _(owner):
            seen[owner] = 0

        @pl.loop(0, blocks, unroll=4)
        def _(block):
            owner = plan[0, stream % terms, block]
            slot = seen[owner]
            seen[owner] = slot + 1
            codes[0, owner, stream * capacity + slot] = block
            codes[1, owner, stream * capacity + slot] = plan[1, stream % terms, block]

    lane = lax.broadcasted_iota(jnp.int32, (PART, width), 1)
    row = lax.broadcasted_iota(jnp.int32, (PART, width), 0)
    copies = []
    for mask in order:
        owner = me ^ mask
        labels = jnp.zeros((PART, width), jnp.int32)
        for stream in range(2 * terms):
            for slot in range(capacity):
                at = stream * capacity + slot
                block = codes[0, owner, at]
                if stream < terms:
                    value = left_ref[stream, block, pl.ds(start, rows), :]
                else:
                    value = other_ref[stream - terms, block]
                value = pltpu.roll(value.astype(jnp.float32), half * rows, 1)
                built[mask, at * parts : (at + 1) * parts] = value.astype(jnp.bfloat16).reshape(
                    parts, PART, width
                )
                label = jnp.where(row == 0, block, codes[1, owner, at])
                labels = jnp.where(lane == at, label, labels)
        built[mask, 2 * terms * capacity * parts] = labels.astype(jnp.float32).astype(jnp.bfloat16)
        copies.append(pltpu.make_async_copy(built.at[mask], pieces[mask], sems.at[mask]))
        copies[-1].start()
    for copy in copies:
        copy.wait()


def pack(ids, plan, other_plan, left, other, order, capacity):
    terms, blocks, rows, width = other.shape
    owners = len(order)
    scalars = pl.BlockSpec(memory_space=pltpu.SMEM)
    whole = pl.BlockSpec(memory_space=pltpu.VMEM)
    anywhere = pl.BlockSpec(memory_space=pl.ANY)
    shape = (2 * terms * capacity * rows // PART + 1, PART, width)
    return pl.pallas_call(
        functools.partial(pack_kernel, order, capacity, blocks, terms),
        out_shape=[jax.ShapeDtypeStruct(shape, jnp.bfloat16)] * owners,
        in_specs=[scalars] * 3 + [whole, whole],
        out_specs=[anywhere] * owners,
        scratch_shapes=[
            pltpu.SMEM((2, owners, 2 * terms * capacity), jnp.int32),
            pltpu.SMEM((owners,), jnp.int32),
            pltpu.VMEM((owners,) + shape, jnp.bfloat16),
            pltpu.SemaphoreType.DMA((owners,)),
        ],
        compiler_params=pltpu.CompilerParams(vmem_limit_bytes=VMEM_LIMIT),
        cost_estimate=busy(5.0),
    )(ids, plan, other_plan, left, other)


def busy(microseconds):
    return pl.CostEstimate(
        flops=int(1.15e9 * microseconds), bytes_accessed=0, transcendentals=0
    )


def add_products(piece, labels, near, far, rights, total, streams, capacity):
    terms = streams // 2
    blocks, rows, width = near.shape
    parts = rows // PART
    for side in range(2):
        moved, where = [], []
        for stream in range(terms * side, terms * side + terms):
            for slot in range(capacity):
                at = stream * capacity + slot
                source, target = labels[0, at], labels[1, at]
                block = jnp.concatenate([near[source], far[source]], axis=0)
                left = piece[at * parts : (at + 1) * parts].reshape(rows, width)
                product = jnp.dot(left, block, preferred_element_type=jnp.float32)
                moved.append(product.astype(jnp.bfloat16))
                where.append((stream - terms * side, target))
        for value, (term, target) in zip(moved, where):
            total[target] += jnp.dot(
                value,
                rights[side][term, jnp.minimum(target, blocks - 1)],
                preferred_element_type=jnp.float32,
            )


def apply_kernel(sources, first, choices, last, streams, capacity, ids_ref, *refs):
    refs = list(refs)
    lefts = [refs.pop(0) for _ in range(choices or sources)]
    vectors = [(refs.pop(0), refs.pop(0)) for _ in range(sources)]
    rights = refs.pop(0), refs.pop(0)
    total_in = None if first else refs.pop(0)
    out = refs.pop(0) if last else None
    total = refs.pop(0)
    spread_labels, labels, label_sems = refs.pop(0), refs.pop(0), refs.pop(0)
    blocks = vectors[0][0].shape[0]

    if choices:
        chosen, chosen_sems = refs.pop(0), refs.pop(0)
        for index in range(sources):
            for choice, left in enumerate(lefts):

                @pl.when(ids_ref[index] == choice)
                def _():
                    pltpu.make_async_copy(left, chosen.at[index], chosen_sems.at[index]).start()

    total[...] = jnp.zeros_like(total) if first else total_in[...]
    pieces = []
    for index in range(sources):
        if choices:
            pltpu.make_async_copy(lefts[0], chosen.at[index], chosen_sems.at[index]).wait()
            piece = chosen.at[index]
        else:
            piece = lefts[index]
        pieces.append(piece)
        values = piece[piece.shape[0] - 1].astype(jnp.float32).astype(jnp.int32)
        spread_labels[index] = values[:8]
        pltpu.make_async_copy(
            spread_labels.at[index], labels.at[index], label_sems.at[index]
        ).start()
    for index, (near, far) in enumerate(vectors):
        pltpu.make_async_copy(
            spread_labels.at[index], labels.at[index], label_sems.at[index]
        ).wait()
        add_products(
            pieces[index], labels.at[index], near, far, rights, total, streams, capacity
        )
    if last:
        out[...] = total[:blocks].astype(out.dtype)


def apply_group(ids, lefts, vectors, rights, total, choices, last):
    blocks, rows, width = vectors[0][0].shape
    streams = 2 * rights[0].shape[0]
    capacity = (lefts[0].shape[0] - 1) * PART // (streams * rows)
    sources = len(vectors)
    first = total is None
    arrays = list(lefts) + [unit for pair in vectors for unit in pair] + list(rights)
    if not first:
        arrays.append(total)
    whole = pl.BlockSpec(memory_space=pltpu.VMEM)
    total_shape = (blocks + 1, rows, width)
    scratch = [
        pltpu.VMEM((sources, 8, width), jnp.int32),
        pltpu.SMEM((sources, 8, width), jnp.int32),
        pltpu.SemaphoreType.DMA((sources,)),
    ]
    specs = [whole] * len(arrays)
    if choices:
        scratch += [
            pltpu.VMEM((sources,) + lefts[0].shape, lefts[0].dtype),
            pltpu.SemaphoreType.DMA((sources,)),
        ]
        specs[: len(lefts)] = [pl.BlockSpec(memory_space=pl.ANY)] * len(lefts)
    aliases = {}
    if last:
        out_shape = jax.ShapeDtypeStruct((blocks, rows, width), jnp.bfloat16)
        scratch = [pltpu.VMEM(total_shape, jnp.float32)] + scratch
    else:
        out_shape = jax.ShapeDtypeStruct(total_shape, jnp.float32)
        if not first:
            aliases = {len(arrays): 0}
    return pl.pallas_call(
        functools.partial(
            apply_kernel, sources, first, len(lefts) if choices else 0, last, streams, capacity
        ),
        out_shape=out_shape,
        in_specs=[pl.BlockSpec(memory_space=pltpu.SMEM)] + specs,
        out_specs=whole,
        scratch_shapes=scratch,
        input_output_aliases=aliases,
        compiler_params=pltpu.CompilerParams(vmem_limit_bytes=VMEM_LIMIT),
        cost_estimate=busy(0.7 + 1.4 * sources),
    )(ids, *arrays)


def stats_kernel(ids_ref, total_ref, wave_ref, stats_ref):
    blocks = wave_ref.shape[0]
    zero = jnp.zeros(wave_ref.shape[1:], jnp.float32)

    def sums(block, carry):
        cross, own = carry
        wave = wave_ref[block].astype(jnp.float32)
        return cross + wave * total_ref[block], own + wave * wave

    cross, own = lax.fori_loop(0, blocks, sums, (zero, zero), unroll=4)
    cross, own = jnp.sum(cross, keepdims=True), jnp.sum(own, keepdims=True)
    local = jnp.where(own > 0, cross / own, 0.0)

    def squares(block, carry):
        rest = total_ref[block] - local * wave_ref[block].astype(jnp.float32)
        return carry + rest * rest

    about = jnp.sum(lax.fori_loop(0, blocks, squares, zero, unroll=4), keepdims=True)
    lane = lax.broadcasted_iota(jnp.int32, stats_ref.shape, 1)
    row = lax.broadcasted_iota(jnp.int32, stats_ref.shape, 0)
    values = jnp.where(lane == 0, about, jnp.where(lane == 1, cross, jnp.where(lane == 2, own, local)))
    stats_ref[...] = jnp.where((row == ids_ref[2]) & (lane < 4), values, 0.0)


def direction_kernel(entries, total_ref, wave_ref, stats_ref, out_ref, rayleigh_ref):
    blocks = wave_ref.shape[0]
    stats = stats_ref[...]
    about, cross, own, local = (stats[:, lane : lane + 1] for lane in range(4))
    rayleigh = jnp.sum(cross, keepdims=True) / jnp.sum(own, keepdims=True)
    offset = local - rayleigh
    residual_sq = jnp.sum(about + offset * offset * own, keepdims=True)
    factor = lax.rsqrt(residual_sq / entries + 1e-06)
    rayleigh_ref[...] = rayleigh

    @pl.loop(0, blocks, unroll=4)
    def _(block):
        rest = total_ref[block] - rayleigh * wave_ref[block].astype(jnp.float32)
        out_ref[block] = (rest * factor).astype(jnp.bfloat16)


def new_direction(ids, total, wave, owners, halves, entries):
    devices = owners * halves
    scalars = pl.BlockSpec(memory_space=pltpu.SMEM)
    whole = pl.BlockSpec(memory_space=pltpu.VMEM)
    params = pltpu.CompilerParams(vmem_limit_bytes=VMEM_LIMIT)
    stats = pl.pallas_call(
        stats_kernel,
        out_shape=jax.ShapeDtypeStruct((devices, 128), jnp.float32),
        in_specs=[scalars, whole, whole],
        out_specs=whole,
        compiler_params=params,
    )(ids, total, wave)
    stats = doubled(stats, devices, BOTH, 1)
    return pl.pallas_call(
        functools.partial(direction_kernel, entries),
        out_shape=(
            jax.ShapeDtypeStruct(wave.shape, jnp.bfloat16),
            jax.ShapeDtypeStruct((1, 1), jnp.float32),
        ),
        in_specs=[whole] * 3,
        out_specs=(whole, whole),
        compiler_params=params,
    )(total, wave, stats)


def per_device_ring(wavefunction, left_operator, right_operator, target_owner, target_local):
    owners, halves = lax.axis_size("sec"), lax.axis_size("term")
    me, half = lax.axis_index("sec"), lax.axis_index("term")
    terms, blocks, height, width = left_operator.shape
    rows = height // halves
    capacity = 2 * blocks // owners
    place = ring_place(me, owners)
    ids = jnp.stack([me, half, me * halves + half]).astype(jnp.int32)

    own_rows = lax.dynamic_slice_in_dim(wavefunction, half * rows, rows, 1)
    other_rows = lax.dynamic_slice_in_dim(wavefunction, (1 - half) * rows, rows, 1)
    plan = jnp.stack([target_owner[:, :, 0], target_local])
    other_left = swap(
        lax.dynamic_slice_in_dim(left_operator, (1 - half) * rows, rows, 2), owners, halves
    )
    order = [m for pair in zip(range(owners // 2), range(owners // 2, owners)) for m in pair]
    order = order[:-2] + order[-1:] + order[-2:-1]
    pieces = pack(
        ids,
        plan,
        swap(plan, owners, halves),
        left_operator,
        other_left,
        order[1:] + order[:1],
        capacity,
    )
    lefts = [exchange(piece, owners, halves, m) if m else piece for m, piece in enumerate(pieces)]
    rights = (right_operator, swap(right_operator, owners, halves))
    near = mask_gather(own_rows, lefts, owners, halves)
    far = {m: swap(unit, owners, halves) if m else other_rows for m, unit in near.items()}

    total = None
    no_choice = jnp.zeros((1,), jnp.int32)
    for m in order:
        total = apply_group(
            no_choice, [lefts[m]], [(near[m], far[m])], rights, total, False, False
        )

    entries = blocks * owners * height * width
    direction, rayleigh = new_direction(ids, total, own_rows, owners, halves, entries)
    near = ring_gather(direction, owners, halves, half)
    far = {s: swap(unit, owners, halves) for s, unit in near.items()}
    reach = (owners - 1) // 2
    groups = [[0]] + [[step, -step] for step in range(1, reach + 1)]
    if owners % 2 == 0:
        groups.append([owners // 2])
    total = None
    for group in groups:
        choice = jnp.stack([ring_owner(place - s, owners) ^ me for s in group])
        total = apply_group(
            choice.astype(jnp.int32),
            lefts,
            [(near[s], far[s]) for s in group],
            rights,
            total,
            True,
            group is groups[-1],
        )
    return (total, rayleigh[0])


def slot_codes(target_owner, target_local, owners, capacity):
    terms, blocks = target_local.shape
    owner = target_owner[:, :, 0]
    place = jnp.arange(blocks, dtype=jnp.int32)
    same = (owner[:, :, None] == owner[:, None, :]) & (place[None, :] < place[:, None])[None]
    position = jnp.sum(same.astype(jnp.int32), axis=2)
    hit = (
        owner[:, None, None, :] == jnp.arange(owners, dtype=jnp.int32)[None, :, None, None]
    ) & (position[:, None, None, :] == jnp.arange(capacity, dtype=jnp.int32)[None, None, :, None])
    code = place[None, :] * (2 * blocks) + target_local - blocks
    return blocks + jnp.sum(jnp.where(hit, code[:, None, None, :], 0), axis=3)


def stream_kernel(first, capacity, blocks, code_ref, left_ref, vector_ref, right_ref, *rest):
    total_in, total = (None, rest[0]) if first else rest
    step = pl.program_id(0)
    rows, width = left_ref.shape[2:]

    @pl.when(step == 0)
    def _():
        total[...] = jnp.zeros_like(total) if first else total_in[...]

    for term in range(2):
        moved, where = [], []
        for slot in range(capacity):
            code = code_ref[2 * step + term, slot]
            source, target = lax.div(code, 2 * blocks), lax.rem(code, 2 * blocks)
            block = vector_ref[0, :, source].reshape(2 * rows, width)
            product = jnp.dot(left_ref[term, slot], block, preferred_element_type=jnp.float32)
            moved.append(product.astype(jnp.bfloat16))
            where.append(target)
        for slot in range(capacity):
            target = where[slot]
            total[target] += jnp.dot(
                moved[slot],
                right_ref[term, jnp.minimum(target, blocks - 1)],
                preferred_element_type=jnp.float32,
            )


def stream_chunk(total, codes, left, vector, right):
    owners, _, blocks, rows, width = vector.shape
    capacity = left.shape[1]
    first = total is None
    spec_total = pl.BlockSpec((blocks + 1, rows, width), lambda s, c: (0, 0, 0))
    return pl.pallas_call(
        functools.partial(stream_kernel, first, capacity, blocks),
        out_shape=jax.ShapeDtypeStruct((blocks + 1, rows, width), jnp.float32),
        grid_spec=pltpu.PrefetchScalarGridSpec(
            num_scalar_prefetch=1,
            grid=(owners,),
            in_specs=[
                pl.BlockSpec((2, capacity, rows, width), lambda s, c: (s, 0, 0, 0)),
                pl.BlockSpec((1, 2, blocks, rows, width), lambda s, c: (s, 0, 0, 0, 0)),
                pl.BlockSpec((2, blocks, width, width), lambda s, c: (0, 0, 0, 0)),
            ]
            + ([] if first else [spec_total]),
            out_specs=spec_total,
        ),
        compiler_params=pltpu.CompilerParams(vmem_limit_bytes=32 * 2**20),
        cost_estimate=pl.CostEstimate(
            flops=owners * 2 * capacity * 2 * 2 * rows * width * width,
            bytes_accessed=left.size * 2 + vector.size * 2 + right.size * 2,
            transcendentals=0,
        ),
    )(codes, left, vector, right, *([] if first else [total]))


def per_device_streamed(wavefunction, left_operator, right_operator, target_owner, target_local):
    owners = lax.axis_size("sec")
    halves = lax.axis_size("term")
    me, half = lax.axis_index("sec"), lax.axis_index("term")
    terms, blocks, height, width = left_operator.shape
    rows = height // halves
    capacity = 2 * blocks // owners

    own_rows = lax.dynamic_slice_in_dim(wavefunction, half * rows, rows, 1)
    codes = slot_codes(target_owner, target_local, owners, capacity)
    sources = codes // (2 * blocks)

    moved_left = []
    for k in range(terms):
        pick = sources[k][:, None, :] * halves + jnp.arange(halves, dtype=jnp.int32)[None, :, None]
        pieces = left_operator[k].reshape(blocks * halves, rows, width)[pick.reshape(-1)]
        pieces = pieces.reshape(owners * halves, capacity, rows, width)
        moved_left.append(lax.all_to_all(pieces, BOTH, split_axis=0, concat_axis=0, tiled=True))
    all_codes = lax.all_gather(codes, BOTH, axis=0)
    my_codes = lax.dynamic_index_in_dim(all_codes, me, axis=3 - 1, keepdims=False)
    gathered = lax.all_gather(own_rows, BOTH, axis=0).reshape(owners, halves, blocks, rows, width)
    right = lax.all_gather(right_operator, "term", axis=1)

    def apply(vector):
        total = None
        for k in range(terms):
            total = stream_chunk(total, my_codes[:, k], moved_left[k], vector, right[k])
        return total[:blocks]

    sigma_rows = apply(gathered)
    wave = own_rows.astype(jnp.float32)
    cross, own = jnp.sum(wave * sigma_rows), jnp.sum(wave * wave)
    local = jnp.where(own > 0, cross / own, 0.0)
    about = jnp.sum(jnp.square(sigma_rows - local * wave))
    stats = lax.all_gather(jnp.stack([about, cross, own, local]), BOTH, axis=0)
    rayleigh = jnp.sum(stats[:, 1]) / jnp.sum(stats[:, 2])
    residual_sq = jnp.sum(stats[:, 0] + jnp.square(stats[:, 3] - rayleigh) * stats[:, 2])
    entries = blocks * owners * height * width
    factor = lax.rsqrt(residual_sq / entries + 1e-06)
    direction = ((sigma_rows - rayleigh * wave) * factor).astype(jnp.bfloat16)
    direction = lax.all_gather(direction, BOTH, axis=0).reshape(gathered.shape)
    sigma_two = apply(direction).astype(jnp.bfloat16)
    return (sigma_two, jnp.reshape(rayleigh, (1,)))


def per_device(wavefunction, *operands):
    gathered_bytes = lax.axis_size("sec") * wavefunction.size * wavefunction.dtype.itemsize
    if 2 * gathered_bytes > RING_BYTES:
        return per_device_streamed(wavefunction, *operands)
    return per_device_ring(wavefunction, *operands)


def solution(mesh):
    placed = (
        P(("rep", "sec"), None, None),
        P("term", ("rep", "sec"), None, None),
        P("term", ("rep", "sec"), None, None),
        P("term", ("rep", "sec"), None),
        P("term", ("rep", "sec")),
    )
    return jax.shard_map(
        per_device,
        mesh=mesh,
        in_specs=placed,
        out_specs=(P(("rep", "sec"), "term", None), P("rep")),
        check_vma=False,
    )
```

```python
import functools

import jax
import jax.numpy as jnp
from jax import lax
from jax.experimental import pallas as pl
from jax.experimental.pallas import tpu as pltpu
from jax.sharding import PartitionSpec as P

BOTH = ("sec", "term")
VMEM_LIMIT = 20 * 2**20
PART = 16
RING_BYTES = 24 * 2**20


def ring_order(owners):
    if owners % 2:
        return list(range(owners))
    return list(range(0, owners, 2)) + list(range(owners - 1, 0, -2))


def ring_place(owner, owners):
    if owners % 2:
        return owner
    return jnp.where(owner % 2 == 0, owner // 2, owners - 1 - owner // 2)


def ring_owner(place, owners):
    place = place % owners
    if owners % 2:
        return place
    return jnp.where(place < owners // 2, 2 * place, 2 * (owners - 1 - place) + 1)


def permute(value, owners, halves, target, flip=0):
    pairs = [
        (chip * halves + half, target(chip, half) * halves + (half ^ flip))
        for chip in range(owners)
        for half in range(halves)
    ]
    return lax.ppermute(value, BOTH, pairs)


def swap(value, owners, halves):
    return permute(value, owners, halves, lambda chip, half: chip, 1)


def exchange(value, owners, halves, mask):
    return permute(value, owners, halves, lambda chip, half: chip ^ mask)


def ring_send(value, owners, halves, shifts):
    ring = ring_order(owners)
    place = {chip: index for index, chip in enumerate(ring)}
    return permute(
        value, owners, halves, lambda chip, half: ring[(place[chip] + shifts[half]) % owners]
    )


def select_kernel(half_ref, lower_ref, upper_ref, *rest):
    out_ref = rest[-1]
    out_ref[...] = jnp.where(half_ref[0] == 0, lower_ref[...], upper_ref[...])


def select_half(half, lower, upper, *others):
    anywhere = pl.BlockSpec(memory_space=pl.ANY)
    whole = pl.BlockSpec(memory_space=pltpu.VMEM)
    return pl.pallas_call(
        select_kernel,
        out_shape=jax.ShapeDtypeStruct(lower.shape, lower.dtype),
        in_specs=[pl.BlockSpec(memory_space=pltpu.SMEM), whole, whole] + [anywhere] * len(others),
        out_specs=whole,
        cost_estimate=busy(0.8),
    )(jnp.reshape(half, (1,)).astype(jnp.int32), lower, upper, *others)


def after_kernel(*refs):
    del refs


def after(value, *others):
    anywhere = pl.BlockSpec(memory_space=pl.ANY)
    return pl.pallas_call(
        after_kernel,
        out_shape=jax.ShapeDtypeStruct(value.shape, value.dtype),
        in_specs=[anywhere] * (1 + len(others)),
        out_specs=anywhere,
        input_output_aliases={0: 0},
        cost_estimate=busy(0.3),
    )(value, *others)


def mask_gather(unit, lefts, owners, halves):
    units = {0: unit}
    step = owners // 2
    masks = []
    while step:
        masks.append(step)
        units[step] = exchange(unit, owners, halves, step)
        step //= 2
    for mask in masks[:-1]:
        units[mask] = after(units[mask], lefts[masks[0]])
    for step in masks[1:]:
        for mask in [m for m in units if m >= 2 * step and m % (2 * step) == 0]:
            units[mask | step] = exchange(units[mask], owners, halves, step)
    return units


def doubled(value, count, axes, stride):
    step = 1
    total = lax.axis_size("sec") * lax.axis_size("term")
    while step < count:
        value = value + lax.ppermute(
            value, axes, [(d, d ^ (step * stride)) for d in range(total)]
        )
        step *= 2
    return value


def pack_kernel(order, capacity, blocks, terms, ids_ref, plan_ref, other_plan_ref, *refs):
    left_ref, other_ref, _, *pieces, codes, seen, built, sems = refs
    owners = len(order)
    me, half = ids_ref[0], ids_ref[1]
    rows, width = other_ref.shape[2:]
    start = pl.multiple_of(half * rows, rows)
    parts = rows // PART

    @pl.loop(0, owners)
    def _(owner):
        for index in range(2 * terms * capacity):
            codes[0, owner, index] = 0
            codes[1, owner, index] = blocks

    for stream in range(2 * terms):
        plan = plan_ref if stream < terms else other_plan_ref

        @pl.loop(0, owners)
        def _(owner):
            seen[owner] = 0

        @pl.loop(0, blocks, unroll=4)
        def _(block):
            owner = plan[0, stream % terms, block]
            slot = seen[owner]
            seen[owner] = slot + 1
            codes[0, owner, stream * capacity + slot] = block
            codes[1, owner, stream * capacity + slot] = plan[1, stream % terms, block]

    lane = lax.broadcasted_iota(jnp.int32, (PART, width), 1)
    row = lax.broadcasted_iota(jnp.int32, (PART, width), 0)
    copies = []
    for mask in order:
        owner = me ^ mask
        labels = jnp.zeros((PART, width), jnp.int32)
        for stream in range(2 * terms):
            for slot in range(capacity):
                at = stream * capacity + slot
                block = codes[0, owner, at]
                if stream < terms:
                    value = left_ref[stream, block, pl.ds(start, rows), :]
                else:
                    value = other_ref[stream - terms, block]
                value = pltpu.roll(value.astype(jnp.float32), half * rows, 1)
                built[mask, at * parts : (at + 1) * parts] = value.astype(jnp.bfloat16).reshape(
                    parts, PART, width
                )
                label = jnp.where(row == 0, block, codes[1, owner, at])
                labels = jnp.where(lane == at, label, labels)
        built[mask, 2 * terms * capacity * parts] = labels.astype(jnp.float32).astype(jnp.bfloat16)
        copies.append(pltpu.make_async_copy(built.at[mask], pieces[mask], sems.at[mask]))
        copies[-1].start()
    for copy in copies:
        copy.wait()


def pack(ids, plan, other_plan, left, other, before, order, capacity):
    terms, blocks, rows, width = other.shape
    owners = len(order)
    scalars = pl.BlockSpec(memory_space=pltpu.SMEM)
    whole = pl.BlockSpec(memory_space=pltpu.VMEM)
    anywhere = pl.BlockSpec(memory_space=pl.ANY)
    shape = (2 * terms * capacity * rows // PART + 1, PART, width)
    return pl.pallas_call(
        functools.partial(pack_kernel, order, capacity, blocks, terms),
        out_shape=[jax.ShapeDtypeStruct(shape, jnp.bfloat16)] * owners,
        in_specs=[scalars] * 3 + [whole, whole, anywhere],
        out_specs=[anywhere] * owners,
        scratch_shapes=[
            pltpu.SMEM((2, owners, 2 * terms * capacity), jnp.int32),
            pltpu.SMEM((owners,), jnp.int32),
            pltpu.VMEM((owners,) + shape, jnp.bfloat16),
            pltpu.SemaphoreType.DMA((owners,)),
        ],
        compiler_params=pltpu.CompilerParams(vmem_limit_bytes=VMEM_LIMIT),
        cost_estimate=busy(5.0),
    )(ids, plan, other_plan, left, other, before)


def busy(microseconds):
    return pl.CostEstimate(
        flops=int(1.15e9 * microseconds), bytes_accessed=0, transcendentals=0
    )


def add_products(piece, labels, near, far, rights, total, streams, capacity):
    terms = streams // 2
    blocks, rows, width = near.shape
    parts = rows // PART
    for side in range(2):
        moved, where = [], []
        for stream in range(terms * side, terms * side + terms):
            for slot in range(capacity):
                at = stream * capacity + slot
                source, target = labels[0, at], labels[1, at]
                block = jnp.concatenate([near[source], far[source]], axis=0)
                left = piece[at * parts : (at + 1) * parts].reshape(rows, width)
                product = jnp.dot(left, block, preferred_element_type=jnp.float32)
                moved.append(product.astype(jnp.bfloat16))
                where.append((stream - terms * side, target))
        for value, (term, target) in zip(moved, where):
            total[target] += jnp.dot(
                value,
                rights[side][term, jnp.minimum(target, blocks - 1)],
                preferred_element_type=jnp.float32,
            )


def apply_kernel(sources, first, choices, last, streams, capacity, ids_ref, *refs):
    refs = list(refs)
    lefts = [refs.pop(0) for _ in range(choices or sources)]
    vectors = [(refs.pop(0), refs.pop(0)) for _ in range(sources)]
    rights = refs.pop(0), refs.pop(0)
    total_in = None if first else refs.pop(0)
    out = refs.pop(0) if last else None
    total = refs.pop(0)
    spread_labels, labels, label_sems = refs.pop(0), refs.pop(0), refs.pop(0)
    blocks = vectors[0][0].shape[0]

    if choices:
        chosen, chosen_sems = refs.pop(0), refs.pop(0)
        for index in range(sources):
            for choice, left in enumerate(lefts):

                @pl.when(ids_ref[index] == choice)
                def _():
                    pltpu.make_async_copy(left, chosen.at[index], chosen_sems.at[index]).start()

    total[...] = jnp.zeros_like(total) if first else total_in[...]
    pieces = []
    for index in range(sources):
        if choices:
            pltpu.make_async_copy(lefts[0], chosen.at[index], chosen_sems.at[index]).wait()
            piece = chosen.at[index]
        else:
            piece = lefts[index]
        pieces.append(piece)
        values = piece[piece.shape[0] - 1].astype(jnp.float32).astype(jnp.int32)
        spread_labels[index] = values[:8]
        pltpu.make_async_copy(
            spread_labels.at[index], labels.at[index], label_sems.at[index]
        ).start()
    for index, (near, far) in enumerate(vectors):
        pltpu.make_async_copy(
            spread_labels.at[index], labels.at[index], label_sems.at[index]
        ).wait()
        add_products(
            pieces[index], labels.at[index], near, far, rights, total, streams, capacity
        )
    if last:
        out[...] = total[:blocks].astype(out.dtype)


def apply_group(ids, lefts, vectors, rights, total, choices, last):
    blocks, rows, width = vectors[0][0].shape
    streams = 2 * rights[0].shape[0]
    capacity = (lefts[0].shape[0] - 1) * PART // (streams * rows)
    sources = len(vectors)
    first = total is None
    arrays = list(lefts) + [unit for pair in vectors for unit in pair] + list(rights)
    if not first:
        arrays.append(total)
    whole = pl.BlockSpec(memory_space=pltpu.VMEM)
    total_shape = (blocks + 1, rows, width)
    scratch = [
        pltpu.VMEM((sources, 8, width), jnp.int32),
        pltpu.SMEM((sources, 8, width), jnp.int32),
        pltpu.SemaphoreType.DMA((sources,)),
    ]
    specs = [whole] * len(arrays)
    if choices:
        scratch += [
            pltpu.VMEM((sources,) + lefts[0].shape, lefts[0].dtype),
            pltpu.SemaphoreType.DMA((sources,)),
        ]
        specs[: len(lefts)] = [pl.BlockSpec(memory_space=pl.ANY)] * len(lefts)
    aliases = {}
    if last:
        out_shape = jax.ShapeDtypeStruct((blocks, rows, width), jnp.bfloat16)
        scratch = [pltpu.VMEM(total_shape, jnp.float32)] + scratch
    else:
        out_shape = jax.ShapeDtypeStruct(total_shape, jnp.float32)
        if not first:
            aliases = {len(arrays): 0}
    return pl.pallas_call(
        functools.partial(
            apply_kernel, sources, first, len(lefts) if choices else 0, last, streams, capacity
        ),
        out_shape=out_shape,
        in_specs=[pl.BlockSpec(memory_space=pltpu.SMEM)] + specs,
        out_specs=whole,
        scratch_shapes=scratch,
        input_output_aliases=aliases,
        compiler_params=pltpu.CompilerParams(vmem_limit_bytes=VMEM_LIMIT),
        cost_estimate=busy(0.7 + 1.4 * sources),
    )(ids, *arrays)


def stats_kernel(ids_ref, total_ref, wave_ref, stats_ref):
    blocks = wave_ref.shape[0]
    zero = jnp.zeros(wave_ref.shape[1:], jnp.float32)

    def sums(block, carry):
        cross, own = carry
        wave = wave_ref[block].astype(jnp.float32)
        return cross + wave * total_ref[block], own + wave * wave

    cross, own = lax.fori_loop(0, blocks, sums, (zero, zero), unroll=4)
    cross, own = jnp.sum(cross, keepdims=True), jnp.sum(own, keepdims=True)
    local = jnp.where(own > 0, cross / own, 0.0)

    def squares(block, carry):
        rest = total_ref[block] - local * wave_ref[block].astype(jnp.float32)
        return carry + rest * rest

    about = jnp.sum(lax.fori_loop(0, blocks, squares, zero, unroll=4), keepdims=True)
    lane = lax.broadcasted_iota(jnp.int32, stats_ref.shape, 1)
    row = lax.broadcasted_iota(jnp.int32, stats_ref.shape, 0)
    values = jnp.where(lane == 0, about, jnp.where(lane == 1, cross, jnp.where(lane == 2, own, local)))
    stats_ref[...] = jnp.where((row == ids_ref[2]) & (lane < 4), values, 0.0)


def direction_kernel(entries, total_ref, wave_ref, stats_ref, out_ref, rayleigh_ref):
    blocks = wave_ref.shape[0]
    stats = stats_ref[...]
    about, cross, own, local = (stats[:, lane : lane + 1] for lane in range(4))
    rayleigh = jnp.sum(cross, keepdims=True) / jnp.sum(own, keepdims=True)
    offset = local - rayleigh
    residual_sq = jnp.sum(about + offset * offset * own, keepdims=True)
    factor = lax.rsqrt(residual_sq / entries + 1e-06)
    rayleigh_ref[...] = rayleigh

    @pl.loop(0, blocks, unroll=4)
    def _(block):
        rest = total_ref[block] - rayleigh * wave_ref[block].astype(jnp.float32)
        out_ref[block] = (rest * factor).astype(jnp.bfloat16)


def new_direction(ids, total, wave, owners, halves, entries):
    devices = owners * halves
    scalars = pl.BlockSpec(memory_space=pltpu.SMEM)
    whole = pl.BlockSpec(memory_space=pltpu.VMEM)
    params = pltpu.CompilerParams(vmem_limit_bytes=VMEM_LIMIT)
    stats = pl.pallas_call(
        stats_kernel,
        out_shape=jax.ShapeDtypeStruct((devices, 128), jnp.float32),
        in_specs=[scalars, whole, whole],
        out_specs=whole,
        compiler_params=params,
    )(ids, total, wave)
    stats = doubled(stats, devices, BOTH, 1)
    return pl.pallas_call(
        functools.partial(direction_kernel, entries),
        out_shape=(
            jax.ShapeDtypeStruct(wave.shape, jnp.bfloat16),
            jax.ShapeDtypeStruct((1, 1), jnp.float32),
        ),
        in_specs=[whole] * 3,
        out_specs=(whole, whole),
        compiler_params=params,
    )(total, wave, stats)


def per_device_ring(wavefunction, left_operator, right_operator, target_owner, target_local):
    owners, halves = lax.axis_size("sec"), lax.axis_size("term")
    me, half = lax.axis_index("sec"), lax.axis_index("term")
    terms, blocks, height, width = left_operator.shape
    rows = height // halves
    capacity = 2 * blocks // owners
    place = ring_place(me, owners)
    ids = jnp.stack([me, half, me * halves + half]).astype(jnp.int32)

    own_rows = lax.dynamic_slice_in_dim(wavefunction, half * rows, rows, 1)
    other_rows = lax.dynamic_slice_in_dim(wavefunction, (1 - half) * rows, rows, 1)
    plan = jnp.stack([target_owner[:, :, 0], target_local])
    other_left = swap(
        lax.dynamic_slice_in_dim(left_operator, (1 - half) * rows, rows, 2), owners, halves
    )
    far_pieces = list(range(owners // 2, owners))
    order = [0, far_pieces[0]]
    for m in range(1, owners // 2):
        order += [far_pieces[m], m]
    rights = (right_operator, swap(right_operator, owners, halves))
    pieces = pack(
        ids,
        plan,
        swap(plan, owners, halves),
        left_operator,
        other_left,
        rights[1],
        order[1:] + order[:1],
        capacity,
    )
    lefts = [exchange(piece, owners, halves, m) if m else piece for m, piece in enumerate(pieces)]
    near = mask_gather(own_rows, lefts, owners, halves)
    far = {m: swap(unit, owners, halves) if m else other_rows for m, unit in near.items()}

    total = None
    no_choice = jnp.zeros((1,), jnp.int32)
    for m in order:
        total = apply_group(
            no_choice, [lefts[m]], [(near[m], far[m])], rights, total, False, False
        )

    entries = blocks * owners * height * width
    direction, rayleigh = new_direction(ids, total, own_rows, owners, halves, entries)
    reach = (owners - 1) // 2

    def add_group(total, units, last):
        choice = jnp.stack([ring_owner(place - s, owners) ^ me for s in units])
        vectors = [
            (unit, swap(unit, owners, halves)) for unit in units.values()
        ]
        return apply_group(choice.astype(jnp.int32), lefts, vectors, rights, total, True, last)

    ahead = behind = direction
    units = {0: direction}
    total = None
    for step in range(1, reach + 1):
        ahead_next = ring_send(ahead, owners, halves, (1,) * halves)
        behind_next = ring_send(behind, owners, halves, (-1,) * halves)
        total = add_group(total, units, False)
        ahead, behind = after(ahead_next, total), behind_next
        units = {step: ahead, -step: behind}
    last = select_half(half, ahead, behind)
    last = ring_send(last, owners, halves, (1, -1))
    total = add_group(total, units, False)
    total = add_group(total, {owners // 2: after(last, total)}, True)
    return (total, rayleigh[0])


def slot_codes(target_owner, target_local, owners, capacity):
    terms, blocks = target_local.shape
    owner = target_owner[:, :, 0]
    place = jnp.arange(blocks, dtype=jnp.int32)
    same = (owner[:, :, None] == owner[:, None, :]) & (place[None, :] < place[:, None])[None]
    position = jnp.sum(same.astype(jnp.int32), axis=2)
    hit = (
        owner[:, None, None, :] == jnp.arange(owners, dtype=jnp.int32)[None, :, None, None]
    ) & (position[:, None, None, :] == jnp.arange(capacity, dtype=jnp.int32)[None, None, :, None])
    code = place[None, :] * (2 * blocks) + target_local - blocks
    return blocks + jnp.sum(jnp.where(hit, code[:, None, None, :], 0), axis=3)


def stream_kernel(first, capacity, blocks, code_ref, left_ref, vector_ref, right_ref, *rest):
    total_in, total = (None, rest[0]) if first else rest
    step = pl.program_id(0)
    rows, width = left_ref.shape[2:]

    @pl.when(step == 0)
    def _():
        total[...] = jnp.zeros_like(total) if first else total_in[...]

    for term in range(2):
        moved, where = [], []
        for slot in range(capacity):
            code = code_ref[2 * step + term, slot]
            source, target = lax.div(code, 2 * blocks), lax.rem(code, 2 * blocks)
            block = vector_ref[0, :, source].reshape(2 * rows, width)
            product = jnp.dot(left_ref[term, slot], block, preferred_element_type=jnp.float32)
            moved.append(product.astype(jnp.bfloat16))
            where.append(target)
        for slot in range(capacity):
            target = where[slot]
            total[target] += jnp.dot(
                moved[slot],
                right_ref[term, jnp.minimum(target, blocks - 1)],
                preferred_element_type=jnp.float32,
            )


def stream_chunk(total, codes, left, vector, right):
    owners, _, blocks, rows, width = vector.shape
    capacity = left.shape[1]
    first = total is None
    spec_total = pl.BlockSpec((blocks + 1, rows, width), lambda s, c: (0, 0, 0))
    return pl.pallas_call(
        functools.partial(stream_kernel, first, capacity, blocks),
        out_shape=jax.ShapeDtypeStruct((blocks + 1, rows, width), jnp.float32),
        grid_spec=pltpu.PrefetchScalarGridSpec(
            num_scalar_prefetch=1,
            grid=(owners,),
            in_specs=[
                pl.BlockSpec((2, capacity, rows, width), lambda s, c: (s, 0, 0, 0)),
                pl.BlockSpec((1, 2, blocks, rows, width), lambda s, c: (s, 0, 0, 0, 0)),
                pl.BlockSpec((2, blocks, width, width), lambda s, c: (0, 0, 0, 0)),
            ]
            + ([] if first else [spec_total]),
            out_specs=spec_total,
        ),
        compiler_params=pltpu.CompilerParams(vmem_limit_bytes=32 * 2**20),
        cost_estimate=pl.CostEstimate(
            flops=owners * 2 * capacity * 2 * 2 * rows * width * width,
            bytes_accessed=left.size * 2 + vector.size * 2 + right.size * 2,
            transcendentals=0,
        ),
    )(codes, left, vector, right, *([] if first else [total]))


def per_device_streamed(wavefunction, left_operator, right_operator, target_owner, target_local):
    owners = lax.axis_size("sec")
    halves = lax.axis_size("term")
    me, half = lax.axis_index("sec"), lax.axis_index("term")
    terms, blocks, height, width = left_operator.shape
    rows = height // halves
    capacity = 2 * blocks // owners

    own_rows = lax.dynamic_slice_in_dim(wavefunction, half * rows, rows, 1)
    codes = slot_codes(target_owner, target_local, owners, capacity)
    sources = codes // (2 * blocks)

    moved_left = []
    for k in range(terms):
        pick = sources[k][:, None, :] * halves + jnp.arange(halves, dtype=jnp.int32)[None, :, None]
        pieces = left_operator[k].reshape(blocks * halves, rows, width)[pick.reshape(-1)]
        pieces = pieces.reshape(owners * halves, capacity, rows, width)
        moved_left.append(lax.all_to_all(pieces, BOTH, split_axis=0, concat_axis=0, tiled=True))
    all_codes = lax.all_gather(codes, BOTH, axis=0)
    my_codes = lax.dynamic_index_in_dim(all_codes, me, axis=3 - 1, keepdims=False)
    gathered = lax.all_gather(own_rows, BOTH, axis=0).reshape(owners, halves, blocks, rows, width)
    right = lax.all_gather(right_operator, "term", axis=1)

    def apply(vector):
        total = None
        for k in range(terms):
            total = stream_chunk(total, my_codes[:, k], moved_left[k], vector, right[k])
        return total[:blocks]

    sigma_rows = apply(gathered)
    wave = own_rows.astype(jnp.float32)
    cross, own = jnp.sum(wave * sigma_rows), jnp.sum(wave * wave)
    local = jnp.where(own > 0, cross / own, 0.0)
    about = jnp.sum(jnp.square(sigma_rows - local * wave))
    stats = lax.all_gather(jnp.stack([about, cross, own, local]), BOTH, axis=0)
    rayleigh = jnp.sum(stats[:, 1]) / jnp.sum(stats[:, 2])
    residual_sq = jnp.sum(stats[:, 0] + jnp.square(stats[:, 3] - rayleigh) * stats[:, 2])
    entries = blocks * owners * height * width
    factor = lax.rsqrt(residual_sq / entries + 1e-06)
    direction = ((sigma_rows - rayleigh * wave) * factor).astype(jnp.bfloat16)
    direction = lax.all_gather(direction, BOTH, axis=0).reshape(gathered.shape)
    sigma_two = apply(direction).astype(jnp.bfloat16)
    return (sigma_two, jnp.reshape(rayleigh, (1,)))


def per_device(wavefunction, *operands):
    gathered_bytes = lax.axis_size("sec") * wavefunction.size * wavefunction.dtype.itemsize
    if 2 * gathered_bytes > RING_BYTES:
        return per_device_streamed(wavefunction, *operands)
    return per_device_ring(wavefunction, *operands)


def solution(mesh):
    placed = (
        P(("rep", "sec"), None, None),
        P("term", ("rep", "sec"), None, None),
        P("term", ("rep", "sec"), None, None),
        P("term", ("rep", "sec"), None),
        P("term", ("rep", "sec")),
    )
    return jax.shard_map(
        per_device,
        mesh=mesh,
        in_specs=placed,
        out_specs=(P(("rep", "sec"), "term", None), P("rep")),
        check_vma=False,
    )
```

```python
import functools

import jax
import jax.numpy as jnp
from jax import lax
from jax.experimental import pallas as pl
from jax.experimental.pallas import tpu as pltpu
from jax.sharding import PartitionSpec as P

BOTH = ("sec", "term")
VMEM_LIMIT = 24 * 2**20
PART = 16
RING_BYTES = 24 * 2**20


def ring_order(owners):
    if owners % 2:
        return list(range(owners))
    return list(range(0, owners, 2)) + list(range(owners - 1, 0, -2))


def ring_place(owner, owners):
    if owners % 2:
        return owner
    return jnp.where(owner % 2 == 0, owner // 2, owners - 1 - owner // 2)


def ring_owner(place, owners):
    place = place % owners
    if owners % 2:
        return place
    return jnp.where(place < owners // 2, 2 * place, 2 * (owners - 1 - place) + 1)


def permute(value, owners, halves, target, flip=0):
    pairs = [
        (chip * halves + half, target(chip, half) * halves + (half ^ flip))
        for chip in range(owners)
        for half in range(halves)
    ]
    return lax.ppermute(value, BOTH, pairs)


def swap(value, owners, halves):
    return permute(value, owners, halves, lambda chip, half: chip, 1)


def exchange(value, owners, halves, mask):
    return permute(value, owners, halves, lambda chip, half: chip ^ mask)


def ring_send(value, owners, halves, shifts):
    ring = ring_order(owners)
    place = {chip: index for index, chip in enumerate(ring)}
    return permute(
        value, owners, halves, lambda chip, half: ring[(place[chip] + shifts[half]) % owners]
    )


def select_kernel(half_ref, lower_ref, upper_ref, *rest):
    out_ref = rest[-1]
    out_ref[...] = jnp.where(half_ref[0] == 0, lower_ref[...], upper_ref[...])


def select_half(half, lower, upper, *others):
    anywhere = pl.BlockSpec(memory_space=pl.ANY)
    whole = pl.BlockSpec(memory_space=pltpu.VMEM)
    return pl.pallas_call(
        select_kernel,
        out_shape=jax.ShapeDtypeStruct(lower.shape, lower.dtype),
        in_specs=[pl.BlockSpec(memory_space=pltpu.SMEM), whole, whole] + [anywhere] * len(others),
        out_specs=whole,
        cost_estimate=busy(0.8),
    )(jnp.reshape(half, (1,)).astype(jnp.int32), lower, upper, *others)


def after_kernel(*refs):
    del refs


def after(value, *others):
    far_memory = pl.BlockSpec(memory_space=pltpu.HBM)
    anywhere = pl.BlockSpec(memory_space=pl.ANY)
    return pl.pallas_call(
        after_kernel,
        out_shape=jax.ShapeDtypeStruct(value.shape, value.dtype),
        in_specs=[far_memory] + [anywhere] * len(others),
        out_specs=far_memory,
        input_output_aliases={0: 0},
        cost_estimate=busy(0.3),
    )(value, *others)


def mask_gather(unit, owners, halves):
    units = {0: unit}
    step = owners // 2
    while step:
        for mask in list(units):
            units[mask | step] = exchange(units[mask], owners, halves, step)
        step //= 2
    return units


def doubled(value, count, axes, stride):
    step = 1
    total = lax.axis_size("sec") * lax.axis_size("term")
    while step < count:
        value = value + lax.ppermute(
            value, axes, [(d, d ^ (step * stride)) for d in range(total)]
        )
        step *= 2
    return value


def pack_kernel(capacity, own_left, half_ref, owner_ref, target_ref, left_ref, out_ref, *scratch):
    codes, seen, left, built, in_sem, sems = scratch
    terms, blocks, rows, width = left.shape
    owners = out_ref.shape[0]
    half = half_ref[0]
    parts = rows // PART
    if own_left:
        start = pl.multiple_of(half * rows, rows)
        load = pltpu.make_async_copy(left_ref.at[:, :, pl.ds(start, rows), :], left, in_sem)
    else:
        load = pltpu.make_async_copy(left_ref, left, in_sem)
    load.start()

    @pl.loop(0, owners)
    def _(owner):
        for index in range(terms * capacity):
            codes[0, owner, index] = 0
            codes[1, owner, index] = blocks

    for term in range(terms):

        @pl.loop(0, owners)
        def _(owner):
            seen[owner] = 0

        @pl.loop(0, blocks, unroll=4)
        def _(block):
            owner = owner_ref[term, block]
            slot = seen[owner]
            seen[owner] = slot + 1
            codes[0, owner, term * capacity + slot] = block
            codes[1, owner, term * capacity + slot] = target_ref[term, block]

    load.wait()
    lane = lax.broadcasted_iota(jnp.int32, (PART, width), 1)
    row = lax.broadcasted_iota(jnp.int32, (PART, width), 0)
    copies = [
        pltpu.make_async_copy(built.at[owner], out_ref.at[owner], sems.at[owner])
        for owner in range(owners)
    ]
    for owner in range(owners):
        labels = jnp.zeros((PART, width), jnp.int32)
        for at in range(terms * capacity):
            block = codes[0, owner, at]
            value = left[at // capacity, block]
            value = pltpu.roll(value.astype(jnp.float32), half * rows, 1)
            built[owner, at * parts : (at + 1) * parts] = value.astype(jnp.bfloat16).reshape(
                parts, PART, width
            )
            labels = jnp.where(
                lane == at, jnp.where(row == 0, block, codes[1, owner, at]), labels
            )
        built[owner, terms * capacity * parts] = labels.astype(jnp.float32).astype(jnp.bfloat16)
        copies[owner].start()
    for copy in copies:
        copy.wait()


def pack(half, target_owner, target_local, left, rows, owners, capacity):
    terms, blocks, height, width = left.shape
    scalars = pl.BlockSpec(memory_space=pltpu.SMEM)
    far_memory = pl.BlockSpec(memory_space=pltpu.HBM)
    shape = (owners, terms * capacity * rows // PART + 1, PART, width)
    return pl.pallas_call(
        functools.partial(pack_kernel, capacity, height != rows),
        out_shape=jax.ShapeDtypeStruct(shape, jnp.bfloat16),
        in_specs=[scalars] * 3 + [far_memory],
        out_specs=far_memory,
        scratch_shapes=[
            pltpu.SMEM((2, owners, terms * capacity), jnp.int32),
            pltpu.SMEM((owners,), jnp.int32),
            pltpu.VMEM((terms, blocks, rows, width), jnp.bfloat16),
            pltpu.VMEM(shape, jnp.bfloat16),
            pltpu.SemaphoreType.DMA,
            pltpu.SemaphoreType.DMA((owners,)),
        ],
        compiler_params=pltpu.CompilerParams(vmem_limit_bytes=VMEM_LIMIT),
        cost_estimate=busy(3.0),
    )(half, target_owner, target_local, left)


def busy(microseconds):
    return pl.CostEstimate(
        flops=int(1.15e9 * microseconds), bytes_accessed=0, transcendentals=0
    )


def add_products(left, labels, near, far, right, total, terms, capacity):
    blocks, rows, width = near.shape
    parts = rows // PART
    moved, where = [], []
    for at in range(terms * capacity):
        block = jnp.concatenate([near[labels[0, at]], far[labels[0, at]]], axis=0)
        piece = left[at * parts : (at + 1) * parts].reshape(rows, width)
        product = jnp.dot(piece, block, preferred_element_type=jnp.float32)
        moved.append(product.astype(jnp.bfloat16))
        where.append(labels[1, at])
    for at in range(terms * capacity):
        target = where[at]
        total[target] += jnp.dot(
            moved[at],
            right[at // capacity, jnp.minimum(target, blocks - 1)],
            preferred_element_type=jnp.float32,
        )


def apply_kernel(sources, sides, first, last, chips_ref, *refs):
    refs = list(refs)
    lefts = [refs.pop(0) for _ in range(sides)]
    rights = [refs.pop(0) for _ in range(sides)]
    vectors = [(refs.pop(0), refs.pop(0)) for _ in range(sources)]
    total_in = None if first else refs.pop(0)
    out = refs.pop(0) if last else None
    total = refs.pop(0)
    left, right, vector, raw, spread, labels = refs[:6]
    left_sems, right_sems, vector_sems, raw_sems, label_sem = refs[6:]
    terms, blocks = right.shape[1:3]
    rows = vector.shape[3]
    parts = left.shape[1]
    capacity = parts * PART // (terms * rows)
    items = [(source, side) for source in range(sources) for side in range(sides)]

    def label_copy(item):
        source, side = items[item]
        return pltpu.make_async_copy(
            lefts[side].at[chips_ref[source], parts], raw.at[item], raw_sems.at[item]
        )

    def left_copy(item):
        source, side = items[item]
        return pltpu.make_async_copy(
            lefts[side].at[chips_ref[source], pl.ds(0, parts)],
            left.at[item % 2],
            left_sems.at[item % 2],
        )

    def vector_copies(source):
        return [
            pltpu.make_async_copy(
                vectors[source][part], vector.at[source % 2, part], vector_sems.at[source % 2, part]
            )
            for part in range(2)
        ]

    def right_copy(side):
        return pltpu.make_async_copy(rights[side], right.at[side], right_sems.at[side])

    for item in range(len(items)):
        label_copy(item).start()
    for copy in [left_copy(0), *vector_copies(0), right_copy(0)]:
        copy.start()
    for side in range(1, sides):
        right_copy(side).start()
    total[...] = jnp.zeros_like(total) if first else total_in[...]
    for item in range(len(items)):
        label_copy(item).wait()
    spread[...] = raw[:, :8].astype(jnp.float32).astype(jnp.int32)
    label_move = pltpu.make_async_copy(spread, labels, label_sem)
    label_move.start()
    label_move.wait()

    for item, (source, side) in enumerate(items):
        if item + 1 < len(items):
            left_copy(item + 1).start()
        if side == 0:
            for copy in vector_copies(source):
                copy.wait()
            if source + 1 < sources:
                for copy in vector_copies(source + 1):
                    copy.start()
        if source == 0:
            right_copy(side).wait()
        left_copy(item).wait()
        add_products(
            left.at[item % 2],
            labels.at[item],
            vector.at[source % 2, 0],
            vector.at[source % 2, 1],
            right.at[side],
            total,
            terms,
            capacity,
        )
    if last:
        out[...] = total[:blocks].astype(out.dtype)


def apply_group(chips, lefts, rights, vectors, total, last):
    blocks, rows, width = vectors[0][0].shape
    terms = rights[0].shape[0]
    parts = lefts[0].shape[1] - 1
    sources, sides = len(vectors), len(lefts)
    first = total is None
    arrays = list(lefts) + list(rights) + [unit for pair in vectors for unit in pair]
    whole = pl.BlockSpec(memory_space=pltpu.VMEM)
    specs = [pl.BlockSpec(memory_space=pltpu.HBM)] * len(arrays)
    if not first:
        arrays.append(total)
        specs.append(whole)
    total_shape = (blocks + 1, rows, width)
    items = sources * sides
    scratch = [
        pltpu.VMEM((2, parts, PART, width), jnp.bfloat16),
        pltpu.VMEM((sides, terms, blocks, width, width), jnp.bfloat16),
        pltpu.VMEM((2, 2, blocks, rows, width), jnp.bfloat16),
        pltpu.VMEM((items, PART, width), jnp.bfloat16),
        pltpu.VMEM((items, 8, width), jnp.int32),
        pltpu.SMEM((items, 8, width), jnp.int32),
        pltpu.SemaphoreType.DMA((2,)),
        pltpu.SemaphoreType.DMA((sides,)),
        pltpu.SemaphoreType.DMA((2, 2)),
        pltpu.SemaphoreType.DMA((items,)),
        pltpu.SemaphoreType.DMA,
    ]
    aliases = {}
    if last:
        out_shape = jax.ShapeDtypeStruct((blocks, rows, width), jnp.bfloat16)
        scratch = [pltpu.VMEM(total_shape, jnp.float32)] + scratch
    else:
        out_shape = jax.ShapeDtypeStruct(total_shape, jnp.float32)
        if not first:
            aliases = {len(arrays): 0}
    return pl.pallas_call(
        functools.partial(apply_kernel, sources, sides, first, last),
        out_shape=out_shape,
        in_specs=[pl.BlockSpec(memory_space=pltpu.SMEM)] + specs,
        out_specs=whole,
        scratch_shapes=scratch,
        input_output_aliases=aliases,
        compiler_params=pltpu.CompilerParams(vmem_limit_bytes=VMEM_LIMIT),
        cost_estimate=busy(1.5 + 0.7 * items),
    )(chips.astype(jnp.int32), *arrays)


def stats_kernel(ids_ref, total_ref, wave_ref, stats_ref):
    blocks = wave_ref.shape[0]
    zero = jnp.zeros(wave_ref.shape[1:], jnp.float32)

    def sums(block, carry):
        cross, own = carry
        wave = wave_ref[block].astype(jnp.float32)
        return cross + wave * total_ref[block], own + wave * wave

    cross, own = lax.fori_loop(0, blocks, sums, (zero, zero), unroll=4)
    cross, own = jnp.sum(cross, keepdims=True), jnp.sum(own, keepdims=True)
    local = jnp.where(own > 0, cross / own, 0.0)

    def squares(block, carry):
        rest = total_ref[block] - local * wave_ref[block].astype(jnp.float32)
        return carry + rest * rest

    about = jnp.sum(lax.fori_loop(0, blocks, squares, zero, unroll=4), keepdims=True)
    lane = lax.broadcasted_iota(jnp.int32, stats_ref.shape, 1)
    row = lax.broadcasted_iota(jnp.int32, stats_ref.shape, 0)
    values = jnp.where(lane == 0, about, jnp.where(lane == 1, cross, jnp.where(lane == 2, own, local)))
    stats_ref[...] = jnp.where((row == ids_ref[2]) & (lane < 4), values, 0.0)


def direction_kernel(entries, total_ref, wave_ref, stats_ref, out_ref, rayleigh_ref):
    blocks = wave_ref.shape[0]
    stats = stats_ref[...]
    about, cross, own, local = (stats[:, lane : lane + 1] for lane in range(4))
    rayleigh = jnp.sum(cross, keepdims=True) / jnp.sum(own, keepdims=True)
    offset = local - rayleigh
    residual_sq = jnp.sum(about + offset * offset * own, keepdims=True)
    factor = lax.rsqrt(residual_sq / entries + 1e-06)
    rayleigh_ref[...] = rayleigh

    @pl.loop(0, blocks, unroll=4)
    def _(block):
        rest = total_ref[block] - rayleigh * wave_ref[block].astype(jnp.float32)
        out_ref[block] = (rest * factor).astype(jnp.bfloat16)


def new_direction(ids, total, wave, owners, halves, entries):
    devices = owners * halves
    scalars = pl.BlockSpec(memory_space=pltpu.SMEM)
    whole = pl.BlockSpec(memory_space=pltpu.VMEM)
    params = pltpu.CompilerParams(vmem_limit_bytes=VMEM_LIMIT)
    stats = pl.pallas_call(
        stats_kernel,
        out_shape=jax.ShapeDtypeStruct((devices, 128), jnp.float32),
        in_specs=[scalars, whole, whole],
        out_specs=whole,
        compiler_params=params,
    )(ids, total, wave)
    stats = doubled(stats, devices, BOTH, 1)
    return pl.pallas_call(
        functools.partial(direction_kernel, entries),
        out_shape=(
            jax.ShapeDtypeStruct(wave.shape, jnp.bfloat16),
            jax.ShapeDtypeStruct((1, 1), jnp.float32),
        ),
        in_specs=[whole] * 3,
        out_specs=(whole, whole),
        compiler_params=params,
    )(total, wave, stats)


def per_device_ring(wavefunction, left_operator, right_operator, target_owner, target_local):
    owners, halves = lax.axis_size("sec"), lax.axis_size("term")
    me, half = lax.axis_index("sec"), lax.axis_index("term")
    terms, blocks, height, width = left_operator.shape
    rows = height // halves
    capacity = 2 * blocks // owners
    place = ring_place(me, owners)
    ids = jnp.stack([me, half, me * halves + half]).astype(jnp.int32)

    own_rows = lax.dynamic_slice_in_dim(wavefunction, half * rows, rows, 1)
    other_rows = lax.dynamic_slice_in_dim(wavefunction, (1 - half) * rows, rows, 1)
    half_scalar = jnp.reshape(half, (1,)).astype(jnp.int32)

    def send_left(owner_of, target_of, left):
        packed = pack(half_scalar, owner_of, target_of, left, rows, owners, capacity)
        return lax.all_to_all(packed, "sec", split_axis=0, concat_axis=0, tiled=True)

    plan = jnp.stack([target_owner[:, :, 0], target_local])
    lefts = [send_left(plan[0], plan[1], left_operator)]
    other_left = swap(
        lax.dynamic_slice_in_dim(left_operator, (1 - half) * rows, rows, 2), owners, halves
    )
    other_plan = swap(plan, owners, halves)
    lefts.append(send_left(other_plan[0], other_plan[1], other_left))
    rights = [right_operator, swap(right_operator, owners, halves)]
    near = mask_gather(own_rows, owners, halves)
    far = {m: swap(unit, owners, halves) if m else other_rows for m, unit in near.items()}
    masks = jnp.array(list(near), jnp.int32)
    vectors = [(near[m], far[m]) for m in near]

    total = None
    for left, right in zip(lefts, rights):
        total = apply_group(me ^ masks, [left], [right], vectors, total, False)

    entries = blocks * owners * height * width
    direction, rayleigh = new_direction(ids, total, own_rows, owners, halves, entries)
    reach = (owners - 1) // 2

    def add_group(total, units, last):
        chips = jnp.stack([ring_owner(place - s, owners) for s in units])
        vectors = [(unit, swap(unit, owners, halves)) for unit in units.values()]
        return apply_group(chips, lefts, rights, vectors, total, last)

    ahead = behind = direction
    units = {0: direction}
    total = None
    for step in range(1, reach + 1):
        ahead_next = ring_send(ahead, owners, halves, (1,) * halves)
        behind_next = ring_send(behind, owners, halves, (-1,) * halves)
        total = add_group(total, units, False)
        ahead, behind = after(ahead_next, total), behind_next
        units = {step: ahead, -step: behind}
    last = select_half(half, ahead, behind)
    last = ring_send(last, owners, halves, (1, -1))
    total = add_group(total, units, False)
    total = add_group(total, {owners // 2: after(last, total)}, True)
    return (total, rayleigh[0])


def slot_codes(target_owner, target_local, owners, capacity):
    terms, blocks = target_local.shape
    owner = target_owner[:, :, 0]
    place = jnp.arange(blocks, dtype=jnp.int32)
    same = (owner[:, :, None] == owner[:, None, :]) & (place[None, :] < place[:, None])[None]
    position = jnp.sum(same.astype(jnp.int32), axis=2)
    hit = (
        owner[:, None, None, :] == jnp.arange(owners, dtype=jnp.int32)[None, :, None, None]
    ) & (position[:, None, None, :] == jnp.arange(capacity, dtype=jnp.int32)[None, None, :, None])
    code = place[None, :] * (2 * blocks) + target_local - blocks
    return blocks + jnp.sum(jnp.where(hit, code[:, None, None, :], 0), axis=3)


def stream_kernel(first, capacity, blocks, code_ref, left_ref, vector_ref, right_ref, *rest):
    total_in, total = (None, rest[0]) if first else rest
    step = pl.program_id(0)
    rows, width = left_ref.shape[2:]

    @pl.when(step == 0)
    def _():
        total[...] = jnp.zeros_like(total) if first else total_in[...]

    for term in range(2):
        moved, where = [], []
        for slot in range(capacity):
            code = code_ref[2 * step + term, slot]
            source, target = lax.div(code, 2 * blocks), lax.rem(code, 2 * blocks)
            block = vector_ref[0, :, source].reshape(2 * rows, width)
            product = jnp.dot(left_ref[term, slot], block, preferred_element_type=jnp.float32)
            moved.append(product.astype(jnp.bfloat16))
            where.append(target)
        for slot in range(capacity):
            target = where[slot]
            total[target] += jnp.dot(
                moved[slot],
                right_ref[term, jnp.minimum(target, blocks - 1)],
                preferred_element_type=jnp.float32,
            )


def stream_chunk(total, codes, left, vector, right):
    owners, _, blocks, rows, width = vector.shape
    capacity = left.shape[1]
    first = total is None
    spec_total = pl.BlockSpec((blocks + 1, rows, width), lambda s, c: (0, 0, 0))
    return pl.pallas_call(
        functools.partial(stream_kernel, first, capacity, blocks),
        out_shape=jax.ShapeDtypeStruct((blocks + 1, rows, width), jnp.float32),
        grid_spec=pltpu.PrefetchScalarGridSpec(
            num_scalar_prefetch=1,
            grid=(owners,),
            in_specs=[
                pl.BlockSpec((2, capacity, rows, width), lambda s, c: (s, 0, 0, 0)),
                pl.BlockSpec((1, 2, blocks, rows, width), lambda s, c: (s, 0, 0, 0, 0)),
                pl.BlockSpec((2, blocks, width, width), lambda s, c: (0, 0, 0, 0)),
            ]
            + ([] if first else [spec_total]),
            out_specs=spec_total,
        ),
        compiler_params=pltpu.CompilerParams(vmem_limit_bytes=32 * 2**20),
        cost_estimate=pl.CostEstimate(
            flops=owners * 2 * capacity * 2 * 2 * rows * width * width,
            bytes_accessed=left.size * 2 + vector.size * 2 + right.size * 2,
            transcendentals=0,
        ),
    )(codes, left, vector, right, *([] if first else [total]))


def per_device_streamed(wavefunction, left_operator, right_operator, target_owner, target_local):
    owners = lax.axis_size("sec")
    halves = lax.axis_size("term")
    me, half = lax.axis_index("sec"), lax.axis_index("term")
    terms, blocks, height, width = left_operator.shape
    rows = height // halves
    capacity = 2 * blocks // owners

    own_rows = lax.dynamic_slice_in_dim(wavefunction, half * rows, rows, 1)
    codes = slot_codes(target_owner, target_local, owners, capacity)
    sources = codes // (2 * blocks)

    moved_left = []
    for k in range(terms):
        pick = sources[k][:, None, :] * halves + jnp.arange(halves, dtype=jnp.int32)[None, :, None]
        pieces = left_operator[k].reshape(blocks * halves, rows, width)[pick.reshape(-1)]
        pieces = pieces.reshape(owners * halves, capacity, rows, width)
        moved_left.append(lax.all_to_all(pieces, BOTH, split_axis=0, concat_axis=0, tiled=True))
    all_codes = lax.all_gather(codes, BOTH, axis=0)
    my_codes = lax.dynamic_index_in_dim(all_codes, me, axis=3 - 1, keepdims=False)
    gathered = lax.all_gather(own_rows, BOTH, axis=0).reshape(owners, halves, blocks, rows, width)
    right = lax.all_gather(right_operator, "term", axis=1)

    def apply(vector):
        total = None
        for k in range(terms):
            total = stream_chunk(total, my_codes[:, k], moved_left[k], vector, right[k])
        return total[:blocks]

    sigma_rows = apply(gathered)
    wave = own_rows.astype(jnp.float32)
    cross, own = jnp.sum(wave * sigma_rows), jnp.sum(wave * wave)
    local = jnp.where(own > 0, cross / own, 0.0)
    about = jnp.sum(jnp.square(sigma_rows - local * wave))
    stats = lax.all_gather(jnp.stack([about, cross, own, local]), BOTH, axis=0)
    rayleigh = jnp.sum(stats[:, 1]) / jnp.sum(stats[:, 2])
    residual_sq = jnp.sum(stats[:, 0] + jnp.square(stats[:, 3] - rayleigh) * stats[:, 2])
    entries = blocks * owners * height * width
    factor = lax.rsqrt(residual_sq / entries + 1e-06)
    direction = ((sigma_rows - rayleigh * wave) * factor).astype(jnp.bfloat16)
    direction = lax.all_gather(direction, BOTH, axis=0).reshape(gathered.shape)
    sigma_two = apply(direction).astype(jnp.bfloat16)
    return (sigma_two, jnp.reshape(rayleigh, (1,)))


def per_device(wavefunction, *operands):
    gathered_bytes = lax.axis_size("sec") * wavefunction.size * wavefunction.dtype.itemsize
    if 2 * gathered_bytes > RING_BYTES:
        return per_device_streamed(wavefunction, *operands)
    return per_device_ring(wavefunction, *operands)


def solution(mesh):
    placed = (
        P(("rep", "sec"), None, None),
        P("term", ("rep", "sec"), None, None),
        P("term", ("rep", "sec"), None, None),
        P("term", ("rep", "sec"), None),
        P("term", ("rep", "sec")),
    )
    return jax.shard_map(
        per_device,
        mesh=mesh,
        in_specs=placed,
        out_specs=(P(("rep", "sec"), "term", None), P("rep")),
        check_vma=False,
    )
```

```python
import functools

import jax
import jax.numpy as jnp
from jax import lax
from jax.experimental import pallas as pl
from jax.experimental.pallas import tpu as pltpu
from jax.sharding import PartitionSpec as P

BOTH = ("sec", "term")
VMEM_LIMIT = 20 * 2**20
PART = 16
ORDER = [0, 4, 5, 1, 2, 6, 3, 7]
WAITS = {4: 1, 2: 5, 6: 2}
PIECE_WAITS = {6: 4, 7: 5}
RING_BYTES = 24 * 2**20


def ring_order(owners):
    if owners % 2:
        return list(range(owners))
    return list(range(0, owners, 2)) + list(range(owners - 1, 0, -2))


def ring_place(owner, owners):
    if owners % 2:
        return owner
    return jnp.where(owner % 2 == 0, owner // 2, owners - 1 - owner // 2)


def ring_owner(place, owners):
    place = place % owners
    if owners % 2:
        return place
    return jnp.where(place < owners // 2, 2 * place, 2 * (owners - 1 - place) + 1)


def permute(value, owners, halves, target, flip=0):
    pairs = [
        (chip * halves + half, target(chip, half) * halves + (half ^ flip))
        for chip in range(owners)
        for half in range(halves)
    ]
    return lax.ppermute(value, BOTH, pairs)


def swap(value, owners, halves):
    return permute(value, owners, halves, lambda chip, half: chip, 1)


def exchange(value, owners, halves, mask):
    return permute(value, owners, halves, lambda chip, half: chip ^ mask)


def ring_send(value, owners, halves, shifts):
    ring = ring_order(owners)
    place = {chip: index for index, chip in enumerate(ring)}
    return permute(
        value, owners, halves, lambda chip, half: ring[(place[chip] + shifts[half]) % owners]
    )


def select_kernel(half_ref, lower_ref, upper_ref, *rest):
    out_ref = rest[-1]
    out_ref[...] = jnp.where(half_ref[0] == 0, lower_ref[...], upper_ref[...])


def select_half(half, lower, upper, *others):
    anywhere = pl.BlockSpec(memory_space=pl.ANY)
    whole = pl.BlockSpec(memory_space=pltpu.VMEM)
    return pl.pallas_call(
        select_kernel,
        out_shape=jax.ShapeDtypeStruct(lower.shape, lower.dtype),
        in_specs=[pl.BlockSpec(memory_space=pltpu.SMEM), whole, whole] + [anywhere] * len(others),
        out_specs=whole,
        cost_estimate=busy(0.8),
    )(jnp.reshape(half, (1,)).astype(jnp.int32), lower, upper, *others)


def after_kernel(*refs):
    del refs


def after(value, *others):
    anywhere = pl.BlockSpec(memory_space=pl.ANY)
    return pl.pallas_call(
        after_kernel,
        out_shape=jax.ShapeDtypeStruct(value.shape, value.dtype),
        in_specs=[anywhere] * (1 + len(others)),
        out_specs=anywhere,
        input_output_aliases={0: 0},
        cost_estimate=busy(0.3),
    )(value, *others)


def mask_gather(unit, lefts, owners, halves):
    units = {0: unit}
    step = owners // 2
    masks = []
    while step:
        masks.append(step)
        units[step] = exchange(unit, owners, halves, step)
        step //= 2
    waits = dict(WAITS)
    for step in masks[1:]:
        for mask in [m for m in units if m >= 2 * step and m % (2 * step) == 0]:
            if mask in waits:
                units[mask] = after(units[mask], lefts[waits.pop(mask)])
            units[mask | step] = exchange(units[mask], owners, halves, step)
    return units


def spread(value, devices):
    step = 1
    while step < devices:
        masks = [step] if 2 * step == devices else [step, 2 * step, 3 * step]
        parts = [lax.ppermute(value, BOTH, [(d, d ^ m) for d in range(devices)]) for m in masks]
        for part in parts:
            value = value + part
        step *= 4
    return value


def pack_kernel(order, capacity, blocks, terms, ids_ref, plan_ref, other_plan_ref, *refs):
    left_ref, other_ref, _, *pieces, codes, seen, built, sems = refs
    owners = len(order)
    me, half = ids_ref[0], ids_ref[1]
    rows, width = other_ref.shape[2:]
    start = pl.multiple_of(half * rows, rows)
    parts = rows // PART

    @pl.loop(0, owners)
    def _(owner):
        for index in range(2 * terms * capacity):
            codes[0, owner, index] = 0
            codes[1, owner, index] = blocks

    for stream in range(2 * terms):
        plan = plan_ref if stream < terms else other_plan_ref

        @pl.loop(0, owners)
        def _(owner):
            seen[owner] = 0

        @pl.loop(0, blocks, unroll=4)
        def _(block):
            owner = plan[0, stream % terms, block]
            slot = seen[owner]
            seen[owner] = slot + 1
            codes[0, owner, stream * capacity + slot] = block
            codes[1, owner, stream * capacity + slot] = plan[1, stream % terms, block]

    lane = lax.broadcasted_iota(jnp.int32, (PART, width), 1)
    row = lax.broadcasted_iota(jnp.int32, (PART, width), 0)
    copies = []
    for mask in order:
        owner = me ^ mask
        labels = jnp.zeros((PART, width), jnp.int32)
        for stream in range(2 * terms):
            for slot in range(capacity):
                at = stream * capacity + slot
                block = codes[0, owner, at]
                if stream < terms:
                    value = left_ref[stream, block, pl.ds(start, rows), :]
                else:
                    value = other_ref[stream - terms, block]
                value = pltpu.roll(value.astype(jnp.float32), half * rows, 1)
                built[mask, at * parts : (at + 1) * parts] = value.astype(jnp.bfloat16).reshape(
                    parts, PART, width
                )
                label = jnp.where(row == 0, block, codes[1, owner, at])
                labels = jnp.where(lane == at, label, labels)
        built[mask, 2 * terms * capacity * parts] = labels.astype(jnp.float32).astype(jnp.bfloat16)
        copies.append(pltpu.make_async_copy(built.at[mask], pieces[mask], sems.at[mask]))
        copies[-1].start()
    for copy in copies:
        copy.wait()


def pack(ids, plan, other_plan, left, other, before, order, capacity):
    terms, blocks, rows, width = other.shape
    owners = len(order)
    scalars = pl.BlockSpec(memory_space=pltpu.SMEM)
    whole = pl.BlockSpec(memory_space=pltpu.VMEM)
    anywhere = pl.BlockSpec(memory_space=pl.ANY)
    shape = (2 * terms * capacity * rows // PART + 1, PART, width)
    return pl.pallas_call(
        functools.partial(pack_kernel, order, capacity, blocks, terms),
        out_shape=[jax.ShapeDtypeStruct(shape, jnp.bfloat16)] * owners,
        in_specs=[scalars] * 3 + [whole, whole, anywhere],
        out_specs=[anywhere] * owners,
        scratch_shapes=[
            pltpu.SMEM((2, owners, 2 * terms * capacity), jnp.int32),
            pltpu.SMEM((owners,), jnp.int32),
            pltpu.VMEM((owners,) + shape, jnp.bfloat16),
            pltpu.SemaphoreType.DMA((owners,)),
        ],
        compiler_params=pltpu.CompilerParams(vmem_limit_bytes=VMEM_LIMIT),
        cost_estimate=busy(5.0),
    )(ids, plan, other_plan, left, other, before)


def busy(microseconds):
    return pl.CostEstimate(
        flops=int(1.15e9 * microseconds), bytes_accessed=0, transcendentals=0
    )


def add_products(piece, labels, near, far, rights, total, streams, capacity):
    terms = streams // 2
    blocks, rows, width = near.shape
    parts = rows // PART
    for side in range(2):
        moved, where = [], []
        for stream in range(terms * side, terms * side + terms):
            for slot in range(capacity):
                at = stream * capacity + slot
                source, target = labels[0, at], labels[1, at]
                block = jnp.concatenate([near[source], far[source]], axis=0)
                left = piece[at * parts : (at + 1) * parts].reshape(rows, width)
                product = jnp.dot(left, block, preferred_element_type=jnp.float32)
                moved.append(product.astype(jnp.bfloat16))
                where.append((stream - terms * side, target))
        for value, (term, target) in zip(moved, where):
            total[target] += jnp.dot(
                value,
                rights[side][term, jnp.minimum(target, blocks - 1)],
                preferred_element_type=jnp.float32,
            )


def read_labels(raw, spread_labels, labels, sem):
    spread_labels[...] = raw[:8].astype(jnp.float32).astype(jnp.int32)
    copy = pltpu.make_async_copy(spread_labels, labels, sem)
    copy.start()
    copy.wait()


def first_kernel(first, streams, capacity, chip_ref, piece, near, far, own, other, *refs):
    refs = list(refs)
    total_in = None if first else refs.pop(0)
    if not first:
        refs.pop(0)
    total, kept, spread_labels, labels, label_sem, kept_sem = refs
    keep = pltpu.make_async_copy(piece, kept.at[chip_ref[0]], kept_sem)
    keep.start()
    total[...] = jnp.zeros_like(total) if first else total_in[...]
    read_labels(piece.at[piece.shape[0] - 1], spread_labels, labels, label_sem)
    add_products(piece, labels, near, far, (own, other), total, streams, capacity)
    keep.wait()


def first_group(chip, piece, near, far, rights, total, kept):
    blocks, rows, width = near.shape
    streams = 2 * rights[0].shape[0]
    capacity = (piece.shape[0] - 1) * PART // (streams * rows)
    first = total is None
    whole = pl.BlockSpec(memory_space=pltpu.VMEM)
    anywhere = pl.BlockSpec(memory_space=pl.ANY)
    arrays, specs, aliases = [piece, near, far, *rights], [whole] * 5, {}
    if not first:
        arrays += [total, kept]
        specs += [whole, anywhere]
        aliases = {6: 0, 7: 1}
    return pl.pallas_call(
        functools.partial(first_kernel, first, streams, capacity),
        out_shape=(
            jax.ShapeDtypeStruct((blocks + 1, rows, width), jnp.float32),
            jax.ShapeDtypeStruct((lax.axis_size("sec"),) + piece.shape, piece.dtype),
        ),
        in_specs=[pl.BlockSpec(memory_space=pltpu.SMEM)] + specs,
        out_specs=(whole, anywhere),
        scratch_shapes=[
            pltpu.VMEM((8, width), jnp.int32),
            pltpu.SMEM((8, width), jnp.int32),
            pltpu.SemaphoreType.DMA,
            pltpu.SemaphoreType.DMA,
        ],
        input_output_aliases=aliases,
        compiler_params=pltpu.CompilerParams(vmem_limit_bytes=VMEM_LIMIT),
        cost_estimate=busy(2.5),
    )(jnp.reshape(chip, (1,)).astype(jnp.int32), *arrays)


def second_kernel(sources, first, last, streams, capacity, chips_ref, kept, *refs):
    refs = list(refs)
    rights = [refs.pop(0), refs.pop(0)]
    vectors = [(refs.pop(0), refs.pop(0)) for _ in range(sources)]
    total_in = None if first else refs.pop(0)
    if last:
        out, total = refs.pop(0), refs.pop(0)
    else:
        total, token = refs.pop(0), refs.pop(0)
        token[...] = jnp.zeros_like(token)
    left, right, vector, spread_labels, labels = refs[:5]
    left_sems, right_sems, vector_sems, label_sem = refs[5:]
    blocks = vector.shape[2]

    def left_copy(source):
        return pltpu.make_async_copy(
            kept.at[chips_ref[source]], left.at[source], left_sems.at[source]
        )

    def right_copy(side):
        return pltpu.make_async_copy(rights[side], right.at[side], right_sems.at[side])

    def vector_copy(source, part):
        return pltpu.make_async_copy(
            vectors[source][part], vector.at[source, part], vector_sems.at[source, part]
        )

    for source in range(sources):
        left_copy(source).start()
        for part in range(2):
            vector_copy(source, part).start()
    for side in range(2):
        right_copy(side).start()
    total[...] = jnp.zeros_like(total) if first else total_in[...]
    for source in range(sources):
        left_copy(source).wait()
        read_labels(
            left.at[source, left.shape[1] - 1],
            spread_labels.at[source],
            labels.at[source],
            label_sem,
        )
    for side in range(2):
        right_copy(side).wait()
    for source in range(sources):
        for part in range(2):
            vector_copy(source, part).wait()
        add_products(
            left.at[source],
            labels.at[source],
            vector.at[source, 0],
            vector.at[source, 1],
            (right.at[0], right.at[1]),
            total,
            streams,
            capacity,
        )
    if last:
        out[...] = total[:blocks].astype(out.dtype)


def second_group(chips, kept, vectors, rights, total, last):
    blocks, rows, width = vectors[0][0].shape
    streams = 2 * rights[0].shape[0]
    capacity = (kept.shape[1] - 1) * PART // (streams * rows)
    sources, first = len(vectors), total is None
    arrays = [kept, *rights] + [unit for pair in vectors for unit in pair]
    whole = pl.BlockSpec(memory_space=pltpu.VMEM)
    specs = [pl.BlockSpec(memory_space=pl.ANY)] * len(arrays)
    if not first:
        arrays.append(total)
        specs.append(whole)
    total_shape = (blocks + 1, rows, width)
    scratch = [
        pltpu.VMEM((sources,) + kept.shape[1:], kept.dtype),
        pltpu.VMEM((2,) + rights[0].shape, rights[0].dtype),
        pltpu.VMEM((sources, 2, blocks, rows, width), jnp.bfloat16),
        pltpu.VMEM((sources, 8, width), jnp.int32),
        pltpu.SMEM((sources, 8, width), jnp.int32),
        pltpu.SemaphoreType.DMA((sources,)),
        pltpu.SemaphoreType.DMA((2,)),
        pltpu.SemaphoreType.DMA((sources, 2)),
        pltpu.SemaphoreType.DMA,
    ]
    aliases = {}
    if last:
        out_shape = jax.ShapeDtypeStruct((blocks, rows, width), jnp.bfloat16)
        out_specs = whole
        scratch = [pltpu.VMEM(total_shape, jnp.float32)] + scratch
    else:
        out_shape = (
            jax.ShapeDtypeStruct(total_shape, jnp.float32),
            jax.ShapeDtypeStruct((8, width), jnp.float32),
        )
        out_specs = (whole, whole)
        if not first:
            aliases = {len(arrays): 0}
    return pl.pallas_call(
        functools.partial(second_kernel, sources, first, last, streams, capacity),
        out_shape=out_shape,
        in_specs=[pl.BlockSpec(memory_space=pltpu.SMEM)] + specs,
        out_specs=out_specs,
        scratch_shapes=scratch,
        input_output_aliases=aliases,
        compiler_params=pltpu.CompilerParams(vmem_limit_bytes=VMEM_LIMIT),
        cost_estimate=busy(1.5 + 1.4 * sources),
    )(chips.astype(jnp.int32), *arrays)


def stats_kernel(ids_ref, total_ref, wave_ref, stats_ref):
    blocks = wave_ref.shape[0]
    zero = jnp.zeros(wave_ref.shape[1:], jnp.float32)

    def sums(block, carry):
        cross, own = carry
        wave = wave_ref[block].astype(jnp.float32)
        return cross + wave * total_ref[block], own + wave * wave

    cross, own = lax.fori_loop(0, blocks, sums, (zero, zero), unroll=4)
    cross, own = jnp.sum(cross, keepdims=True), jnp.sum(own, keepdims=True)
    local = jnp.where(own > 0, cross / own, 0.0)

    def squares(block, carry):
        rest = total_ref[block] - local * wave_ref[block].astype(jnp.float32)
        return carry + rest * rest

    about = jnp.sum(lax.fori_loop(0, blocks, squares, zero, unroll=4), keepdims=True)
    lane = lax.broadcasted_iota(jnp.int32, stats_ref.shape, 1)
    row = lax.broadcasted_iota(jnp.int32, stats_ref.shape, 0)
    values = jnp.where(lane == 0, about, jnp.where(lane == 1, cross, jnp.where(lane == 2, own, local)))
    stats_ref[...] = jnp.where((row == ids_ref[2]) & (lane < 4), values, 0.0)


def direction_kernel(entries, total_ref, wave_ref, stats_ref, out_ref, rayleigh_ref):
    blocks = wave_ref.shape[0]
    stats = stats_ref[...]
    about, cross, own, local = (stats[:, lane : lane + 1] for lane in range(4))
    rayleigh = jnp.sum(cross, keepdims=True) / jnp.sum(own, keepdims=True)
    offset = local - rayleigh
    residual_sq = jnp.sum(about + offset * offset * own, keepdims=True)
    factor = lax.rsqrt(residual_sq / entries + 1e-06)
    rayleigh_ref[...] = rayleigh

    @pl.loop(0, blocks, unroll=4)
    def _(block):
        rest = total_ref[block] - rayleigh * wave_ref[block].astype(jnp.float32)
        out_ref[block] = (rest * factor).astype(jnp.bfloat16)


def new_direction(ids, total, wave, owners, halves, entries):
    devices = owners * halves
    scalars = pl.BlockSpec(memory_space=pltpu.SMEM)
    whole = pl.BlockSpec(memory_space=pltpu.VMEM)
    params = pltpu.CompilerParams(vmem_limit_bytes=VMEM_LIMIT)
    stats = pl.pallas_call(
        stats_kernel,
        out_shape=jax.ShapeDtypeStruct((devices, 128), jnp.float32),
        in_specs=[scalars, whole, whole],
        out_specs=whole,
        compiler_params=params,
    )(ids, total, wave)
    stats = spread(stats, devices)
    return pl.pallas_call(
        functools.partial(direction_kernel, entries),
        out_shape=(
            jax.ShapeDtypeStruct(wave.shape, jnp.bfloat16),
            jax.ShapeDtypeStruct((1, 1), jnp.float32),
        ),
        in_specs=[whole] * 3,
        out_specs=(whole, whole),
        compiler_params=params,
    )(total, wave, stats)


def per_device_ring(wavefunction, left_operator, right_operator, target_owner, target_local):
    owners, halves = lax.axis_size("sec"), lax.axis_size("term")
    me, half = lax.axis_index("sec"), lax.axis_index("term")
    terms, blocks, height, width = left_operator.shape
    rows = height // halves
    capacity = 2 * blocks // owners
    place = ring_place(me, owners)
    ids = jnp.stack([me, half, me * halves + half]).astype(jnp.int32)

    own_rows = lax.dynamic_slice_in_dim(wavefunction, half * rows, rows, 1)
    other_rows = lax.dynamic_slice_in_dim(wavefunction, (1 - half) * rows, rows, 1)
    plan = jnp.stack([target_owner[:, :, 0], target_local])
    other_left = swap(
        lax.dynamic_slice_in_dim(left_operator, (1 - half) * rows, rows, 2), owners, halves
    )
    order = [m for m in ORDER if m < owners] + list(range(len(ORDER), owners))
    rights = (right_operator, swap(right_operator, owners, halves))
    pieces = pack(
        ids,
        plan,
        swap(plan, owners, halves),
        left_operator,
        other_left,
        plan,
        order[1:] + order[:1],
        capacity,
    )
    lefts = [pieces[0]]
    for m in range(1, owners):
        piece = pieces[m]
        if m in PIECE_WAITS:
            piece = after(piece, lefts[PIECE_WAITS[m]])
        lefts.append(exchange(piece, owners, halves, m))
    near = mask_gather(own_rows, lefts, owners, halves)
    far = {m: swap(unit, owners, halves) if m else other_rows for m, unit in near.items()}

    total = kept = None
    for m in order:
        total, kept = first_group(me ^ m, lefts[m], near[m], far[m], rights, total, kept)

    entries = blocks * owners * height * width
    direction, rayleigh = new_direction(ids, total, own_rows, owners, halves, entries)
    reach = (owners - 1) // 2

    def add_group(total, units, last):
        chips = jnp.stack([ring_owner(place - s, owners) for s in units])
        vectors = [(unit, swap(unit, owners, halves)) for unit in units.values()]
        return second_group(chips, kept, vectors, rights, total, last)

    ahead = behind = direction
    units = {0: direction}
    total = None
    for step in range(1, reach + 1):
        ahead_next = ring_send(ahead, owners, halves, (1,) * halves)
        behind_next = ring_send(behind, owners, halves, (-1,) * halves)
        total, token = add_group(total, units, False)
        ahead, behind = after(ahead_next, token), behind_next
        units = {step: ahead, -step: behind}
    last = select_half(half, ahead, behind)
    last = ring_send(last, owners, halves, (1, -1))
    total, token = add_group(total, units, False)
    total = add_group(total, {owners // 2: after(last, token)}, True)
    return (total, rayleigh[0])


def slot_codes(target_owner, target_local, owners, capacity):
    terms, blocks = target_local.shape
    owner = target_owner[:, :, 0]
    place = jnp.arange(blocks, dtype=jnp.int32)
    same = (owner[:, :, None] == owner[:, None, :]) & (place[None, :] < place[:, None])[None]
    position = jnp.sum(same.astype(jnp.int32), axis=2)
    hit = (
        owner[:, None, None, :] == jnp.arange(owners, dtype=jnp.int32)[None, :, None, None]
    ) & (position[:, None, None, :] == jnp.arange(capacity, dtype=jnp.int32)[None, None, :, None])
    code = place[None, :] * (2 * blocks) + target_local - blocks
    return blocks + jnp.sum(jnp.where(hit, code[:, None, None, :], 0), axis=3)


def stream_kernel(first, capacity, blocks, code_ref, left_ref, vector_ref, right_ref, *rest):
    total_in, total = (None, rest[0]) if first else rest
    step = pl.program_id(0)
    rows, width = left_ref.shape[2:]

    @pl.when(step == 0)
    def _():
        total[...] = jnp.zeros_like(total) if first else total_in[...]

    for term in range(2):
        moved, where = [], []
        for slot in range(capacity):
            code = code_ref[2 * step + term, slot]
            source, target = lax.div(code, 2 * blocks), lax.rem(code, 2 * blocks)
            block = vector_ref[0, :, source].reshape(2 * rows, width)
            product = jnp.dot(left_ref[term, slot], block, preferred_element_type=jnp.float32)
            moved.append(product.astype(jnp.bfloat16))
            where.append(target)
        for slot in range(capacity):
            target = where[slot]
            total[target] += jnp.dot(
                moved[slot],
                right_ref[term, jnp.minimum(target, blocks - 1)],
                preferred_element_type=jnp.float32,
            )


def stream_chunk(total, codes, left, vector, right):
    owners, _, blocks, rows, width = vector.shape
    capacity = left.shape[1]
    first = total is None
    spec_total = pl.BlockSpec((blocks + 1, rows, width), lambda s, c: (0, 0, 0))
    return pl.pallas_call(
        functools.partial(stream_kernel, first, capacity, blocks),
        out_shape=jax.ShapeDtypeStruct((blocks + 1, rows, width), jnp.float32),
        grid_spec=pltpu.PrefetchScalarGridSpec(
            num_scalar_prefetch=1,
            grid=(owners,),
            in_specs=[
                pl.BlockSpec((2, capacity, rows, width), lambda s, c: (s, 0, 0, 0)),
                pl.BlockSpec((1, 2, blocks, rows, width), lambda s, c: (s, 0, 0, 0, 0)),
                pl.BlockSpec((2, blocks, width, width), lambda s, c: (0, 0, 0, 0)),
            ]
            + ([] if first else [spec_total]),
            out_specs=spec_total,
        ),
        compiler_params=pltpu.CompilerParams(vmem_limit_bytes=32 * 2**20),
        cost_estimate=pl.CostEstimate(
            flops=owners * 2 * capacity * 2 * 2 * rows * width * width,
            bytes_accessed=left.size * 2 + vector.size * 2 + right.size * 2,
            transcendentals=0,
        ),
    )(codes, left, vector, right, *([] if first else [total]))


def per_device_streamed(wavefunction, left_operator, right_operator, target_owner, target_local):
    owners = lax.axis_size("sec")
    halves = lax.axis_size("term")
    me, half = lax.axis_index("sec"), lax.axis_index("term")
    terms, blocks, height, width = left_operator.shape
    rows = height // halves
    capacity = 2 * blocks // owners

    own_rows = lax.dynamic_slice_in_dim(wavefunction, half * rows, rows, 1)
    codes = slot_codes(target_owner, target_local, owners, capacity)
    sources = codes // (2 * blocks)

    moved_left = []
    for k in range(terms):
        pick = sources[k][:, None, :] * halves + jnp.arange(halves, dtype=jnp.int32)[None, :, None]
        pieces = left_operator[k].reshape(blocks * halves, rows, width)[pick.reshape(-1)]
        pieces = pieces.reshape(owners * halves, capacity, rows, width)
        moved_left.append(lax.all_to_all(pieces, BOTH, split_axis=0, concat_axis=0, tiled=True))
    all_codes = lax.all_gather(codes, BOTH, axis=0)
    my_codes = lax.dynamic_index_in_dim(all_codes, me, axis=3 - 1, keepdims=False)
    gathered = lax.all_gather(own_rows, BOTH, axis=0).reshape(owners, halves, blocks, rows, width)
    right = lax.all_gather(right_operator, "term", axis=1)

    def apply(vector):
        total = None
        for k in range(terms):
            total = stream_chunk(total, my_codes[:, k], moved_left[k], vector, right[k])
        return total[:blocks]

    sigma_rows = apply(gathered)
    wave = own_rows.astype(jnp.float32)
    cross, own = jnp.sum(wave * sigma_rows), jnp.sum(wave * wave)
    local = jnp.where(own > 0, cross / own, 0.0)
    about = jnp.sum(jnp.square(sigma_rows - local * wave))
    stats = lax.all_gather(jnp.stack([about, cross, own, local]), BOTH, axis=0)
    rayleigh = jnp.sum(stats[:, 1]) / jnp.sum(stats[:, 2])
    residual_sq = jnp.sum(stats[:, 0] + jnp.square(stats[:, 3] - rayleigh) * stats[:, 2])
    entries = blocks * owners * height * width
    factor = lax.rsqrt(residual_sq / entries + 1e-06)
    direction = ((sigma_rows - rayleigh * wave) * factor).astype(jnp.bfloat16)
    direction = lax.all_gather(direction, BOTH, axis=0).reshape(gathered.shape)
    sigma_two = apply(direction).astype(jnp.bfloat16)
    return (sigma_two, jnp.reshape(rayleigh, (1,)))


def per_device(wavefunction, *operands):
    gathered_bytes = lax.axis_size("sec") * wavefunction.size * wavefunction.dtype.itemsize
    if 2 * gathered_bytes > RING_BYTES:
        return per_device_streamed(wavefunction, *operands)
    return per_device_ring(wavefunction, *operands)


def solution(mesh):
    placed = (
        P(("rep", "sec"), None, None),
        P("term", ("rep", "sec"), None, None),
        P("term", ("rep", "sec"), None, None),
        P("term", ("rep", "sec"), None),
        P("term", ("rep", "sec")),
    )
    return jax.shard_map(
        per_device,
        mesh=mesh,
        in_specs=placed,
        out_specs=(P(("rep", "sec"), "term", None), P("rep")),
        check_vma=False,
    )
```

```python
import functools

import jax
import jax.numpy as jnp
from jax import lax
from jax.experimental import pallas as pl
from jax.experimental.pallas import tpu as pltpu
from jax.sharding import PartitionSpec as P

BOTH = ("sec", "term")
VMEM_LIMIT = 60 * 2**20
PART = 16
ORDER = [0, 4, 5, 1, 2, 6, 3, 7]
WAITS = {4: 1, 2: 5, 6: 2}
PIECE_WAITS = {6: 4, 7: 5}
RING_BYTES = 24 * 2**20


def ring_order(owners):
    if owners % 2:
        return list(range(owners))
    return list(range(0, owners, 2)) + list(range(owners - 1, 0, -2))


def ring_place(owner, owners):
    if owners % 2:
        return owner
    return jnp.where(owner % 2 == 0, owner // 2, owners - 1 - owner // 2)


def ring_owner(place, owners):
    place = place % owners
    if owners % 2:
        return place
    return jnp.where(place < owners // 2, 2 * place, 2 * (owners - 1 - place) + 1)


def permute(value, owners, halves, target, flip=0):
    pairs = [
        (chip * halves + half, target(chip, half) * halves + (half ^ flip))
        for chip in range(owners)
        for half in range(halves)
    ]
    return lax.ppermute(value, BOTH, pairs)


def swap(value, owners, halves):
    return permute(value, owners, halves, lambda chip, half: chip, 1)


def exchange(value, owners, halves, mask):
    return permute(value, owners, halves, lambda chip, half: chip ^ mask)


def ring_send(value, owners, halves, shifts):
    ring = ring_order(owners)
    place = {chip: index for index, chip in enumerate(ring)}
    return permute(
        value, owners, halves, lambda chip, half: ring[(place[chip] + shifts[half]) % owners]
    )


def select_kernel(half_ref, lower_ref, upper_ref, *rest):
    out_ref = rest[-1]
    out_ref[...] = jnp.where(half_ref[0] == 0, lower_ref[...], upper_ref[...])


def select_half(half, lower, upper, *others):
    anywhere = pl.BlockSpec(memory_space=pl.ANY)
    whole = pl.BlockSpec(memory_space=pltpu.VMEM)
    return pl.pallas_call(
        select_kernel,
        out_shape=jax.ShapeDtypeStruct(lower.shape, lower.dtype),
        in_specs=[pl.BlockSpec(memory_space=pltpu.SMEM), whole, whole] + [anywhere] * len(others),
        out_specs=whole,
        cost_estimate=busy(0.8),
    )(jnp.reshape(half, (1,)).astype(jnp.int32), lower, upper, *others)


def after_kernel(*refs):
    del refs


def after(value, *others):
    anywhere = pl.BlockSpec(memory_space=pl.ANY)
    return pl.pallas_call(
        after_kernel,
        out_shape=jax.ShapeDtypeStruct(value.shape, value.dtype),
        in_specs=[anywhere] * (1 + len(others)),
        out_specs=anywhere,
        input_output_aliases={0: 0},
        cost_estimate=busy(0.3),
    )(value, *others)


def mask_gather(unit, lefts, owners, halves):
    units = {0: unit}
    step = owners // 2
    masks = []
    while step:
        masks.append(step)
        units[step] = exchange(unit, owners, halves, step)
        step //= 2
    waits = dict(WAITS)
    for step in masks[1:]:
        for mask in [m for m in units if m >= 2 * step and m % (2 * step) == 0]:
            if mask in waits:
                units[mask] = after(units[mask], lefts[waits.pop(mask)])
            units[mask | step] = exchange(units[mask], owners, halves, step)
    return units


def spread(value, devices):
    step = 1
    while step < devices:
        masks = [step] if 2 * step == devices else [step, 2 * step, 3 * step]
        parts = [lax.ppermute(value, BOTH, [(d, d ^ m) for d in range(devices)]) for m in masks]
        for part in parts:
            value = value + part
        step *= 4
    return value


def pack_kernel(order, capacity, blocks, terms, ids_ref, plan_ref, other_plan_ref, *refs):
    left_ref, other_ref, _, *pieces, codes, seen, built, sems = refs
    owners = len(order)
    me, half = ids_ref[0], ids_ref[1]
    rows, width = other_ref.shape[2:]
    start = pl.multiple_of(half * rows, rows)
    parts = rows // PART

    @pl.loop(0, owners)
    def _(owner):
        for index in range(2 * terms * capacity):
            codes[0, owner, index] = 0
            codes[1, owner, index] = blocks

    for stream in range(2 * terms):
        plan = plan_ref if stream < terms else other_plan_ref

        @pl.loop(0, owners)
        def _(owner):
            seen[owner] = 0

        @pl.loop(0, blocks, unroll=4)
        def _(block):
            owner = plan[0, stream % terms, block]
            slot = seen[owner]
            seen[owner] = slot + 1
            codes[0, owner, stream * capacity + slot] = block
            codes[1, owner, stream * capacity + slot] = plan[1, stream % terms, block]

    lane = lax.broadcasted_iota(jnp.int32, (PART, width), 1)
    row = lax.broadcasted_iota(jnp.int32, (PART, width), 0)
    copies = []
    for mask in order:
        owner = me ^ mask
        labels = jnp.zeros((PART, width), jnp.int32)
        for stream in range(2 * terms):
            for slot in range(capacity):
                at = stream * capacity + slot
                block = codes[0, owner, at]
                if stream < terms:
                    value = left_ref[stream, block, pl.ds(start, rows), :]
                else:
                    value = other_ref[stream - terms, block]
                value = pltpu.roll(value.astype(jnp.float32), half * rows, 1)
                built[mask, at * parts : (at + 1) * parts] = value.astype(jnp.bfloat16).reshape(
                    parts, PART, width
                )
                label = jnp.where(row == 0, block, codes[1, owner, at])
                labels = jnp.where(lane == at, label, labels)
        built[mask, 2 * terms * capacity * parts] = labels.astype(jnp.float32).astype(jnp.bfloat16)
        copies.append(pltpu.make_async_copy(built.at[mask], pieces[mask], sems.at[mask]))
        copies[-1].start()
    for copy in copies:
        copy.wait()


def pack(ids, plan, other_plan, left, other, before, order, capacity):
    terms, blocks, rows, width = other.shape
    owners = len(order)
    scalars = pl.BlockSpec(memory_space=pltpu.SMEM)
    whole = pl.BlockSpec(memory_space=pltpu.VMEM)
    anywhere = pl.BlockSpec(memory_space=pl.ANY)
    shape = (2 * terms * capacity * rows // PART + 1, PART, width)
    return pl.pallas_call(
        functools.partial(pack_kernel, order, capacity, blocks, terms),
        out_shape=[jax.ShapeDtypeStruct(shape, jnp.bfloat16)] * owners,
        in_specs=[scalars] * 3 + [whole, whole, anywhere],
        out_specs=[anywhere] * owners,
        scratch_shapes=[
            pltpu.SMEM((2, owners, 2 * terms * capacity), jnp.int32),
            pltpu.SMEM((owners,), jnp.int32),
            pltpu.VMEM((owners,) + shape, jnp.bfloat16),
            pltpu.SemaphoreType.DMA((owners,)),
        ],
        compiler_params=pltpu.CompilerParams(vmem_limit_bytes=VMEM_LIMIT),
        cost_estimate=busy(5.0),
    )(ids, plan, other_plan, left, other, before)


def busy(microseconds):
    return pl.CostEstimate(
        flops=int(1.15e9 * microseconds), bytes_accessed=0, transcendentals=0
    )


def add_products(piece, labels, near, far, rights, total, streams, capacity):
    terms = streams // 2
    blocks, rows, width = near.shape
    parts = rows // PART
    for side in range(2):
        moved, where = [], []
        for stream in range(terms * side, terms * side + terms):
            for slot in range(capacity):
                at = stream * capacity + slot
                source, target = labels[0, at], labels[1, at]
                block = jnp.concatenate([near[source], far[source]], axis=0)
                left = piece[at * parts : (at + 1) * parts].reshape(rows, width)
                product = jnp.dot(left, block, preferred_element_type=jnp.float32)
                moved.append(product.astype(jnp.bfloat16))
                where.append((stream - terms * side, target))
        for value, (term, target) in zip(moved, where):
            total[target] += jnp.dot(
                value,
                rights[side][term, jnp.minimum(target, blocks - 1)],
                preferred_element_type=jnp.float32,
            )


def read_labels(raw, spread_labels, labels, sem):
    spread_labels[...] = raw[:8].astype(jnp.float32).astype(jnp.int32)
    copy = pltpu.make_async_copy(spread_labels, labels, sem)
    copy.start()
    copy.wait()


def first_kernel(first, streams, capacity, chip_ref, piece, near, far, own, other, *refs):
    refs = list(refs)
    total_in = None if first else refs.pop(0)
    if not first:
        refs.pop(0)
    total, kept, spread_labels, labels, label_sem, kept_sem = refs
    keep = pltpu.make_async_copy(piece, kept.at[chip_ref[0]], kept_sem)
    keep.start()
    total[...] = jnp.zeros_like(total) if first else total_in[...]
    read_labels(piece.at[piece.shape[0] - 1], spread_labels, labels, label_sem)
    add_products(piece, labels, near, far, (own, other), total, streams, capacity)
    keep.wait()


def first_group(chip, piece, near, far, rights, total, kept):
    blocks, rows, width = near.shape
    streams = 2 * rights[0].shape[0]
    capacity = (piece.shape[0] - 1) * PART // (streams * rows)
    first = total is None
    whole = pl.BlockSpec(memory_space=pltpu.VMEM)
    anywhere = pl.BlockSpec(memory_space=pl.ANY)
    arrays, specs, aliases = [piece, near, far, *rights], [whole] * 5, {}
    if not first:
        arrays += [total, kept]
        specs += [whole, anywhere]
        aliases = {6: 0, 7: 1}
    return pl.pallas_call(
        functools.partial(first_kernel, first, streams, capacity),
        out_shape=(
            jax.ShapeDtypeStruct((blocks + 1, rows, width), jnp.float32),
            jax.ShapeDtypeStruct((lax.axis_size("sec"),) + piece.shape, piece.dtype),
        ),
        in_specs=[pl.BlockSpec(memory_space=pltpu.SMEM)] + specs,
        out_specs=(whole, anywhere),
        scratch_shapes=[
            pltpu.VMEM((8, width), jnp.int32),
            pltpu.SMEM((8, width), jnp.int32),
            pltpu.SemaphoreType.DMA,
            pltpu.SemaphoreType.DMA,
        ],
        input_output_aliases=aliases,
        compiler_params=pltpu.CompilerParams(vmem_limit_bytes=VMEM_LIMIT),
        cost_estimate=busy(2.5),
    )(jnp.reshape(chip, (1,)).astype(jnp.int32), *arrays)


def second_kernel(sources, first, last, streams, capacity, chips_ref, kept, *refs):
    refs = list(refs)
    rights = [refs.pop(0), refs.pop(0)]
    vectors = [(refs.pop(0), refs.pop(0)) for _ in range(sources)]
    total_in = None if first else refs.pop(0)
    if last:
        out, total = refs.pop(0), refs.pop(0)
    else:
        total, token = refs.pop(0), refs.pop(0)
        token[...] = jnp.zeros_like(token)
    left, right, vector, spread_labels, labels = refs[:5]
    left_sems, right_sems, vector_sems, label_sem = refs[5:]
    blocks = vector.shape[2]

    def left_copy(source):
        return pltpu.make_async_copy(
            kept.at[chips_ref[source]], left.at[source], left_sems.at[source]
        )

    def right_copy(side):
        return pltpu.make_async_copy(rights[side], right.at[side], right_sems.at[side])

    def vector_copy(source, part):
        return pltpu.make_async_copy(
            vectors[source][part], vector.at[source, part], vector_sems.at[source, part]
        )

    for source in range(sources):
        left_copy(source).start()
        for part in range(2):
            vector_copy(source, part).start()
    for side in range(2):
        right_copy(side).start()
    total[...] = jnp.zeros_like(total) if first else total_in[...]
    for source in range(sources):
        left_copy(source).wait()
        read_labels(
            left.at[source, left.shape[1] - 1],
            spread_labels.at[source],
            labels.at[source],
            label_sem,
        )
    for side in range(2):
        right_copy(side).wait()
    for source in range(sources):
        for part in range(2):
            vector_copy(source, part).wait()
        add_products(
            left.at[source],
            labels.at[source],
            vector.at[source, 0],
            vector.at[source, 1],
            (right.at[0], right.at[1]),
            total,
            streams,
            capacity,
        )
    if last:
        out[...] = total[:blocks].astype(out.dtype)


def second_group(chips, kept, vectors, rights, total, last):
    blocks, rows, width = vectors[0][0].shape
    streams = 2 * rights[0].shape[0]
    capacity = (kept.shape[1] - 1) * PART // (streams * rows)
    sources, first = len(vectors), total is None
    arrays = [kept, *rights] + [unit for pair in vectors for unit in pair]
    whole = pl.BlockSpec(memory_space=pltpu.VMEM)
    specs = [pl.BlockSpec(memory_space=pl.ANY)] * len(arrays)
    if not first:
        arrays.append(total)
        specs.append(whole)
    total_shape = (blocks + 1, rows, width)
    scratch = [
        pltpu.VMEM((sources,) + kept.shape[1:], kept.dtype),
        pltpu.VMEM((2,) + rights[0].shape, rights[0].dtype),
        pltpu.VMEM((sources, 2, blocks, rows, width), jnp.bfloat16),
        pltpu.VMEM((sources, 8, width), jnp.int32),
        pltpu.SMEM((sources, 8, width), jnp.int32),
        pltpu.SemaphoreType.DMA((sources,)),
        pltpu.SemaphoreType.DMA((2,)),
        pltpu.SemaphoreType.DMA((sources, 2)),
        pltpu.SemaphoreType.DMA,
    ]
    aliases = {}
    if last:
        out_shape = jax.ShapeDtypeStruct((blocks, rows, width), jnp.bfloat16)
        out_specs = whole
        scratch = [pltpu.VMEM(total_shape, jnp.float32)] + scratch
    else:
        out_shape = (
            jax.ShapeDtypeStruct(total_shape, jnp.float32),
            jax.ShapeDtypeStruct((8, width), jnp.float32),
        )
        out_specs = (whole, whole)
        if not first:
            aliases = {len(arrays): 0}
    return pl.pallas_call(
        functools.partial(second_kernel, sources, first, last, streams, capacity),
        out_shape=out_shape,
        in_specs=[pl.BlockSpec(memory_space=pltpu.SMEM)] + specs,
        out_specs=out_specs,
        scratch_shapes=scratch,
        input_output_aliases=aliases,
        compiler_params=pltpu.CompilerParams(vmem_limit_bytes=VMEM_LIMIT),
        cost_estimate=busy(1.5 + 1.4 * sources),
    )(chips.astype(jnp.int32), *arrays)


def stats_kernel(ids_ref, total_ref, wave_ref, stats_ref):
    blocks = wave_ref.shape[0]
    zero = jnp.zeros(wave_ref.shape[1:], jnp.float32)

    def sums(block, carry):
        cross, own = carry
        wave = wave_ref[block].astype(jnp.float32)
        return cross + wave * total_ref[block], own + wave * wave

    cross, own = lax.fori_loop(0, blocks, sums, (zero, zero), unroll=4)
    cross, own = jnp.sum(cross, keepdims=True), jnp.sum(own, keepdims=True)
    local = jnp.where(own > 0, cross / own, 0.0)

    def squares(block, carry):
        rest = total_ref[block] - local * wave_ref[block].astype(jnp.float32)
        return carry + rest * rest

    about = jnp.sum(lax.fori_loop(0, blocks, squares, zero, unroll=4), keepdims=True)
    lane = lax.broadcasted_iota(jnp.int32, stats_ref.shape, 1)
    row = lax.broadcasted_iota(jnp.int32, stats_ref.shape, 0)
    values = jnp.where(lane == 0, about, jnp.where(lane == 1, cross, jnp.where(lane == 2, own, local)))
    stats_ref[...] = jnp.where((row == ids_ref[2]) & (lane < 4), values, 0.0)


def direction_kernel(entries, total_ref, wave_ref, stats_ref, out_ref, rayleigh_ref):
    blocks = wave_ref.shape[0]
    stats = stats_ref[...]
    about, cross, own, local = (stats[:, lane : lane + 1] for lane in range(4))
    rayleigh = jnp.sum(cross, keepdims=True) / jnp.sum(own, keepdims=True)
    offset = local - rayleigh
    residual_sq = jnp.sum(about + offset * offset * own, keepdims=True)
    factor = lax.rsqrt(residual_sq / entries + 1e-06)
    rayleigh_ref[...] = rayleigh

    @pl.loop(0, blocks, unroll=4)
    def _(block):
        rest = total_ref[block] - rayleigh * wave_ref[block].astype(jnp.float32)
        out_ref[block] = (rest * factor).astype(jnp.bfloat16)


def new_direction(ids, total, wave, owners, halves, entries):
    devices = owners * halves
    scalars = pl.BlockSpec(memory_space=pltpu.SMEM)
    whole = pl.BlockSpec(memory_space=pltpu.VMEM)
    params = pltpu.CompilerParams(vmem_limit_bytes=VMEM_LIMIT)
    stats = pl.pallas_call(
        stats_kernel,
        out_shape=jax.ShapeDtypeStruct((devices, 128), jnp.float32),
        in_specs=[scalars, whole, whole],
        out_specs=whole,
        compiler_params=params,
    )(ids, total, wave)
    stats = spread(stats, devices)
    return pl.pallas_call(
        functools.partial(direction_kernel, entries),
        out_shape=(
            jax.ShapeDtypeStruct(wave.shape, jnp.bfloat16),
            jax.ShapeDtypeStruct((1, 1), jnp.float32),
        ),
        in_specs=[whole] * 3,
        out_specs=(whole, whole),
        compiler_params=params,
    )(total, wave, stats)


def per_device_ring(wavefunction, left_operator, right_operator, target_owner, target_local):
    owners, halves = lax.axis_size("sec"), lax.axis_size("term")
    me, half = lax.axis_index("sec"), lax.axis_index("term")
    terms, blocks, height, width = left_operator.shape
    rows = height // halves
    capacity = 2 * blocks // owners
    place = ring_place(me, owners)
    ids = jnp.stack([me, half, me * halves + half]).astype(jnp.int32)

    own_rows = lax.dynamic_slice_in_dim(wavefunction, half * rows, rows, 1)
    other_rows = lax.dynamic_slice_in_dim(wavefunction, (1 - half) * rows, rows, 1)
    plan = jnp.stack([target_owner[:, :, 0], target_local])
    other_left = swap(
        lax.dynamic_slice_in_dim(left_operator, (1 - half) * rows, rows, 2), owners, halves
    )
    order = [m for m in ORDER if m < owners] + list(range(len(ORDER), owners))
    rights = (right_operator, swap(right_operator, owners, halves))
    pieces = pack(
        ids,
        plan,
        swap(plan, owners, halves),
        left_operator,
        other_left,
        plan,
        order[1:] + order[:1],
        capacity,
    )
    lefts = [pieces[0]]
    for m in range(1, owners):
        piece = pieces[m]
        if m in PIECE_WAITS:
            piece = after(piece, lefts[PIECE_WAITS[m]])
        lefts.append(exchange(piece, owners, halves, m))
    near = mask_gather(own_rows, lefts, owners, halves)
    far = {m: swap(unit, owners, halves) if m else other_rows for m, unit in near.items()}

    total = kept = None
    for m in order:
        total, kept = first_group(me ^ m, lefts[m], near[m], far[m], rights, total, kept)

    entries = blocks * owners * height * width
    direction, rayleigh = new_direction(ids, total, own_rows, owners, halves, entries)
    reach = (owners - 1) // 2

    def add_group(total, units, last):
        chips = jnp.stack([ring_owner(place - s, owners) for s in units])
        vectors = [(unit, swap(unit, owners, halves)) for unit in units.values()]
        return second_group(chips, kept, vectors, rights, total, last)

    ahead = behind = direction
    units = {0: direction}
    total = None
    for step in range(1, reach + 1):
        ahead_next = ring_send(ahead, owners, halves, (1,) * halves)
        behind_next = ring_send(behind, owners, halves, (-1,) * halves)
        total, token = add_group(total, units, False)
        ahead, behind = after(ahead_next, token), behind_next
        units = {step: ahead, -step: behind}
    last = select_half(half, ahead, behind)
    last = ring_send(last, owners, halves, (1, -1))
    total, token = add_group(total, units, False)
    total = add_group(total, {owners // 2: after(last, token)}, True)
    return (total, rayleigh[0])


def slot_codes(target_owner, target_local, owners, capacity):
    terms, blocks = target_local.shape
    owner = target_owner[:, :, 0]
    place = jnp.arange(blocks, dtype=jnp.int32)
    same = (owner[:, :, None] == owner[:, None, :]) & (place[None, :] < place[:, None])[None]
    position = jnp.sum(same.astype(jnp.int32), axis=2)
    hit = (
        owner[:, None, None, :] == jnp.arange(owners, dtype=jnp.int32)[None, :, None, None]
    ) & (position[:, None, None, :] == jnp.arange(capacity, dtype=jnp.int32)[None, None, :, None])
    code = place[None, :] * (2 * blocks) + target_local - blocks
    return blocks + jnp.sum(jnp.where(hit, code[:, None, None, :], 0), axis=3)


def stream_kernel(first, capacity, blocks, code_ref, left_ref, vector_ref, right_ref, *rest):
    total_in, total = (None, rest[0]) if first else rest
    step = pl.program_id(0)
    rows, width = left_ref.shape[2:]

    @pl.when(step == 0)
    def _():
        total[...] = jnp.zeros_like(total) if first else total_in[...]

    for term in range(2):
        moved, where = [], []
        for slot in range(capacity):
            code = code_ref[2 * step + term, slot]
            source, target = lax.div(code, 2 * blocks), lax.rem(code, 2 * blocks)
            block = vector_ref[0, :, source].reshape(2 * rows, width)
            product = jnp.dot(left_ref[term, slot], block, preferred_element_type=jnp.float32)
            moved.append(product.astype(jnp.bfloat16))
            where.append(target)
        for slot in range(capacity):
            target = where[slot]
            total[target] += jnp.dot(
                moved[slot],
                right_ref[term, jnp.minimum(target, blocks - 1)],
                preferred_element_type=jnp.float32,
            )


def stream_chunk(total, codes, left, vector, right):
    owners, _, blocks, rows, width = vector.shape
    capacity = left.shape[1]
    first = total is None
    spec_total = pl.BlockSpec((blocks + 1, rows, width), lambda s, c: (0, 0, 0))
    return pl.pallas_call(
        functools.partial(stream_kernel, first, capacity, blocks),
        out_shape=jax.ShapeDtypeStruct((blocks + 1, rows, width), jnp.float32),
        grid_spec=pltpu.PrefetchScalarGridSpec(
            num_scalar_prefetch=1,
            grid=(owners,),
            in_specs=[
                pl.BlockSpec((2, capacity, rows, width), lambda s, c: (s, 0, 0, 0)),
                pl.BlockSpec((1, 2, blocks, rows, width), lambda s, c: (s, 0, 0, 0, 0)),
                pl.BlockSpec((2, blocks, width, width), lambda s, c: (0, 0, 0, 0)),
            ]
            + ([] if first else [spec_total]),
            out_specs=spec_total,
        ),
        compiler_params=pltpu.CompilerParams(vmem_limit_bytes=32 * 2**20),
        cost_estimate=pl.CostEstimate(
            flops=owners * 2 * capacity * 2 * 2 * rows * width * width,
            bytes_accessed=left.size * 2 + vector.size * 2 + right.size * 2,
            transcendentals=0,
        ),
    )(codes, left, vector, right, *([] if first else [total]))


def per_device_streamed(wavefunction, left_operator, right_operator, target_owner, target_local):
    owners = lax.axis_size("sec")
    halves = lax.axis_size("term")
    me, half = lax.axis_index("sec"), lax.axis_index("term")
    terms, blocks, height, width = left_operator.shape
    rows = height // halves
    capacity = 2 * blocks // owners

    own_rows = lax.dynamic_slice_in_dim(wavefunction, half * rows, rows, 1)
    codes = slot_codes(target_owner, target_local, owners, capacity)
    sources = codes // (2 * blocks)

    moved_left = []
    for k in range(terms):
        pick = sources[k][:, None, :] * halves + jnp.arange(halves, dtype=jnp.int32)[None, :, None]
        pieces = left_operator[k].reshape(blocks * halves, rows, width)[pick.reshape(-1)]
        pieces = pieces.reshape(owners * halves, capacity, rows, width)
        moved_left.append(lax.all_to_all(pieces, BOTH, split_axis=0, concat_axis=0, tiled=True))
    all_codes = lax.all_gather(codes, BOTH, axis=0)
    my_codes = lax.dynamic_index_in_dim(all_codes, me, axis=3 - 1, keepdims=False)
    gathered = lax.all_gather(own_rows, BOTH, axis=0).reshape(owners, halves, blocks, rows, width)
    right = lax.all_gather(right_operator, "term", axis=1)

    def apply(vector):
        total = None
        for k in range(terms):
            total = stream_chunk(total, my_codes[:, k], moved_left[k], vector, right[k])
        return total[:blocks]

    sigma_rows = apply(gathered)
    wave = own_rows.astype(jnp.float32)
    cross, own = jnp.sum(wave * sigma_rows), jnp.sum(wave * wave)
    local = jnp.where(own > 0, cross / own, 0.0)
    about = jnp.sum(jnp.square(sigma_rows - local * wave))
    stats = lax.all_gather(jnp.stack([about, cross, own, local]), BOTH, axis=0)
    rayleigh = jnp.sum(stats[:, 1]) / jnp.sum(stats[:, 2])
    residual_sq = jnp.sum(stats[:, 0] + jnp.square(stats[:, 3] - rayleigh) * stats[:, 2])
    entries = blocks * owners * height * width
    factor = lax.rsqrt(residual_sq / entries + 1e-06)
    direction = ((sigma_rows - rayleigh * wave) * factor).astype(jnp.bfloat16)
    direction = lax.all_gather(direction, BOTH, axis=0).reshape(gathered.shape)
    sigma_two = apply(direction).astype(jnp.bfloat16)
    return (sigma_two, jnp.reshape(rayleigh, (1,)))


def per_device(wavefunction, *operands):
    gathered_bytes = lax.axis_size("sec") * wavefunction.size * wavefunction.dtype.itemsize
    if 2 * gathered_bytes > RING_BYTES:
        return per_device_streamed(wavefunction, *operands)
    return per_device_ring(wavefunction, *operands)


def solution(mesh):
    placed = (
        P(("rep", "sec"), None, None),
        P("term", ("rep", "sec"), None, None),
        P("term", ("rep", "sec"), None, None),
        P("term", ("rep", "sec"), None),
        P("term", ("rep", "sec")),
    )
    return jax.shard_map(
        per_device,
        mesh=mesh,
        in_specs=placed,
        out_specs=(P(("rep", "sec"), "term", None), P("rep")),
        check_vma=False,
    )
```

```python
import functools

import jax
import jax.numpy as jnp
from jax import lax
from jax.experimental import pallas as pl
from jax.experimental.pallas import tpu as pltpu
from jax.sharding import PartitionSpec as P

BOTH = ("sec", "term")
VMEM_LIMIT = 60 * 2**20
PART = 16
ORDER = [0, 4, 5, 1, 2, 6, 3, 7]
WAITS = {4: 1, 2: 5, 6: 2}
PIECE_WAITS = {6: 4, 7: 5}
RING_BYTES = 24 * 2**20


def ring_order(owners):
    if owners % 2:
        return list(range(owners))
    return list(range(0, owners, 2)) + list(range(owners - 1, 0, -2))


def ring_place(owner, owners):
    if owners % 2:
        return owner
    return jnp.where(owner % 2 == 0, owner // 2, owners - 1 - owner // 2)


def ring_owner(place, owners):
    place = place % owners
    if owners % 2:
        return place
    return jnp.where(place < owners // 2, 2 * place, 2 * (owners - 1 - place) + 1)


def permute(value, owners, halves, target, flip=0):
    pairs = [
        (chip * halves + half, target(chip, half) * halves + (half ^ flip))
        for chip in range(owners)
        for half in range(halves)
    ]
    return lax.ppermute(value, BOTH, pairs)


def swap(value, owners, halves):
    return permute(value, owners, halves, lambda chip, half: chip, 1)


def exchange(value, owners, halves, mask):
    return permute(value, owners, halves, lambda chip, half: chip ^ mask)


def ring_send(value, owners, halves, shifts):
    ring = ring_order(owners)
    place = {chip: index for index, chip in enumerate(ring)}
    return permute(
        value, owners, halves, lambda chip, half: ring[(place[chip] + shifts[half]) % owners]
    )


def select_kernel(half_ref, lower_ref, upper_ref, *rest):
    out_ref = rest[-1]
    out_ref[...] = jnp.where(half_ref[0] == 0, lower_ref[...], upper_ref[...])


def select_half(half, lower, upper, *others):
    anywhere = pl.BlockSpec(memory_space=pl.ANY)
    whole = pl.BlockSpec(memory_space=pltpu.VMEM)
    return pl.pallas_call(
        select_kernel,
        out_shape=jax.ShapeDtypeStruct(lower.shape, lower.dtype),
        in_specs=[pl.BlockSpec(memory_space=pltpu.SMEM), whole, whole] + [anywhere] * len(others),
        out_specs=whole,
        cost_estimate=busy(0.8),
    )(jnp.reshape(half, (1,)).astype(jnp.int32), lower, upper, *others)


def after_kernel(*refs):
    del refs


def after(value, *others):
    anywhere = pl.BlockSpec(memory_space=pl.ANY)
    return pl.pallas_call(
        after_kernel,
        out_shape=jax.ShapeDtypeStruct(value.shape, value.dtype),
        in_specs=[anywhere] * (1 + len(others)),
        out_specs=anywhere,
        input_output_aliases={0: 0},
        cost_estimate=busy(0.3),
    )(value, *others)


def mask_gather(unit, lefts, owners, halves):
    units = {0: unit}
    step = owners // 2
    masks = []
    while step:
        masks.append(step)
        units[step] = exchange(unit, owners, halves, step)
        step //= 2
    waits = dict(WAITS)
    for step in masks[1:]:
        for mask in [m for m in units if m >= 2 * step and m % (2 * step) == 0]:
            if mask in waits:
                units[mask] = after(units[mask], lefts[waits.pop(mask)])
            units[mask | step] = exchange(units[mask], owners, halves, step)
    return units


def spread(value, devices):
    step = 1
    while step < devices:
        masks = [step] if 2 * step == devices else [step, 2 * step, 3 * step]
        parts = [lax.ppermute(value, BOTH, [(d, d ^ m) for d in range(devices)]) for m in masks]
        for part in parts:
            value = value + part
        step *= 4
    return value


def pack_kernel(order, capacity, blocks, terms, ids_ref, plan_ref, other_plan_ref, *refs):
    left_ref, other_ref, _, *pieces, codes, seen, built, sems = refs
    owners = len(order)
    me, half = ids_ref[0], ids_ref[1]
    rows, width = other_ref.shape[2:]
    start = pl.multiple_of(half * rows, rows)
    parts = rows // PART

    @pl.loop(0, owners)
    def _(owner):
        for index in range(2 * terms * capacity):
            codes[0, owner, index] = 0
            codes[1, owner, index] = blocks

    for stream in range(2 * terms):
        plan = plan_ref if stream < terms else other_plan_ref

        @pl.loop(0, owners)
        def _(owner):
            seen[owner] = 0

        @pl.loop(0, blocks, unroll=4)
        def _(block):
            owner = plan[0, stream % terms, block]
            slot = seen[owner]
            seen[owner] = slot + 1
            codes[0, owner, stream * capacity + slot] = block
            codes[1, owner, stream * capacity + slot] = plan[1, stream % terms, block]

    lane = lax.broadcasted_iota(jnp.int32, (PART, width), 1)
    row = lax.broadcasted_iota(jnp.int32, (PART, width), 0)
    copies = []
    for mask in order:
        owner = me ^ mask
        labels = jnp.zeros((PART, width), jnp.int32)
        for stream in range(2 * terms):
            for slot in range(capacity):
                at = stream * capacity + slot
                block = codes[0, owner, at]
                if stream < terms:
                    value = left_ref[stream, block, pl.ds(start, rows), :]
                else:
                    value = other_ref[stream - terms, block]
                built[mask, at * parts : (at + 1) * parts] = value.reshape(parts, PART, width)
                label = jnp.where(row == 0, block, codes[1, owner, at])
                labels = jnp.where(lane == at, label, labels)
        built[mask, 2 * terms * capacity * parts] = labels.astype(jnp.float32).astype(jnp.bfloat16)
        copies.append(pltpu.make_async_copy(built.at[mask], pieces[mask], sems.at[mask]))
        copies[-1].start()
    for copy in copies:
        copy.wait()


def pack(ids, plan, other_plan, left, other, before, order, capacity):
    terms, blocks, rows, width = other.shape
    owners = len(order)
    scalars = pl.BlockSpec(memory_space=pltpu.SMEM)
    whole = pl.BlockSpec(memory_space=pltpu.VMEM)
    anywhere = pl.BlockSpec(memory_space=pl.ANY)
    shape = (2 * terms * capacity * rows // PART + 1, PART, width)
    return pl.pallas_call(
        functools.partial(pack_kernel, order, capacity, blocks, terms),
        out_shape=[jax.ShapeDtypeStruct(shape, jnp.bfloat16)] * owners,
        in_specs=[scalars] * 3 + [whole, whole, anywhere],
        out_specs=[anywhere] * owners,
        scratch_shapes=[
            pltpu.SMEM((2, owners, 2 * terms * capacity), jnp.int32),
            pltpu.SMEM((owners,), jnp.int32),
            pltpu.VMEM((owners,) + shape, jnp.bfloat16),
            pltpu.SemaphoreType.DMA((owners,)),
        ],
        compiler_params=pltpu.CompilerParams(vmem_limit_bytes=VMEM_LIMIT),
        cost_estimate=busy(5.0),
    )(ids, plan, other_plan, left, other, before)


def busy(microseconds):
    return pl.CostEstimate(
        flops=int(1.15e9 * microseconds), bytes_accessed=0, transcendentals=0
    )


def add_products(left, labels, vector, right, total, side, terms, capacity):
    blocks, rows, width = vector.shape[1:]
    parts = rows // PART
    moved, where = [], []
    for slot in range(terms * capacity):
        at = side * terms * capacity + slot
        block = vector[:, labels[0, at]].reshape(2 * rows, width)
        piece = left[at * parts : (at + 1) * parts].reshape(rows, width)
        product = jnp.dot(piece, block, preferred_element_type=jnp.float32)
        moved.append(product.astype(jnp.bfloat16))
        where.append(labels[1, at])
    for slot in range(terms * capacity):
        target = where[slot]
        total[target] += jnp.dot(
            moved[slot],
            right[slot // capacity, jnp.minimum(target, blocks - 1)],
            preferred_element_type=jnp.float32,
        )


def local_stats(total, wave_ref, device, stats_ref):
    blocks = wave_ref.shape[0]
    zero = jnp.zeros(wave_ref.shape[1:], jnp.float32)

    def sums(block, carry):
        cross, own = carry
        wave = wave_ref[block].astype(jnp.float32)
        return cross + wave * total[block], own + wave * wave

    cross, own = lax.fori_loop(0, blocks, sums, (zero, zero), unroll=4)
    cross, own = jnp.sum(cross, keepdims=True), jnp.sum(own, keepdims=True)
    local = jnp.where(own > 0, cross / own, 0.0)

    def squares(block, carry):
        rest = total[block] - local * wave_ref[block].astype(jnp.float32)
        return carry + rest * rest

    about = jnp.sum(lax.fori_loop(0, blocks, squares, zero, unroll=4), keepdims=True)
    lane = lax.broadcasted_iota(jnp.int32, stats_ref.shape, 1)
    row = lax.broadcasted_iota(jnp.int32, stats_ref.shape, 0)
    values = jnp.where(lane == 0, about, jnp.where(lane == 1, cross, jnp.where(lane == 2, own, local)))
    stats_ref[...] = jnp.where((row == device) & (lane < 4), values, 0.0)


def apply_kernel(sources, choices, first, end, terms, capacity, ids_ref, *refs):
    refs = list(refs)

    def take(count):
        taken, refs[:count] = refs[:count], []
        return taken

    lefts = take(choices or sources)
    rights = take(2)
    vectors = [take(2) for _ in range(sources)]
    (wave_in,) = take(1) if end == "stats" else (None,)
    (total_in,) = (None,) if first else take(1)
    (total_out,) = (None,) if end == "result" else take(1)
    (last_out,) = take(1)
    total, left, right, vector, raw, spread_labels, labels = take(7)
    left_sems, right_sems, vector_sems, raw_sems, label_sem, total_sem = take(6)
    (wave, wave_sem) = take(2) if end == "stats" else (None, None)
    half = ids_ref[0]
    blocks = vector.shape[2]
    parts = left.shape[1]

    def left_copies(source, piece):
        return [
            pltpu.make_async_copy(piece.at[parts], raw.at[source], raw_sems.at[source]),
            pltpu.make_async_copy(
                piece.at[pl.ds(0, parts)], left.at[source], left_sems.at[source]
            ),
        ]

    def vector_copies(source):
        return [
            pltpu.make_async_copy(
                vectors[source][part],
                vector.at[source, half if part == 0 else 1 - half],
                vector_sems.at[source, part],
            )
            for part in range(2)
        ]

    def right_copy(side):
        return pltpu.make_async_copy(rights[side], right.at[side], right_sems.at[side])

    for source in range(sources):
        if choices:
            for choice, piece in enumerate(lefts):

                @pl.when(ids_ref[2 + source] == choice)
                def _():
                    for copy in left_copies(source, piece):
                        copy.start()

        else:
            for copy in left_copies(source, lefts[source]):
                copy.start()
    for copy in [*vector_copies(0), right_copy(0)]:
        copy.start()
    for source in range(1, sources):
        for copy in vector_copies(source):
            copy.start()
    right_copy(1).start()
    if first:
        total[...] = jnp.zeros_like(total)
    else:
        load_total = pltpu.make_async_copy(total_in, total, total_sem)
        load_total.start()
    if end == "stats":
        load_wave = pltpu.make_async_copy(wave_in, wave, wave_sem)
        load_wave.start()
    if end == "go on":
        last_out[...] = jnp.zeros_like(last_out)

    for source in range(sources):
        left_copies(source, lefts[0])[0].wait()
    spread_labels[...] = raw[:, :8].astype(jnp.float32).astype(jnp.int32)
    move_labels = pltpu.make_async_copy(spread_labels, labels, label_sem)
    move_labels.start()
    move_labels.wait()
    if not first:
        load_total.wait()
    for side in range(2):
        right_copy(side).wait()
        for source in range(sources):
            if side == 0:
                left_copies(source, lefts[0])[1].wait()
                for copy in vector_copies(source):
                    copy.wait()
            add_products(
                left.at[source],
                labels.at[source],
                vector.at[source],
                right.at[side],
                total,
                side,
                terms,
                capacity,
            )
    if end == "result":
        last_out[...] = total[:blocks].astype(last_out.dtype)
    else:
        store_total = pltpu.make_async_copy(total, total_out, total_sem)
        store_total.start()
        if end == "stats":
            load_wave.wait()
            local_stats(total, wave, ids_ref[1], last_out)
        store_total.wait()


def apply_group(ids, lefts, rights, vectors, total, end, wave=None):
    blocks, rows, width = vectors[0][0].shape
    terms = rights[0].shape[0]
    parts = lefts[0].shape[0] - 1
    capacity = parts * PART // (2 * terms * rows)
    sources, first = len(vectors), total is None
    arrays = [*lefts, *rights] + [unit for pair in vectors for unit in pair]
    arrays += [wave] if end == "stats" else []
    arrays += [] if first else [total]
    whole = pl.BlockSpec(memory_space=pltpu.VMEM)
    anywhere = pl.BlockSpec(memory_space=pl.ANY)
    total_shape = (blocks + 1, rows, width)
    scratch = [
        pltpu.VMEM(total_shape, jnp.float32),
        pltpu.VMEM((sources, parts, PART, width), jnp.bfloat16),
        pltpu.VMEM((2,) + rights[0].shape, jnp.bfloat16),
        pltpu.VMEM((sources, 2, blocks, rows, width), jnp.bfloat16),
        pltpu.VMEM((sources, PART, width), jnp.bfloat16),
        pltpu.VMEM((sources, 8, width), jnp.int32),
        pltpu.SMEM((sources, 8, width), jnp.int32),
        pltpu.SemaphoreType.DMA((sources,)),
        pltpu.SemaphoreType.DMA((2,)),
        pltpu.SemaphoreType.DMA((sources, 2)),
        pltpu.SemaphoreType.DMA((sources,)),
        pltpu.SemaphoreType.DMA,
        pltpu.SemaphoreType.DMA,
    ]
    if end == "stats":
        scratch += [pltpu.VMEM(wave.shape, wave.dtype), pltpu.SemaphoreType.DMA]
    devices = lax.axis_size("sec") * lax.axis_size("term")
    total_out = jax.ShapeDtypeStruct(total_shape, jnp.float32)
    out_shape, out_specs = {
        "go on": ((total_out, jax.ShapeDtypeStruct((8, width), jnp.float32)), (anywhere, whole)),
        "stats": (
            (total_out, jax.ShapeDtypeStruct((devices, 128), jnp.float32)),
            (anywhere, whole),
        ),
        "result": (jax.ShapeDtypeStruct((blocks, rows, width), jnp.bfloat16), whole),
    }[end]
    choices = len(lefts) if ids.shape[0] > 2 else 0
    return pl.pallas_call(
        functools.partial(apply_kernel, sources, choices, first, end, terms, capacity),
        out_shape=out_shape,
        in_specs=[pl.BlockSpec(memory_space=pltpu.SMEM)] + [anywhere] * len(arrays),
        out_specs=out_specs,
        scratch_shapes=scratch,
        compiler_params=pltpu.CompilerParams(vmem_limit_bytes=VMEM_LIMIT),
        cost_estimate=busy(2.0 + 1.4 * sources),
    )(ids, *arrays)


def direction_kernel(entries, total_ref, wave_ref, stats_ref, out_ref, rayleigh_ref):
    blocks = wave_ref.shape[0]
    stats = stats_ref[...]
    about, cross, own, local = (stats[:, lane : lane + 1] for lane in range(4))
    rayleigh = jnp.sum(cross, keepdims=True) / jnp.sum(own, keepdims=True)
    offset = local - rayleigh
    residual_sq = jnp.sum(about + offset * offset * own, keepdims=True)
    factor = lax.rsqrt(residual_sq / entries + 1e-06)
    rayleigh_ref[...] = rayleigh

    @pl.loop(0, blocks, unroll=4)
    def _(block):
        rest = total_ref[block] - rayleigh * wave_ref[block].astype(jnp.float32)
        out_ref[block] = (rest * factor).astype(jnp.bfloat16)


def new_direction(total, wave, stats, entries):
    whole = pl.BlockSpec(memory_space=pltpu.VMEM)
    return pl.pallas_call(
        functools.partial(direction_kernel, entries),
        out_shape=(
            jax.ShapeDtypeStruct(wave.shape, jnp.bfloat16),
            jax.ShapeDtypeStruct((1, 1), jnp.float32),
        ),
        in_specs=[whole] * 3,
        out_specs=(whole, whole),
        compiler_params=pltpu.CompilerParams(vmem_limit_bytes=VMEM_LIMIT),
        cost_estimate=busy(2.0),
    )(total, wave, stats)


def per_device_ring(wavefunction, left_operator, right_operator, target_owner, target_local):
    owners, halves = lax.axis_size("sec"), lax.axis_size("term")
    me, half = lax.axis_index("sec"), lax.axis_index("term")
    terms, blocks, height, width = left_operator.shape
    rows = height // halves
    capacity = 2 * blocks // owners
    place = ring_place(me, owners)
    ids = jnp.stack([me, half]).astype(jnp.int32)

    own_rows = lax.dynamic_slice_in_dim(wavefunction, half * rows, rows, 1)
    other_rows = lax.dynamic_slice_in_dim(wavefunction, (1 - half) * rows, rows, 1)
    plan = jnp.stack([target_owner[:, :, 0], target_local])
    other_left = swap(
        lax.dynamic_slice_in_dim(left_operator, (1 - half) * rows, rows, 2), owners, halves
    )
    order = [m for m in ORDER if m < owners] + list(range(len(ORDER), owners))
    rights = (right_operator, swap(right_operator, owners, halves))
    pieces = pack(
        ids,
        plan,
        swap(plan, owners, halves),
        left_operator,
        other_left,
        plan,
        order[1:] + order[:1],
        capacity,
    )
    lefts = [pieces[0]]
    for m in range(1, owners):
        piece = pieces[m]
        if m in PIECE_WAITS:
            piece = after(piece, lefts[PIECE_WAITS[m]])
        lefts.append(exchange(piece, owners, halves, m))
    near = mask_gather(own_rows, lefts, owners, halves)
    far = {m: swap(unit, owners, halves) if m else other_rows for m, unit in near.items()}

    here = [half, me * halves + half]
    no_choice = jnp.stack(here).astype(jnp.int32)
    total = None
    for at in range(0, owners, 2):
        group = order[at : at + 2]
        total, stats = apply_group(
            no_choice,
            [lefts[m] for m in group],
            rights,
            [(near[m], far[m]) for m in group],
            total,
            "go on" if at + 2 < owners else "stats",
            own_rows,
        )

    entries = blocks * owners * height * width
    stats = spread(stats, owners * halves)
    direction, rayleigh = new_direction(total, own_rows, stats, entries)
    reach = (owners - 1) // 2

    def add_group(total, units, last):
        choices = [me ^ ring_owner(place - s, owners) for s in units]
        vectors = [(unit, swap(unit, owners, halves)) for unit in units.values()]
        ids = jnp.stack(here + choices).astype(jnp.int32)
        return apply_group(ids, lefts, rights, vectors, total, "result" if last else "go on")

    ahead = behind = direction
    units = {0: direction}
    total = None
    for step in range(1, reach + 1):
        ahead_next = ring_send(ahead, owners, halves, (1,) * halves)
        behind_next = ring_send(behind, owners, halves, (-1,) * halves)
        total, token = add_group(total, units, False)
        ahead, behind = after(ahead_next, token), behind_next
        units = {step: ahead, -step: behind}
    last = select_half(half, ahead, behind)
    last = ring_send(last, owners, halves, (1, -1))
    total, token = add_group(total, units, False)
    total = add_group(total, {owners // 2: after(last, token)}, True)
    return (total, rayleigh[0])


def slot_codes(target_owner, target_local, owners, capacity):
    terms, blocks = target_local.shape
    owner = target_owner[:, :, 0]
    place = jnp.arange(blocks, dtype=jnp.int32)
    same = (owner[:, :, None] == owner[:, None, :]) & (place[None, :] < place[:, None])[None]
    position = jnp.sum(same.astype(jnp.int32), axis=2)
    hit = (
        owner[:, None, None, :] == jnp.arange(owners, dtype=jnp.int32)[None, :, None, None]
    ) & (position[:, None, None, :] == jnp.arange(capacity, dtype=jnp.int32)[None, None, :, None])
    code = place[None, :] * (2 * blocks) + target_local - blocks
    return blocks + jnp.sum(jnp.where(hit, code[:, None, None, :], 0), axis=3)


def stream_kernel(first, capacity, blocks, code_ref, left_ref, vector_ref, right_ref, *rest):
    total_in, total = (None, rest[0]) if first else rest
    step = pl.program_id(0)
    rows, width = left_ref.shape[2:]

    @pl.when(step == 0)
    def _():
        total[...] = jnp.zeros_like(total) if first else total_in[...]

    for term in range(2):
        moved, where = [], []
        for slot in range(capacity):
            code = code_ref[2 * step + term, slot]
            source, target = lax.div(code, 2 * blocks), lax.rem(code, 2 * blocks)
            block = vector_ref[0, :, source].reshape(2 * rows, width)
            product = jnp.dot(left_ref[term, slot], block, preferred_element_type=jnp.float32)
            moved.append(product.astype(jnp.bfloat16))
            where.append(target)
        for slot in range(capacity):
            target = where[slot]
            total[target] += jnp.dot(
                moved[slot],
                right_ref[term, jnp.minimum(target, blocks - 1)],
                preferred_element_type=jnp.float32,
            )


def stream_chunk(total, codes, left, vector, right):
    owners, _, blocks, rows, width = vector.shape
    capacity = left.shape[1]
    first = total is None
    spec_total = pl.BlockSpec((blocks + 1, rows, width), lambda s, c: (0, 0, 0))
    return pl.pallas_call(
        functools.partial(stream_kernel, first, capacity, blocks),
        out_shape=jax.ShapeDtypeStruct((blocks + 1, rows, width), jnp.float32),
        grid_spec=pltpu.PrefetchScalarGridSpec(
            num_scalar_prefetch=1,
            grid=(owners,),
            in_specs=[
                pl.BlockSpec((2, capacity, rows, width), lambda s, c: (s, 0, 0, 0)),
                pl.BlockSpec((1, 2, blocks, rows, width), lambda s, c: (s, 0, 0, 0, 0)),
                pl.BlockSpec((2, blocks, width, width), lambda s, c: (0, 0, 0, 0)),
            ]
            + ([] if first else [spec_total]),
            out_specs=spec_total,
        ),
        compiler_params=pltpu.CompilerParams(vmem_limit_bytes=32 * 2**20),
        cost_estimate=pl.CostEstimate(
            flops=owners * 2 * capacity * 2 * 2 * rows * width * width,
            bytes_accessed=left.size * 2 + vector.size * 2 + right.size * 2,
            transcendentals=0,
        ),
    )(codes, left, vector, right, *([] if first else [total]))


def per_device_streamed(wavefunction, left_operator, right_operator, target_owner, target_local):
    owners = lax.axis_size("sec")
    halves = lax.axis_size("term")
    me, half = lax.axis_index("sec"), lax.axis_index("term")
    terms, blocks, height, width = left_operator.shape
    rows = height // halves
    capacity = 2 * blocks // owners

    own_rows = lax.dynamic_slice_in_dim(wavefunction, half * rows, rows, 1)
    codes = slot_codes(target_owner, target_local, owners, capacity)
    sources = codes // (2 * blocks)

    moved_left = []
    for k in range(terms):
        pick = sources[k][:, None, :] * halves + jnp.arange(halves, dtype=jnp.int32)[None, :, None]
        pieces = left_operator[k].reshape(blocks * halves, rows, width)[pick.reshape(-1)]
        pieces = pieces.reshape(owners * halves, capacity, rows, width)
        moved_left.append(lax.all_to_all(pieces, BOTH, split_axis=0, concat_axis=0, tiled=True))
    all_codes = lax.all_gather(codes, BOTH, axis=0)
    my_codes = lax.dynamic_index_in_dim(all_codes, me, axis=3 - 1, keepdims=False)
    gathered = lax.all_gather(own_rows, BOTH, axis=0).reshape(owners, halves, blocks, rows, width)
    right = lax.all_gather(right_operator, "term", axis=1)

    def apply(vector):
        total = None
        for k in range(terms):
            total = stream_chunk(total, my_codes[:, k], moved_left[k], vector, right[k])
        return total[:blocks]

    sigma_rows = apply(gathered)
    wave = own_rows.astype(jnp.float32)
    cross, own = jnp.sum(wave * sigma_rows), jnp.sum(wave * wave)
    local = jnp.where(own > 0, cross / own, 0.0)
    about = jnp.sum(jnp.square(sigma_rows - local * wave))
    stats = lax.all_gather(jnp.stack([about, cross, own, local]), BOTH, axis=0)
    rayleigh = jnp.sum(stats[:, 1]) / jnp.sum(stats[:, 2])
    residual_sq = jnp.sum(stats[:, 0] + jnp.square(stats[:, 3] - rayleigh) * stats[:, 2])
    entries = blocks * owners * height * width
    factor = lax.rsqrt(residual_sq / entries + 1e-06)
    direction = ((sigma_rows - rayleigh * wave) * factor).astype(jnp.bfloat16)
    direction = lax.all_gather(direction, BOTH, axis=0).reshape(gathered.shape)
    sigma_two = apply(direction).astype(jnp.bfloat16)
    return (sigma_two, jnp.reshape(rayleigh, (1,)))


def per_device(wavefunction, *operands):
    gathered_bytes = lax.axis_size("sec") * wavefunction.size * wavefunction.dtype.itemsize
    if 2 * gathered_bytes > RING_BYTES:
        return per_device_streamed(wavefunction, *operands)
    return per_device_ring(wavefunction, *operands)


def solution(mesh):
    placed = (
        P(("rep", "sec"), None, None),
        P("term", ("rep", "sec"), None, None),
        P("term", ("rep", "sec"), None, None),
        P("term", ("rep", "sec"), None),
        P("term", ("rep", "sec")),
    )
    return jax.shard_map(
        per_device,
        mesh=mesh,
        in_specs=placed,
        out_specs=(P(("rep", "sec"), "term", None), P("rep")),
        check_vma=False,
    )
```

```python
import functools

import jax
import jax.numpy as jnp
from jax import lax
from jax.experimental import pallas as pl
from jax.experimental.pallas import tpu as pltpu
from jax.sharding import PartitionSpec as P

BOTH = ("sec", "term")
VMEM_LIMIT = 60 * 2**20
PART = 16
ORDER = [0, 4, 5, 1, 2, 6, 3, 7]
WAITS = {4: 1, 2: 5, 6: 2}
PIECE_WAITS = {6: 4, 7: 5}
RING_BYTES = 24 * 2**20


def ring_order(owners):
    if owners % 2:
        return list(range(owners))
    return list(range(0, owners, 2)) + list(range(owners - 1, 0, -2))


def ring_place(owner, owners):
    if owners % 2:
        return owner
    return jnp.where(owner % 2 == 0, owner // 2, owners - 1 - owner // 2)


def ring_owner(place, owners):
    place = place % owners
    if owners % 2:
        return place
    return jnp.where(place < owners // 2, 2 * place, 2 * (owners - 1 - place) + 1)


def permute(value, owners, halves, target, flip=0):
    pairs = [
        (chip * halves + half, target(chip, half) * halves + (half ^ flip))
        for chip in range(owners)
        for half in range(halves)
    ]
    return lax.ppermute(value, BOTH, pairs)


def swap(value, owners, halves):
    return permute(value, owners, halves, lambda chip, half: chip, 1)


def exchange(value, owners, halves, mask):
    return permute(value, owners, halves, lambda chip, half: chip ^ mask)


def ring_send(value, owners, halves, shifts):
    ring = ring_order(owners)
    place = {chip: index for index, chip in enumerate(ring)}
    return permute(
        value, owners, halves, lambda chip, half: ring[(place[chip] + shifts[half]) % owners]
    )


def select_kernel(half_ref, lower_ref, upper_ref, *rest):
    out_ref = rest[-1]
    out_ref[...] = jnp.where(half_ref[0] == 0, lower_ref[...], upper_ref[...])


def select_half(half, lower, upper, *others):
    anywhere = pl.BlockSpec(memory_space=pl.ANY)
    whole = pl.BlockSpec(memory_space=pltpu.VMEM)
    return pl.pallas_call(
        select_kernel,
        out_shape=jax.ShapeDtypeStruct(lower.shape, lower.dtype),
        in_specs=[pl.BlockSpec(memory_space=pltpu.SMEM), whole, whole] + [anywhere] * len(others),
        out_specs=whole,
        cost_estimate=busy(0.8),
    )(jnp.reshape(half, (1,)).astype(jnp.int32), lower, upper, *others)


def after_kernel(*refs):
    del refs


def after(value, *others):
    anywhere = pl.BlockSpec(memory_space=pl.ANY)
    return pl.pallas_call(
        after_kernel,
        out_shape=jax.ShapeDtypeStruct(value.shape, value.dtype),
        in_specs=[anywhere] * (1 + len(others)),
        out_specs=anywhere,
        input_output_aliases={0: 0},
        cost_estimate=busy(0.3),
    )(value, *others)


def mask_gather(unit, lefts, owners, halves):
    units = {0: unit}
    step = owners // 2
    masks = []
    while step:
        masks.append(step)
        units[step] = exchange(unit, owners, halves, step)
        step //= 2
    waits = dict(WAITS)
    for step in masks[1:]:
        for mask in [m for m in units if m >= 2 * step and m % (2 * step) == 0]:
            if mask in waits:
                units[mask] = after(units[mask], lefts[waits.pop(mask)])
            units[mask | step] = exchange(units[mask], owners, halves, step)
    return units


def spread(value, devices):
    step = 1
    while step < devices:
        masks = [step] if 2 * step == devices else [step, 2 * step, 3 * step]
        parts = [lax.ppermute(value, BOTH, [(d, d ^ m) for d in range(devices)]) for m in masks]
        for part in parts:
            value = value + part
        step *= 4
    return value


def pack_kernel(order, capacity, blocks, terms, ids_ref, plan_ref, other_plan_ref, *refs):
    left_ref, other_ref, _, *pieces, codes, seen, built, sems = refs
    owners = len(order)
    me, half = ids_ref[0], ids_ref[1]
    rows, width = other_ref.shape[2:]
    start = pl.multiple_of(half * rows, rows)
    parts = rows // PART

    @pl.loop(0, owners)
    def _(owner):
        for index in range(2 * terms * capacity):
            codes[0, owner, index] = 0
            codes[1, owner, index] = blocks

    for stream in range(2 * terms):
        plan = plan_ref if stream < terms else other_plan_ref

        @pl.loop(0, owners)
        def _(owner):
            seen[owner] = 0

        @pl.loop(0, blocks, unroll=4)
        def _(block):
            owner = plan[0, stream % terms, block]
            slot = seen[owner]
            seen[owner] = slot + 1
            codes[0, owner, stream * capacity + slot] = block
            codes[1, owner, stream * capacity + slot] = plan[1, stream % terms, block]

    lane = lax.broadcasted_iota(jnp.int32, (PART, width), 1)
    row = lax.broadcasted_iota(jnp.int32, (PART, width), 0)
    copies = []
    for mask in order:
        owner = me ^ mask
        labels = jnp.zeros((PART, width), jnp.int32)
        for stream in range(2 * terms):
            for slot in range(capacity):
                at = stream * capacity + slot
                block = codes[0, owner, at]
                if stream < terms:
                    value = left_ref[stream, block, pl.ds(start, rows), :]
                else:
                    value = other_ref[stream - terms, block]
                built[mask, at * parts : (at + 1) * parts] = value.reshape(parts, PART, width)
                label = jnp.where(row == 0, block, codes[1, owner, at])
                labels = jnp.where(lane == at, label, labels)
        built[mask, 2 * terms * capacity * parts] = labels.astype(jnp.float32).astype(jnp.bfloat16)
        copies.append(pltpu.make_async_copy(built.at[mask], pieces[mask], sems.at[mask]))
        copies[-1].start()
    for copy in copies:
        copy.wait()


def pack(ids, plan, other_plan, left, other, before, order, capacity):
    terms, blocks, rows, width = other.shape
    owners = len(order)
    scalars = pl.BlockSpec(memory_space=pltpu.SMEM)
    whole = pl.BlockSpec(memory_space=pltpu.VMEM)
    anywhere = pl.BlockSpec(memory_space=pl.ANY)
    shape = (2 * terms * capacity * rows // PART + 1, PART, width)
    return pl.pallas_call(
        functools.partial(pack_kernel, order, capacity, blocks, terms),
        out_shape=[jax.ShapeDtypeStruct(shape, jnp.bfloat16)] * owners,
        in_specs=[scalars] * 3 + [whole, whole, anywhere],
        out_specs=[anywhere] * owners,
        scratch_shapes=[
            pltpu.SMEM((2, owners, 2 * terms * capacity), jnp.int32),
            pltpu.SMEM((owners,), jnp.int32),
            pltpu.VMEM((owners,) + shape, jnp.bfloat16),
            pltpu.SemaphoreType.DMA((owners,)),
        ],
        compiler_params=pltpu.CompilerParams(vmem_limit_bytes=VMEM_LIMIT),
        cost_estimate=busy(5.0),
    )(ids, plan, other_plan, left, other, before)


def busy(microseconds):
    return pl.CostEstimate(
        flops=int(1.15e9 * microseconds), bytes_accessed=0, transcendentals=0
    )


def add_products(left, labels, vector, right, total, side, terms, capacity):
    blocks, rows, width = vector.shape[1:]
    parts = rows // PART
    moved, where = [], []
    for slot in range(terms * capacity):
        at = side * terms * capacity + slot
        block = vector[:, labels[0, at]].reshape(2 * rows, width)
        piece = left[at * parts : (at + 1) * parts].reshape(rows, width)
        product = jnp.dot(piece, block, preferred_element_type=jnp.float32)
        moved.append(product.astype(jnp.bfloat16))
        where.append(labels[1, at])
    for slot in range(terms * capacity):
        target = where[slot]
        total[target] += jnp.dot(
            moved[slot],
            right[slot // capacity, jnp.minimum(target, blocks - 1)],
            preferred_element_type=jnp.float32,
        )


def local_residual(total, wave_ref, device, rest_ref, stats_ref):
    blocks = wave_ref.shape[0]
    zero = jnp.zeros(wave_ref.shape[1:], jnp.float32)

    def sums(block, carry):
        cross, own = carry
        wave = wave_ref[block].astype(jnp.float32)
        return cross + wave * total[block], own + wave * wave

    cross, own = lax.fori_loop(0, blocks, sums, (zero, zero), unroll=4)
    cross, own = jnp.sum(cross, keepdims=True), jnp.sum(own, keepdims=True)
    local = jnp.where(own > 0, cross / own, 0.0)

    def squares(block, carry):
        rest = total[block] - local * wave_ref[block].astype(jnp.float32)
        rest_ref[block] = rest.astype(rest_ref.dtype)
        return carry + rest * rest

    about = jnp.sum(lax.fori_loop(0, blocks, squares, zero, unroll=4), keepdims=True)
    lane = lax.broadcasted_iota(jnp.int32, stats_ref.shape, 1)
    row = lax.broadcasted_iota(jnp.int32, stats_ref.shape, 0)
    values = jnp.where(lane == 0, about, jnp.where(lane == 1, cross, jnp.where(lane == 2, own, local)))
    stats_ref[...] = jnp.where((row == device) & (lane < 4), values, 0.0)


def form_direction(vector, wave, scale, chip):
    factor = scale[0, 1]
    for part in range(2):
        shift = scale[2 * chip + part, 0]

        @pl.loop(0, vector.shape[1], unroll=4)
        def _(block):
            rest = vector[part, block].astype(jnp.float32)
            rest = rest + shift * wave[part, block].astype(jnp.float32)
            vector[part, block] = (rest * factor).astype(vector.dtype)


def apply_kernel(sources, choices, first, end, terms, capacity, ids_ref, *refs):
    refs = list(refs)

    def take(count):
        taken, refs[:count] = refs[:count], []
        return taken

    (scale,) = take(1) if choices else (None,)
    lefts = take(choices or sources)
    rights = take(2)
    vectors = [take(2) for _ in range(sources)]
    waves = [take(2) for _ in range(choices)]
    (wave_in,) = take(1) if end == "stats" else (None,)
    (total_in,) = (None,) if first else take(1)
    (total_out,) = (None,) if end == "result" else take(1)
    (last_out,) = take(1)
    total, left, right, vector, raw, spread_labels, labels = take(7)
    left_sems, right_sems, vector_sems, raw_sems, label_sem, total_sem = take(6)
    wave, wave_sems = take(2) if choices or end == "stats" else (None, None)
    half = ids_ref[0]
    blocks = vector.shape[2]
    parts = left.shape[1]

    def left_copies(source, piece):
        return [
            pltpu.make_async_copy(piece.at[parts], raw.at[source], raw_sems.at[source]),
            pltpu.make_async_copy(
                piece.at[pl.ds(0, parts)], left.at[source], left_sems.at[source]
            ),
        ]

    def vector_copies(source):
        return [
            pltpu.make_async_copy(
                vectors[source][part],
                vector.at[source, half if part == 0 else 1 - half],
                vector_sems.at[source, part],
            )
            for part in range(2)
        ]

    def wave_copies(source, pair):
        return [
            pltpu.make_async_copy(
                pair[part],
                wave.at[source, half if part == 0 else 1 - half],
                wave_sems.at[source, part],
            )
            for part in range(2)
        ]

    def right_copy(side):
        return pltpu.make_async_copy(rights[side], right.at[side], right_sems.at[side])

    for source in range(sources):
        if choices:
            for choice, piece in enumerate(lefts):

                @pl.when(ids_ref[2 + source] == choice)
                def _():
                    for copy in left_copies(source, piece) + wave_copies(source, waves[choice]):
                        copy.start()

        else:
            for copy in left_copies(source, lefts[source]):
                copy.start()
    for copy in [*vector_copies(0), right_copy(0)]:
        copy.start()
    for source in range(1, sources):
        for copy in vector_copies(source):
            copy.start()
    right_copy(1).start()
    if first:
        total[...] = jnp.zeros_like(total)
    else:
        load_total = pltpu.make_async_copy(total_in, total, total_sem)
        load_total.start()
    if end == "stats":
        load_wave = pltpu.make_async_copy(wave_in, wave.at[0, 0], wave_sems.at[0, 0])
        load_wave.start()
    if end == "go on":
        last_out[...] = jnp.zeros_like(last_out)

    for source in range(sources):
        left_copies(source, lefts[0])[0].wait()
    spread_labels[...] = raw[:, :8].astype(jnp.float32).astype(jnp.int32)
    move_labels = pltpu.make_async_copy(spread_labels, labels, label_sem)
    move_labels.start()
    move_labels.wait()
    if not first:
        load_total.wait()
    for side in range(2):
        right_copy(side).wait()
        for source in range(sources):
            if side == 0:
                left_copies(source, lefts[0])[1].wait()
                for copy in vector_copies(source):
                    copy.wait()
                if choices:
                    for copy in wave_copies(source, waves[0]):
                        copy.wait()
                    chip = lax.div(ids_ref[1], 2) ^ ids_ref[2 + source]
                    form_direction(vector.at[source], wave.at[source], scale, chip)
            add_products(
                left.at[source],
                labels.at[source],
                vector.at[source],
                right.at[side],
                total,
                side,
                terms,
                capacity,
            )
    if end == "result":
        last_out[...] = total[:blocks].astype(last_out.dtype)
    elif end == "stats":
        load_wave.wait()
        local_residual(total, wave.at[0, 0], ids_ref[1], total_out, last_out)
    else:
        store_total = pltpu.make_async_copy(total, total_out, total_sem)
        store_total.start()
        store_total.wait()


def apply_group(ids, lefts, rights, vectors, total, end, wave=None, waves=(), scale=None):
    blocks, rows, width = vectors[0][0].shape
    terms = rights[0].shape[0]
    parts = lefts[0].shape[0] - 1
    capacity = parts * PART // (2 * terms * rows)
    sources, first = len(vectors), total is None
    arrays = [*lefts, *rights] + [unit for pair in [*vectors, *waves] for unit in pair]
    arrays += [wave] if end == "stats" else []
    arrays += [] if first else [total]
    whole = pl.BlockSpec(memory_space=pltpu.VMEM)
    anywhere = pl.BlockSpec(memory_space=pl.ANY)
    total_shape = (blocks + 1, rows, width)
    scratch = [
        pltpu.VMEM(total_shape, jnp.float32),
        pltpu.VMEM((sources, parts, PART, width), jnp.bfloat16),
        pltpu.VMEM((2,) + rights[0].shape, jnp.bfloat16),
        pltpu.VMEM((sources, 2, blocks, rows, width), jnp.bfloat16),
        pltpu.VMEM((sources, PART, width), jnp.bfloat16),
        pltpu.VMEM((sources, 8, width), jnp.int32),
        pltpu.SMEM((sources, 8, width), jnp.int32),
        pltpu.SemaphoreType.DMA((sources,)),
        pltpu.SemaphoreType.DMA((2,)),
        pltpu.SemaphoreType.DMA((sources, 2)),
        pltpu.SemaphoreType.DMA((sources,)),
        pltpu.SemaphoreType.DMA,
        pltpu.SemaphoreType.DMA,
    ]
    if waves or end == "stats":
        scratch += [
            pltpu.VMEM((sources, 2, blocks, rows, width), jnp.bfloat16),
            pltpu.SemaphoreType.DMA((sources, 2)),
        ]
    devices = lax.axis_size("sec") * lax.axis_size("term")
    total_out = jax.ShapeDtypeStruct(total_shape, jnp.float32)
    out_shape, out_specs = {
        "go on": ((total_out, jax.ShapeDtypeStruct((8, width), jnp.float32)), (anywhere, whole)),
        "stats": (
            (
                jax.ShapeDtypeStruct((blocks, rows, width), jnp.bfloat16),
                jax.ShapeDtypeStruct((devices, 128), jnp.float32),
            ),
            (whole, whole),
        ),
        "result": (jax.ShapeDtypeStruct((blocks, rows, width), jnp.bfloat16), whole),
    }[end]
    choices = len(waves)
    scalars = [ids] if scale is None else [ids, scale]
    return pl.pallas_call(
        functools.partial(apply_kernel, sources, choices, first, end, terms, capacity),
        out_shape=out_shape,
        in_specs=[pl.BlockSpec(memory_space=pltpu.SMEM)] * len(scalars) + [anywhere] * len(arrays),
        out_specs=out_specs,
        scratch_shapes=scratch,
        compiler_params=pltpu.CompilerParams(vmem_limit_bytes=VMEM_LIMIT),
        cost_estimate=busy(3.5 + (2.7 if waves else 1.8) * sources),
    )(*scalars, *arrays)


def scale_kernel(entries, stats_ref, scale_ref, rayleigh_ref):
    stats = stats_ref[...]
    about, cross, own, local = (stats[:, lane : lane + 1] for lane in range(4))
    rayleigh = jnp.sum(cross, keepdims=True) / jnp.sum(own, keepdims=True)
    offset = local - rayleigh
    residual_sq = jnp.sum(about + offset * offset * own, keepdims=True)
    factor = lax.rsqrt(residual_sq / entries + 1e-06)
    lane = lax.broadcasted_iota(jnp.int32, scale_ref.shape, 1)
    scale_ref[...] = jnp.where(lane == 0, offset, factor)
    rayleigh_ref[...] = rayleigh


def scales(stats, entries):
    whole = pl.BlockSpec(memory_space=pltpu.VMEM)
    return pl.pallas_call(
        functools.partial(scale_kernel, entries),
        out_shape=(
            jax.ShapeDtypeStruct(stats.shape, jnp.float32),
            jax.ShapeDtypeStruct((1, 1), jnp.float32),
        ),
        in_specs=[whole],
        out_specs=(whole, whole),
        cost_estimate=busy(0.7),
    )(stats)


def per_device_ring(wavefunction, left_operator, right_operator, target_owner, target_local):
    owners, halves = lax.axis_size("sec"), lax.axis_size("term")
    me, half = lax.axis_index("sec"), lax.axis_index("term")
    terms, blocks, height, width = left_operator.shape
    rows = height // halves
    capacity = 2 * blocks // owners
    place = ring_place(me, owners)
    ids = jnp.stack([me, half]).astype(jnp.int32)

    own_rows = lax.dynamic_slice_in_dim(wavefunction, half * rows, rows, 1)
    other_rows = lax.dynamic_slice_in_dim(wavefunction, (1 - half) * rows, rows, 1)
    plan = jnp.stack([target_owner[:, :, 0], target_local])
    other_left = swap(
        lax.dynamic_slice_in_dim(left_operator, (1 - half) * rows, rows, 2), owners, halves
    )
    order = [m for m in ORDER if m < owners] + list(range(len(ORDER), owners))
    rights = (right_operator, swap(right_operator, owners, halves))
    pieces = pack(
        ids,
        plan,
        swap(plan, owners, halves),
        left_operator,
        other_left,
        plan,
        order[1:] + order[:1],
        capacity,
    )
    lefts = [pieces[0]]
    for m in range(1, owners):
        piece = pieces[m]
        if m in PIECE_WAITS:
            piece = after(piece, lefts[PIECE_WAITS[m]])
        lefts.append(exchange(piece, owners, halves, m))
    near = mask_gather(own_rows, lefts, owners, halves)
    far = {m: swap(unit, owners, halves) if m else other_rows for m, unit in near.items()}

    here = [half, me * halves + half]
    no_choice = jnp.stack(here).astype(jnp.int32)
    total = None
    for at in range(0, owners, 2):
        group = order[at : at + 2]
        total, stats = apply_group(
            no_choice,
            [lefts[m] for m in group],
            rights,
            [(near[m], far[m]) for m in group],
            total,
            "go on" if at + 2 < owners else "stats",
            own_rows,
        )

    rest = total
    entries = blocks * owners * height * width
    scale, rayleigh = scales(spread(stats, owners * halves), entries)
    reach = (owners - 1) // 2
    waves = [(near[m], far[m]) for m in range(owners)]

    def add_group(total, units, end):
        choices = [me ^ ring_owner(place - s, owners) for s in units]
        vectors = [(unit, swap(unit, owners, halves)) for unit in units.values()]
        ids = jnp.stack(here + choices).astype(jnp.int32)
        return apply_group(
            ids, lefts, rights, vectors, total, end, waves=waves, scale=scale
        )

    total = token = None
    ready = [{0: rest}]
    ahead = behind = rest
    for step in range(1, reach + 1):
        ahead = ring_send(ahead, owners, halves, (1,) * halves)
        behind = ring_send(behind, owners, halves, (-1,) * halves)
        if step > 1:
            total, token = add_group(total, ready.pop(0), "go on")
            ahead = after(ahead, token)
        ready.append({step: ahead, -step: behind})
    last = ring_send(select_half(half, ahead, behind), owners, halves, (1, -1))
    total, token = add_group(total, ready.pop(0), "go on")
    last = after(last, token)
    total = add_group(total, {**ready.pop(0), owners // 2: last}, "result")
    return (total, rayleigh[0])


def slot_codes(target_owner, target_local, owners, capacity):
    terms, blocks = target_local.shape
    owner = target_owner[:, :, 0]
    place = jnp.arange(blocks, dtype=jnp.int32)
    same = (owner[:, :, None] == owner[:, None, :]) & (place[None, :] < place[:, None])[None]
    position = jnp.sum(same.astype(jnp.int32), axis=2)
    hit = (
        owner[:, None, None, :] == jnp.arange(owners, dtype=jnp.int32)[None, :, None, None]
    ) & (position[:, None, None, :] == jnp.arange(capacity, dtype=jnp.int32)[None, None, :, None])
    code = place[None, :] * (2 * blocks) + target_local - blocks
    return blocks + jnp.sum(jnp.where(hit, code[:, None, None, :], 0), axis=3)


def stream_kernel(first, capacity, blocks, code_ref, left_ref, vector_ref, right_ref, *rest):
    total_in, total = (None, rest[0]) if first else rest
    step = pl.program_id(0)
    rows, width = left_ref.shape[2:]

    @pl.when(step == 0)
    def _():
        total[...] = jnp.zeros_like(total) if first else total_in[...]

    for term in range(2):
        moved, where = [], []
        for slot in range(capacity):
            code = code_ref[2 * step + term, slot]
            source, target = lax.div(code, 2 * blocks), lax.rem(code, 2 * blocks)
            block = vector_ref[0, :, source].reshape(2 * rows, width)
            product = jnp.dot(left_ref[term, slot], block, preferred_element_type=jnp.float32)
            moved.append(product.astype(jnp.bfloat16))
            where.append(target)
        for slot in range(capacity):
            target = where[slot]
            total[target] += jnp.dot(
                moved[slot],
                right_ref[term, jnp.minimum(target, blocks - 1)],
                preferred_element_type=jnp.float32,
            )


def stream_chunk(total, codes, left, vector, right):
    owners, _, blocks, rows, width = vector.shape
    capacity = left.shape[1]
    first = total is None
    spec_total = pl.BlockSpec((blocks + 1, rows, width), lambda s, c: (0, 0, 0))
    return pl.pallas_call(
        functools.partial(stream_kernel, first, capacity, blocks),
        out_shape=jax.ShapeDtypeStruct((blocks + 1, rows, width), jnp.float32),
        grid_spec=pltpu.PrefetchScalarGridSpec(
            num_scalar_prefetch=1,
            grid=(owners,),
            in_specs=[
                pl.BlockSpec((2, capacity, rows, width), lambda s, c: (s, 0, 0, 0)),
                pl.BlockSpec((1, 2, blocks, rows, width), lambda s, c: (s, 0, 0, 0, 0)),
                pl.BlockSpec((2, blocks, width, width), lambda s, c: (0, 0, 0, 0)),
            ]
            + ([] if first else [spec_total]),
            out_specs=spec_total,
        ),
        compiler_params=pltpu.CompilerParams(vmem_limit_bytes=32 * 2**20),
        cost_estimate=pl.CostEstimate(
            flops=owners * 2 * capacity * 2 * 2 * rows * width * width,
            bytes_accessed=left.size * 2 + vector.size * 2 + right.size * 2,
            transcendentals=0,
        ),
    )(codes, left, vector, right, *([] if first else [total]))


def per_device_streamed(wavefunction, left_operator, right_operator, target_owner, target_local):
    owners = lax.axis_size("sec")
    halves = lax.axis_size("term")
    me, half = lax.axis_index("sec"), lax.axis_index("term")
    terms, blocks, height, width = left_operator.shape
    rows = height // halves
    capacity = 2 * blocks // owners

    own_rows = lax.dynamic_slice_in_dim(wavefunction, half * rows, rows, 1)
    codes = slot_codes(target_owner, target_local, owners, capacity)
    sources = codes // (2 * blocks)

    moved_left = []
    for k in range(terms):
        pick = sources[k][:, None, :] * halves + jnp.arange(halves, dtype=jnp.int32)[None, :, None]
        pieces = left_operator[k].reshape(blocks * halves, rows, width)[pick.reshape(-1)]
        pieces = pieces.reshape(owners * halves, capacity, rows, width)
        moved_left.append(lax.all_to_all(pieces, BOTH, split_axis=0, concat_axis=0, tiled=True))
    all_codes = lax.all_gather(codes, BOTH, axis=0)
    my_codes = lax.dynamic_index_in_dim(all_codes, me, axis=3 - 1, keepdims=False)
    gathered = lax.all_gather(own_rows, BOTH, axis=0).reshape(owners, halves, blocks, rows, width)
    right = lax.all_gather(right_operator, "term", axis=1)

    def apply(vector):
        total = None
        for k in range(terms):
            total = stream_chunk(total, my_codes[:, k], moved_left[k], vector, right[k])
        return total[:blocks]

    sigma_rows = apply(gathered)
    wave = own_rows.astype(jnp.float32)
    cross, own = jnp.sum(wave * sigma_rows), jnp.sum(wave * wave)
    local = jnp.where(own > 0, cross / own, 0.0)
    about = jnp.sum(jnp.square(sigma_rows - local * wave))
    stats = lax.all_gather(jnp.stack([about, cross, own, local]), BOTH, axis=0)
    rayleigh = jnp.sum(stats[:, 1]) / jnp.sum(stats[:, 2])
    residual_sq = jnp.sum(stats[:, 0] + jnp.square(stats[:, 3] - rayleigh) * stats[:, 2])
    entries = blocks * owners * height * width
    factor = lax.rsqrt(residual_sq / entries + 1e-06)
    direction = ((sigma_rows - rayleigh * wave) * factor).astype(jnp.bfloat16)
    direction = lax.all_gather(direction, BOTH, axis=0).reshape(gathered.shape)
    sigma_two = apply(direction).astype(jnp.bfloat16)
    return (sigma_two, jnp.reshape(rayleigh, (1,)))


def per_device(wavefunction, *operands):
    gathered_bytes = lax.axis_size("sec") * wavefunction.size * wavefunction.dtype.itemsize
    if 2 * gathered_bytes > RING_BYTES:
        return per_device_streamed(wavefunction, *operands)
    return per_device_ring(wavefunction, *operands)


def solution(mesh):
    placed = (
        P(("rep", "sec"), None, None),
        P("term", ("rep", "sec"), None, None),
        P("term", ("rep", "sec"), None, None),
        P("term", ("rep", "sec"), None),
        P("term", ("rep", "sec")),
    )
    return jax.shard_map(
        per_device,
        mesh=mesh,
        in_specs=placed,
        out_specs=(P(("rep", "sec"), "term", None), P("rep")),
        check_vma=False,
    )
```

```python
import functools

import jax
import jax.numpy as jnp
from jax import lax
from jax.experimental import pallas as pl
from jax.experimental.pallas import tpu as pltpu
from jax.sharding import PartitionSpec as P

BOTH = ("sec", "term")
VMEM_LIMIT = 60 * 2**20
PART = 16
ORDER = [0, 4, 5, 1, 2, 6, 3, 7]
WAITS = {4: 1, 2: 5, 6: 2}
PIECE_WAITS = {6: 4, 7: 5}
RING_BYTES = 24 * 2**20


def ring_order(owners):
    if owners % 2:
        return list(range(owners))
    return list(range(0, owners, 2)) + list(range(owners - 1, 0, -2))


def ring_place(owner, owners):
    if owners % 2:
        return owner
    return jnp.where(owner % 2 == 0, owner // 2, owners - 1 - owner // 2)


def ring_owner(place, owners):
    place = place % owners
    if owners % 2:
        return place
    return jnp.where(place < owners // 2, 2 * place, 2 * (owners - 1 - place) + 1)


def permute(value, owners, halves, target, flip=0):
    pairs = [
        (chip * halves + half, target(chip, half) * halves + (half ^ flip))
        for chip in range(owners)
        for half in range(halves)
    ]
    return lax.ppermute(value, BOTH, pairs)


def swap(value, owners, halves):
    return permute(value, owners, halves, lambda chip, half: chip, 1)


def exchange(value, owners, halves, mask):
    return permute(value, owners, halves, lambda chip, half: chip ^ mask)


def ring_send(value, owners, halves, shifts):
    ring = ring_order(owners)
    place = {chip: index for index, chip in enumerate(ring)}
    return permute(
        value, owners, halves, lambda chip, half: ring[(place[chip] + shifts[half]) % owners]
    )


def select_kernel(half_ref, lower_ref, upper_ref, *rest):
    out_ref = rest[-1]
    out_ref[...] = jnp.where(half_ref[0] == 0, lower_ref[...], upper_ref[...])


def select_half(half, lower, upper, *others):
    anywhere = pl.BlockSpec(memory_space=pl.ANY)
    whole = pl.BlockSpec(memory_space=pltpu.VMEM)
    return pl.pallas_call(
        select_kernel,
        out_shape=jax.ShapeDtypeStruct(lower.shape, lower.dtype),
        in_specs=[pl.BlockSpec(memory_space=pltpu.SMEM), whole, whole] + [anywhere] * len(others),
        out_specs=whole,
        cost_estimate=busy(0.8),
    )(jnp.reshape(half, (1,)).astype(jnp.int32), lower, upper, *others)


def after_kernel(*refs):
    del refs


def after(value, *others):
    anywhere = pl.BlockSpec(memory_space=pl.ANY)
    return pl.pallas_call(
        after_kernel,
        out_shape=jax.ShapeDtypeStruct(value.shape, value.dtype),
        in_specs=[anywhere] * (1 + len(others)),
        out_specs=anywhere,
        input_output_aliases={0: 0},
        cost_estimate=busy(0.3),
    )(value, *others)


def mask_gather(unit, lefts, owners, halves):
    units = {0: unit}
    step = owners // 2
    masks = []
    while step:
        masks.append(step)
        units[step] = exchange(unit, owners, halves, step)
        step //= 2
    waits = dict(WAITS)
    for step in masks[1:]:
        for mask in [m for m in units if m >= 2 * step and m % (2 * step) == 0]:
            if mask in waits:
                units[mask] = after(units[mask], lefts[waits.pop(mask)])
            units[mask | step] = exchange(units[mask], owners, halves, step)
    return units


def spread(value, devices):
    step = 1
    values = []
    while step < devices:
        masks = [step] if 2 * step == devices else [step, 2 * step, 3 * step]
        parts = [lax.ppermute(value, BOTH, [(d, d ^ m) for d in range(devices)]) for m in masks]
        for part in parts:
            value = value + part
        values.append(value)
        step *= 4
    return values


def pack_kernel(order, capacity, blocks, terms, ids_ref, plan_ref, other_plan_ref, *refs):
    left_ref, other_ref, _, *pieces, codes, seen, built, sems = refs
    owners = len(order)
    me, half = ids_ref[0], ids_ref[1]
    rows, width = other_ref.shape[2:]
    start = pl.multiple_of(half * rows, rows)
    parts = rows // PART

    @pl.loop(0, owners)
    def _(owner):
        for index in range(2 * terms * capacity):
            codes[0, owner, index] = 0
            codes[1, owner, index] = blocks

    for stream in range(2 * terms):
        plan = plan_ref if stream < terms else other_plan_ref

        @pl.loop(0, owners)
        def _(owner):
            seen[owner] = 0

        @pl.loop(0, blocks, unroll=4)
        def _(block):
            owner = plan[0, stream % terms, block]
            slot = seen[owner]
            seen[owner] = slot + 1
            codes[0, owner, stream * capacity + slot] = block
            codes[1, owner, stream * capacity + slot] = plan[1, stream % terms, block]

    lane = lax.broadcasted_iota(jnp.int32, (PART, width), 1)
    row = lax.broadcasted_iota(jnp.int32, (PART, width), 0)
    copies = []
    for mask in order:
        owner = me ^ mask
        labels = jnp.zeros((PART, width), jnp.int32)
        for stream in range(2 * terms):
            for slot in range(capacity):
                at = stream * capacity + slot
                block = codes[0, owner, at]
                if stream < terms:
                    value = left_ref[stream, block, pl.ds(start, rows), :]
                else:
                    value = other_ref[stream - terms, block]
                built[mask, at * parts : (at + 1) * parts] = value.reshape(parts, PART, width)
                label = jnp.where(row == 0, block, codes[1, owner, at])
                labels = jnp.where(lane == at, label, labels)
        built[mask, 2 * terms * capacity * parts] = labels.astype(jnp.float32).astype(jnp.bfloat16)
        copies.append(pltpu.make_async_copy(built.at[mask], pieces[mask], sems.at[mask]))
        copies[-1].start()
    for copy in copies:
        copy.wait()


def pack(ids, plan, other_plan, left, other, before, order, capacity):
    terms, blocks, rows, width = other.shape
    owners = len(order)
    scalars = pl.BlockSpec(memory_space=pltpu.SMEM)
    whole = pl.BlockSpec(memory_space=pltpu.VMEM)
    anywhere = pl.BlockSpec(memory_space=pl.ANY)
    shape = (2 * terms * capacity * rows // PART + 1, PART, width)
    return pl.pallas_call(
        functools.partial(pack_kernel, order, capacity, blocks, terms),
        out_shape=[jax.ShapeDtypeStruct(shape, jnp.bfloat16)] * owners,
        in_specs=[scalars] * 3 + [whole, whole, anywhere],
        out_specs=[anywhere] * owners,
        scratch_shapes=[
            pltpu.SMEM((2, owners, 2 * terms * capacity), jnp.int32),
            pltpu.SMEM((owners,), jnp.int32),
            pltpu.VMEM((owners,) + shape, jnp.bfloat16),
            pltpu.SemaphoreType.DMA((owners,)),
        ],
        compiler_params=pltpu.CompilerParams(vmem_limit_bytes=VMEM_LIMIT),
        cost_estimate=busy(5.0),
    )(ids, plan, other_plan, left, other, before)


def busy(microseconds):
    return pl.CostEstimate(
        flops=int(1.15e9 * microseconds), bytes_accessed=0, transcendentals=0
    )


def add_products(left, labels, vector, right, total, side, terms, capacity):
    blocks, rows, width = vector.shape[1:]
    parts = rows // PART
    moved, where = [], []
    for slot in range(terms * capacity):
        at = side * terms * capacity + slot
        block = vector[:, labels[0, at]].reshape(2 * rows, width)
        piece = left[at * parts : (at + 1) * parts].reshape(rows, width)
        product = jnp.dot(piece, block, preferred_element_type=jnp.float32)
        moved.append(product.astype(jnp.bfloat16))
        where.append(labels[1, at])
    for slot in range(terms * capacity):
        target = where[slot]
        total[target] += jnp.dot(
            moved[slot],
            right[slot // capacity, jnp.minimum(target, blocks - 1)],
            preferred_element_type=jnp.float32,
        )


def local_residual(total, wave_ref, device, rest_ref, stats_ref):
    blocks = wave_ref.shape[0]
    zero = jnp.zeros(wave_ref.shape[1:], jnp.float32)

    def sums(block, carry):
        cross, own = carry
        wave = wave_ref[block].astype(jnp.float32)
        return cross + wave * total[block], own + wave * wave

    cross, own = lax.fori_loop(0, blocks, sums, (zero, zero), unroll=4)
    cross, own = jnp.sum(cross, keepdims=True), jnp.sum(own, keepdims=True)
    local = jnp.where(own > 0, cross / own, 0.0)

    def squares(block, carry):
        rest = total[block] - local * wave_ref[block].astype(jnp.float32)
        rest_ref[block] = rest.astype(rest_ref.dtype)
        return carry + rest * rest

    about = jnp.sum(lax.fori_loop(0, blocks, squares, zero, unroll=4), keepdims=True)
    lane = lax.broadcasted_iota(jnp.int32, stats_ref.shape, 1)
    row = lax.broadcasted_iota(jnp.int32, stats_ref.shape, 0)
    values = jnp.where(lane == 0, about, jnp.where(lane == 1, cross, jnp.where(lane == 2, own, local)))
    stats_ref[...] = jnp.where((row == device) & (lane < 4), values, 0.0)


def form_direction(vector, wave, scale, chip):
    factor = scale[0, 1]
    for part in range(2):
        shift = scale[2 * chip + part, 0]

        @pl.loop(0, vector.shape[1], unroll=4)
        def _(block):
            rest = vector[part, block].astype(jnp.float32)
            rest = rest + shift * wave[part, block].astype(jnp.float32)
            vector[part, block] = (rest * factor).astype(vector.dtype)


def apply_kernel(sources, choices, first, end, terms, capacity, ids_ref, *refs):
    refs = list(refs)

    def take(count):
        taken, refs[:count] = refs[:count], []
        return taken

    (scale,) = take(1) if choices else (None,)
    lefts = take(choices or sources)
    rights = take(2)
    vectors = [take(2) for _ in range(sources)]
    waves = [take(2) for _ in range(choices)]
    (wave_in,) = take(1) if end == "stats" else (None,)
    (total_in,) = (None,) if first else take(1)
    (total_out,) = (None,) if end == "result" else take(1)
    (last_out,) = take(1)
    total, left, right, vector, raw, spread_labels, labels = take(7)
    left_sems, right_sems, vector_sems, raw_sems, label_sem, total_sem = take(6)
    wave, wave_sems = take(2) if choices or end == "stats" else (None, None)
    half = ids_ref[0]
    blocks = vector.shape[2]
    parts = left.shape[1]

    def left_copies(source, piece):
        return [
            pltpu.make_async_copy(piece.at[parts], raw.at[source], raw_sems.at[source]),
            pltpu.make_async_copy(
                piece.at[pl.ds(0, parts)], left.at[source], left_sems.at[source]
            ),
        ]

    def vector_copies(source):
        return [
            pltpu.make_async_copy(
                vectors[source][part],
                vector.at[source, half if part == 0 else 1 - half],
                vector_sems.at[source, part],
            )
            for part in range(2)
        ]

    def wave_copies(source, pair):
        return [
            pltpu.make_async_copy(
                pair[part],
                wave.at[source, half if part == 0 else 1 - half],
                wave_sems.at[source, part],
            )
            for part in range(2)
        ]

    def right_copy(side):
        return pltpu.make_async_copy(rights[side], right.at[side], right_sems.at[side])

    for source in range(sources):
        if choices:
            for choice, piece in enumerate(lefts):

                @pl.when(ids_ref[2 + source] == choice)
                def _():
                    for copy in left_copies(source, piece) + wave_copies(source, waves[choice]):
                        copy.start()

        else:
            for copy in left_copies(source, lefts[source]):
                copy.start()
    for copy in [*vector_copies(0), right_copy(0)]:
        copy.start()
    for source in range(1, sources):
        for copy in vector_copies(source):
            copy.start()
    right_copy(1).start()
    if first:
        total[...] = jnp.zeros_like(total)
    else:
        load_total = pltpu.make_async_copy(total_in, total, total_sem)
        load_total.start()
    if end == "stats":
        load_wave = pltpu.make_async_copy(wave_in, wave.at[0, 0], wave_sems.at[0, 0])
        load_wave.start()
    if end == "go on":
        last_out[...] = jnp.zeros_like(last_out)

    for source in range(sources):
        left_copies(source, lefts[0])[0].wait()
    spread_labels[...] = raw[:, :8].astype(jnp.float32).astype(jnp.int32)
    move_labels = pltpu.make_async_copy(spread_labels, labels, label_sem)
    move_labels.start()
    move_labels.wait()
    if not first:
        load_total.wait()
    for side in range(2):
        right_copy(side).wait()
        for source in range(sources):
            if side == 0:
                left_copies(source, lefts[0])[1].wait()
                for copy in vector_copies(source):
                    copy.wait()
                if choices:
                    for copy in wave_copies(source, waves[0]):
                        copy.wait()
                    chip = lax.div(ids_ref[1], 2) ^ ids_ref[2 + source]
                    form_direction(vector.at[source], wave.at[source], scale, chip)
            add_products(
                left.at[source],
                labels.at[source],
                vector.at[source],
                right.at[side],
                total,
                side,
                terms,
                capacity,
            )
    if end == "result":
        last_out[...] = total[:blocks].astype(last_out.dtype)
    elif end == "stats":
        load_wave.wait()
        local_residual(total, wave.at[0, 0], ids_ref[1], total_out, last_out)
    else:
        store_total = pltpu.make_async_copy(total, total_out, total_sem)
        store_total.start()
        store_total.wait()


def apply_group(ids, lefts, rights, vectors, total, end, wave=None, waves=(), scale=None):
    blocks, rows, width = vectors[0][0].shape
    terms = rights[0].shape[0]
    parts = lefts[0].shape[0] - 1
    capacity = parts * PART // (2 * terms * rows)
    sources, first = len(vectors), total is None
    arrays = [*lefts, *rights] + [unit for pair in [*vectors, *waves] for unit in pair]
    arrays += [wave] if end == "stats" else []
    arrays += [] if first else [total]
    whole = pl.BlockSpec(memory_space=pltpu.VMEM)
    anywhere = pl.BlockSpec(memory_space=pl.ANY)
    total_shape = (blocks + 1, rows, width)
    scratch = [
        pltpu.VMEM(total_shape, jnp.float32),
        pltpu.VMEM((sources, parts, PART, width), jnp.bfloat16),
        pltpu.VMEM((2,) + rights[0].shape, jnp.bfloat16),
        pltpu.VMEM((sources, 2, blocks, rows, width), jnp.bfloat16),
        pltpu.VMEM((sources, PART, width), jnp.bfloat16),
        pltpu.VMEM((sources, 8, width), jnp.int32),
        pltpu.SMEM((sources, 8, width), jnp.int32),
        pltpu.SemaphoreType.DMA((sources,)),
        pltpu.SemaphoreType.DMA((2,)),
        pltpu.SemaphoreType.DMA((sources, 2)),
        pltpu.SemaphoreType.DMA((sources,)),
        pltpu.SemaphoreType.DMA,
        pltpu.SemaphoreType.DMA,
    ]
    if waves or end == "stats":
        scratch += [
            pltpu.VMEM((sources, 2, blocks, rows, width), jnp.bfloat16),
            pltpu.SemaphoreType.DMA((sources, 2)),
        ]
    devices = lax.axis_size("sec") * lax.axis_size("term")
    total_out = jax.ShapeDtypeStruct(total_shape, jnp.float32)
    out_shape, out_specs = {
        "go on": ((total_out, jax.ShapeDtypeStruct((8, width), jnp.float32)), (anywhere, whole)),
        "stats": (
            (
                jax.ShapeDtypeStruct((blocks, rows, width), jnp.bfloat16),
                jax.ShapeDtypeStruct((devices, 128), jnp.float32),
            ),
            (whole, whole),
        ),
        "result": (jax.ShapeDtypeStruct((blocks, rows, width), jnp.bfloat16), whole),
    }[end]
    choices = len(waves)
    scalars = [ids] if scale is None else [ids, scale]
    return pl.pallas_call(
        functools.partial(apply_kernel, sources, choices, first, end, terms, capacity),
        out_shape=out_shape,
        in_specs=[pl.BlockSpec(memory_space=pltpu.SMEM)] * len(scalars) + [anywhere] * len(arrays),
        out_specs=out_specs,
        scratch_shapes=scratch,
        compiler_params=pltpu.CompilerParams(vmem_limit_bytes=VMEM_LIMIT),
        cost_estimate=busy(3.5 + (2.7 if waves else 1.8) * sources),
    )(*scalars, *arrays)


def scale_kernel(entries, stats_ref, scale_ref, rayleigh_ref):
    stats = stats_ref[...]
    about, cross, own, local = (stats[:, lane : lane + 1] for lane in range(4))
    rayleigh = jnp.sum(cross, keepdims=True) / jnp.sum(own, keepdims=True)
    offset = local - rayleigh
    residual_sq = jnp.sum(about + offset * offset * own, keepdims=True)
    factor = lax.rsqrt(residual_sq / entries + 1e-06)
    lane = lax.broadcasted_iota(jnp.int32, scale_ref.shape, 1)
    scale_ref[...] = jnp.where(lane == 0, offset, factor)
    rayleigh_ref[...] = rayleigh


def scales(stats, entries):
    whole = pl.BlockSpec(memory_space=pltpu.VMEM)
    return pl.pallas_call(
        functools.partial(scale_kernel, entries),
        out_shape=(
            jax.ShapeDtypeStruct(stats.shape, jnp.float32),
            jax.ShapeDtypeStruct((1, 1), jnp.float32),
        ),
        in_specs=[whole],
        out_specs=(whole, whole),
        cost_estimate=busy(0.7),
    )(stats)


def per_device_ring(wavefunction, left_operator, right_operator, target_owner, target_local):
    owners, halves = lax.axis_size("sec"), lax.axis_size("term")
    me, half = lax.axis_index("sec"), lax.axis_index("term")
    terms, blocks, height, width = left_operator.shape
    rows = height // halves
    capacity = 2 * blocks // owners
    place = ring_place(me, owners)
    ids = jnp.stack([me, half]).astype(jnp.int32)

    own_rows = lax.dynamic_slice_in_dim(wavefunction, half * rows, rows, 1)
    other_rows = lax.dynamic_slice_in_dim(wavefunction, (1 - half) * rows, rows, 1)
    plan = jnp.stack([target_owner[:, :, 0], target_local])
    other_left = swap(
        lax.dynamic_slice_in_dim(left_operator, (1 - half) * rows, rows, 2), owners, halves
    )
    order = [m for m in ORDER if m < owners] + list(range(len(ORDER), owners))
    rights = (right_operator, swap(right_operator, owners, halves))
    pieces = pack(
        ids,
        plan,
        swap(plan, owners, halves),
        left_operator,
        other_left,
        plan,
        order[1:] + order[:1],
        capacity,
    )
    lefts = [pieces[0]]
    for m in range(1, owners):
        piece = pieces[m]
        if m in PIECE_WAITS:
            piece = after(piece, lefts[PIECE_WAITS[m]])
        lefts.append(exchange(piece, owners, halves, m))
    near = mask_gather(own_rows, lefts, owners, halves)
    far = {m: swap(unit, owners, halves) if m else other_rows for m, unit in near.items()}

    here = [half, me * halves + half]
    no_choice = jnp.stack(here).astype(jnp.int32)
    total = None
    for at in range(0, owners, 2):
        group = order[at : at + 2]
        total, stats = apply_group(
            no_choice,
            [lefts[m] for m in group],
            rights,
            [(near[m], far[m]) for m in group],
            total,
            "go on" if at + 2 < owners else "stats",
            own_rows,
        )

    stats = spread(stats, owners * halves)
    rest = after(total, stats[0])
    entries = blocks * owners * height * width
    scale, rayleigh = scales(stats[-1], entries)
    reach = (owners - 1) // 2
    waves = [(near[m], far[m]) for m in range(owners)]

    def add_group(total, units, end):
        choices = [me ^ ring_owner(place - s, owners) for s in units]
        vectors = [(unit, swap(unit, owners, halves)) for unit in units.values()]
        ids = jnp.stack(here + choices).astype(jnp.int32)
        return apply_group(
            ids, lefts, rights, vectors, total, end, waves=waves, scale=scale
        )

    total = token = None
    ready = [{0: rest}]
    ahead = behind = rest
    for step in range(1, reach + 1):
        ahead = ring_send(ahead, owners, halves, (1,) * halves)
        behind = ring_send(behind, owners, halves, (-1,) * halves)
        if step > 1:
            total, token = add_group(total, ready.pop(0), "go on")
            ahead = after(ahead, token)
        ready.append({step: ahead, -step: behind})
    last = ring_send(select_half(half, ahead, behind), owners, halves, (1, -1))
    total, token = add_group(total, ready.pop(0), "go on")
    last = after(last, token)
    total = add_group(total, {**ready.pop(0), owners // 2: last}, "result")
    return (total, rayleigh[0])


def slot_codes(target_owner, target_local, owners, capacity):
    terms, blocks = target_local.shape
    owner = target_owner[:, :, 0]
    place = jnp.arange(blocks, dtype=jnp.int32)
    same = (owner[:, :, None] == owner[:, None, :]) & (place[None, :] < place[:, None])[None]
    position = jnp.sum(same.astype(jnp.int32), axis=2)
    hit = (
        owner[:, None, None, :] == jnp.arange(owners, dtype=jnp.int32)[None, :, None, None]
    ) & (position[:, None, None, :] == jnp.arange(capacity, dtype=jnp.int32)[None, None, :, None])
    code = place[None, :] * (2 * blocks) + target_local - blocks
    return blocks + jnp.sum(jnp.where(hit, code[:, None, None, :], 0), axis=3)


def stream_kernel(first, capacity, blocks, code_ref, left_ref, vector_ref, right_ref, *rest):
    total_in, total = (None, rest[0]) if first else rest
    step = pl.program_id(0)
    rows, width = left_ref.shape[2:]

    @pl.when(step == 0)
    def _():
        total[...] = jnp.zeros_like(total) if first else total_in[...]

    for term in range(2):
        moved, where = [], []
        for slot in range(capacity):
            code = code_ref[2 * step + term, slot]
            source, target = lax.div(code, 2 * blocks), lax.rem(code, 2 * blocks)
            block = vector_ref[0, :, source].reshape(2 * rows, width)
            product = jnp.dot(left_ref[term, slot], block, preferred_element_type=jnp.float32)
            moved.append(product.astype(jnp.bfloat16))
            where.append(target)
        for slot in range(capacity):
            target = where[slot]
            total[target] += jnp.dot(
                moved[slot],
                right_ref[term, jnp.minimum(target, blocks - 1)],
                preferred_element_type=jnp.float32,
            )


def stream_chunk(total, codes, left, vector, right):
    owners, _, blocks, rows, width = vector.shape
    capacity = left.shape[1]
    first = total is None
    spec_total = pl.BlockSpec((blocks + 1, rows, width), lambda s, c: (0, 0, 0))
    return pl.pallas_call(
        functools.partial(stream_kernel, first, capacity, blocks),
        out_shape=jax.ShapeDtypeStruct((blocks + 1, rows, width), jnp.float32),
        grid_spec=pltpu.PrefetchScalarGridSpec(
            num_scalar_prefetch=1,
            grid=(owners,),
            in_specs=[
                pl.BlockSpec((2, capacity, rows, width), lambda s, c: (s, 0, 0, 0)),
                pl.BlockSpec((1, 2, blocks, rows, width), lambda s, c: (s, 0, 0, 0, 0)),
                pl.BlockSpec((2, blocks, width, width), lambda s, c: (0, 0, 0, 0)),
            ]
            + ([] if first else [spec_total]),
            out_specs=spec_total,
        ),
        compiler_params=pltpu.CompilerParams(vmem_limit_bytes=32 * 2**20),
        cost_estimate=pl.CostEstimate(
            flops=owners * 2 * capacity * 2 * 2 * rows * width * width,
            bytes_accessed=left.size * 2 + vector.size * 2 + right.size * 2,
            transcendentals=0,
        ),
    )(codes, left, vector, right, *([] if first else [total]))


def per_device_streamed(wavefunction, left_operator, right_operator, target_owner, target_local):
    owners = lax.axis_size("sec")
    halves = lax.axis_size("term")
    me, half = lax.axis_index("sec"), lax.axis_index("term")
    terms, blocks, height, width = left_operator.shape
    rows = height // halves
    capacity = 2 * blocks // owners

    own_rows = lax.dynamic_slice_in_dim(wavefunction, half * rows, rows, 1)
    codes = slot_codes(target_owner, target_local, owners, capacity)
    sources = codes // (2 * blocks)

    moved_left = []
    for k in range(terms):
        pick = sources[k][:, None, :] * halves + jnp.arange(halves, dtype=jnp.int32)[None, :, None]
        pieces = left_operator[k].reshape(blocks * halves, rows, width)[pick.reshape(-1)]
        pieces = pieces.reshape(owners * halves, capacity, rows, width)
        moved_left.append(lax.all_to_all(pieces, BOTH, split_axis=0, concat_axis=0, tiled=True))
    all_codes = lax.all_gather(codes, BOTH, axis=0)
    my_codes = lax.dynamic_index_in_dim(all_codes, me, axis=3 - 1, keepdims=False)
    gathered = lax.all_gather(own_rows, BOTH, axis=0).reshape(owners, halves, blocks, rows, width)
    right = lax.all_gather(right_operator, "term", axis=1)

    def apply(vector):
        total = None
        for k in range(terms):
            total = stream_chunk(total, my_codes[:, k], moved_left[k], vector, right[k])
        return total[:blocks]

    sigma_rows = apply(gathered)
    wave = own_rows.astype(jnp.float32)
    cross, own = jnp.sum(wave * sigma_rows), jnp.sum(wave * wave)
    local = jnp.where(own > 0, cross / own, 0.0)
    about = jnp.sum(jnp.square(sigma_rows - local * wave))
    stats = lax.all_gather(jnp.stack([about, cross, own, local]), BOTH, axis=0)
    rayleigh = jnp.sum(stats[:, 1]) / jnp.sum(stats[:, 2])
    residual_sq = jnp.sum(stats[:, 0] + jnp.square(stats[:, 3] - rayleigh) * stats[:, 2])
    entries = blocks * owners * height * width
    factor = lax.rsqrt(residual_sq / entries + 1e-06)
    direction = ((sigma_rows - rayleigh * wave) * factor).astype(jnp.bfloat16)
    direction = lax.all_gather(direction, BOTH, axis=0).reshape(gathered.shape)
    sigma_two = apply(direction).astype(jnp.bfloat16)
    return (sigma_two, jnp.reshape(rayleigh, (1,)))


def per_device(wavefunction, *operands):
    gathered_bytes = lax.axis_size("sec") * wavefunction.size * wavefunction.dtype.itemsize
    if 2 * gathered_bytes > RING_BYTES:
        return per_device_streamed(wavefunction, *operands)
    return per_device_ring(wavefunction, *operands)


def solution(mesh):
    placed = (
        P(("rep", "sec"), None, None),
        P("term", ("rep", "sec"), None, None),
        P("term", ("rep", "sec"), None, None),
        P("term", ("rep", "sec"), None),
        P("term", ("rep", "sec")),
    )
    return jax.shard_map(
        per_device,
        mesh=mesh,
        in_specs=placed,
        out_specs=(P(("rep", "sec"), "term", None), P("rep")),
        check_vma=False,
    )
```

```python
import functools

import jax
import jax.numpy as jnp
from jax import lax
from jax.experimental import pallas as pl
from jax.experimental.pallas import tpu as pltpu
from jax.sharding import PartitionSpec as P

BOTH = ("sec", "term")
VMEM_LIMIT = 60 * 2**20
PART = 16
ORDER = [0, 4, 5, 1, 2, 6, 3, 7]
WAITS = {4: 1, 2: 5, 6: 2}
PIECE_WAITS = {6: 4, 7: 5}
RING_BYTES = 24 * 2**20


def ring_order(owners):
    if owners % 2:
        return list(range(owners))
    return list(range(0, owners, 2)) + list(range(owners - 1, 0, -2))


def ring_place(owner, owners):
    if owners % 2:
        return owner
    return jnp.where(owner % 2 == 0, owner // 2, owners - 1 - owner // 2)


def ring_owner(place, owners):
    place = place % owners
    if owners % 2:
        return place
    return jnp.where(place < owners // 2, 2 * place, 2 * (owners - 1 - place) + 1)


def permute(value, owners, halves, target, flip=0):
    pairs = [
        (chip * halves + half, target(chip, half) * halves + (half ^ flip))
        for chip in range(owners)
        for half in range(halves)
    ]
    return lax.ppermute(value, BOTH, pairs)


def swap(value, owners, halves):
    return permute(value, owners, halves, lambda chip, half: chip, 1)


def exchange(value, owners, halves, mask):
    return permute(value, owners, halves, lambda chip, half: chip ^ mask)


def ring_send(value, owners, halves, shifts):
    ring = ring_order(owners)
    place = {chip: index for index, chip in enumerate(ring)}
    return permute(
        value, owners, halves, lambda chip, half: ring[(place[chip] + shifts[half]) % owners]
    )


def select_kernel(half_ref, lower_ref, upper_ref, *rest):
    out_ref = rest[-1]
    out_ref[...] = jnp.where(half_ref[0] == 0, lower_ref[...], upper_ref[...])


def select_half(half, lower, upper, *others):
    anywhere = pl.BlockSpec(memory_space=pl.ANY)
    whole = pl.BlockSpec(memory_space=pltpu.VMEM)
    return pl.pallas_call(
        select_kernel,
        out_shape=jax.ShapeDtypeStruct(lower.shape, lower.dtype),
        in_specs=[pl.BlockSpec(memory_space=pltpu.SMEM), whole, whole] + [anywhere] * len(others),
        out_specs=whole,
        cost_estimate=busy(0.8),
    )(jnp.reshape(half, (1,)).astype(jnp.int32), lower, upper, *others)


def after_kernel(*refs):
    del refs


def after(value, *others):
    anywhere = pl.BlockSpec(memory_space=pl.ANY)
    return pl.pallas_call(
        after_kernel,
        out_shape=jax.ShapeDtypeStruct(value.shape, value.dtype),
        in_specs=[anywhere] * (1 + len(others)),
        out_specs=anywhere,
        input_output_aliases={0: 0},
        cost_estimate=busy(0.3),
    )(value, *others)


def mask_gather(unit, lefts, owners, halves):
    units = {0: unit}
    step = owners // 2
    masks = []
    while step:
        masks.append(step)
        units[step] = exchange(unit, owners, halves, step)
        step //= 2
    waits = dict(WAITS)
    for step in masks[1:]:
        for mask in [m for m in units if m >= 2 * step and m % (2 * step) == 0]:
            if mask in waits:
                units[mask] = after(units[mask], lefts[waits.pop(mask)])
            units[mask | step] = exchange(units[mask], owners, halves, step)
    return units


def spread(value, devices):
    step = 1
    values = []
    while step < devices:
        masks = [step] if 2 * step == devices else [step, 2 * step, 3 * step]
        parts = [lax.ppermute(value, BOTH, [(d, d ^ m) for d in range(devices)]) for m in masks]
        for part in parts:
            value = value + part
        values.append(value)
        step *= 4
    return values


def pack_kernel(order, capacity, blocks, terms, ids_ref, plan_ref, other_plan_ref, *refs):
    left_ref, other_ref, _, *pieces, codes, seen, built, sems = refs
    owners = len(order)
    me, half = ids_ref[0], ids_ref[1]
    rows, width = other_ref.shape[2:]
    start = pl.multiple_of(half * rows, rows)
    parts = rows // PART

    @pl.loop(0, owners)
    def _(owner):
        for index in range(2 * terms * capacity):
            codes[0, owner, index] = 0
            codes[1, owner, index] = blocks

    for stream in range(2 * terms):
        plan = plan_ref if stream < terms else other_plan_ref

        @pl.loop(0, owners)
        def _(owner):
            seen[owner] = 0

        @pl.loop(0, blocks, unroll=4)
        def _(block):
            owner = plan[0, stream % terms, block]
            slot = seen[owner]
            seen[owner] = slot + 1
            codes[0, owner, stream * capacity + slot] = block
            codes[1, owner, stream * capacity + slot] = plan[1, stream % terms, block]

    lane = lax.broadcasted_iota(jnp.int32, (PART, width), 1)
    row = lax.broadcasted_iota(jnp.int32, (PART, width), 0)
    copies = []
    for mask in order:
        owner = me ^ mask
        labels = jnp.zeros((PART, width), jnp.int32)
        for stream in range(2 * terms):
            for slot in range(capacity):
                at = stream * capacity + slot
                block = codes[0, owner, at]
                if stream < terms:
                    value = left_ref[stream, block, pl.ds(start, rows), :]
                else:
                    value = other_ref[stream - terms, block]
                built[mask, at * parts : (at + 1) * parts] = value.reshape(parts, PART, width)
                label = jnp.where(row == 0, block, codes[1, owner, at])
                labels = jnp.where(lane == at, label, labels)
        built[mask, 2 * terms * capacity * parts] = labels.astype(jnp.float32).astype(jnp.bfloat16)
        copies.append(pltpu.make_async_copy(built.at[mask], pieces[mask], sems.at[mask]))
        copies[-1].start()
    for copy in copies:
        copy.wait()


def pack(ids, plan, other_plan, left, other, before, order, capacity):
    terms, blocks, rows, width = other.shape
    owners = len(order)
    scalars = pl.BlockSpec(memory_space=pltpu.SMEM)
    whole = pl.BlockSpec(memory_space=pltpu.VMEM)
    anywhere = pl.BlockSpec(memory_space=pl.ANY)
    shape = (2 * terms * capacity * rows // PART + 1, PART, width)
    return pl.pallas_call(
        functools.partial(pack_kernel, order, capacity, blocks, terms),
        out_shape=[jax.ShapeDtypeStruct(shape, jnp.bfloat16)] * owners,
        in_specs=[scalars] * 3 + [whole, whole, anywhere],
        out_specs=[anywhere] * owners,
        scratch_shapes=[
            pltpu.SMEM((2, owners, 2 * terms * capacity), jnp.int32),
            pltpu.SMEM((owners,), jnp.int32),
            pltpu.VMEM((owners,) + shape, jnp.bfloat16),
            pltpu.SemaphoreType.DMA((owners,)),
        ],
        compiler_params=pltpu.CompilerParams(vmem_limit_bytes=VMEM_LIMIT),
        cost_estimate=busy(5.0),
    )(ids, plan, other_plan, left, other, before)


def busy(microseconds):
    return pl.CostEstimate(
        flops=int(1.15e9 * microseconds), bytes_accessed=0, transcendentals=0
    )


def add_products(left, labels, vector, right, total, side, terms, capacity):
    blocks, rows, width = vector.shape[1:]
    parts = rows // PART
    moved, where = [], []
    for slot in range(terms * capacity):
        at = side * terms * capacity + slot
        block = vector[:, labels[0, at]].reshape(2 * rows, width)
        piece = left[at * parts : (at + 1) * parts].reshape(rows, width)
        product = jnp.dot(piece, block, preferred_element_type=jnp.float32)
        moved.append(product.astype(jnp.bfloat16))
        where.append(labels[1, at])
    for slot in range(terms * capacity):
        total[where[slot]] += jnp.dot(
            moved[slot], right[slot], preferred_element_type=jnp.float32
        )


def local_residual(total, wave_ref, device, rest_ref, stats_ref):
    blocks = wave_ref.shape[0]
    zero = jnp.zeros(wave_ref.shape[1:], jnp.float32)

    def sums(block, carry):
        cross, own = carry
        wave = wave_ref[block].astype(jnp.float32)
        return cross + wave * total[block], own + wave * wave

    cross, own = lax.fori_loop(0, blocks, sums, (zero, zero), unroll=4)
    cross, own = jnp.sum(cross, keepdims=True), jnp.sum(own, keepdims=True)
    local = jnp.where(own > 0, cross / own, 0.0)

    def squares(block, carry):
        rest = total[block] - local * wave_ref[block].astype(jnp.float32)
        rest_ref[block] = rest.astype(rest_ref.dtype)
        return carry + rest * rest

    about = jnp.sum(lax.fori_loop(0, blocks, squares, zero, unroll=4), keepdims=True)
    lane = lax.broadcasted_iota(jnp.int32, stats_ref.shape, 1)
    row = lax.broadcasted_iota(jnp.int32, stats_ref.shape, 0)
    values = jnp.where(lane == 0, about, jnp.where(lane == 1, cross, jnp.where(lane == 2, own, local)))
    stats_ref[...] = jnp.where((row == device) & (lane < 4), values, 0.0)


def form_direction(vector, wave, scale, chip):
    factor = scale[0, 1]
    for part in range(2):
        shift = scale[2 * chip + part, 0]

        @pl.loop(0, vector.shape[1], unroll=4)
        def _(block):
            rest = vector[part, block].astype(jnp.float32)
            rest = rest + shift * wave[part, block].astype(jnp.float32)
            vector[part, block] = (rest * factor).astype(vector.dtype)


def apply_kernel(sources, choices, first, end, terms, capacity, ids_ref, *refs):
    refs = list(refs)

    def take(count):
        taken, refs[:count] = refs[:count], []
        return taken

    (scale,) = take(1) if choices else (None,)
    lefts = take(choices or sources)
    rights = take(2)
    vectors = [take(2) for _ in range(sources)]
    waves = [take(2) for _ in range(choices)]
    (wave_in,) = take(1) if end == "stats" else (None,)
    (total_in,) = (None,) if first else take(1)
    (total_out,) = (None,) if end == "result" else take(1)
    (last_out,) = take(1)
    total, left, right, vector, raw, spread_labels, labels = take(7)
    left_sems, right_sems, vector_sems, raw_sems, label_sem, total_sem = take(6)
    wave, wave_sems = take(2) if choices or end == "stats" else (None, None)
    half = ids_ref[0]
    blocks = vector.shape[2]
    parts = left.shape[1]

    def left_copies(source, piece):
        return [
            pltpu.make_async_copy(piece.at[parts], raw.at[source], raw_sems.at[source]),
            pltpu.make_async_copy(
                piece.at[pl.ds(0, parts)], left.at[source], left_sems.at[source]
            ),
        ]

    def vector_copies(source):
        return [
            pltpu.make_async_copy(
                vectors[source][part],
                vector.at[source, half if part == 0 else 1 - half],
                vector_sems.at[source, part],
            )
            for part in range(2)
        ]

    def wave_copies(source, pair):
        return [
            pltpu.make_async_copy(
                pair[part],
                wave.at[source, half if part == 0 else 1 - half],
                wave_sems.at[source, part],
            )
            for part in range(2)
        ]

    def load_right(source, side):
        for slot in range(terms * capacity):
            target = jnp.minimum(labels[source, 1, side * terms * capacity + slot], blocks - 1)
            pltpu.make_async_copy(
                rights[side].at[slot // capacity, target],
                right.at[source, side, slot],
                right_sems.at[source, side],
            ).start()

    def wait_right(source, side):
        whole = right.at[source, side]
        pltpu.make_async_copy(whole, whole, right_sems.at[source, side]).wait()

    for source in range(sources):
        if choices:
            for choice, piece in enumerate(lefts):

                @pl.when(ids_ref[2 + source] == choice)
                def _():
                    for copy in left_copies(source, piece) + wave_copies(source, waves[choice]):
                        copy.start()

        else:
            for copy in left_copies(source, lefts[source]):
                copy.start()
    for source in range(sources):
        for copy in vector_copies(source):
            copy.start()
    if first:
        total[...] = jnp.zeros_like(total)
    else:
        load_total = pltpu.make_async_copy(total_in, total, total_sem)
        load_total.start()
    if end == "stats":
        load_wave = pltpu.make_async_copy(wave_in, wave.at[0, 0], wave_sems.at[0, 0])
        load_wave.start()
    if end == "go on":
        last_out[...] = jnp.zeros_like(last_out)

    for source in range(sources):
        left_copies(source, lefts[0])[0].wait()
    spread_labels[...] = raw[:, :8].astype(jnp.float32).astype(jnp.int32)
    move_labels = pltpu.make_async_copy(spread_labels, labels, label_sem)
    move_labels.start()
    move_labels.wait()
    for source in range(sources):
        for side in range(2):
            load_right(source, side)
    if not first:
        load_total.wait()
    for source in range(sources):
        for side in range(2):
            if side == 0:
                left_copies(source, lefts[0])[1].wait()
                for copy in vector_copies(source):
                    copy.wait()
                if choices:
                    for copy in wave_copies(source, waves[0]):
                        copy.wait()
                    chip = lax.div(ids_ref[1], 2) ^ ids_ref[2 + source]
                    form_direction(vector.at[source], wave.at[source], scale, chip)
            wait_right(source, side)
            add_products(
                left.at[source],
                labels.at[source],
                vector.at[source],
                right.at[source, side],
                total,
                side,
                terms,
                capacity,
            )
    if end == "result":
        last_out[...] = total[:blocks].astype(last_out.dtype)
    elif end == "stats":
        load_wave.wait()
        local_residual(total, wave.at[0, 0], ids_ref[1], total_out, last_out)
    else:
        store_total = pltpu.make_async_copy(total, total_out, total_sem)
        store_total.start()
        store_total.wait()


def apply_group(ids, lefts, rights, vectors, total, end, wave=None, waves=(), scale=None):
    blocks, rows, width = vectors[0][0].shape
    terms = rights[0].shape[0]
    parts = lefts[0].shape[0] - 1
    capacity = parts * PART // (2 * terms * rows)
    sources, first = len(vectors), total is None
    arrays = [*lefts, *rights] + [unit for pair in [*vectors, *waves] for unit in pair]
    arrays += [wave] if end == "stats" else []
    arrays += [] if first else [total]
    whole = pl.BlockSpec(memory_space=pltpu.VMEM)
    anywhere = pl.BlockSpec(memory_space=pl.ANY)
    total_shape = (blocks + 1, rows, width)
    scratch = [
        pltpu.VMEM(total_shape, jnp.float32),
        pltpu.VMEM((sources, parts, PART, width), jnp.bfloat16),
        pltpu.VMEM((sources, 2, terms * capacity, width, width), jnp.bfloat16),
        pltpu.VMEM((sources, 2, blocks, rows, width), jnp.bfloat16),
        pltpu.VMEM((sources, PART, width), jnp.bfloat16),
        pltpu.VMEM((sources, 8, width), jnp.int32),
        pltpu.SMEM((sources, 8, width), jnp.int32),
        pltpu.SemaphoreType.DMA((sources,)),
        pltpu.SemaphoreType.DMA((sources, 2)),
        pltpu.SemaphoreType.DMA((sources, 2)),
        pltpu.SemaphoreType.DMA((sources,)),
        pltpu.SemaphoreType.DMA,
        pltpu.SemaphoreType.DMA,
    ]
    if waves or end == "stats":
        scratch += [
            pltpu.VMEM((sources, 2, blocks, rows, width), jnp.bfloat16),
            pltpu.SemaphoreType.DMA((sources, 2)),
        ]
    devices = lax.axis_size("sec") * lax.axis_size("term")
    total_out = jax.ShapeDtypeStruct(total_shape, jnp.float32)
    out_shape, out_specs = {
        "go on": ((total_out, jax.ShapeDtypeStruct((8, width), jnp.float32)), (anywhere, whole)),
        "stats": (
            (
                jax.ShapeDtypeStruct((blocks, rows, width), jnp.bfloat16),
                jax.ShapeDtypeStruct((devices, 128), jnp.float32),
            ),
            (whole, whole),
        ),
        "result": (jax.ShapeDtypeStruct((blocks, rows, width), jnp.bfloat16), whole),
    }[end]
    choices = len(waves)
    scalars = [ids] if scale is None else [ids, scale]
    return pl.pallas_call(
        functools.partial(apply_kernel, sources, choices, first, end, terms, capacity),
        out_shape=out_shape,
        in_specs=[pl.BlockSpec(memory_space=pltpu.SMEM)] * len(scalars) + [anywhere] * len(arrays),
        out_specs=out_specs,
        scratch_shapes=scratch,
        compiler_params=pltpu.CompilerParams(vmem_limit_bytes=VMEM_LIMIT),
        cost_estimate=busy(3.5 + (2.7 if waves else 1.8) * sources),
    )(*scalars, *arrays)


def scale_kernel(entries, stats_ref, scale_ref, rayleigh_ref):
    stats = stats_ref[...]
    about, cross, own, local = (stats[:, lane : lane + 1] for lane in range(4))
    rayleigh = jnp.sum(cross, keepdims=True) / jnp.sum(own, keepdims=True)
    offset = local - rayleigh
    residual_sq = jnp.sum(about + offset * offset * own, keepdims=True)
    factor = lax.rsqrt(residual_sq / entries + 1e-06)
    lane = lax.broadcasted_iota(jnp.int32, scale_ref.shape, 1)
    scale_ref[...] = jnp.where(lane == 0, offset, factor)
    rayleigh_ref[...] = rayleigh


def scales(stats, entries):
    whole = pl.BlockSpec(memory_space=pltpu.VMEM)
    return pl.pallas_call(
        functools.partial(scale_kernel, entries),
        out_shape=(
            jax.ShapeDtypeStruct(stats.shape, jnp.float32),
            jax.ShapeDtypeStruct((1, 1), jnp.float32),
        ),
        in_specs=[whole],
        out_specs=(whole, whole),
        cost_estimate=busy(0.7),
    )(stats)


def per_device_ring(wavefunction, left_operator, right_operator, target_owner, target_local):
    owners, halves = lax.axis_size("sec"), lax.axis_size("term")
    me, half = lax.axis_index("sec"), lax.axis_index("term")
    terms, blocks, height, width = left_operator.shape
    rows = height // halves
    capacity = 2 * blocks // owners
    place = ring_place(me, owners)
    ids = jnp.stack([me, half]).astype(jnp.int32)

    own_rows = lax.dynamic_slice_in_dim(wavefunction, half * rows, rows, 1)
    other_rows = lax.dynamic_slice_in_dim(wavefunction, (1 - half) * rows, rows, 1)
    plan = jnp.stack([target_owner[:, :, 0], target_local])
    other_left = swap(
        lax.dynamic_slice_in_dim(left_operator, (1 - half) * rows, rows, 2), owners, halves
    )
    order = [m for m in ORDER if m < owners] + list(range(len(ORDER), owners))
    rights = (right_operator, swap(right_operator, owners, halves))
    pieces = pack(
        ids,
        plan,
        swap(plan, owners, halves),
        left_operator,
        other_left,
        plan,
        order[1:] + order[:1],
        capacity,
    )
    lefts = [pieces[0]]
    for m in range(1, owners):
        piece = pieces[m]
        if m in PIECE_WAITS:
            piece = after(piece, lefts[PIECE_WAITS[m]])
        lefts.append(exchange(piece, owners, halves, m))
    near = mask_gather(own_rows, lefts, owners, halves)
    far = {m: swap(unit, owners, halves) if m else other_rows for m, unit in near.items()}

    here = [half, me * halves + half]
    no_choice = jnp.stack(here).astype(jnp.int32)
    total = None
    for at in range(0, owners, 2):
        group = order[at : at + 2]
        total, stats = apply_group(
            no_choice,
            [lefts[m] for m in group],
            rights,
            [(near[m], far[m]) for m in group],
            total,
            "go on" if at + 2 < owners else "stats",
            own_rows,
        )

    stats = spread(stats, owners * halves)
    rest = after(total, stats[0])
    entries = blocks * owners * height * width
    scale, rayleigh = scales(stats[-1], entries)
    reach = (owners - 1) // 2
    waves = [(near[m], far[m]) for m in range(owners)]

    def add_group(total, units, end):
        choices = [me ^ ring_owner(place - s, owners) for s in units]
        vectors = [(unit, swap(unit, owners, halves)) for unit in units.values()]
        ids = jnp.stack(here + choices).astype(jnp.int32)
        return apply_group(
            ids, lefts, rights, vectors, total, end, waves=waves, scale=scale
        )

    total = token = None
    units = {0: rest}
    waiting = {}
    ahead = behind = rest
    for step in range(1, reach + 1):
        ahead = ring_send(ahead, owners, halves, (1,) * halves)
        behind = ring_send(behind, owners, halves, (-1,) * halves)
        if step == reach:
            total, token = add_group(total, waiting, "go on")
            waiting = {}
            ahead = after(ahead, token)
        waiting.update(units)
        units = {step: ahead, -step: behind}
    last = ring_send(select_half(half, ahead, behind), owners, halves, (1, -1))
    total, token = add_group(total, waiting, "go on")
    last = after(last, token)
    total = add_group(total, {**units, owners // 2: last}, "result")
    return (total, rayleigh[0])


def slot_codes(target_owner, target_local, owners, capacity):
    terms, blocks = target_local.shape
    owner = target_owner[:, :, 0]
    place = jnp.arange(blocks, dtype=jnp.int32)
    same = (owner[:, :, None] == owner[:, None, :]) & (place[None, :] < place[:, None])[None]
    position = jnp.sum(same.astype(jnp.int32), axis=2)
    hit = (
        owner[:, None, None, :] == jnp.arange(owners, dtype=jnp.int32)[None, :, None, None]
    ) & (position[:, None, None, :] == jnp.arange(capacity, dtype=jnp.int32)[None, None, :, None])
    code = place[None, :] * (2 * blocks) + target_local - blocks
    return blocks + jnp.sum(jnp.where(hit, code[:, None, None, :], 0), axis=3)


def stream_kernel(first, capacity, blocks, code_ref, left_ref, vector_ref, right_ref, *rest):
    total_in, total = (None, rest[0]) if first else rest
    step = pl.program_id(0)
    rows, width = left_ref.shape[2:]

    @pl.when(step == 0)
    def _():
        total[...] = jnp.zeros_like(total) if first else total_in[...]

    for term in range(2):
        moved, where = [], []
        for slot in range(capacity):
            code = code_ref[2 * step + term, slot]
            source, target = lax.div(code, 2 * blocks), lax.rem(code, 2 * blocks)
            block = vector_ref[0, :, source].reshape(2 * rows, width)
            product = jnp.dot(left_ref[term, slot], block, preferred_element_type=jnp.float32)
            moved.append(product.astype(jnp.bfloat16))
            where.append(target)
        for slot in range(capacity):
            target = where[slot]
            total[target] += jnp.dot(
                moved[slot],
                right_ref[term, jnp.minimum(target, blocks - 1)],
                preferred_element_type=jnp.float32,
            )


def stream_chunk(total, codes, left, vector, right):
    owners, _, blocks, rows, width = vector.shape
    capacity = left.shape[1]
    first = total is None
    spec_total = pl.BlockSpec((blocks + 1, rows, width), lambda s, c: (0, 0, 0))
    return pl.pallas_call(
        functools.partial(stream_kernel, first, capacity, blocks),
        out_shape=jax.ShapeDtypeStruct((blocks + 1, rows, width), jnp.float32),
        grid_spec=pltpu.PrefetchScalarGridSpec(
            num_scalar_prefetch=1,
            grid=(owners,),
            in_specs=[
                pl.BlockSpec((2, capacity, rows, width), lambda s, c: (s, 0, 0, 0)),
                pl.BlockSpec((1, 2, blocks, rows, width), lambda s, c: (s, 0, 0, 0, 0)),
                pl.BlockSpec((2, blocks, width, width), lambda s, c: (0, 0, 0, 0)),
            ]
            + ([] if first else [spec_total]),
            out_specs=spec_total,
        ),
        compiler_params=pltpu.CompilerParams(vmem_limit_bytes=32 * 2**20),
        cost_estimate=pl.CostEstimate(
            flops=owners * 2 * capacity * 2 * 2 * rows * width * width,
            bytes_accessed=left.size * 2 + vector.size * 2 + right.size * 2,
            transcendentals=0,
        ),
    )(codes, left, vector, right, *([] if first else [total]))


def per_device_streamed(wavefunction, left_operator, right_operator, target_owner, target_local):
    owners = lax.axis_size("sec")
    halves = lax.axis_size("term")
    me, half = lax.axis_index("sec"), lax.axis_index("term")
    terms, blocks, height, width = left_operator.shape
    rows = height // halves
    capacity = 2 * blocks // owners

    own_rows = lax.dynamic_slice_in_dim(wavefunction, half * rows, rows, 1)
    codes = slot_codes(target_owner, target_local, owners, capacity)
    sources = codes // (2 * blocks)

    moved_left = []
    for k in range(terms):
        pick = sources[k][:, None, :] * halves + jnp.arange(halves, dtype=jnp.int32)[None, :, None]
        pieces = left_operator[k].reshape(blocks * halves, rows, width)[pick.reshape(-1)]
        pieces = pieces.reshape(owners * halves, capacity, rows, width)
        moved_left.append(lax.all_to_all(pieces, BOTH, split_axis=0, concat_axis=0, tiled=True))
    all_codes = lax.all_gather(codes, BOTH, axis=0)
    my_codes = lax.dynamic_index_in_dim(all_codes, me, axis=3 - 1, keepdims=False)
    gathered = lax.all_gather(own_rows, BOTH, axis=0).reshape(owners, halves, blocks, rows, width)
    right = lax.all_gather(right_operator, "term", axis=1)

    def apply(vector):
        total = None
        for k in range(terms):
            total = stream_chunk(total, my_codes[:, k], moved_left[k], vector, right[k])
        return total[:blocks]

    sigma_rows = apply(gathered)
    wave = own_rows.astype(jnp.float32)
    cross, own = jnp.sum(wave * sigma_rows), jnp.sum(wave * wave)
    local = jnp.where(own > 0, cross / own, 0.0)
    about = jnp.sum(jnp.square(sigma_rows - local * wave))
    stats = lax.all_gather(jnp.stack([about, cross, own, local]), BOTH, axis=0)
    rayleigh = jnp.sum(stats[:, 1]) / jnp.sum(stats[:, 2])
    residual_sq = jnp.sum(stats[:, 0] + jnp.square(stats[:, 3] - rayleigh) * stats[:, 2])
    entries = blocks * owners * height * width
    factor = lax.rsqrt(residual_sq / entries + 1e-06)
    direction = ((sigma_rows - rayleigh * wave) * factor).astype(jnp.bfloat16)
    direction = lax.all_gather(direction, BOTH, axis=0).reshape(gathered.shape)
    sigma_two = apply(direction).astype(jnp.bfloat16)
    return (sigma_two, jnp.reshape(rayleigh, (1,)))


def per_device(wavefunction, *operands):
    gathered_bytes = lax.axis_size("sec") * wavefunction.size * wavefunction.dtype.itemsize
    if 2 * gathered_bytes > RING_BYTES:
        return per_device_streamed(wavefunction, *operands)
    return per_device_ring(wavefunction, *operands)


def solution(mesh):
    placed = (
        P(("rep", "sec"), None, None),
        P("term", ("rep", "sec"), None, None),
        P("term", ("rep", "sec"), None, None),
        P("term", ("rep", "sec"), None),
        P("term", ("rep", "sec")),
    )
    return jax.shard_map(
        per_device,
        mesh=mesh,
        in_specs=placed,
        out_specs=(P(("rep", "sec"), "term", None), P("rep")),
        check_vma=False,
    )
```

```python
import functools

import jax
import jax.numpy as jnp
from jax import lax
from jax.experimental import pallas as pl
from jax.experimental.pallas import tpu as pltpu
from jax.sharding import PartitionSpec as P

BOTH = ("sec", "term")
VMEM_LIMIT = 60 * 2**20
PART = 16
ORDER = [0, 4, 5, 1, 2, 6, 3, 7]
WAITS = {4: 1, 2: 5, 6: 2}
PIECE_WAITS = {6: 4, 7: 5}
RING_BYTES = 24 * 2**20


def ring_order(owners):
    if owners % 2:
        return list(range(owners))
    return list(range(0, owners, 2)) + list(range(owners - 1, 0, -2))


def ring_place(owner, owners):
    if owners % 2:
        return owner
    return jnp.where(owner % 2 == 0, owner // 2, owners - 1 - owner // 2)


def ring_owner(place, owners):
    place = place % owners
    if owners % 2:
        return place
    return jnp.where(place < owners // 2, 2 * place, 2 * (owners - 1 - place) + 1)


def permute(value, owners, halves, target, flip=0):
    pairs = [
        (chip * halves + half, target(chip, half) * halves + (half ^ flip))
        for chip in range(owners)
        for half in range(halves)
    ]
    return lax.ppermute(value, BOTH, pairs)


def swap(value, owners, halves):
    return permute(value, owners, halves, lambda chip, half: chip, 1)


def exchange(value, owners, halves, mask):
    return permute(value, owners, halves, lambda chip, half: chip ^ mask)


def ring_send(value, owners, halves, shifts):
    ring = ring_order(owners)
    place = {chip: index for index, chip in enumerate(ring)}
    return permute(
        value, owners, halves, lambda chip, half: ring[(place[chip] + shifts[half]) % owners]
    )


def select_kernel(half_ref, lower_ref, upper_ref, *rest):
    out_ref = rest[-1]
    out_ref[...] = jnp.where(half_ref[0] == 0, lower_ref[...], upper_ref[...])


def select_half(half, lower, upper, *others):
    anywhere = pl.BlockSpec(memory_space=pl.ANY)
    whole = pl.BlockSpec(memory_space=pltpu.VMEM)
    return pl.pallas_call(
        select_kernel,
        out_shape=jax.ShapeDtypeStruct(lower.shape, lower.dtype),
        in_specs=[pl.BlockSpec(memory_space=pltpu.SMEM), whole, whole] + [anywhere] * len(others),
        out_specs=whole,
        cost_estimate=busy(0.8),
    )(jnp.reshape(half, (1,)).astype(jnp.int32), lower, upper, *others)


def after_kernel(*refs):
    del refs


def after(value, *others):
    anywhere = pl.BlockSpec(memory_space=pl.ANY)
    return pl.pallas_call(
        after_kernel,
        out_shape=jax.ShapeDtypeStruct(value.shape, value.dtype),
        in_specs=[anywhere] * (1 + len(others)),
        out_specs=anywhere,
        input_output_aliases={0: 0},
        cost_estimate=busy(0.3),
    )(value, *others)


def mask_gather(unit, lefts, owners, halves):
    units = {0: unit}
    step = owners // 2
    masks = []
    while step:
        masks.append(step)
        units[step] = exchange(unit, owners, halves, step)
        step //= 2
    waits = dict(WAITS)
    for step in masks[1:]:
        for mask in [m for m in units if m >= 2 * step and m % (2 * step) == 0]:
            if mask in waits:
                units[mask] = after(units[mask], lefts[waits.pop(mask)])
            units[mask | step] = exchange(units[mask], owners, halves, step)
    return units


def spread(value, devices, before):
    step = 1
    while step < devices:
        if step > 1:
            value = after(value, before)
        masks = [step] if 2 * step == devices else [step, 2 * step, 3 * step]
        parts = [lax.ppermute(value, BOTH, [(d, d ^ m) for d in range(devices)]) for m in masks]
        for part in parts:
            value = value + part
        step *= 4
    return value


def pack_kernel(order, capacity, blocks, terms, ids_ref, plan_ref, other_plan_ref, *refs):
    left_ref, other_ref, _, *pieces, codes, seen, built, sems = refs
    owners = len(order)
    me, half = ids_ref[0], ids_ref[1]
    rows, width = other_ref.shape[2:]
    start = pl.multiple_of(half * rows, rows)
    parts = rows // PART

    @pl.loop(0, owners)
    def _(owner):
        for index in range(2 * terms * capacity):
            codes[0, owner, index] = 0
            codes[1, owner, index] = blocks

    for stream in range(2 * terms):
        plan = plan_ref if stream < terms else other_plan_ref

        @pl.loop(0, owners)
        def _(owner):
            seen[owner] = 0

        @pl.loop(0, blocks, unroll=4)
        def _(block):
            owner = plan[0, stream % terms, block]
            slot = seen[owner]
            seen[owner] = slot + 1
            codes[0, owner, stream * capacity + slot] = block
            codes[1, owner, stream * capacity + slot] = plan[1, stream % terms, block]

    lane = lax.broadcasted_iota(jnp.int32, (PART, width), 1)
    row = lax.broadcasted_iota(jnp.int32, (PART, width), 0)
    copies = []
    for mask in order:
        owner = me ^ mask
        labels = jnp.zeros((PART, width), jnp.int32)
        for stream in range(2 * terms):
            for slot in range(capacity):
                at = stream * capacity + slot
                block = codes[0, owner, at]
                if stream < terms:
                    value = left_ref[stream, block, pl.ds(start, rows), :]
                else:
                    value = other_ref[stream - terms, block]
                built[mask, at * parts : (at + 1) * parts] = value.reshape(parts, PART, width)
                label = jnp.where(row == 0, block, codes[1, owner, at])
                labels = jnp.where(lane == at, label, labels)
        built[mask, 2 * terms * capacity * parts] = labels.astype(jnp.float32).astype(jnp.bfloat16)
        copies.append(pltpu.make_async_copy(built.at[mask], pieces[mask], sems.at[mask]))
        copies[-1].start()
    for copy in copies:
        copy.wait()


def pack(ids, plan, other_plan, left, other, before, order, capacity):
    terms, blocks, rows, width = other.shape
    owners = len(order)
    scalars = pl.BlockSpec(memory_space=pltpu.SMEM)
    whole = pl.BlockSpec(memory_space=pltpu.VMEM)
    anywhere = pl.BlockSpec(memory_space=pl.ANY)
    shape = (2 * terms * capacity * rows // PART + 1, PART, width)
    return pl.pallas_call(
        functools.partial(pack_kernel, order, capacity, blocks, terms),
        out_shape=[jax.ShapeDtypeStruct(shape, jnp.bfloat16)] * owners,
        in_specs=[scalars] * 3 + [whole, whole, anywhere],
        out_specs=[anywhere] * owners,
        scratch_shapes=[
            pltpu.SMEM((2, owners, 2 * terms * capacity), jnp.int32),
            pltpu.SMEM((owners,), jnp.int32),
            pltpu.VMEM((owners,) + shape, jnp.bfloat16),
            pltpu.SemaphoreType.DMA((owners,)),
        ],
        compiler_params=pltpu.CompilerParams(vmem_limit_bytes=VMEM_LIMIT),
        cost_estimate=busy(5.0),
    )(ids, plan, other_plan, left, other, before)


def busy(microseconds):
    return pl.CostEstimate(
        flops=int(1.15e9 * microseconds), bytes_accessed=0, transcendentals=0
    )


def add_products(left, labels, vector, right, total, side, terms, capacity):
    blocks, rows, width = vector.shape[1:]
    parts = rows // PART
    moved, where = [], []
    for slot in range(terms * capacity):
        at = side * terms * capacity + slot
        block = vector[:, labels[0, at]].reshape(2 * rows, width)
        piece = left[at * parts : (at + 1) * parts].reshape(rows, width)
        product = jnp.dot(piece, block, preferred_element_type=jnp.float32)
        moved.append(product.astype(jnp.bfloat16))
        where.append(labels[1, at])
    for slot in range(terms * capacity):
        total[where[slot]] += jnp.dot(
            moved[slot], right[slot], preferred_element_type=jnp.float32
        )


def local_residual(total, wave_ref, device, rest_ref, stats_ref):
    blocks = wave_ref.shape[0]
    zero = jnp.zeros(wave_ref.shape[1:], jnp.float32)

    def sums(block, carry):
        cross, own = carry
        wave = wave_ref[block].astype(jnp.float32)
        return cross + wave * total[block], own + wave * wave

    cross, own = lax.fori_loop(0, blocks, sums, (zero, zero), unroll=4)
    cross, own = jnp.sum(cross, keepdims=True), jnp.sum(own, keepdims=True)
    local = jnp.where(own > 0, cross / own, 0.0)

    def squares(block, carry):
        rest = total[block] - local * wave_ref[block].astype(jnp.float32)
        rest_ref[block] = rest.astype(rest_ref.dtype)
        return carry + rest * rest

    about = jnp.sum(lax.fori_loop(0, blocks, squares, zero, unroll=4), keepdims=True)
    lane = lax.broadcasted_iota(jnp.int32, stats_ref.shape, 1)
    row = lax.broadcasted_iota(jnp.int32, stats_ref.shape, 0)
    values = jnp.where(lane == 0, about, jnp.where(lane == 1, cross, jnp.where(lane == 2, own, local)))
    stats_ref[...] = jnp.where((row == device) & (lane < 4), values, 0.0)


def form_direction(vector, wave, scale, chip):
    factor = scale[0, 1]
    for part in range(2):
        shift = scale[2 * chip + part, 0]

        @pl.loop(0, vector.shape[1], unroll=4)
        def _(block):
            rest = vector[part, block].astype(jnp.float32)
            rest = rest + shift * wave[part, block].astype(jnp.float32)
            vector[part, block] = (rest * factor).astype(vector.dtype)


def apply_kernel(sources, choices, first, end, terms, capacity, ids_ref, *refs):
    refs = list(refs)

    def take(count):
        taken, refs[:count] = refs[:count], []
        return taken

    (scale,) = take(1) if choices else (None,)
    lefts = take(choices or sources)
    rights = take(2)
    vectors = [take(2) for _ in range(sources)]
    waves = [take(2) for _ in range(choices)]
    (wave_in,) = take(1) if end == "stats" else (None,)
    (total_in,) = (None,) if first else take(1)
    (total_out,) = (None,) if end == "result" else take(1)
    (last_out,) = take(1)
    total, left, right, vector, raw, spread_labels, labels = take(7)
    left_sems, right_sems, vector_sems, raw_sems, label_sem, total_sem = take(6)
    wave, wave_sems = take(2) if choices or end == "stats" else (None, None)
    half = ids_ref[0]
    blocks = vector.shape[2]
    parts = left.shape[1]

    def left_copies(source, piece):
        return [
            pltpu.make_async_copy(piece.at[parts], raw.at[source], raw_sems.at[source]),
            pltpu.make_async_copy(
                piece.at[pl.ds(0, parts)], left.at[source], left_sems.at[source]
            ),
        ]

    def vector_copies(source):
        return [
            pltpu.make_async_copy(
                vectors[source][part],
                vector.at[source, half if part == 0 else 1 - half],
                vector_sems.at[source, part],
            )
            for part in range(2)
        ]

    def wave_copies(source, pair):
        return [
            pltpu.make_async_copy(
                pair[part],
                wave.at[source, half if part == 0 else 1 - half],
                wave_sems.at[source, part],
            )
            for part in range(2)
        ]

    def load_right(source, side):
        for slot in range(terms * capacity):
            target = jnp.minimum(labels[source, 1, side * terms * capacity + slot], blocks - 1)
            pltpu.make_async_copy(
                rights[side].at[slot // capacity, target],
                right.at[source, side, slot],
                right_sems.at[source, side],
            ).start()

    def wait_right(source, side):
        whole = right.at[source, side]
        pltpu.make_async_copy(whole, whole, right_sems.at[source, side]).wait()

    for source in range(sources):
        if choices:
            for choice, piece in enumerate(lefts):

                @pl.when(ids_ref[2 + source] == choice)
                def _():
                    for copy in left_copies(source, piece) + wave_copies(source, waves[choice]):
                        copy.start()

        else:
            for copy in left_copies(source, lefts[source]):
                copy.start()
    for source in range(sources):
        for copy in vector_copies(source):
            copy.start()
    if first:
        total[...] = jnp.zeros_like(total)
    else:
        load_total = pltpu.make_async_copy(total_in, total, total_sem)
        load_total.start()
    if end == "stats":
        load_wave = pltpu.make_async_copy(wave_in, wave.at[0, 0], wave_sems.at[0, 0])
        load_wave.start()
    if end == "go on":
        last_out[...] = jnp.zeros_like(last_out)

    for source in range(sources):
        left_copies(source, lefts[0])[0].wait()
    spread_labels[...] = raw[:, :8].astype(jnp.float32).astype(jnp.int32)
    move_labels = pltpu.make_async_copy(spread_labels, labels, label_sem)
    move_labels.start()
    move_labels.wait()
    for source in range(sources):
        for side in range(2):
            load_right(source, side)
    if not first:
        load_total.wait()
    for source in range(sources):
        for side in range(2):
            if side == 0:
                left_copies(source, lefts[0])[1].wait()
                for copy in vector_copies(source):
                    copy.wait()
                if choices:
                    for copy in wave_copies(source, waves[0]):
                        copy.wait()
                    chip = lax.div(ids_ref[1], 2) ^ ids_ref[2 + source]
                    form_direction(vector.at[source], wave.at[source], scale, chip)
            wait_right(source, side)
            add_products(
                left.at[source],
                labels.at[source],
                vector.at[source],
                right.at[source, side],
                total,
                side,
                terms,
                capacity,
            )
    if end == "result":
        last_out[...] = total[:blocks].astype(last_out.dtype)
    elif end == "stats":
        load_wave.wait()
        local_residual(total, wave.at[0, 0], ids_ref[1], total_out, last_out)
    else:
        store_total = pltpu.make_async_copy(total, total_out, total_sem)
        store_total.start()
        store_total.wait()


def apply_group(ids, lefts, rights, vectors, total, end, wave=None, waves=(), scale=None):
    blocks, rows, width = vectors[0][0].shape
    terms = rights[0].shape[0]
    parts = lefts[0].shape[0] - 1
    capacity = parts * PART // (2 * terms * rows)
    sources, first = len(vectors), total is None
    arrays = [*lefts, *rights] + [unit for pair in [*vectors, *waves] for unit in pair]
    arrays += [wave] if end == "stats" else []
    arrays += [] if first else [total]
    whole = pl.BlockSpec(memory_space=pltpu.VMEM)
    anywhere = pl.BlockSpec(memory_space=pl.ANY)
    total_shape = (blocks + 1, rows, width)
    scratch = [
        pltpu.VMEM(total_shape, jnp.float32),
        pltpu.VMEM((sources, parts, PART, width), jnp.bfloat16),
        pltpu.VMEM((sources, 2, terms * capacity, width, width), jnp.bfloat16),
        pltpu.VMEM((sources, 2, blocks, rows, width), jnp.bfloat16),
        pltpu.VMEM((sources, PART, width), jnp.bfloat16),
        pltpu.VMEM((sources, 8, width), jnp.int32),
        pltpu.SMEM((sources, 8, width), jnp.int32),
        pltpu.SemaphoreType.DMA((sources,)),
        pltpu.SemaphoreType.DMA((sources, 2)),
        pltpu.SemaphoreType.DMA((sources, 2)),
        pltpu.SemaphoreType.DMA((sources,)),
        pltpu.SemaphoreType.DMA,
        pltpu.SemaphoreType.DMA,
    ]
    if waves or end == "stats":
        scratch += [
            pltpu.VMEM((sources, 2, blocks, rows, width), jnp.bfloat16),
            pltpu.SemaphoreType.DMA((sources, 2)),
        ]
    devices = lax.axis_size("sec") * lax.axis_size("term")
    total_out = jax.ShapeDtypeStruct(total_shape, jnp.float32)
    out_shape, out_specs = {
        "go on": ((total_out, jax.ShapeDtypeStruct((8, width), jnp.float32)), (anywhere, whole)),
        "stats": (
            (
                jax.ShapeDtypeStruct((blocks, rows, width), jnp.bfloat16),
                jax.ShapeDtypeStruct((devices, 128), jnp.float32),
            ),
            (whole, whole),
        ),
        "result": (jax.ShapeDtypeStruct((blocks, rows, width), jnp.bfloat16), whole),
    }[end]
    choices = len(waves)
    scalars = [ids] if scale is None else [ids, scale]
    return pl.pallas_call(
        functools.partial(apply_kernel, sources, choices, first, end, terms, capacity),
        out_shape=out_shape,
        in_specs=[pl.BlockSpec(memory_space=pltpu.SMEM)] * len(scalars) + [anywhere] * len(arrays),
        out_specs=out_specs,
        scratch_shapes=scratch,
        compiler_params=pltpu.CompilerParams(vmem_limit_bytes=VMEM_LIMIT),
        cost_estimate=busy(0.5 if waves else 3.5 + 1.8 * sources),
    )(*scalars, *arrays)


def scale_kernel(entries, stats_ref, scale_ref, rayleigh_ref):
    stats = stats_ref[...]
    about, cross, own, local = (stats[:, lane : lane + 1] for lane in range(4))
    rayleigh = jnp.sum(cross, keepdims=True) / jnp.sum(own, keepdims=True)
    offset = local - rayleigh
    residual_sq = jnp.sum(about + offset * offset * own, keepdims=True)
    factor = lax.rsqrt(residual_sq / entries + 1e-06)
    lane = lax.broadcasted_iota(jnp.int32, scale_ref.shape, 1)
    scale_ref[...] = jnp.where(lane == 0, offset, factor)
    rayleigh_ref[...] = rayleigh


def scales(stats, entries):
    whole = pl.BlockSpec(memory_space=pltpu.VMEM)
    return pl.pallas_call(
        functools.partial(scale_kernel, entries),
        out_shape=(
            jax.ShapeDtypeStruct(stats.shape, jnp.float32),
            jax.ShapeDtypeStruct((1, 1), jnp.float32),
        ),
        in_specs=[whole],
        out_specs=(whole, whole),
        cost_estimate=busy(0.7),
    )(stats)


def per_device_ring(wavefunction, left_operator, right_operator, target_owner, target_local):
    owners, halves = lax.axis_size("sec"), lax.axis_size("term")
    me, half = lax.axis_index("sec"), lax.axis_index("term")
    terms, blocks, height, width = left_operator.shape
    rows = height // halves
    capacity = 2 * blocks // owners
    place = ring_place(me, owners)
    ids = jnp.stack([me, half]).astype(jnp.int32)

    own_rows = lax.dynamic_slice_in_dim(wavefunction, half * rows, rows, 1)
    other_rows = lax.dynamic_slice_in_dim(wavefunction, (1 - half) * rows, rows, 1)
    plan = jnp.stack([target_owner[:, :, 0], target_local])
    other_left = swap(
        lax.dynamic_slice_in_dim(left_operator, (1 - half) * rows, rows, 2), owners, halves
    )
    order = [m for m in ORDER if m < owners] + list(range(len(ORDER), owners))
    rights = (right_operator, swap(right_operator, owners, halves))
    pieces = pack(
        ids,
        plan,
        swap(plan, owners, halves),
        left_operator,
        other_left,
        plan,
        order[1:] + order[:1],
        capacity,
    )
    lefts = [pieces[0]]
    for m in range(1, owners):
        piece = pieces[m]
        if m in PIECE_WAITS:
            piece = after(piece, lefts[PIECE_WAITS[m]])
        lefts.append(exchange(piece, owners, halves, m))
    near = mask_gather(own_rows, lefts, owners, halves)
    far = {m: swap(unit, owners, halves) if m else other_rows for m, unit in near.items()}

    here = [half, me * halves + half]
    no_choice = jnp.stack(here).astype(jnp.int32)
    total = None
    for at in range(0, owners, 2):
        group = order[at : at + 2]
        total, stats = apply_group(
            no_choice,
            [lefts[m] for m in group],
            rights,
            [(near[m], far[m]) for m in group],
            total,
            "go on" if at + 2 < owners else "stats",
            own_rows,
        )

    rest = total
    ahead = ring_send(rest, owners, halves, (1,) * halves)
    behind = ring_send(rest, owners, halves, (-1,) * halves)
    entries = blocks * owners * height * width
    scale, rayleigh = scales(spread(stats, owners * halves, ahead), entries)
    reach = (owners - 1) // 2
    waves = [(near[m], far[m]) for m in range(owners)]

    def add_group(total, units, end):
        choices = [me ^ ring_owner(place - s, owners) for s in units]
        vectors = [(unit, swap(unit, owners, halves)) for unit in units.values()]
        ids = jnp.stack(here + choices).astype(jnp.int32)
        return apply_group(
            ids, lefts, rights, vectors, total, end, waves=waves, scale=scale
        )

    total, token = None, None
    units, waiting = {1: ahead, -1: behind}, {0: rest}
    for step in range(2, reach + 1):
        ahead = ring_send(ahead, owners, halves, (1,) * halves)
        behind = ring_send(behind, owners, halves, (-1,) * halves)
        total, token = add_group(total, waiting, "go on")
        ahead = after(ahead, token)
        waiting = units if step == 2 else {}
        units = {step: ahead, -step: behind}
        waiting = {**waiting, **units}
    last = ring_send(select_half(half, ahead, behind), owners, halves, (1, -1))
    total, token = add_group(total, waiting, "go on")
    total = add_group(total, {owners // 2: after(last, token)}, "result")
    return (total, rayleigh[0])


def slot_codes(target_owner, target_local, owners, capacity):
    terms, blocks = target_local.shape
    owner = target_owner[:, :, 0]
    place = jnp.arange(blocks, dtype=jnp.int32)
    same = (owner[:, :, None] == owner[:, None, :]) & (place[None, :] < place[:, None])[None]
    position = jnp.sum(same.astype(jnp.int32), axis=2)
    hit = (
        owner[:, None, None, :] == jnp.arange(owners, dtype=jnp.int32)[None, :, None, None]
    ) & (position[:, None, None, :] == jnp.arange(capacity, dtype=jnp.int32)[None, None, :, None])
    code = place[None, :] * (2 * blocks) + target_local - blocks
    return blocks + jnp.sum(jnp.where(hit, code[:, None, None, :], 0), axis=3)


def stream_kernel(first, capacity, blocks, code_ref, left_ref, vector_ref, right_ref, *rest):
    total_in, total = (None, rest[0]) if first else rest
    step = pl.program_id(0)
    rows, width = left_ref.shape[2:]

    @pl.when(step == 0)
    def _():
        total[...] = jnp.zeros_like(total) if first else total_in[...]

    for term in range(2):
        moved, where = [], []
        for slot in range(capacity):
            code = code_ref[2 * step + term, slot]
            source, target = lax.div(code, 2 * blocks), lax.rem(code, 2 * blocks)
            block = vector_ref[0, :, source].reshape(2 * rows, width)
            product = jnp.dot(left_ref[term, slot], block, preferred_element_type=jnp.float32)
            moved.append(product.astype(jnp.bfloat16))
            where.append(target)
        for slot in range(capacity):
            target = where[slot]
            total[target] += jnp.dot(
                moved[slot],
                right_ref[term, jnp.minimum(target, blocks - 1)],
                preferred_element_type=jnp.float32,
            )


def stream_chunk(total, codes, left, vector, right):
    owners, _, blocks, rows, width = vector.shape
    capacity = left.shape[1]
    first = total is None
    spec_total = pl.BlockSpec((blocks + 1, rows, width), lambda s, c: (0, 0, 0))
    return pl.pallas_call(
        functools.partial(stream_kernel, first, capacity, blocks),
        out_shape=jax.ShapeDtypeStruct((blocks + 1, rows, width), jnp.float32),
        grid_spec=pltpu.PrefetchScalarGridSpec(
            num_scalar_prefetch=1,
            grid=(owners,),
            in_specs=[
                pl.BlockSpec((2, capacity, rows, width), lambda s, c: (s, 0, 0, 0)),
                pl.BlockSpec((1, 2, blocks, rows, width), lambda s, c: (s, 0, 0, 0, 0)),
                pl.BlockSpec((2, blocks, width, width), lambda s, c: (0, 0, 0, 0)),
            ]
            + ([] if first else [spec_total]),
            out_specs=spec_total,
        ),
        compiler_params=pltpu.CompilerParams(vmem_limit_bytes=32 * 2**20),
        cost_estimate=pl.CostEstimate(
            flops=owners * 2 * capacity * 2 * 2 * rows * width * width,
            bytes_accessed=left.size * 2 + vector.size * 2 + right.size * 2,
            transcendentals=0,
        ),
    )(codes, left, vector, right, *([] if first else [total]))


def per_device_streamed(wavefunction, left_operator, right_operator, target_owner, target_local):
    owners = lax.axis_size("sec")
    halves = lax.axis_size("term")
    me, half = lax.axis_index("sec"), lax.axis_index("term")
    terms, blocks, height, width = left_operator.shape
    rows = height // halves
    capacity = 2 * blocks // owners

    own_rows = lax.dynamic_slice_in_dim(wavefunction, half * rows, rows, 1)
    codes = slot_codes(target_owner, target_local, owners, capacity)
    sources = codes // (2 * blocks)

    moved_left = []
    for k in range(terms):
        pick = sources[k][:, None, :] * halves + jnp.arange(halves, dtype=jnp.int32)[None, :, None]
        pieces = left_operator[k].reshape(blocks * halves, rows, width)[pick.reshape(-1)]
        pieces = pieces.reshape(owners * halves, capacity, rows, width)
        moved_left.append(lax.all_to_all(pieces, BOTH, split_axis=0, concat_axis=0, tiled=True))
    all_codes = lax.all_gather(codes, BOTH, axis=0)
    my_codes = lax.dynamic_index_in_dim(all_codes, me, axis=3 - 1, keepdims=False)
    gathered = lax.all_gather(own_rows, BOTH, axis=0).reshape(owners, halves, blocks, rows, width)
    right = lax.all_gather(right_operator, "term", axis=1)

    def apply(vector):
        total = None
        for k in range(terms):
            total = stream_chunk(total, my_codes[:, k], moved_left[k], vector, right[k])
        return total[:blocks]

    sigma_rows = apply(gathered)
    wave = own_rows.astype(jnp.float32)
    cross, own = jnp.sum(wave * sigma_rows), jnp.sum(wave * wave)
    local = jnp.where(own > 0, cross / own, 0.0)
    about = jnp.sum(jnp.square(sigma_rows - local * wave))
    stats = lax.all_gather(jnp.stack([about, cross, own, local]), BOTH, axis=0)
    rayleigh = jnp.sum(stats[:, 1]) / jnp.sum(stats[:, 2])
    residual_sq = jnp.sum(stats[:, 0] + jnp.square(stats[:, 3] - rayleigh) * stats[:, 2])
    entries = blocks * owners * height * width
    factor = lax.rsqrt(residual_sq / entries + 1e-06)
    direction = ((sigma_rows - rayleigh * wave) * factor).astype(jnp.bfloat16)
    direction = lax.all_gather(direction, BOTH, axis=0).reshape(gathered.shape)
    sigma_two = apply(direction).astype(jnp.bfloat16)
    return (sigma_two, jnp.reshape(rayleigh, (1,)))


def per_device(wavefunction, *operands):
    owners = lax.axis_size("sec")
    gathered_bytes = owners * wavefunction.size * wavefunction.dtype.itemsize
    if owners < 8 or owners & (owners - 1) or 2 * gathered_bytes > RING_BYTES:
        return per_device_streamed(wavefunction, *operands)
    return per_device_ring(wavefunction, *operands)


def solution(mesh):
    placed = (
        P(("rep", "sec"), None, None),
        P("term", ("rep", "sec"), None, None),
        P("term", ("rep", "sec"), None, None),
        P("term", ("rep", "sec"), None),
        P("term", ("rep", "sec")),
    )
    return jax.shard_map(
        per_device,
        mesh=mesh,
        in_specs=placed,
        out_specs=(P(("rep", "sec"), "term", None), P("rep")),
        check_vma=False,
    )
```

```python
import functools

import jax
import jax.numpy as jnp
from jax import lax
from jax.experimental import pallas as pl
from jax.experimental.pallas import tpu as pltpu
from jax.sharding import PartitionSpec as P

BOTH = ("sec", "term")
VMEM_LIMIT = 60 * 2**20
PART = 16
ORDER = [0, 4, 5, 1, 2, 6, 3, 7]
WAITS = {4: 1, 2: 5, 6: 2}
PIECE_WAITS = {6: 4, 7: 5}
RING_BYTES = 24 * 2**20


def ring_order(owners):
    if owners % 2:
        return list(range(owners))
    return list(range(0, owners, 2)) + list(range(owners - 1, 0, -2))


def ring_place(owner, owners):
    if owners % 2:
        return owner
    return jnp.where(owner % 2 == 0, owner // 2, owners - 1 - owner // 2)


def ring_owner(place, owners):
    place = place % owners
    if owners % 2:
        return place
    return jnp.where(place < owners // 2, 2 * place, 2 * (owners - 1 - place) + 1)


def permute(value, owners, halves, target, flip=0):
    pairs = [
        (chip * halves + half, target(chip, half) * halves + (half ^ flip))
        for chip in range(owners)
        for half in range(halves)
    ]
    return lax.ppermute(value, BOTH, pairs)


def swap(value, owners, halves):
    return permute(value, owners, halves, lambda chip, half: chip, 1)


def exchange(value, owners, halves, mask):
    return permute(value, owners, halves, lambda chip, half: chip ^ mask)


def ring_send(value, owners, halves, shifts):
    ring = ring_order(owners)
    place = {chip: index for index, chip in enumerate(ring)}
    return permute(
        value, owners, halves, lambda chip, half: ring[(place[chip] + shifts[half]) % owners]
    )


def select_kernel(half_ref, lower_ref, upper_ref, *rest):
    out_ref = rest[-1]
    out_ref[...] = jnp.where(half_ref[0] == 0, lower_ref[...], upper_ref[...])


def select_half(half, lower, upper, *others):
    anywhere = pl.BlockSpec(memory_space=pl.ANY)
    whole = pl.BlockSpec(memory_space=pltpu.VMEM)
    return pl.pallas_call(
        select_kernel,
        out_shape=jax.ShapeDtypeStruct(lower.shape, lower.dtype),
        in_specs=[pl.BlockSpec(memory_space=pltpu.SMEM), whole, whole] + [anywhere] * len(others),
        out_specs=whole,
        cost_estimate=busy(0.8),
    )(jnp.reshape(half, (1,)).astype(jnp.int32), lower, upper, *others)


def after_kernel(*refs):
    del refs


def after(value, *others):
    anywhere = pl.BlockSpec(memory_space=pl.ANY)
    return pl.pallas_call(
        after_kernel,
        out_shape=jax.ShapeDtypeStruct(value.shape, value.dtype),
        in_specs=[anywhere] * (1 + len(others)),
        out_specs=anywhere,
        input_output_aliases={0: 0},
        cost_estimate=busy(0.3),
    )(value, *others)


def mask_gather(unit, lefts, owners, halves):
    units = {0: unit}
    step = owners // 2
    masks = []
    while step:
        masks.append(step)
        units[step] = exchange(unit, owners, halves, step)
        step //= 2
    waits = dict(WAITS)
    for step in masks[1:]:
        for mask in [m for m in units if m >= 2 * step and m % (2 * step) == 0]:
            if mask in waits:
                units[mask] = after(units[mask], lefts[waits.pop(mask)])
            units[mask | step] = exchange(units[mask], owners, halves, step)
    return units


def spread(value, devices):
    step = 1
    values = []
    while step < devices:
        masks = [step] if 2 * step == devices else [step, 2 * step, 3 * step]
        parts = [lax.ppermute(value, BOTH, [(d, d ^ m) for d in range(devices)]) for m in masks]
        for part in parts:
            value = value + part
        values.append(value)
        step *= 4
    return values


def pack_kernel(order, capacity, blocks, terms, ids_ref, plan_ref, other_plan_ref, *refs):
    left_ref, other_ref, _, *pieces, codes, seen, built, sems = refs
    owners = len(order)
    me, half = ids_ref[0], ids_ref[1]
    rows, width = other_ref.shape[2:]
    start = pl.multiple_of(half * rows, rows)
    parts = rows // PART

    @pl.loop(0, owners)
    def _(owner):
        for index in range(2 * terms * capacity):
            codes[0, owner, index] = 0
            codes[1, owner, index] = blocks

    for stream in range(2 * terms):
        plan = plan_ref if stream < terms else other_plan_ref

        @pl.loop(0, owners)
        def _(owner):
            seen[owner] = 0

        @pl.loop(0, blocks, unroll=4)
        def _(block):
            owner = plan[0, stream % terms, block]
            slot = seen[owner]
            seen[owner] = slot + 1
            codes[0, owner, stream * capacity + slot] = block
            codes[1, owner, stream * capacity + slot] = plan[1, stream % terms, block]

    lane = lax.broadcasted_iota(jnp.int32, (PART, width), 1)
    row = lax.broadcasted_iota(jnp.int32, (PART, width), 0)
    copies = []
    for mask in order:
        owner = me ^ mask
        labels = jnp.zeros((PART, width), jnp.int32)
        for stream in range(2 * terms):
            for slot in range(capacity):
                at = stream * capacity + slot
                block = codes[0, owner, at]
                if stream < terms:
                    value = left_ref[stream, block, pl.ds(start, rows), :]
                else:
                    value = other_ref[stream - terms, block]
                built[mask, at * parts : (at + 1) * parts] = value.reshape(parts, PART, width)
                label = jnp.where(row == 0, block, codes[1, owner, at])
                labels = jnp.where(lane == at, label, labels)
        built[mask, 2 * terms * capacity * parts] = labels.astype(jnp.float32).astype(jnp.bfloat16)
        copies.append(pltpu.make_async_copy(built.at[mask], pieces[mask], sems.at[mask]))
        copies[-1].start()
    for copy in copies:
        copy.wait()


def pack(ids, plan, other_plan, left, other, before, order, capacity):
    terms, blocks, rows, width = other.shape
    owners = len(order)
    scalars = pl.BlockSpec(memory_space=pltpu.SMEM)
    whole = pl.BlockSpec(memory_space=pltpu.VMEM)
    anywhere = pl.BlockSpec(memory_space=pl.ANY)
    shape = (2 * terms * capacity * rows // PART + 1, PART, width)
    return pl.pallas_call(
        functools.partial(pack_kernel, order, capacity, blocks, terms),
        out_shape=[jax.ShapeDtypeStruct(shape, jnp.bfloat16)] * owners,
        in_specs=[scalars] * 3 + [whole, whole, anywhere],
        out_specs=[anywhere] * owners,
        scratch_shapes=[
            pltpu.SMEM((2, owners, 2 * terms * capacity), jnp.int32),
            pltpu.SMEM((owners,), jnp.int32),
            pltpu.VMEM((owners,) + shape, jnp.bfloat16),
            pltpu.SemaphoreType.DMA((owners,)),
        ],
        compiler_params=pltpu.CompilerParams(vmem_limit_bytes=VMEM_LIMIT),
        cost_estimate=busy(5.0),
    )(ids, plan, other_plan, left, other, before)


def busy(microseconds):
    return pl.CostEstimate(
        flops=int(1.15e9 * microseconds), bytes_accessed=0, transcendentals=0
    )


def add_products(left, labels, vector, right, total, side, terms, capacity):
    blocks, rows, width = vector.shape[1:]
    parts = rows // PART
    moved, where = [], []
    for slot in range(terms * capacity):
        at = side * terms * capacity + slot
        block = vector[:, labels[0, at]].reshape(2 * rows, width)
        piece = left[at * parts : (at + 1) * parts].reshape(rows, width)
        product = jnp.dot(piece, block, preferred_element_type=jnp.float32)
        moved.append(product.astype(jnp.bfloat16))
        where.append(labels[1, at])
    for slot in range(terms * capacity):
        total[where[slot]] += jnp.dot(
            moved[slot], right[slot], preferred_element_type=jnp.float32
        )


def local_residual(total, wave_ref, device, rest_ref, stats_ref):
    blocks = wave_ref.shape[0]
    zero = jnp.zeros(wave_ref.shape[1:], jnp.float32)

    def sums(block, carry):
        cross, own = carry
        wave = wave_ref[block].astype(jnp.float32)
        return cross + wave * total[block], own + wave * wave

    cross, own = lax.fori_loop(0, blocks, sums, (zero, zero), unroll=4)
    cross, own = jnp.sum(cross, keepdims=True), jnp.sum(own, keepdims=True)
    local = jnp.where(own > 0, cross / own, 0.0)

    def squares(block, carry):
        rest = total[block] - local * wave_ref[block].astype(jnp.float32)
        rest_ref[block] = rest.astype(rest_ref.dtype)
        return carry + rest * rest

    about = jnp.sum(lax.fori_loop(0, blocks, squares, zero, unroll=4), keepdims=True)
    lane = lax.broadcasted_iota(jnp.int32, stats_ref.shape, 1)
    row = lax.broadcasted_iota(jnp.int32, stats_ref.shape, 0)
    values = jnp.where(lane == 0, about, jnp.where(lane == 1, cross, jnp.where(lane == 2, own, local)))
    stats_ref[...] = jnp.where((row == device) & (lane < 4), values, 0.0)


def form_direction(vector, wave, scale, chip):
    factor = scale[0, 1]
    for part in range(2):
        shift = scale[2 * chip + part, 0]

        @pl.loop(0, vector.shape[1], unroll=4)
        def _(block):
            rest = vector[part, block].astype(jnp.float32)
            rest = rest + shift * wave[part, block].astype(jnp.float32)
            vector[part, block] = (rest * factor).astype(vector.dtype)


def apply_kernel(sources, choices, first, end, terms, capacity, ids_ref, *refs):
    refs = list(refs)

    def take(count):
        taken, refs[:count] = refs[:count], []
        return taken

    (scale,) = take(1) if choices else (None,)
    lefts = take(choices or sources)
    rights = take(2)
    vectors = [take(2) for _ in range(sources)]
    waves = [take(2) for _ in range(choices)]
    (wave_in,) = take(1) if end == "stats" else (None,)
    (total_in,) = (None,) if first else take(1)
    (total_out,) = (None,) if end == "result" else take(1)
    (last_out,) = take(1)
    total, left, right, vector, raw, spread_labels, labels = take(7)
    left_sems, right_sems, vector_sems, raw_sems, label_sem, total_sem = take(6)
    wave, wave_sems = take(2) if choices or end == "stats" else (None, None)
    half = ids_ref[0]
    blocks = vector.shape[2]
    parts = left.shape[1]

    def left_copies(source, piece):
        return [
            pltpu.make_async_copy(piece.at[parts], raw.at[source], raw_sems.at[source]),
            pltpu.make_async_copy(
                piece.at[pl.ds(0, parts)], left.at[source], left_sems.at[source]
            ),
        ]

    def vector_copies(source):
        return [
            pltpu.make_async_copy(
                vectors[source][part],
                vector.at[source, half if part == 0 else 1 - half],
                vector_sems.at[source, part],
            )
            for part in range(2)
        ]

    def wave_copies(source, pair):
        return [
            pltpu.make_async_copy(
                pair[part],
                wave.at[source, half if part == 0 else 1 - half],
                wave_sems.at[source, part],
            )
            for part in range(2)
        ]

    def load_right(source, side):
        for slot in range(terms * capacity):
            target = jnp.minimum(labels[source, 1, side * terms * capacity + slot], blocks - 1)
            pltpu.make_async_copy(
                rights[side].at[slot // capacity, target],
                right.at[source, side, slot],
                right_sems.at[source, side],
            ).start()

    def wait_right(source, side):
        whole = right.at[source, side]
        pltpu.make_async_copy(whole, whole, right_sems.at[source, side]).wait()

    for source in range(sources):
        if choices:
            for choice, piece in enumerate(lefts):

                @pl.when(ids_ref[2 + source] == choice)
                def _():
                    for copy in left_copies(source, piece) + wave_copies(source, waves[choice]):
                        copy.start()

        else:
            for copy in left_copies(source, lefts[source]):
                copy.start()
    for source in range(sources):
        for copy in vector_copies(source):
            copy.start()
    if first:
        total[...] = jnp.zeros_like(total)
    else:
        load_total = pltpu.make_async_copy(total_in, total, total_sem)
        load_total.start()
    if end == "stats":
        load_wave = pltpu.make_async_copy(wave_in, wave.at[0, 0], wave_sems.at[0, 0])
        load_wave.start()
    if end == "go on":
        last_out[...] = jnp.zeros_like(last_out)

    for source in range(sources):
        left_copies(source, lefts[0])[0].wait()
    spread_labels[...] = raw[:, :8].astype(jnp.float32).astype(jnp.int32)
    move_labels = pltpu.make_async_copy(spread_labels, labels, label_sem)
    move_labels.start()
    move_labels.wait()
    for source in range(sources):
        for side in range(2):
            load_right(source, side)
    if not first:
        load_total.wait()
    for source in range(sources):
        for side in range(2):
            if side == 0:
                left_copies(source, lefts[0])[1].wait()
                for copy in vector_copies(source):
                    copy.wait()
                if choices:
                    for copy in wave_copies(source, waves[0]):
                        copy.wait()
                    chip = lax.div(ids_ref[1], 2) ^ ids_ref[2 + source]
                    form_direction(vector.at[source], wave.at[source], scale, chip)
            wait_right(source, side)
            add_products(
                left.at[source],
                labels.at[source],
                vector.at[source],
                right.at[source, side],
                total,
                side,
                terms,
                capacity,
            )
    if end == "result":
        last_out[...] = total[:blocks].astype(last_out.dtype)
    elif end == "stats":
        load_wave.wait()
        local_residual(total, wave.at[0, 0], ids_ref[1], total_out, last_out)
    else:
        store_total = pltpu.make_async_copy(total, total_out, total_sem)
        store_total.start()
        store_total.wait()


def apply_group(ids, lefts, rights, vectors, total, end, wave=None, waves=(), scale=None):
    blocks, rows, width = vectors[0][0].shape
    terms = rights[0].shape[0]
    parts = lefts[0].shape[0] - 1
    capacity = parts * PART // (2 * terms * rows)
    sources, first = len(vectors), total is None
    arrays = [*lefts, *rights] + [unit for pair in [*vectors, *waves] for unit in pair]
    arrays += [wave] if end == "stats" else []
    arrays += [] if first else [total]
    whole = pl.BlockSpec(memory_space=pltpu.VMEM)
    anywhere = pl.BlockSpec(memory_space=pl.ANY)
    total_shape = (blocks + 1, rows, width)
    scratch = [
        pltpu.VMEM(total_shape, jnp.float32),
        pltpu.VMEM((sources, parts, PART, width), jnp.bfloat16),
        pltpu.VMEM((sources, 2, terms * capacity, width, width), jnp.bfloat16),
        pltpu.VMEM((sources, 2, blocks, rows, width), jnp.bfloat16),
        pltpu.VMEM((sources, PART, width), jnp.bfloat16),
        pltpu.VMEM((sources, 8, width), jnp.int32),
        pltpu.SMEM((sources, 8, width), jnp.int32),
        pltpu.SemaphoreType.DMA((sources,)),
        pltpu.SemaphoreType.DMA((sources, 2)),
        pltpu.SemaphoreType.DMA((sources, 2)),
        pltpu.SemaphoreType.DMA((sources,)),
        pltpu.SemaphoreType.DMA,
        pltpu.SemaphoreType.DMA,
    ]
    if waves or end == "stats":
        scratch += [
            pltpu.VMEM((sources, 2, blocks, rows, width), jnp.bfloat16),
            pltpu.SemaphoreType.DMA((sources, 2)),
        ]
    devices = lax.axis_size("sec") * lax.axis_size("term")
    total_out = jax.ShapeDtypeStruct(total_shape, jnp.float32)
    out_shape, out_specs = {
        "go on": ((total_out, jax.ShapeDtypeStruct((8, width), jnp.float32)), (anywhere, whole)),
        "stats": (
            (
                jax.ShapeDtypeStruct((blocks, rows, width), jnp.bfloat16),
                jax.ShapeDtypeStruct((devices, 128), jnp.float32),
            ),
            (whole, whole),
        ),
        "result": (jax.ShapeDtypeStruct((blocks, rows, width), jnp.bfloat16), whole),
    }[end]
    choices = len(waves)
    scalars = [ids] if scale is None else [ids, scale]
    return pl.pallas_call(
        functools.partial(apply_kernel, sources, choices, first, end, terms, capacity),
        out_shape=out_shape,
        in_specs=[pl.BlockSpec(memory_space=pltpu.SMEM)] * len(scalars) + [anywhere] * len(arrays),
        out_specs=out_specs,
        scratch_shapes=scratch,
        compiler_params=pltpu.CompilerParams(vmem_limit_bytes=VMEM_LIMIT),
        cost_estimate=busy(0.5 if waves else 3.5 + 1.8 * sources),
    )(*scalars, *arrays)


def scale_kernel(entries, stats_ref, scale_ref, rayleigh_ref):
    stats = stats_ref[...]
    about, cross, own, local = (stats[:, lane : lane + 1] for lane in range(4))
    rayleigh = jnp.sum(cross, keepdims=True) / jnp.sum(own, keepdims=True)
    offset = local - rayleigh
    residual_sq = jnp.sum(about + offset * offset * own, keepdims=True)
    factor = lax.rsqrt(residual_sq / entries + 1e-06)
    lane = lax.broadcasted_iota(jnp.int32, scale_ref.shape, 1)
    scale_ref[...] = jnp.where(lane == 0, offset, factor)
    rayleigh_ref[...] = rayleigh


def scales(stats, entries):
    whole = pl.BlockSpec(memory_space=pltpu.VMEM)
    return pl.pallas_call(
        functools.partial(scale_kernel, entries),
        out_shape=(
            jax.ShapeDtypeStruct(stats.shape, jnp.float32),
            jax.ShapeDtypeStruct((1, 1), jnp.float32),
        ),
        in_specs=[whole],
        out_specs=(whole, whole),
        cost_estimate=busy(0.7),
    )(stats)


def per_device_ring(wavefunction, left_operator, right_operator, target_owner, target_local):
    owners, halves = lax.axis_size("sec"), lax.axis_size("term")
    me, half = lax.axis_index("sec"), lax.axis_index("term")
    terms, blocks, height, width = left_operator.shape
    rows = height // halves
    capacity = 2 * blocks // owners
    place = ring_place(me, owners)
    ids = jnp.stack([me, half]).astype(jnp.int32)

    own_rows = lax.dynamic_slice_in_dim(wavefunction, half * rows, rows, 1)
    other_rows = lax.dynamic_slice_in_dim(wavefunction, (1 - half) * rows, rows, 1)
    plan = jnp.stack([target_owner[:, :, 0], target_local])
    other_left = swap(
        lax.dynamic_slice_in_dim(left_operator, (1 - half) * rows, rows, 2), owners, halves
    )
    order = [m for m in ORDER if m < owners] + list(range(len(ORDER), owners))
    rights = (right_operator, swap(right_operator, owners, halves))
    pieces = pack(
        ids,
        plan,
        swap(plan, owners, halves),
        left_operator,
        other_left,
        plan,
        order[1:] + order[:1],
        capacity,
    )
    lefts = [pieces[0]]
    for m in range(1, owners):
        piece = pieces[m]
        if m in PIECE_WAITS:
            piece = after(piece, lefts[PIECE_WAITS[m]])
        lefts.append(exchange(piece, owners, halves, m))
    near = mask_gather(own_rows, lefts, owners, halves)
    far = {m: swap(unit, owners, halves) if m else other_rows for m, unit in near.items()}

    here = [half, me * halves + half]
    no_choice = jnp.stack(here).astype(jnp.int32)
    total = None
    for at in range(0, owners, 2):
        group = order[at : at + 2]
        total, stats = apply_group(
            no_choice,
            [lefts[m] for m in group],
            rights,
            [(near[m], far[m]) for m in group],
            total,
            "go on" if at + 2 < owners else "stats",
            own_rows,
        )

    stats = spread(stats, owners * halves)
    rest = after(total, stats[0])
    ahead = ring_send(rest, owners, halves, (1,) * halves)
    behind = ring_send(rest, owners, halves, (-1,) * halves)
    entries = blocks * owners * height * width
    scale, rayleigh = scales(stats[-1], entries)
    reach = (owners - 1) // 2
    waves = [(near[m], far[m]) for m in range(owners)]

    def add_group(total, units, end):
        choices = [me ^ ring_owner(place - s, owners) for s in units]
        vectors = [(unit, swap(unit, owners, halves)) for unit in units.values()]
        ids = jnp.stack(here + choices).astype(jnp.int32)
        return apply_group(
            ids, lefts, rights, vectors, total, end, waves=waves, scale=scale
        )

    total, token = None, None
    units, waiting = {1: ahead, -1: behind}, {0: rest}
    for step in range(2, reach + 1):
        ahead = ring_send(ahead, owners, halves, (1,) * halves)
        behind = ring_send(behind, owners, halves, (-1,) * halves)
        total, token = add_group(total, waiting, "go on")
        ahead = after(ahead, token)
        waiting = units if step == 2 else {}
        units = {step: ahead, -step: behind}
        waiting = {**waiting, **units}
    last = ring_send(select_half(half, ahead, behind), owners, halves, (1, -1))
    total, token = add_group(total, waiting, "go on")
    total = add_group(total, {owners // 2: after(last, token)}, "result")
    return (total, rayleigh[0])


def slot_codes(target_owner, target_local, owners, capacity):
    terms, blocks = target_local.shape
    owner = target_owner[:, :, 0]
    place = jnp.arange(blocks, dtype=jnp.int32)
    same = (owner[:, :, None] == owner[:, None, :]) & (place[None, :] < place[:, None])[None]
    position = jnp.sum(same.astype(jnp.int32), axis=2)
    hit = (
        owner[:, None, None, :] == jnp.arange(owners, dtype=jnp.int32)[None, :, None, None]
    ) & (position[:, None, None, :] == jnp.arange(capacity, dtype=jnp.int32)[None, None, :, None])
    code = place[None, :] * (2 * blocks) + target_local - blocks
    return blocks + jnp.sum(jnp.where(hit, code[:, None, None, :], 0), axis=3)


def stream_kernel(first, capacity, blocks, code_ref, left_ref, vector_ref, right_ref, *rest):
    total_in, total = (None, rest[0]) if first else rest
    step = pl.program_id(0)
    rows, width = left_ref.shape[2:]

    @pl.when(step == 0)
    def _():
        total[...] = jnp.zeros_like(total) if first else total_in[...]

    for term in range(2):
        moved, where = [], []
        for slot in range(capacity):
            code = code_ref[2 * step + term, slot]
            source, target = lax.div(code, 2 * blocks), lax.rem(code, 2 * blocks)
            block = vector_ref[0, :, source].reshape(2 * rows, width)
            product = jnp.dot(left_ref[term, slot], block, preferred_element_type=jnp.float32)
            moved.append(product.astype(jnp.bfloat16))
            where.append(target)
        for slot in range(capacity):
            target = where[slot]
            total[target] += jnp.dot(
                moved[slot],
                right_ref[term, jnp.minimum(target, blocks - 1)],
                preferred_element_type=jnp.float32,
            )


def stream_chunk(total, codes, left, vector, right):
    owners, _, blocks, rows, width = vector.shape
    capacity = left.shape[1]
    first = total is None
    spec_total = pl.BlockSpec((blocks + 1, rows, width), lambda s, c: (0, 0, 0))
    return pl.pallas_call(
        functools.partial(stream_kernel, first, capacity, blocks),
        out_shape=jax.ShapeDtypeStruct((blocks + 1, rows, width), jnp.float32),
        grid_spec=pltpu.PrefetchScalarGridSpec(
            num_scalar_prefetch=1,
            grid=(owners,),
            in_specs=[
                pl.BlockSpec((2, capacity, rows, width), lambda s, c: (s, 0, 0, 0)),
                pl.BlockSpec((1, 2, blocks, rows, width), lambda s, c: (s, 0, 0, 0, 0)),
                pl.BlockSpec((2, blocks, width, width), lambda s, c: (0, 0, 0, 0)),
            ]
            + ([] if first else [spec_total]),
            out_specs=spec_total,
        ),
        compiler_params=pltpu.CompilerParams(vmem_limit_bytes=32 * 2**20),
        cost_estimate=pl.CostEstimate(
            flops=owners * 2 * capacity * 2 * 2 * rows * width * width,
            bytes_accessed=left.size * 2 + vector.size * 2 + right.size * 2,
            transcendentals=0,
        ),
    )(codes, left, vector, right, *([] if first else [total]))


def per_device_streamed(wavefunction, left_operator, right_operator, target_owner, target_local):
    owners = lax.axis_size("sec")
    halves = lax.axis_size("term")
    me, half = lax.axis_index("sec"), lax.axis_index("term")
    terms, blocks, height, width = left_operator.shape
    rows = height // halves
    capacity = 2 * blocks // owners

    own_rows = lax.dynamic_slice_in_dim(wavefunction, half * rows, rows, 1)
    codes = slot_codes(target_owner, target_local, owners, capacity)
    sources = codes // (2 * blocks)

    moved_left = []
    for k in range(terms):
        pick = sources[k][:, None, :] * halves + jnp.arange(halves, dtype=jnp.int32)[None, :, None]
        pieces = left_operator[k].reshape(blocks * halves, rows, width)[pick.reshape(-1)]
        pieces = pieces.reshape(owners * halves, capacity, rows, width)
        moved_left.append(lax.all_to_all(pieces, BOTH, split_axis=0, concat_axis=0, tiled=True))
    all_codes = lax.all_gather(codes, BOTH, axis=0)
    my_codes = lax.dynamic_index_in_dim(all_codes, me, axis=3 - 1, keepdims=False)
    gathered = lax.all_gather(own_rows, BOTH, axis=0).reshape(owners, halves, blocks, rows, width)
    right = lax.all_gather(right_operator, "term", axis=1)

    def apply(vector):
        total = None
        for k in range(terms):
            total = stream_chunk(total, my_codes[:, k], moved_left[k], vector, right[k])
        return total[:blocks]

    sigma_rows = apply(gathered)
    wave = own_rows.astype(jnp.float32)
    cross, own = jnp.sum(wave * sigma_rows), jnp.sum(wave * wave)
    local = jnp.where(own > 0, cross / own, 0.0)
    about = jnp.sum(jnp.square(sigma_rows - local * wave))
    stats = lax.all_gather(jnp.stack([about, cross, own, local]), BOTH, axis=0)
    rayleigh = jnp.sum(stats[:, 1]) / jnp.sum(stats[:, 2])
    residual_sq = jnp.sum(stats[:, 0] + jnp.square(stats[:, 3] - rayleigh) * stats[:, 2])
    entries = blocks * owners * height * width
    factor = lax.rsqrt(residual_sq / entries + 1e-06)
    direction = ((sigma_rows - rayleigh * wave) * factor).astype(jnp.bfloat16)
    direction = lax.all_gather(direction, BOTH, axis=0).reshape(gathered.shape)
    sigma_two = apply(direction).astype(jnp.bfloat16)
    return (sigma_two, jnp.reshape(rayleigh, (1,)))


def per_device(wavefunction, *operands):
    owners = lax.axis_size("sec")
    gathered_bytes = owners * wavefunction.size * wavefunction.dtype.itemsize
    if owners < 8 or owners & (owners - 1) or 2 * gathered_bytes > RING_BYTES:
        return per_device_streamed(wavefunction, *operands)
    return per_device_ring(wavefunction, *operands)


def solution(mesh):
    placed = (
        P(("rep", "sec"), None, None),
        P("term", ("rep", "sec"), None, None),
        P("term", ("rep", "sec"), None, None),
        P("term", ("rep", "sec"), None),
        P("term", ("rep", "sec")),
    )
    return jax.shard_map(
        per_device,
        mesh=mesh,
        in_specs=placed,
        out_specs=(P(("rep", "sec"), "term", None), P("rep")),
        check_vma=False,
    )
```

```python
import functools

import jax
import jax.numpy as jnp
from jax import lax
from jax.experimental import pallas as pl
from jax.experimental.pallas import tpu as pltpu
from jax.sharding import PartitionSpec as P

BOTH = ("sec", "term")
VMEM_LIMIT = 60 * 2**20
PART = 16
ORDER = [0, 4, 5, 1, 2, 6, 3, 7]
WAITS = {4: 1, 2: 5, 6: 2}
PIECE_WAITS = {6: 4, 7: 5}
RING_BYTES = 24 * 2**20


def ring_order(owners):
    if owners % 2:
        return list(range(owners))
    return list(range(0, owners, 2)) + list(range(owners - 1, 0, -2))


def ring_place(owner, owners):
    if owners % 2:
        return owner
    return jnp.where(owner % 2 == 0, owner // 2, owners - 1 - owner // 2)


def ring_owner(place, owners):
    place = place % owners
    if owners % 2:
        return place
    return jnp.where(place < owners // 2, 2 * place, 2 * (owners - 1 - place) + 1)


def permute(value, owners, halves, target, flip=0):
    pairs = [
        (chip * halves + half, target(chip, half) * halves + (half ^ flip))
        for chip in range(owners)
        for half in range(halves)
    ]
    return lax.ppermute(value, BOTH, pairs)


def swap(value, owners, halves):
    return permute(value, owners, halves, lambda chip, half: chip, 1)


def exchange(value, owners, halves, mask):
    return permute(value, owners, halves, lambda chip, half: chip ^ mask)


def ring_send(value, owners, halves, shifts):
    ring = ring_order(owners)
    place = {chip: index for index, chip in enumerate(ring)}
    return permute(
        value, owners, halves, lambda chip, half: ring[(place[chip] + shifts[half]) % owners]
    )


def select_kernel(half_ref, lower_ref, upper_ref, *rest):
    out_ref = rest[-1]
    out_ref[...] = jnp.where(half_ref[0] == 0, lower_ref[...], upper_ref[...])


def select_half(half, lower, upper, *others):
    anywhere = pl.BlockSpec(memory_space=pl.ANY)
    whole = pl.BlockSpec(memory_space=pltpu.VMEM)
    return pl.pallas_call(
        select_kernel,
        out_shape=jax.ShapeDtypeStruct(lower.shape, lower.dtype),
        in_specs=[pl.BlockSpec(memory_space=pltpu.SMEM), whole, whole] + [anywhere] * len(others),
        out_specs=whole,
        cost_estimate=busy(0.8),
    )(jnp.reshape(half, (1,)).astype(jnp.int32), lower, upper, *others)


def after_kernel(*refs):
    del refs


def after(value, *others):
    anywhere = pl.BlockSpec(memory_space=pl.ANY)
    return pl.pallas_call(
        after_kernel,
        out_shape=jax.ShapeDtypeStruct(value.shape, value.dtype),
        in_specs=[anywhere] * (1 + len(others)),
        out_specs=anywhere,
        input_output_aliases={0: 0},
        cost_estimate=busy(0.3),
    )(value, *others)


def mask_gather(unit, lefts, owners, halves):
    units = {0: unit}
    step = owners // 2
    masks = []
    while step:
        masks.append(step)
        units[step] = exchange(unit, owners, halves, step)
        step //= 2
    waits = dict(WAITS)
    for step in masks[1:]:
        for mask in [m for m in units if m >= 2 * step and m % (2 * step) == 0]:
            if mask in waits:
                units[mask] = after(units[mask], lefts[waits.pop(mask)])
            units[mask | step] = exchange(units[mask], owners, halves, step)
    return units


def spread(value, devices):
    step = 1
    while step < devices:
        masks = [step] if 2 * step == devices else [step, 2 * step, 3 * step]
        parts = [lax.ppermute(value, BOTH, [(d, d ^ m) for d in range(devices)]) for m in masks]
        for part in parts:
            value = value + part
        step *= 4
    return value


def pack_kernel(order, capacity, blocks, terms, ids_ref, plan_ref, other_plan_ref, *refs):
    left_ref, other_ref, _, *pieces, codes, seen, built, sems = refs
    owners = len(order)
    me, half = ids_ref[0], ids_ref[1]
    rows, width = other_ref.shape[2:]
    start = pl.multiple_of(half * rows, rows)
    parts = rows // PART

    @pl.loop(0, owners)
    def _(owner):
        for index in range(2 * terms * capacity):
            codes[0, owner, index] = 0
            codes[1, owner, index] = blocks

    for stream in range(2 * terms):
        plan = plan_ref if stream < terms else other_plan_ref

        @pl.loop(0, owners)
        def _(owner):
            seen[owner] = 0

        @pl.loop(0, blocks, unroll=4)
        def _(block):
            owner = plan[0, stream % terms, block]
            slot = seen[owner]
            seen[owner] = slot + 1
            codes[0, owner, stream * capacity + slot] = block
            codes[1, owner, stream * capacity + slot] = plan[1, stream % terms, block]

    lane = lax.broadcasted_iota(jnp.int32, (PART, width), 1)
    row = lax.broadcasted_iota(jnp.int32, (PART, width), 0)
    copies = []
    for mask in order:
        owner = me ^ mask
        labels = jnp.zeros((PART, width), jnp.int32)
        for stream in range(2 * terms):
            for slot in range(capacity):
                at = stream * capacity + slot
                block = codes[0, owner, at]
                if stream < terms:
                    value = left_ref[stream, block, pl.ds(start, rows), :]
                else:
                    value = other_ref[stream - terms, block]
                built[mask, at * parts : (at + 1) * parts] = value.reshape(parts, PART, width)
                label = jnp.where(row == 0, block, codes[1, owner, at])
                labels = jnp.where(lane == at, label, labels)
        built[mask, 2 * terms * capacity * parts] = labels.astype(jnp.float32).astype(jnp.bfloat16)
        copies.append(pltpu.make_async_copy(built.at[mask], pieces[mask], sems.at[mask]))
        copies[-1].start()
    for copy in copies:
        copy.wait()


def pack(ids, plan, other_plan, left, other, before, order, capacity):
    terms, blocks, rows, width = other.shape
    owners = len(order)
    scalars = pl.BlockSpec(memory_space=pltpu.SMEM)
    whole = pl.BlockSpec(memory_space=pltpu.VMEM)
    anywhere = pl.BlockSpec(memory_space=pl.ANY)
    shape = (2 * terms * capacity * rows // PART + 1, PART, width)
    return pl.pallas_call(
        functools.partial(pack_kernel, order, capacity, blocks, terms),
        out_shape=[jax.ShapeDtypeStruct(shape, jnp.bfloat16)] * owners,
        in_specs=[scalars] * 3 + [whole, whole, anywhere],
        out_specs=[anywhere] * owners,
        scratch_shapes=[
            pltpu.SMEM((2, owners, 2 * terms * capacity), jnp.int32),
            pltpu.SMEM((owners,), jnp.int32),
            pltpu.VMEM((owners,) + shape, jnp.bfloat16),
            pltpu.SemaphoreType.DMA((owners,)),
        ],
        compiler_params=pltpu.CompilerParams(vmem_limit_bytes=VMEM_LIMIT),
        cost_estimate=busy(5.0),
    )(ids, plan, other_plan, left, other, before)


def busy(microseconds):
    return pl.CostEstimate(
        flops=int(1.15e9 * microseconds), bytes_accessed=0, transcendentals=0
    )


def add_products(left, labels, vector, right, total, side, terms, capacity):
    blocks, rows, width = vector.shape[1:]
    parts = rows // PART
    moved, where = [], []
    for slot in range(terms * capacity):
        at = side * terms * capacity + slot
        block = vector[:, labels[0, at]].reshape(2 * rows, width)
        piece = left[at * parts : (at + 1) * parts].reshape(rows, width)
        product = jnp.dot(piece, block, preferred_element_type=jnp.float32)
        moved.append(product.astype(jnp.bfloat16))
        where.append(labels[1, at])
    for slot in range(terms * capacity):
        total[where[slot]] += jnp.dot(
            moved[slot], right[slot], preferred_element_type=jnp.float32
        )


def local_stats(total, wave_ref, device, stats_ref):
    blocks = wave_ref.shape[0]
    zero = jnp.zeros(wave_ref.shape[1:], jnp.float32)

    def sums(block, carry):
        cross, own = carry
        wave = wave_ref[block].astype(jnp.float32)
        return cross + wave * total[block], own + wave * wave

    cross, own = lax.fori_loop(0, blocks, sums, (zero, zero), unroll=4)
    cross, own = jnp.sum(cross, keepdims=True), jnp.sum(own, keepdims=True)
    local = jnp.where(own > 0, cross / own, 0.0)

    def squares(block, carry):
        rest = total[block] - local * wave_ref[block].astype(jnp.float32)
        return carry + rest * rest

    about = jnp.sum(lax.fori_loop(0, blocks, squares, zero, unroll=4), keepdims=True)
    lane = lax.broadcasted_iota(jnp.int32, stats_ref.shape, 1)
    row = lax.broadcasted_iota(jnp.int32, stats_ref.shape, 0)
    values = jnp.where(lane == 0, about, jnp.where(lane == 1, cross, jnp.where(lane == 2, own, local)))
    stats_ref[...] = jnp.where((row == device) & (lane < 4), values, 0.0)


def apply_kernel(sources, choices, first, end, terms, capacity, ids_ref, *refs):
    refs = list(refs)

    def take(count):
        taken, refs[:count] = refs[:count], []
        return taken

    lefts = take(choices or sources)
    rights = take(2)
    vectors = [take(2) for _ in range(sources)]
    (wave_in,) = take(1) if end == "stats" else (None,)
    (total_in,) = (None,) if first else take(1)
    (total_out,) = (None,) if end == "result" else take(1)
    (last_out,) = take(1)
    total, left, right, vector, raw, spread_labels, labels = take(7)
    left_sems, right_sems, vector_sems, raw_sems, label_sem, total_sem = take(6)
    wave, wave_sem = take(2) if end == "stats" else (None, None)
    half = ids_ref[0]
    blocks = vector.shape[2]
    parts = left.shape[1]

    def left_copies(source, piece):
        return [
            pltpu.make_async_copy(piece.at[parts], raw.at[source], raw_sems.at[source]),
            pltpu.make_async_copy(
                piece.at[pl.ds(0, parts)], left.at[source], left_sems.at[source]
            ),
        ]

    def vector_copies(source):
        return [
            pltpu.make_async_copy(
                vectors[source][part],
                vector.at[source, half if part == 0 else 1 - half],
                vector_sems.at[source, part],
            )
            for part in range(2)
        ]

    def load_right(source, side):
        for slot in range(terms * capacity):
            target = jnp.minimum(labels[source, 1, side * terms * capacity + slot], blocks - 1)
            pltpu.make_async_copy(
                rights[side].at[slot // capacity, target],
                right.at[source, side, slot],
                right_sems.at[source, side],
            ).start()

    def wait_right(source, side):
        whole = right.at[source, side]
        pltpu.make_async_copy(whole, whole, right_sems.at[source, side]).wait()

    for source in range(sources):
        if choices:
            for choice, piece in enumerate(lefts):

                @pl.when(ids_ref[2 + source] == choice)
                def _():
                    for copy in left_copies(source, piece):
                        copy.start()

        else:
            for copy in left_copies(source, lefts[source]):
                copy.start()
    for source in range(sources):
        for copy in vector_copies(source):
            copy.start()
    if first:
        total[...] = jnp.zeros_like(total)
    else:
        load_total = pltpu.make_async_copy(total_in, total, total_sem)
        load_total.start()
    if end == "stats":
        load_wave = pltpu.make_async_copy(wave_in, wave, wave_sem)
        load_wave.start()
    if end == "go on":
        last_out[...] = jnp.zeros_like(last_out)

    for source in range(sources):
        left_copies(source, lefts[0])[0].wait()
    spread_labels[...] = raw[:, :8].astype(jnp.float32).astype(jnp.int32)
    move_labels = pltpu.make_async_copy(spread_labels, labels, label_sem)
    move_labels.start()
    move_labels.wait()
    for source in range(sources):
        for side in range(2):
            load_right(source, side)
    if not first:
        load_total.wait()
    for source in range(sources):
        for side in range(2):
            if side == 0:
                left_copies(source, lefts[0])[1].wait()
                for copy in vector_copies(source):
                    copy.wait()
            wait_right(source, side)
            add_products(
                left.at[source],
                labels.at[source],
                vector.at[source],
                right.at[source, side],
                total,
                side,
                terms,
                capacity,
            )
    if end == "result":
        last_out[...] = total[:blocks].astype(last_out.dtype)
    elif end == "stats":
        load_wave.wait()
        local_stats(total, wave, ids_ref[1], last_out)
        total_out[...] = total[:blocks]
    else:
        store_total = pltpu.make_async_copy(total, total_out, total_sem)
        store_total.start()
        store_total.wait()


def apply_group(ids, lefts, rights, vectors, total, end, wave=None):
    blocks, rows, width = vectors[0][0].shape
    terms = rights[0].shape[0]
    parts = lefts[0].shape[0] - 1
    capacity = parts * PART // (2 * terms * rows)
    sources, first = len(vectors), total is None
    arrays = [*lefts, *rights] + [unit for pair in vectors for unit in pair]
    arrays += [wave] if end == "stats" else []
    arrays += [] if first else [total]
    whole = pl.BlockSpec(memory_space=pltpu.VMEM)
    anywhere = pl.BlockSpec(memory_space=pl.ANY)
    total_shape = (blocks + 1, rows, width)
    scratch = [
        pltpu.VMEM(total_shape, jnp.float32),
        pltpu.VMEM((sources, parts, PART, width), jnp.bfloat16),
        pltpu.VMEM((sources, 2, terms * capacity, width, width), jnp.bfloat16),
        pltpu.VMEM((sources, 2, blocks, rows, width), jnp.bfloat16),
        pltpu.VMEM((sources, PART, width), jnp.bfloat16),
        pltpu.VMEM((sources, 8, width), jnp.int32),
        pltpu.SMEM((sources, 8, width), jnp.int32),
        pltpu.SemaphoreType.DMA((sources,)),
        pltpu.SemaphoreType.DMA((sources, 2)),
        pltpu.SemaphoreType.DMA((sources, 2)),
        pltpu.SemaphoreType.DMA((sources,)),
        pltpu.SemaphoreType.DMA,
        pltpu.SemaphoreType.DMA,
    ]
    if end == "stats":
        scratch += [pltpu.VMEM(wave.shape, wave.dtype), pltpu.SemaphoreType.DMA]
    devices = lax.axis_size("sec") * lax.axis_size("term")
    total_out = jax.ShapeDtypeStruct(total_shape, jnp.float32)
    out_shape, out_specs = {
        "go on": ((total_out, jax.ShapeDtypeStruct((8, width), jnp.float32)), (anywhere, whole)),
        "stats": (
            (
                jax.ShapeDtypeStruct((blocks, rows, width), jnp.float32),
                jax.ShapeDtypeStruct((devices, 128), jnp.float32),
            ),
            (whole, whole),
        ),
        "result": (jax.ShapeDtypeStruct((blocks, rows, width), jnp.bfloat16), whole),
    }[end]
    choices = len(lefts) if ids.shape[0] > 2 else 0
    return pl.pallas_call(
        functools.partial(apply_kernel, sources, choices, first, end, terms, capacity),
        out_shape=out_shape,
        in_specs=[pl.BlockSpec(memory_space=pltpu.SMEM)] + [anywhere] * len(arrays),
        out_specs=out_specs,
        scratch_shapes=scratch,
        compiler_params=pltpu.CompilerParams(vmem_limit_bytes=VMEM_LIMIT),
        cost_estimate=busy(3.5 + 1.8 * sources),
    )(ids, *arrays)


def direction_kernel(entries, total_ref, wave_ref, stats_ref, out_ref, rayleigh_ref):
    blocks = wave_ref.shape[0]
    stats = stats_ref[...]
    about, cross, own, local = (stats[:, lane : lane + 1] for lane in range(4))
    rayleigh = jnp.sum(cross, keepdims=True) / jnp.sum(own, keepdims=True)
    offset = local - rayleigh
    residual_sq = jnp.sum(about + offset * offset * own, keepdims=True)
    factor = lax.rsqrt(residual_sq / entries + 1e-06)
    rayleigh_ref[...] = rayleigh

    @pl.loop(0, blocks, unroll=4)
    def _(block):
        rest = total_ref[block] - rayleigh * wave_ref[block].astype(jnp.float32)
        out_ref[block] = (rest * factor).astype(jnp.bfloat16)


def new_direction(total, wave, stats, entries):
    whole = pl.BlockSpec(memory_space=pltpu.VMEM)
    return pl.pallas_call(
        functools.partial(direction_kernel, entries),
        out_shape=(
            jax.ShapeDtypeStruct(wave.shape, jnp.bfloat16),
            jax.ShapeDtypeStruct((1, 1), jnp.float32),
        ),
        in_specs=[whole] * 3,
        out_specs=(whole, whole),
        compiler_params=pltpu.CompilerParams(vmem_limit_bytes=8 * 2**20),
        cost_estimate=busy(2.0),
    )(total, wave, stats)


def per_device_ring(wavefunction, left_operator, right_operator, target_owner, target_local):
    owners, halves = lax.axis_size("sec"), lax.axis_size("term")
    me, half = lax.axis_index("sec"), lax.axis_index("term")
    terms, blocks, height, width = left_operator.shape
    rows = height // halves
    capacity = 2 * blocks // owners
    place = ring_place(me, owners)
    ids = jnp.stack([me, half]).astype(jnp.int32)

    own_rows = lax.dynamic_slice_in_dim(wavefunction, half * rows, rows, 1)
    other_rows = lax.dynamic_slice_in_dim(wavefunction, (1 - half) * rows, rows, 1)
    plan = jnp.stack([target_owner[:, :, 0], target_local])
    other_left = swap(
        lax.dynamic_slice_in_dim(left_operator, (1 - half) * rows, rows, 2), owners, halves
    )
    order = [m for m in ORDER if m < owners] + list(range(len(ORDER), owners))
    rights = (right_operator, swap(right_operator, owners, halves))
    pieces = pack(
        ids,
        plan,
        swap(plan, owners, halves),
        left_operator,
        other_left,
        plan,
        order[1:] + order[:1],
        capacity,
    )
    lefts = [pieces[0]]
    for m in range(1, owners):
        piece = pieces[m]
        if m in PIECE_WAITS:
            piece = after(piece, lefts[PIECE_WAITS[m]])
        lefts.append(exchange(piece, owners, halves, m))
    near = mask_gather(own_rows, lefts, owners, halves)
    far = {m: swap(unit, owners, halves) if m else other_rows for m, unit in near.items()}

    here = [half, me * halves + half]
    no_choice = jnp.stack(here).astype(jnp.int32)
    total = None
    for at in range(0, owners, 2):
        group = order[at : at + 2]
        total, stats = apply_group(
            no_choice,
            [lefts[m] for m in group],
            rights,
            [(near[m], far[m]) for m in group],
            total,
            "go on" if at + 2 < owners else "stats",
            own_rows,
        )

    entries = blocks * owners * height * width
    stats = spread(stats, owners * halves)
    direction, rayleigh = new_direction(total, own_rows, stats, entries)
    reach = (owners - 1) // 2

    def add_group(total, units, end):
        choices = [me ^ ring_owner(place - s, owners) for s in units]
        vectors = [(unit, swap(unit, owners, halves)) for unit in units.values()]
        ids = jnp.stack(here + choices).astype(jnp.int32)
        return apply_group(ids, lefts, rights, vectors, total, end)

    total, waiting = None, {0: direction}
    ahead = behind = direction
    for step in range(1, reach + 1):
        ahead = ring_send(ahead, owners, halves, (1,) * halves)
        behind = ring_send(behind, owners, halves, (-1,) * halves)
        if step > 1:
            total, token = add_group(total, waiting, "go on")
            ahead, waiting = after(ahead, token), {}
        waiting.update({step: ahead, -step: behind})
    last = ring_send(select_half(half, ahead, behind), owners, halves, (1, -1))
    total, token = add_group(total, waiting, "go on")
    total = add_group(total, {owners // 2: after(last, token)}, "result")
    return (total, rayleigh[0])


def slot_codes(target_owner, target_local, owners, capacity):
    terms, blocks = target_local.shape
    owner = target_owner[:, :, 0]
    place = jnp.arange(blocks, dtype=jnp.int32)
    same = (owner[:, :, None] == owner[:, None, :]) & (place[None, :] < place[:, None])[None]
    position = jnp.sum(same.astype(jnp.int32), axis=2)
    hit = (
        owner[:, None, None, :] == jnp.arange(owners, dtype=jnp.int32)[None, :, None, None]
    ) & (position[:, None, None, :] == jnp.arange(capacity, dtype=jnp.int32)[None, None, :, None])
    code = place[None, :] * (2 * blocks) + target_local - blocks
    return blocks + jnp.sum(jnp.where(hit, code[:, None, None, :], 0), axis=3)


def stream_kernel(first, capacity, blocks, code_ref, left_ref, vector_ref, right_ref, *rest):
    total_in, total = (None, rest[0]) if first else rest
    step = pl.program_id(0)
    rows, width = left_ref.shape[2:]

    @pl.when(step == 0)
    def _():
        total[...] = jnp.zeros_like(total) if first else total_in[...]

    for term in range(2):
        moved, where = [], []
        for slot in range(capacity):
            code = code_ref[2 * step + term, slot]
            source, target = lax.div(code, 2 * blocks), lax.rem(code, 2 * blocks)
            block = vector_ref[0, :, source].reshape(2 * rows, width)
            product = jnp.dot(left_ref[term, slot], block, preferred_element_type=jnp.float32)
            moved.append(product.astype(jnp.bfloat16))
            where.append(target)
        for slot in range(capacity):
            target = where[slot]
            total[target] += jnp.dot(
                moved[slot],
                right_ref[term, jnp.minimum(target, blocks - 1)],
                preferred_element_type=jnp.float32,
            )


def stream_chunk(total, codes, left, vector, right):
    owners, _, blocks, rows, width = vector.shape
    capacity = left.shape[1]
    first = total is None
    spec_total = pl.BlockSpec((blocks + 1, rows, width), lambda s, c: (0, 0, 0))
    return pl.pallas_call(
        functools.partial(stream_kernel, first, capacity, blocks),
        out_shape=jax.ShapeDtypeStruct((blocks + 1, rows, width), jnp.float32),
        grid_spec=pltpu.PrefetchScalarGridSpec(
            num_scalar_prefetch=1,
            grid=(owners,),
            in_specs=[
                pl.BlockSpec((2, capacity, rows, width), lambda s, c: (s, 0, 0, 0)),
                pl.BlockSpec((1, 2, blocks, rows, width), lambda s, c: (s, 0, 0, 0, 0)),
                pl.BlockSpec((2, blocks, width, width), lambda s, c: (0, 0, 0, 0)),
            ]
            + ([] if first else [spec_total]),
            out_specs=spec_total,
        ),
        compiler_params=pltpu.CompilerParams(vmem_limit_bytes=32 * 2**20),
        cost_estimate=pl.CostEstimate(
            flops=owners * 2 * capacity * 2 * 2 * rows * width * width,
            bytes_accessed=left.size * 2 + vector.size * 2 + right.size * 2,
            transcendentals=0,
        ),
    )(codes, left, vector, right, *([] if first else [total]))


def per_device_streamed(wavefunction, left_operator, right_operator, target_owner, target_local):
    owners = lax.axis_size("sec")
    halves = lax.axis_size("term")
    me, half = lax.axis_index("sec"), lax.axis_index("term")
    terms, blocks, height, width = left_operator.shape
    rows = height // halves
    capacity = 2 * blocks // owners

    own_rows = lax.dynamic_slice_in_dim(wavefunction, half * rows, rows, 1)
    codes = slot_codes(target_owner, target_local, owners, capacity)
    sources = codes // (2 * blocks)

    moved_left = []
    for k in range(terms):
        pick = sources[k][:, None, :] * halves + jnp.arange(halves, dtype=jnp.int32)[None, :, None]
        pieces = left_operator[k].reshape(blocks * halves, rows, width)[pick.reshape(-1)]
        pieces = pieces.reshape(owners * halves, capacity, rows, width)
        moved_left.append(lax.all_to_all(pieces, BOTH, split_axis=0, concat_axis=0, tiled=True))
    all_codes = lax.all_gather(codes, BOTH, axis=0)
    my_codes = lax.dynamic_index_in_dim(all_codes, me, axis=3 - 1, keepdims=False)
    gathered = lax.all_gather(own_rows, BOTH, axis=0).reshape(owners, halves, blocks, rows, width)
    right = lax.all_gather(right_operator, "term", axis=1)

    def apply(vector):
        total = None
        for k in range(terms):
            total = stream_chunk(total, my_codes[:, k], moved_left[k], vector, right[k])
        return total[:blocks]

    sigma_rows = apply(gathered)
    wave = own_rows.astype(jnp.float32)
    cross, own = jnp.sum(wave * sigma_rows), jnp.sum(wave * wave)
    local = jnp.where(own > 0, cross / own, 0.0)
    about = jnp.sum(jnp.square(sigma_rows - local * wave))
    stats = lax.all_gather(jnp.stack([about, cross, own, local]), BOTH, axis=0)
    rayleigh = jnp.sum(stats[:, 1]) / jnp.sum(stats[:, 2])
    residual_sq = jnp.sum(stats[:, 0] + jnp.square(stats[:, 3] - rayleigh) * stats[:, 2])
    entries = blocks * owners * height * width
    factor = lax.rsqrt(residual_sq / entries + 1e-06)
    direction = ((sigma_rows - rayleigh * wave) * factor).astype(jnp.bfloat16)
    direction = lax.all_gather(direction, BOTH, axis=0).reshape(gathered.shape)
    sigma_two = apply(direction).astype(jnp.bfloat16)
    return (sigma_two, jnp.reshape(rayleigh, (1,)))


def per_device(wavefunction, *operands):
    owners = lax.axis_size("sec")
    gathered_bytes = owners * wavefunction.size * wavefunction.dtype.itemsize
    if owners < 8 or owners & (owners - 1) or 2 * gathered_bytes > RING_BYTES:
        return per_device_streamed(wavefunction, *operands)
    return per_device_ring(wavefunction, *operands)


def solution(mesh):
    placed = (
        P(("rep", "sec"), None, None),
        P("term", ("rep", "sec"), None, None),
        P("term", ("rep", "sec"), None, None),
        P("term", ("rep", "sec"), None),
        P("term", ("rep", "sec")),
    )
    return jax.shard_map(
        per_device,
        mesh=mesh,
        in_specs=placed,
        out_specs=(P(("rep", "sec"), "term", None), P("rep")),
        check_vma=False,
    )
```

```python
import functools

import jax
import jax.numpy as jnp
from jax import lax
from jax.experimental import pallas as pl
from jax.experimental.pallas import tpu as pltpu
from jax.sharding import PartitionSpec as P

BOTH = ("sec", "term")
VMEM_LIMIT = 60 * 2**20
PART = 16
ORDER = [0, 4, 5, 1, 2, 6, 3, 7]
WAITS = {4: 1, 2: 5, 6: 2}
PIECE_WAITS = {6: 4, 7: 5}
RING_BYTES = 24 * 2**20


def ring_order(owners):
    if owners % 2:
        return list(range(owners))
    return list(range(0, owners, 2)) + list(range(owners - 1, 0, -2))


def ring_place(owner, owners):
    if owners % 2:
        return owner
    return jnp.where(owner % 2 == 0, owner // 2, owners - 1 - owner // 2)


def ring_owner(place, owners):
    place = place % owners
    if owners % 2:
        return place
    return jnp.where(place < owners // 2, 2 * place, 2 * (owners - 1 - place) + 1)


def permute(value, owners, halves, target, flip=0):
    pairs = [
        (chip * halves + half, target(chip, half) * halves + (half ^ flip))
        for chip in range(owners)
        for half in range(halves)
    ]
    return lax.ppermute(value, BOTH, pairs)


def swap(value, owners, halves):
    return permute(value, owners, halves, lambda chip, half: chip, 1)


def exchange(value, owners, halves, mask):
    return permute(value, owners, halves, lambda chip, half: chip ^ mask)


def ring_send(value, owners, halves, shifts):
    ring = ring_order(owners)
    place = {chip: index for index, chip in enumerate(ring)}
    return permute(
        value, owners, halves, lambda chip, half: ring[(place[chip] + shifts[half]) % owners]
    )


def after_kernel(*refs):
    del refs


def after(value, *others):
    anywhere = pl.BlockSpec(memory_space=pl.ANY)
    return pl.pallas_call(
        after_kernel,
        out_shape=jax.ShapeDtypeStruct(value.shape, value.dtype),
        in_specs=[anywhere] * (1 + len(others)),
        out_specs=anywhere,
        input_output_aliases={0: 0},
        cost_estimate=busy(0.3),
    )(value, *others)


def mask_gather(unit, lefts, owners, halves):
    units = {0: unit}
    step = owners // 2
    masks = []
    while step:
        masks.append(step)
        units[step] = exchange(unit, owners, halves, step)
        step //= 2
    waits = dict(WAITS)
    for step in masks[1:]:
        for mask in [m for m in units if m >= 2 * step and m % (2 * step) == 0]:
            if mask in waits:
                units[mask] = after(units[mask], lefts[waits.pop(mask)])
            units[mask | step] = exchange(units[mask], owners, halves, step)
    return units


def spread(value, devices):
    step = 1
    while step < devices:
        masks = [step] if 2 * step == devices else [step, 2 * step, 3 * step]
        parts = [lax.ppermute(value, BOTH, [(d, d ^ m) for d in range(devices)]) for m in masks]
        for part in parts:
            value = value + part
        step *= 4
    return value


def pack_kernel(order, capacity, blocks, terms, ids_ref, plan_ref, other_plan_ref, *refs):
    left_ref, other_ref, _, *pieces, codes, seen, built, sems = refs
    owners = len(order)
    me, half = ids_ref[0], ids_ref[1]
    rows, width = other_ref.shape[2:]
    start = pl.multiple_of(half * rows, rows)
    parts = rows // PART

    @pl.loop(0, owners)
    def _(owner):
        for index in range(2 * terms * capacity):
            codes[0, owner, index] = 0
            codes[1, owner, index] = blocks

    for stream in range(2 * terms):
        plan = plan_ref if stream < terms else other_plan_ref

        @pl.loop(0, owners)
        def _(owner):
            seen[owner] = 0

        @pl.loop(0, blocks, unroll=4)
        def _(block):
            owner = plan[0, stream % terms, block]
            slot = seen[owner]
            seen[owner] = slot + 1
            codes[0, owner, stream * capacity + slot] = block
            codes[1, owner, stream * capacity + slot] = plan[1, stream % terms, block]

    lane = lax.broadcasted_iota(jnp.int32, (PART, width), 1)
    row = lax.broadcasted_iota(jnp.int32, (PART, width), 0)
    copies = []
    for mask in order:
        owner = me ^ mask
        labels = jnp.zeros((PART, width), jnp.int32)
        for stream in range(2 * terms):
            for slot in range(capacity):
                at = stream * capacity + slot
                block = codes[0, owner, at]
                if stream < terms:
                    value = left_ref[stream, block, pl.ds(start, rows), :]
                else:
                    value = other_ref[stream - terms, block]
                built[mask, at * parts : (at + 1) * parts] = value.reshape(parts, PART, width)
                label = jnp.where(row == 0, block, codes[1, owner, at])
                labels = jnp.where(lane == at, label, labels)
        built[mask, 2 * terms * capacity * parts] = labels.astype(jnp.float32).astype(jnp.bfloat16)
        copies.append(pltpu.make_async_copy(built.at[mask], pieces[mask], sems.at[mask]))
        copies[-1].start()
    for copy in copies:
        copy.wait()


def pack(ids, plan, other_plan, left, other, before, order, capacity):
    terms, blocks, rows, width = other.shape
    owners = len(order)
    scalars = pl.BlockSpec(memory_space=pltpu.SMEM)
    whole = pl.BlockSpec(memory_space=pltpu.VMEM)
    anywhere = pl.BlockSpec(memory_space=pl.ANY)
    shape = (2 * terms * capacity * rows // PART + 1, PART, width)
    return pl.pallas_call(
        functools.partial(pack_kernel, order, capacity, blocks, terms),
        out_shape=[jax.ShapeDtypeStruct(shape, jnp.bfloat16)] * owners,
        in_specs=[scalars] * 3 + [whole, whole, anywhere],
        out_specs=[anywhere] * owners,
        scratch_shapes=[
            pltpu.SMEM((2, owners, 2 * terms * capacity), jnp.int32),
            pltpu.SMEM((owners,), jnp.int32),
            pltpu.VMEM((owners,) + shape, jnp.bfloat16),
            pltpu.SemaphoreType.DMA((owners,)),
        ],
        compiler_params=pltpu.CompilerParams(vmem_limit_bytes=VMEM_LIMIT),
        cost_estimate=busy(5.0),
    )(ids, plan, other_plan, left, other, before)


def busy(microseconds):
    return pl.CostEstimate(
        flops=int(1.15e9 * microseconds), bytes_accessed=0, transcendentals=0
    )


def add_products(left, labels, vector, right, total, side, terms, capacity):
    blocks, rows, width = vector.shape[1:]
    parts = rows // PART
    moved, where = [], []
    for slot in range(terms * capacity):
        at = side * terms * capacity + slot
        block = vector[:, labels[0, at]].reshape(2 * rows, width)
        piece = left[at * parts : (at + 1) * parts].reshape(rows, width)
        product = jnp.dot(piece, block, preferred_element_type=jnp.float32)
        moved.append(product.astype(jnp.bfloat16))
        where.append(labels[1, at])
    for slot in range(terms * capacity):
        total[where[slot]] += jnp.dot(
            moved[slot], right[slot], preferred_element_type=jnp.float32
        )


def local_stats(total, wave_ref, device, stats_ref):
    blocks = wave_ref.shape[0]
    zero = jnp.zeros(wave_ref.shape[1:], jnp.float32)

    def sums(block, carry):
        cross, own = carry
        wave = wave_ref[block].astype(jnp.float32)
        return cross + wave * total[block], own + wave * wave

    cross, own = lax.fori_loop(0, blocks, sums, (zero, zero), unroll=4)
    cross, own = jnp.sum(cross, keepdims=True), jnp.sum(own, keepdims=True)
    local = jnp.where(own > 0, cross / own, 0.0)

    def squares(block, carry):
        rest = total[block] - local * wave_ref[block].astype(jnp.float32)
        return carry + rest * rest

    about = jnp.sum(lax.fori_loop(0, blocks, squares, zero, unroll=4), keepdims=True)
    lane = lax.broadcasted_iota(jnp.int32, stats_ref.shape, 1)
    row = lax.broadcasted_iota(jnp.int32, stats_ref.shape, 0)
    values = jnp.where(lane == 0, about, jnp.where(lane == 1, cross, jnp.where(lane == 2, own, local)))
    stats_ref[...] = jnp.where((row == device) & (lane < 4), values, 0.0)


def apply_kernel(sources, choices, chosen, first, end, terms, capacity, ids_ref, *refs):
    refs = list(refs)

    def take(count):
        taken, refs[:count] = refs[:count], []
        return taken

    lefts = take(choices or sources)
    rights = take(2)
    vectors = [take(2) for _ in range(sources)]
    (wave_in,) = take(1) if end == "stats" else (None,)
    (total_in,) = (None,) if first else take(1)
    (total_out,) = (None,) if end == "result" else take(1)
    (last_out,) = take(1)
    total, left, right, vector, raw, spread_labels, labels = take(7)
    left_sems, right_sems, vector_sems, raw_sems, label_sem, total_sem = take(6)
    wave, wave_sem = take(2) if end == "stats" else (None, None)
    half = ids_ref[0]
    blocks = vector.shape[2]
    parts = left.shape[1]

    def left_copies(source, piece):
        return [
            pltpu.make_async_copy(piece.at[parts], raw.at[source], raw_sems.at[source]),
            pltpu.make_async_copy(
                piece.at[pl.ds(0, parts)], left.at[source], left_sems.at[source]
            ),
        ]

    def vector_copies(source):
        return [
            pltpu.make_async_copy(
                vectors[source][part],
                vector.at[source, half if part == 0 else 1 - half],
                vector_sems.at[source, part],
            )
            for part in range(2)
        ]

    def load_right(source, side):
        for slot in range(terms * capacity):
            target = jnp.minimum(labels[source, 1, side * terms * capacity + slot], blocks - 1)
            pltpu.make_async_copy(
                rights[side].at[slot // capacity, target],
                right.at[source, side, slot],
                right_sems.at[source, side],
            ).start()

    def wait_right(source, side):
        whole = right.at[source, side]
        pltpu.make_async_copy(whole, whole, right_sems.at[source, side]).wait()

    for source in range(sources):
        if choices:
            for choice, piece in enumerate(lefts):

                @pl.when(ids_ref[chosen + source] == choice)
                def _():
                    for copy in left_copies(source, piece):
                        copy.start()

        else:
            for copy in left_copies(source, lefts[source]):
                copy.start()
    for source in range(sources):
        for copy in vector_copies(source):
            copy.start()
    if first:
        total[...] = jnp.zeros_like(total)
    else:
        load_total = pltpu.make_async_copy(total_in, total, total_sem)
        load_total.start()
    if end == "stats":
        load_wave = pltpu.make_async_copy(wave_in, wave, wave_sem)
        load_wave.start()
    if end == "go on":
        last_out[...] = jnp.zeros_like(last_out)

    for source in range(sources):
        left_copies(source, lefts[0])[0].wait()
    spread_labels[...] = raw[:, :8].astype(jnp.float32).astype(jnp.int32)
    move_labels = pltpu.make_async_copy(spread_labels, labels, label_sem)
    move_labels.start()
    move_labels.wait()
    for source in range(sources):
        for side in range(2):
            load_right(source, side)
    if not first:
        load_total.wait()
    for source in range(sources):
        for side in range(2):
            if side == 0:
                left_copies(source, lefts[0])[1].wait()
                for copy in vector_copies(source):
                    copy.wait()
            wait_right(source, side)
            add_products(
                left.at[source],
                labels.at[source],
                vector.at[source],
                right.at[source, side],
                total,
                side,
                terms,
                capacity,
            )
    if end == "result":
        last_out[...] = total[:blocks].astype(last_out.dtype)
    elif end == "stats":
        load_wave.wait()
        local_stats(total, wave, ids_ref[1], last_out)
        total_out[...] = total[:blocks]
    else:
        store_total = pltpu.make_async_copy(total, total_out, total_sem)
        store_total.start()
        store_total.wait()


def apply_group(ids, lefts, rights, vectors, total, end, wave=None, chosen=0):
    blocks, rows, width = vectors[0][0].shape
    terms = rights[0].shape[0]
    parts = lefts[0].shape[0] - 1
    capacity = parts * PART // (2 * terms * rows)
    sources, first = len(vectors), total is None
    arrays = [*lefts, *rights] + [unit for pair in vectors for unit in pair]
    arrays += [wave] if end == "stats" else []
    arrays += [] if first else [total]
    whole = pl.BlockSpec(memory_space=pltpu.VMEM)
    anywhere = pl.BlockSpec(memory_space=pl.ANY)
    total_shape = (blocks + 1, rows, width)
    scratch = [
        pltpu.VMEM(total_shape, jnp.float32),
        pltpu.VMEM((sources, parts, PART, width), jnp.bfloat16),
        pltpu.VMEM((sources, 2, terms * capacity, width, width), jnp.bfloat16),
        pltpu.VMEM((sources, 2, blocks, rows, width), jnp.bfloat16),
        pltpu.VMEM((sources, PART, width), jnp.bfloat16),
        pltpu.VMEM((sources, 8, width), jnp.int32),
        pltpu.SMEM((sources, 8, width), jnp.int32),
        pltpu.SemaphoreType.DMA((sources,)),
        pltpu.SemaphoreType.DMA((sources, 2)),
        pltpu.SemaphoreType.DMA((sources, 2)),
        pltpu.SemaphoreType.DMA((sources,)),
        pltpu.SemaphoreType.DMA,
        pltpu.SemaphoreType.DMA,
    ]
    if end == "stats":
        scratch += [pltpu.VMEM(wave.shape, wave.dtype), pltpu.SemaphoreType.DMA]
    devices = lax.axis_size("sec") * lax.axis_size("term")
    total_out = jax.ShapeDtypeStruct(total_shape, jnp.float32)
    out_shape, out_specs = {
        "go on": ((total_out, jax.ShapeDtypeStruct((8, width), jnp.float32)), (anywhere, whole)),
        "stats": (
            (
                jax.ShapeDtypeStruct((blocks, rows, width), jnp.float32),
                jax.ShapeDtypeStruct((devices, 128), jnp.float32),
            ),
            (whole, whole),
        ),
        "result": (jax.ShapeDtypeStruct((blocks, rows, width), jnp.bfloat16), whole),
    }[end]
    choices = len(lefts) if chosen else 0
    return pl.pallas_call(
        functools.partial(apply_kernel, sources, choices, chosen, first, end, terms, capacity),
        out_shape=out_shape,
        in_specs=[pl.BlockSpec(memory_space=pltpu.SMEM)] + [anywhere] * len(arrays),
        out_specs=out_specs,
        scratch_shapes=scratch,
        compiler_params=pltpu.CompilerParams(vmem_limit_bytes=VMEM_LIMIT),
        cost_estimate=busy(3.5 + 1.8 * sources),
    )(ids, *arrays)


def direction_kernel(entries, total_ref, wave_ref, stats_ref, out_ref, rayleigh_ref):
    blocks = wave_ref.shape[0]
    stats = stats_ref[...]
    about, cross, own, local = (stats[:, lane : lane + 1] for lane in range(4))
    rayleigh = jnp.sum(cross, keepdims=True) / jnp.sum(own, keepdims=True)
    offset = local - rayleigh
    residual_sq = jnp.sum(about + offset * offset * own, keepdims=True)
    factor = lax.rsqrt(residual_sq / entries + 1e-06)
    rayleigh_ref[...] = rayleigh

    @pl.loop(0, blocks, unroll=4)
    def _(block):
        rest = total_ref[block] - rayleigh * wave_ref[block].astype(jnp.float32)
        out_ref[block] = (rest * factor).astype(jnp.bfloat16)


def new_direction(total, wave, stats, entries):
    whole = pl.BlockSpec(memory_space=pltpu.VMEM)
    return pl.pallas_call(
        functools.partial(direction_kernel, entries),
        out_shape=(
            jax.ShapeDtypeStruct(wave.shape, jnp.bfloat16),
            jax.ShapeDtypeStruct((1, 1), jnp.float32),
        ),
        in_specs=[whole] * 3,
        out_specs=(whole, whole),
        compiler_params=pltpu.CompilerParams(vmem_limit_bytes=8 * 2**20),
        cost_estimate=busy(2.0),
    )(total, wave, stats)


def per_device_ring(wavefunction, left_operator, right_operator, target_owner, target_local):
    owners, halves = lax.axis_size("sec"), lax.axis_size("term")
    me, half = lax.axis_index("sec"), lax.axis_index("term")
    terms, blocks, height, width = left_operator.shape
    rows = height // halves
    capacity = 2 * blocks // owners
    place = ring_place(me, owners)
    ids = jnp.stack([me, half]).astype(jnp.int32)

    own_rows = lax.dynamic_slice_in_dim(wavefunction, half * rows, rows, 1)
    other_rows = lax.dynamic_slice_in_dim(wavefunction, (1 - half) * rows, rows, 1)
    plan = jnp.stack([target_owner[:, :, 0], target_local])
    other_left = swap(
        lax.dynamic_slice_in_dim(left_operator, (1 - half) * rows, rows, 2), owners, halves
    )
    order = [m for m in ORDER if m < owners] + list(range(len(ORDER), owners))
    rights = (right_operator, swap(right_operator, owners, halves))
    pieces = pack(
        ids,
        plan,
        swap(plan, owners, halves),
        left_operator,
        other_left,
        plan,
        order[1:] + order[:1],
        capacity,
    )
    lefts = [pieces[0]]
    for m in range(1, owners):
        piece = pieces[m]
        if m in PIECE_WAITS:
            piece = after(piece, lefts[PIECE_WAITS[m]])
        lefts.append(exchange(piece, owners, halves, m))
    near = mask_gather(own_rows, lefts, owners, halves)
    far = {m: swap(unit, owners, halves) if m else other_rows for m, unit in near.items()}

    reach = (owners - 1) // 2
    turn = 1 - 2 * half
    distances = [0] + [s for step in range(1, reach + 1) for s in (step, -step)] + [owners // 2]
    whose = [me ^ ring_owner(place - s * turn, owners) for s in distances]
    numbers = jnp.stack([half, me * halves + half, *whose]).astype(jnp.int32)
    total = None
    groups = [order[at : at + 2] for at in range(0, owners, 2)]
    for group in groups:
        total, stats = apply_group(
            numbers,
            [lefts[m] for m in group],
            rights,
            [(near[m], far[m]) for m in group],
            total,
            "go on" if group is not groups[-1] else "stats",
            own_rows,
        )

    entries = blocks * owners * height * width
    stats = spread(stats, owners * halves)
    direction, rayleigh = new_direction(total, own_rows, stats, entries)
    def add_group(total, units, end):
        vectors = [(unit, swap(units[-s], owners, halves)) for s, unit in units.items()]
        chosen = 2 + distances.index(next(iter(units)))
        return apply_group(numbers, lefts, rights, vectors, total, end, chosen=chosen)

    total, waiting = None, {0: direction}
    ahead = behind = direction
    for step in range(1, reach + 1):
        ahead = ring_send(ahead, owners, halves, (1, -1))
        behind = ring_send(behind, owners, halves, (-1, 1))
        if step > 1:
            total, token = add_group(total, waiting, "go on")
            ahead, waiting = after(ahead, token), {}
        waiting.update({step: ahead, -step: behind})
    last = ring_send(ahead, owners, halves, (1, -1))
    total, token = add_group(total, waiting, "go on")
    last = after(last, token)
    vectors = [(last, swap(last, owners, halves))]
    chosen = 2 + distances.index(owners // 2)
    total = apply_group(numbers, lefts, rights, vectors, total, "result", chosen=chosen)
    return (total, rayleigh[0])


def slot_codes(target_owner, target_local, owners, capacity):
    terms, blocks = target_local.shape
    owner = target_owner[:, :, 0]
    place = jnp.arange(blocks, dtype=jnp.int32)
    same = (owner[:, :, None] == owner[:, None, :]) & (place[None, :] < place[:, None])[None]
    position = jnp.sum(same.astype(jnp.int32), axis=2)
    hit = (
        owner[:, None, None, :] == jnp.arange(owners, dtype=jnp.int32)[None, :, None, None]
    ) & (position[:, None, None, :] == jnp.arange(capacity, dtype=jnp.int32)[None, None, :, None])
    code = place[None, :] * (2 * blocks) + target_local - blocks
    return blocks + jnp.sum(jnp.where(hit, code[:, None, None, :], 0), axis=3)


def stream_kernel(first, capacity, blocks, code_ref, left_ref, vector_ref, right_ref, *rest):
    total_in, total = (None, rest[0]) if first else rest
    step = pl.program_id(0)
    rows, width = left_ref.shape[2:]

    @pl.when(step == 0)
    def _():
        total[...] = jnp.zeros_like(total) if first else total_in[...]

    for term in range(2):
        moved, where = [], []
        for slot in range(capacity):
            code = code_ref[2 * step + term, slot]
            source, target = lax.div(code, 2 * blocks), lax.rem(code, 2 * blocks)
            block = vector_ref[0, :, source].reshape(2 * rows, width)
            product = jnp.dot(left_ref[term, slot], block, preferred_element_type=jnp.float32)
            moved.append(product.astype(jnp.bfloat16))
            where.append(target)
        for slot in range(capacity):
            target = where[slot]
            total[target] += jnp.dot(
                moved[slot],
                right_ref[term, jnp.minimum(target, blocks - 1)],
                preferred_element_type=jnp.float32,
            )


def stream_chunk(total, codes, left, vector, right):
    owners, _, blocks, rows, width = vector.shape
    capacity = left.shape[1]
    first = total is None
    spec_total = pl.BlockSpec((blocks + 1, rows, width), lambda s, c: (0, 0, 0))
    return pl.pallas_call(
        functools.partial(stream_kernel, first, capacity, blocks),
        out_shape=jax.ShapeDtypeStruct((blocks + 1, rows, width), jnp.float32),
        grid_spec=pltpu.PrefetchScalarGridSpec(
            num_scalar_prefetch=1,
            grid=(owners,),
            in_specs=[
                pl.BlockSpec((2, capacity, rows, width), lambda s, c: (s, 0, 0, 0)),
                pl.BlockSpec((1, 2, blocks, rows, width), lambda s, c: (s, 0, 0, 0, 0)),
                pl.BlockSpec((2, blocks, width, width), lambda s, c: (0, 0, 0, 0)),
            ]
            + ([] if first else [spec_total]),
            out_specs=spec_total,
        ),
        compiler_params=pltpu.CompilerParams(vmem_limit_bytes=32 * 2**20),
        cost_estimate=pl.CostEstimate(
            flops=owners * 2 * capacity * 2 * 2 * rows * width * width,
            bytes_accessed=left.size * 2 + vector.size * 2 + right.size * 2,
            transcendentals=0,
        ),
    )(codes, left, vector, right, *([] if first else [total]))


def per_device_streamed(wavefunction, left_operator, right_operator, target_owner, target_local):
    owners = lax.axis_size("sec")
    halves = lax.axis_size("term")
    me, half = lax.axis_index("sec"), lax.axis_index("term")
    terms, blocks, height, width = left_operator.shape
    rows = height // halves
    capacity = 2 * blocks // owners

    own_rows = lax.dynamic_slice_in_dim(wavefunction, half * rows, rows, 1)
    codes = slot_codes(target_owner, target_local, owners, capacity)
    sources = codes // (2 * blocks)

    moved_left = []
    for k in range(terms):
        pick = sources[k][:, None, :] * halves + jnp.arange(halves, dtype=jnp.int32)[None, :, None]
        pieces = left_operator[k].reshape(blocks * halves, rows, width)[pick.reshape(-1)]
        pieces = pieces.reshape(owners * halves, capacity, rows, width)
        moved_left.append(lax.all_to_all(pieces, BOTH, split_axis=0, concat_axis=0, tiled=True))
    all_codes = lax.all_gather(codes, BOTH, axis=0)
    my_codes = lax.dynamic_index_in_dim(all_codes, me, axis=3 - 1, keepdims=False)
    gathered = lax.all_gather(own_rows, BOTH, axis=0).reshape(owners, halves, blocks, rows, width)
    right = lax.all_gather(right_operator, "term", axis=1)

    def apply(vector):
        total = None
        for k in range(terms):
            total = stream_chunk(total, my_codes[:, k], moved_left[k], vector, right[k])
        return total[:blocks]

    sigma_rows = apply(gathered)
    wave = own_rows.astype(jnp.float32)
    cross, own = jnp.sum(wave * sigma_rows), jnp.sum(wave * wave)
    local = jnp.where(own > 0, cross / own, 0.0)
    about = jnp.sum(jnp.square(sigma_rows - local * wave))
    stats = lax.all_gather(jnp.stack([about, cross, own, local]), BOTH, axis=0)
    rayleigh = jnp.sum(stats[:, 1]) / jnp.sum(stats[:, 2])
    residual_sq = jnp.sum(stats[:, 0] + jnp.square(stats[:, 3] - rayleigh) * stats[:, 2])
    entries = blocks * owners * height * width
    factor = lax.rsqrt(residual_sq / entries + 1e-06)
    direction = ((sigma_rows - rayleigh * wave) * factor).astype(jnp.bfloat16)
    direction = lax.all_gather(direction, BOTH, axis=0).reshape(gathered.shape)
    sigma_two = apply(direction).astype(jnp.bfloat16)
    return (sigma_two, jnp.reshape(rayleigh, (1,)))


def per_device(wavefunction, *operands):
    owners = lax.axis_size("sec")
    gathered_bytes = owners * wavefunction.size * wavefunction.dtype.itemsize
    if owners < 8 or owners & (owners - 1) or 2 * gathered_bytes > RING_BYTES:
        return per_device_streamed(wavefunction, *operands)
    return per_device_ring(wavefunction, *operands)


def solution(mesh):
    placed = (
        P(("rep", "sec"), None, None),
        P("term", ("rep", "sec"), None, None),
        P("term", ("rep", "sec"), None, None),
        P("term", ("rep", "sec"), None),
        P("term", ("rep", "sec")),
    )
    return jax.shard_map(
        per_device,
        mesh=mesh,
        in_specs=placed,
        out_specs=(P(("rep", "sec"), "term", None), P("rep")),
        check_vma=False,
    )
```

```python
import functools

import jax
import jax.numpy as jnp
from jax import lax
from jax.experimental import pallas as pl
from jax.experimental.pallas import tpu as pltpu
from jax.sharding import PartitionSpec as P

BOTH = ("sec", "term")
VMEM_LIMIT = 60 * 2**20
PART = 16
ORDER = [0, 1, 4, 2, 5, 6, 3, 7]
WAITS = {4: 1, 2: 4, 6: 2}
PIECE_WAITS = {6: 4, 7: 5}
RING_BYTES = 24 * 2**20


def ring_order(owners):
    if owners % 2:
        return list(range(owners))
    return list(range(0, owners, 2)) + list(range(owners - 1, 0, -2))


def ring_place(owner, owners):
    if owners % 2:
        return owner
    return jnp.where(owner % 2 == 0, owner // 2, owners - 1 - owner // 2)


def ring_owner(place, owners):
    place = place % owners
    if owners % 2:
        return place
    return jnp.where(place < owners // 2, 2 * place, 2 * (owners - 1 - place) + 1)


def permute(value, owners, halves, target, flip=0):
    pairs = [
        (chip * halves + half, target(chip, half) * halves + (half ^ flip))
        for chip in range(owners)
        for half in range(halves)
    ]
    return lax.ppermute(value, BOTH, pairs)


def swap(value, owners, halves):
    return permute(value, owners, halves, lambda chip, half: chip, 1)


def exchange(value, owners, halves, mask):
    return permute(value, owners, halves, lambda chip, half: chip ^ mask)


def ring_send(value, owners, halves, shifts):
    ring = ring_order(owners)
    place = {chip: index for index, chip in enumerate(ring)}
    return permute(
        value, owners, halves, lambda chip, half: ring[(place[chip] + shifts[half]) % owners]
    )


def after_kernel(*refs):
    del refs


def after(value, *others):
    anywhere = pl.BlockSpec(memory_space=pl.ANY)
    return pl.pallas_call(
        after_kernel,
        out_shape=jax.ShapeDtypeStruct(value.shape, value.dtype),
        in_specs=[anywhere] * (1 + len(others)),
        out_specs=anywhere,
        input_output_aliases={0: 0},
        cost_estimate=busy(0.3),
    )(value, *others)


def mask_gather(unit, lefts, owners, halves):
    units = {0: unit}
    step = owners // 2
    masks = []
    while step:
        masks.append(step)
        units[step] = exchange(unit, owners, halves, step)
        step //= 2
    waits = dict(WAITS)
    for step in masks[1:]:
        for mask in [m for m in units if m >= 2 * step and m % (2 * step) == 0]:
            if mask in waits:
                units[mask] = after(units[mask], lefts[waits.pop(mask)])
            units[mask | step] = exchange(units[mask], owners, halves, step)
    return units


def spread(value, devices):
    step = 1
    while step < devices:
        masks = [step] if 2 * step == devices else [step, 2 * step, 3 * step]
        parts = [lax.ppermute(value, BOTH, [(d, d ^ m) for d in range(devices)]) for m in masks]
        for part in parts:
            value = value + part
        step *= 4
    return value


def pack_kernel(order, capacity, blocks, terms, ids_ref, plan_ref, other_plan_ref, *refs):
    left_ref, other_ref, _, *pieces, codes, seen, built, sems = refs
    owners = len(order)
    me, half = ids_ref[0], ids_ref[1]
    rows, width = other_ref.shape[2:]
    start = pl.multiple_of(half * rows, rows)
    parts = rows // PART

    @pl.loop(0, owners)
    def _(owner):
        for index in range(2 * terms * capacity):
            codes[0, owner, index] = 0
            codes[1, owner, index] = blocks

    for stream in range(2 * terms):
        plan = plan_ref if stream < terms else other_plan_ref

        @pl.loop(0, owners)
        def _(owner):
            seen[owner] = 0

        @pl.loop(0, blocks, unroll=4)
        def _(block):
            owner = plan[0, stream % terms, block]
            slot = seen[owner]
            seen[owner] = slot + 1
            codes[0, owner, stream * capacity + slot] = block
            codes[1, owner, stream * capacity + slot] = plan[1, stream % terms, block]

    lane = lax.broadcasted_iota(jnp.int32, (PART, width), 1)
    row = lax.broadcasted_iota(jnp.int32, (PART, width), 0)
    copies = []
    for mask in order:
        owner = me ^ mask
        labels = jnp.zeros((PART, width), jnp.int32)
        for stream in range(2 * terms):
            for slot in range(capacity):
                at = stream * capacity + slot
                block = codes[0, owner, at]
                if stream < terms:
                    value = left_ref[stream, block, pl.ds(start, rows), :]
                else:
                    value = other_ref[stream - terms, block]
                built[mask, at * parts : (at + 1) * parts] = value.reshape(parts, PART, width)
                label = jnp.where(row == 0, block, codes[1, owner, at])
                labels = jnp.where(lane == at, label, labels)
        built[mask, 2 * terms * capacity * parts] = labels.astype(jnp.float32).astype(jnp.bfloat16)
        copies.append(pltpu.make_async_copy(built.at[mask], pieces[mask], sems.at[mask]))
        copies[-1].start()
    for copy in copies:
        copy.wait()


def pack(ids, plan, other_plan, left, other, before, order, capacity):
    terms, blocks, rows, width = other.shape
    owners = len(order)
    scalars = pl.BlockSpec(memory_space=pltpu.SMEM)
    whole = pl.BlockSpec(memory_space=pltpu.VMEM)
    anywhere = pl.BlockSpec(memory_space=pl.ANY)
    shape = (2 * terms * capacity * rows // PART + 1, PART, width)
    return pl.pallas_call(
        functools.partial(pack_kernel, order, capacity, blocks, terms),
        out_shape=[jax.ShapeDtypeStruct(shape, jnp.bfloat16)] * owners,
        in_specs=[scalars] * 3 + [whole, whole, anywhere],
        out_specs=[anywhere] * owners,
        scratch_shapes=[
            pltpu.SMEM((2, owners, 2 * terms * capacity), jnp.int32),
            pltpu.SMEM((owners,), jnp.int32),
            pltpu.VMEM((owners,) + shape, jnp.bfloat16),
            pltpu.SemaphoreType.DMA((owners,)),
        ],
        compiler_params=pltpu.CompilerParams(vmem_limit_bytes=VMEM_LIMIT),
        cost_estimate=busy(5.0),
    )(ids, plan, other_plan, left, other, before)


def busy(microseconds):
    return pl.CostEstimate(
        flops=int(1.15e9 * microseconds), bytes_accessed=0, transcendentals=0
    )


def add_products(left, labels, vector, right, total, side, terms, capacity):
    blocks, rows, width = vector.shape[1:]
    parts = rows // PART
    moved, where = [], []
    for slot in range(terms * capacity):
        at = side * terms * capacity + slot
        block = vector[:, labels[0, at]].reshape(2 * rows, width)
        piece = left[at * parts : (at + 1) * parts].reshape(rows, width)
        product = jnp.dot(piece, block, preferred_element_type=jnp.float32)
        moved.append(product.astype(jnp.bfloat16))
        where.append(labels[1, at])
    for slot in range(terms * capacity):
        total[where[slot]] += jnp.dot(
            moved[slot], right[slot], preferred_element_type=jnp.float32
        )


def local_stats(total, wave_ref, device, stats_ref):
    blocks = wave_ref.shape[0]
    zero = jnp.zeros(wave_ref.shape[1:], jnp.float32)

    def sums(block, carry):
        cross, own = carry
        wave = wave_ref[block].astype(jnp.float32)
        return cross + wave * total[block], own + wave * wave

    cross, own = lax.fori_loop(0, blocks, sums, (zero, zero), unroll=4)
    cross, own = jnp.sum(cross, keepdims=True), jnp.sum(own, keepdims=True)
    local = jnp.where(own > 0, cross / own, 0.0)

    def squares(block, carry):
        rest = total[block] - local * wave_ref[block].astype(jnp.float32)
        return carry + rest * rest

    about = jnp.sum(lax.fori_loop(0, blocks, squares, zero, unroll=4), keepdims=True)
    lane = lax.broadcasted_iota(jnp.int32, stats_ref.shape, 1)
    row = lax.broadcasted_iota(jnp.int32, stats_ref.shape, 0)
    values = jnp.where(lane == 0, about, jnp.where(lane == 1, cross, jnp.where(lane == 2, own, local)))
    stats_ref[...] = jnp.where((row == device) & (lane < 4), values, 0.0)


def apply_kernel(sources, choices, chosen, first, end, terms, capacity, ids_ref, *refs):
    refs = list(refs)

    def take(count):
        taken, refs[:count] = refs[:count], []
        return taken

    lefts = take(choices or sources)
    rights = take(2)
    vectors = [take(2) for _ in range(sources)]
    (wave_in,) = take(1) if end == "stats" else (None,)
    (total_in,) = (None,) if first else take(1)
    (total_out,) = (None,) if end == "result" else take(1)
    (last_out,) = take(1)
    total, left, right, vector, raw, spread_labels, labels = take(7)
    left_sems, right_sems, vector_sems, raw_sems, label_sem, total_sem = take(6)
    wave, wave_sem = take(2) if end == "stats" else (None, None)
    half = ids_ref[0]
    blocks = vector.shape[2]
    parts = left.shape[1]

    def left_copies(source, piece):
        return [
            pltpu.make_async_copy(piece.at[parts], raw.at[source], raw_sems.at[source]),
            pltpu.make_async_copy(
                piece.at[pl.ds(0, parts)], left.at[source], left_sems.at[source]
            ),
        ]

    def vector_copies(source):
        return [
            pltpu.make_async_copy(
                vectors[source][part],
                vector.at[source, half if part == 0 else 1 - half],
                vector_sems.at[source, part],
            )
            for part in range(2)
        ]

    def load_right(source, side):
        for slot in range(terms * capacity):
            target = jnp.minimum(labels[source, 1, side * terms * capacity + slot], blocks - 1)
            pltpu.make_async_copy(
                rights[side].at[slot // capacity, target],
                right.at[source, side, slot],
                right_sems.at[source, side],
            ).start()

    def wait_right(source, side):
        whole = right.at[source, side]
        pltpu.make_async_copy(whole, whole, right_sems.at[source, side]).wait()

    for source in range(sources):
        if choices:
            for choice, piece in enumerate(lefts):

                @pl.when(ids_ref[chosen + source] == choice)
                def _():
                    for copy in left_copies(source, piece):
                        copy.start()

        else:
            for copy in left_copies(source, lefts[source]):
                copy.start()
    for source in range(sources):
        for copy in vector_copies(source):
            copy.start()
    if first:
        total[...] = jnp.zeros_like(total)
    else:
        load_total = pltpu.make_async_copy(total_in, total, total_sem)
        load_total.start()
    if end == "stats":
        load_wave = pltpu.make_async_copy(wave_in, wave, wave_sem)
        load_wave.start()
    if end == "go on":
        last_out[...] = jnp.zeros_like(last_out)

    for source in range(sources):
        left_copies(source, lefts[0])[0].wait()
    spread_labels[...] = raw[:, :8].astype(jnp.float32).astype(jnp.int32)
    move_labels = pltpu.make_async_copy(spread_labels, labels, label_sem)
    move_labels.start()
    move_labels.wait()
    for source in range(sources):
        for side in range(2):
            load_right(source, side)
    if not first:
        load_total.wait()
    for source in range(sources):
        for side in range(2):
            if side == 0:
                left_copies(source, lefts[0])[1].wait()
                for copy in vector_copies(source):
                    copy.wait()
            wait_right(source, side)
            add_products(
                left.at[source],
                labels.at[source],
                vector.at[source],
                right.at[source, side],
                total,
                side,
                terms,
                capacity,
            )
    if end == "result":
        last_out[...] = total[:blocks].astype(last_out.dtype)
    elif end == "stats":
        load_wave.wait()
        local_stats(total, wave, ids_ref[1], last_out)
        total_out[...] = total[:blocks]
    else:
        store_total = pltpu.make_async_copy(total, total_out, total_sem)
        store_total.start()
        store_total.wait()


def apply_group(ids, lefts, rights, vectors, total, end, wave=None, chosen=0):
    blocks, rows, width = vectors[0][0].shape
    terms = rights[0].shape[0]
    parts = lefts[0].shape[0] - 1
    capacity = parts * PART // (2 * terms * rows)
    sources, first = len(vectors), total is None
    arrays = [*lefts, *rights] + [unit for pair in vectors for unit in pair]
    arrays += [wave] if end == "stats" else []
    arrays += [] if first else [total]
    whole = pl.BlockSpec(memory_space=pltpu.VMEM)
    anywhere = pl.BlockSpec(memory_space=pl.ANY)
    total_shape = (blocks + 1, rows, width)
    scratch = [
        pltpu.VMEM(total_shape, jnp.float32),
        pltpu.VMEM((sources, parts, PART, width), jnp.bfloat16),
        pltpu.VMEM((sources, 2, terms * capacity, width, width), jnp.bfloat16),
        pltpu.VMEM((sources, 2, blocks, rows, width), jnp.bfloat16),
        pltpu.VMEM((sources, PART, width), jnp.bfloat16),
        pltpu.VMEM((sources, 8, width), jnp.int32),
        pltpu.SMEM((sources, 8, width), jnp.int32),
        pltpu.SemaphoreType.DMA((sources,)),
        pltpu.SemaphoreType.DMA((sources, 2)),
        pltpu.SemaphoreType.DMA((sources, 2)),
        pltpu.SemaphoreType.DMA((sources,)),
        pltpu.SemaphoreType.DMA,
        pltpu.SemaphoreType.DMA,
    ]
    if end == "stats":
        scratch += [pltpu.VMEM(wave.shape, wave.dtype), pltpu.SemaphoreType.DMA]
    devices = lax.axis_size("sec") * lax.axis_size("term")
    total_out = jax.ShapeDtypeStruct(total_shape, jnp.float32)
    out_shape, out_specs = {
        "go on": ((total_out, jax.ShapeDtypeStruct((8, width), jnp.float32)), (anywhere, whole)),
        "stats": (
            (
                jax.ShapeDtypeStruct((blocks, rows, width), jnp.float32),
                jax.ShapeDtypeStruct((devices, 128), jnp.float32),
            ),
            (whole, whole),
        ),
        "result": (jax.ShapeDtypeStruct((blocks, rows, width), jnp.bfloat16), whole),
    }[end]
    choices = len(lefts) if chosen else 0
    return pl.pallas_call(
        functools.partial(apply_kernel, sources, choices, chosen, first, end, terms, capacity),
        out_shape=out_shape,
        in_specs=[pl.BlockSpec(memory_space=pltpu.SMEM)] + [anywhere] * len(arrays),
        out_specs=out_specs,
        scratch_shapes=scratch,
        compiler_params=pltpu.CompilerParams(vmem_limit_bytes=VMEM_LIMIT),
        cost_estimate=busy(3.5 + 1.8 * sources),
    )(ids, *arrays)


def direction_kernel(entries, total_ref, wave_ref, stats_ref, out_ref, rayleigh_ref):
    blocks = wave_ref.shape[0]
    stats = stats_ref[...]
    about, cross, own, local = (stats[:, lane : lane + 1] for lane in range(4))
    rayleigh = jnp.sum(cross, keepdims=True) / jnp.sum(own, keepdims=True)
    offset = local - rayleigh
    residual_sq = jnp.sum(about + offset * offset * own, keepdims=True)
    factor = lax.rsqrt(residual_sq / entries + 1e-06)
    rayleigh_ref[...] = rayleigh

    @pl.loop(0, blocks, unroll=4)
    def _(block):
        rest = total_ref[block] - rayleigh * wave_ref[block].astype(jnp.float32)
        out_ref[block] = (rest * factor).astype(jnp.bfloat16)


def new_direction(total, wave, stats, entries):
    whole = pl.BlockSpec(memory_space=pltpu.VMEM)
    return pl.pallas_call(
        functools.partial(direction_kernel, entries),
        out_shape=(
            jax.ShapeDtypeStruct(wave.shape, jnp.bfloat16),
            jax.ShapeDtypeStruct((1, 1), jnp.float32),
        ),
        in_specs=[whole] * 3,
        out_specs=(whole, whole),
        compiler_params=pltpu.CompilerParams(vmem_limit_bytes=8 * 2**20),
        cost_estimate=busy(2.0),
    )(total, wave, stats)


def per_device_ring(wavefunction, left_operator, right_operator, target_owner, target_local):
    owners, halves = lax.axis_size("sec"), lax.axis_size("term")
    me, half = lax.axis_index("sec"), lax.axis_index("term")
    terms, blocks, height, width = left_operator.shape
    rows = height // halves
    capacity = 2 * blocks // owners
    place = ring_place(me, owners)
    ids = jnp.stack([me, half]).astype(jnp.int32)

    own_rows = lax.dynamic_slice_in_dim(wavefunction, half * rows, rows, 1)
    other_rows = lax.dynamic_slice_in_dim(wavefunction, (1 - half) * rows, rows, 1)
    plan = jnp.stack([target_owner[:, :, 0], target_local])
    other_left = swap(
        lax.dynamic_slice_in_dim(left_operator, (1 - half) * rows, rows, 2), owners, halves
    )
    order = [m for m in ORDER if m < owners] + list(range(len(ORDER), owners))
    rights = (right_operator, swap(right_operator, owners, halves))
    pieces = pack(
        ids,
        plan,
        swap(plan, owners, halves),
        left_operator,
        other_left,
        plan,
        order[1:] + order[:1],
        capacity,
    )
    lefts = [pieces[0]]
    for m in range(1, owners):
        piece = pieces[m]
        if m in PIECE_WAITS:
            piece = after(piece, lefts[PIECE_WAITS[m]])
        lefts.append(exchange(piece, owners, halves, m))
    near = mask_gather(own_rows, lefts, owners, halves)
    far = {m: swap(unit, owners, halves) if m else other_rows for m, unit in near.items()}

    reach = (owners - 1) // 2
    turn = 1 - 2 * half
    distances = [0] + [s for step in range(1, reach + 1) for s in (step, -step)] + [owners // 2]
    whose = [me ^ ring_owner(place - s * turn, owners) for s in distances]
    numbers = jnp.stack([half, me * halves + half, *whose]).astype(jnp.int32)
    total = None
    groups = [order[at : at + 2] for at in range(0, owners, 2)]
    for group in groups:
        total, stats = apply_group(
            numbers,
            [lefts[m] for m in group],
            rights,
            [(near[m], far[m]) for m in group],
            total,
            "go on" if group is not groups[-1] else "stats",
            own_rows,
        )

    entries = blocks * owners * height * width
    stats = spread(stats, owners * halves)
    direction, rayleigh = new_direction(total, own_rows, stats, entries)
    def add_group(total, units, end):
        vectors = [(unit, swap(units[-s], owners, halves)) for s, unit in units.items()]
        chosen = 2 + distances.index(next(iter(units)))
        return apply_group(numbers, lefts, rights, vectors, total, end, chosen=chosen)

    total, waiting = None, {0: direction}
    ahead = behind = direction
    for step in range(1, reach + 1):
        ahead = ring_send(ahead, owners, halves, (1, -1))
        behind = ring_send(behind, owners, halves, (-1, 1))
        if step > 1:
            total, token = add_group(total, waiting, "go on")
            ahead, waiting = after(ahead, token), {}
        waiting.update({step: ahead, -step: behind})
    last = ring_send(ahead, owners, halves, (1, -1))
    total, token = add_group(total, waiting, "go on")
    last = after(last, token)
    vectors = [(last, swap(last, owners, halves))]
    chosen = 2 + distances.index(owners // 2)
    total = apply_group(numbers, lefts, rights, vectors, total, "result", chosen=chosen)
    return (total, rayleigh[0])


def slot_codes(target_owner, target_local, owners, capacity):
    terms, blocks = target_local.shape
    owner = target_owner[:, :, 0]
    place = jnp.arange(blocks, dtype=jnp.int32)
    same = (owner[:, :, None] == owner[:, None, :]) & (place[None, :] < place[:, None])[None]
    position = jnp.sum(same.astype(jnp.int32), axis=2)
    hit = (
        owner[:, None, None, :] == jnp.arange(owners, dtype=jnp.int32)[None, :, None, None]
    ) & (position[:, None, None, :] == jnp.arange(capacity, dtype=jnp.int32)[None, None, :, None])
    code = place[None, :] * (2 * blocks) + target_local - blocks
    return blocks + jnp.sum(jnp.where(hit, code[:, None, None, :], 0), axis=3)


def stream_kernel(first, capacity, blocks, code_ref, left_ref, vector_ref, right_ref, *rest):
    total_in, total = (None, rest[0]) if first else rest
    step = pl.program_id(0)
    rows, width = left_ref.shape[2:]

    @pl.when(step == 0)
    def _():
        total[...] = jnp.zeros_like(total) if first else total_in[...]

    for term in range(2):
        moved, where = [], []
        for slot in range(capacity):
            code = code_ref[2 * step + term, slot]
            source, target = lax.div(code, 2 * blocks), lax.rem(code, 2 * blocks)
            block = vector_ref[0, :, source].reshape(2 * rows, width)
            product = jnp.dot(left_ref[term, slot], block, preferred_element_type=jnp.float32)
            moved.append(product.astype(jnp.bfloat16))
            where.append(target)
        for slot in range(capacity):
            target = where[slot]
            total[target] += jnp.dot(
                moved[slot],
                right_ref[term, jnp.minimum(target, blocks - 1)],
                preferred_element_type=jnp.float32,
            )


def stream_chunk(total, codes, left, vector, right):
    owners, _, blocks, rows, width = vector.shape
    capacity = left.shape[1]
    first = total is None
    spec_total = pl.BlockSpec((blocks + 1, rows, width), lambda s, c: (0, 0, 0))
    return pl.pallas_call(
        functools.partial(stream_kernel, first, capacity, blocks),
        out_shape=jax.ShapeDtypeStruct((blocks + 1, rows, width), jnp.float32),
        grid_spec=pltpu.PrefetchScalarGridSpec(
            num_scalar_prefetch=1,
            grid=(owners,),
            in_specs=[
                pl.BlockSpec((2, capacity, rows, width), lambda s, c: (s, 0, 0, 0)),
                pl.BlockSpec((1, 2, blocks, rows, width), lambda s, c: (s, 0, 0, 0, 0)),
                pl.BlockSpec((2, blocks, width, width), lambda s, c: (0, 0, 0, 0)),
            ]
            + ([] if first else [spec_total]),
            out_specs=spec_total,
        ),
        compiler_params=pltpu.CompilerParams(vmem_limit_bytes=32 * 2**20),
        cost_estimate=pl.CostEstimate(
            flops=owners * 2 * capacity * 2 * 2 * rows * width * width,
            bytes_accessed=left.size * 2 + vector.size * 2 + right.size * 2,
            transcendentals=0,
        ),
    )(codes, left, vector, right, *([] if first else [total]))


def per_device_streamed(wavefunction, left_operator, right_operator, target_owner, target_local):
    owners = lax.axis_size("sec")
    halves = lax.axis_size("term")
    me, half = lax.axis_index("sec"), lax.axis_index("term")
    terms, blocks, height, width = left_operator.shape
    rows = height // halves
    capacity = 2 * blocks // owners

    own_rows = lax.dynamic_slice_in_dim(wavefunction, half * rows, rows, 1)
    codes = slot_codes(target_owner, target_local, owners, capacity)
    sources = codes // (2 * blocks)

    moved_left = []
    for k in range(terms):
        pick = sources[k][:, None, :] * halves + jnp.arange(halves, dtype=jnp.int32)[None, :, None]
        pieces = left_operator[k].reshape(blocks * halves, rows, width)[pick.reshape(-1)]
        pieces = pieces.reshape(owners * halves, capacity, rows, width)
        moved_left.append(lax.all_to_all(pieces, BOTH, split_axis=0, concat_axis=0, tiled=True))
    all_codes = lax.all_gather(codes, BOTH, axis=0)
    my_codes = lax.dynamic_index_in_dim(all_codes, me, axis=3 - 1, keepdims=False)
    gathered = lax.all_gather(own_rows, BOTH, axis=0).reshape(owners, halves, blocks, rows, width)
    right = lax.all_gather(right_operator, "term", axis=1)

    def apply(vector):
        total = None
        for k in range(terms):
            total = stream_chunk(total, my_codes[:, k], moved_left[k], vector, right[k])
        return total[:blocks]

    sigma_rows = apply(gathered)
    wave = own_rows.astype(jnp.float32)
    cross, own = jnp.sum(wave * sigma_rows), jnp.sum(wave * wave)
    local = jnp.where(own > 0, cross / own, 0.0)
    about = jnp.sum(jnp.square(sigma_rows - local * wave))
    stats = lax.all_gather(jnp.stack([about, cross, own, local]), BOTH, axis=0)
    rayleigh = jnp.sum(stats[:, 1]) / jnp.sum(stats[:, 2])
    residual_sq = jnp.sum(stats[:, 0] + jnp.square(stats[:, 3] - rayleigh) * stats[:, 2])
    entries = blocks * owners * height * width
    factor = lax.rsqrt(residual_sq / entries + 1e-06)
    direction = ((sigma_rows - rayleigh * wave) * factor).astype(jnp.bfloat16)
    direction = lax.all_gather(direction, BOTH, axis=0).reshape(gathered.shape)
    sigma_two = apply(direction).astype(jnp.bfloat16)
    return (sigma_two, jnp.reshape(rayleigh, (1,)))


def per_device(wavefunction, *operands):
    owners = lax.axis_size("sec")
    gathered_bytes = owners * wavefunction.size * wavefunction.dtype.itemsize
    if owners < 8 or owners & (owners - 1) or 2 * gathered_bytes > RING_BYTES:
        return per_device_streamed(wavefunction, *operands)
    return per_device_ring(wavefunction, *operands)


def solution(mesh):
    placed = (
        P(("rep", "sec"), None, None),
        P("term", ("rep", "sec"), None, None),
        P("term", ("rep", "sec"), None, None),
        P("term", ("rep", "sec"), None),
        P("term", ("rep", "sec")),
    )
    return jax.shard_map(
        per_device,
        mesh=mesh,
        in_specs=placed,
        out_specs=(P(("rep", "sec"), "term", None), P("rep")),
        check_vma=False,
    )
```

```python
import functools

import jax
import jax.numpy as jnp
from jax import lax
from jax.experimental import pallas as pl
from jax.experimental.pallas import tpu as pltpu
from jax.sharding import PartitionSpec as P

BOTH = ("sec", "term")
VMEM_LIMIT = 64 * 2**20
PART = 16
ORDER = [0, 1, 4, 2, 5, 6, 3, 7]
WAITS = {4: 1, 2: 4, 6: 2}
PIECE_WAITS = {6: 4, 7: 5}
RING_BYTES = 24 * 2**20


def ring_order(owners):
    if owners % 2:
        return list(range(owners))
    return list(range(0, owners, 2)) + list(range(owners - 1, 0, -2))


def ring_place(owner, owners):
    if owners % 2:
        return owner
    return jnp.where(owner % 2 == 0, owner // 2, owners - 1 - owner // 2)


def ring_owner(place, owners):
    place = place % owners
    if owners % 2:
        return place
    return jnp.where(place < owners // 2, 2 * place, 2 * (owners - 1 - place) + 1)


def permute(value, owners, halves, target, flip=0):
    pairs = [
        (chip * halves + half, target(chip, half) * halves + (half ^ flip))
        for chip in range(owners)
        for half in range(halves)
    ]
    return lax.ppermute(value, BOTH, pairs)


def swap(value, owners, halves):
    return permute(value, owners, halves, lambda chip, half: chip, 1)


def exchange(value, owners, halves, mask):
    return permute(value, owners, halves, lambda chip, half: chip ^ mask)


def ring_send(value, owners, halves, shifts):
    ring = ring_order(owners)
    place = {chip: index for index, chip in enumerate(ring)}
    return permute(
        value, owners, halves, lambda chip, half: ring[(place[chip] + shifts[half]) % owners]
    )


def after_kernel(*refs):
    del refs


def after(value, *others):
    anywhere = pl.BlockSpec(memory_space=pl.ANY)
    return pl.pallas_call(
        after_kernel,
        out_shape=jax.ShapeDtypeStruct(value.shape, value.dtype),
        in_specs=[anywhere] * (1 + len(others)),
        out_specs=anywhere,
        input_output_aliases={0: 0},
        cost_estimate=busy(0.3),
    )(value, *others)


def mask_gather(unit, lefts, owners, halves):
    units = {0: unit}
    step = owners // 2
    masks = []
    while step:
        masks.append(step)
        units[step] = exchange(unit, owners, halves, step)
        step //= 2
    waits = dict(WAITS)
    for step in masks[1:]:
        for mask in [m for m in units if m >= 2 * step and m % (2 * step) == 0]:
            if mask in waits:
                units[mask] = after(units[mask], lefts[waits.pop(mask)])
            units[mask | step] = exchange(units[mask], owners, halves, step)
    return units


def spread(value, devices):
    step = 1
    while step < devices:
        masks = [step] if 2 * step == devices else [step, 2 * step, 3 * step]
        parts = [lax.ppermute(value, BOTH, [(d, d ^ m) for d in range(devices)]) for m in masks]
        for part in parts:
            value = value + part
        step *= 4
    return value


def pack_kernel(order, capacity, blocks, terms, ids_ref, plan_ref, other_plan_ref, *refs):
    left_ref, other_ref, _, *pieces, codes, seen, built, sems = refs
    owners = len(order)
    me, half = ids_ref[0], ids_ref[1]
    rows, width = other_ref.shape[2:]
    start = pl.multiple_of(half * rows, rows)
    parts = rows // PART

    @pl.loop(0, owners)
    def _(owner):
        for index in range(2 * terms * capacity):
            codes[0, owner, index] = 0
            codes[1, owner, index] = blocks

    for stream in range(2 * terms):
        plan = plan_ref if stream < terms else other_plan_ref

        @pl.loop(0, owners)
        def _(owner):
            seen[owner] = 0

        @pl.loop(0, blocks, unroll=4)
        def _(block):
            owner = plan[0, stream % terms, block]
            slot = seen[owner]
            seen[owner] = slot + 1
            codes[0, owner, stream * capacity + slot] = block
            codes[1, owner, stream * capacity + slot] = plan[1, stream % terms, block]

    lane = lax.broadcasted_iota(jnp.int32, (PART, width), 1)
    row = lax.broadcasted_iota(jnp.int32, (PART, width), 0)
    copies = []
    for mask in order:
        owner = me ^ mask
        labels = jnp.zeros((PART, width), jnp.int32)
        for stream in range(2 * terms):
            for slot in range(capacity):
                at = stream * capacity + slot
                block = codes[0, owner, at]
                if stream < terms:
                    value = left_ref[stream, block, pl.ds(start, rows), :]
                else:
                    value = other_ref[stream - terms, block]
                built[mask, at * parts : (at + 1) * parts] = value.reshape(parts, PART, width)
                label = jnp.where(row == 0, block, codes[1, owner, at])
                labels = jnp.where(lane == at, label, labels)
        built[mask, 2 * terms * capacity * parts] = labels.astype(jnp.float32).astype(jnp.bfloat16)
        copies.append(pltpu.make_async_copy(built.at[mask], pieces[mask], sems.at[mask]))
        copies[-1].start()
    for copy in copies:
        copy.wait()


def pack(ids, plan, other_plan, left, other, before, order, capacity):
    terms, blocks, rows, width = other.shape
    owners = len(order)
    scalars = pl.BlockSpec(memory_space=pltpu.SMEM)
    whole = pl.BlockSpec(memory_space=pltpu.VMEM)
    anywhere = pl.BlockSpec(memory_space=pl.ANY)
    shape = (2 * terms * capacity * rows // PART + 1, PART, width)
    return pl.pallas_call(
        functools.partial(pack_kernel, order, capacity, blocks, terms),
        out_shape=[jax.ShapeDtypeStruct(shape, jnp.bfloat16)] * owners,
        in_specs=[scalars] * 3 + [whole, whole, anywhere],
        out_specs=[anywhere] * owners,
        scratch_shapes=[
            pltpu.SMEM((2, owners, 2 * terms * capacity), jnp.int32),
            pltpu.SMEM((owners,), jnp.int32),
            pltpu.VMEM((owners,) + shape, jnp.bfloat16),
            pltpu.SemaphoreType.DMA((owners,)),
        ],
        compiler_params=pltpu.CompilerParams(vmem_limit_bytes=VMEM_LIMIT),
        cost_estimate=busy(5.0),
    )(ids, plan, other_plan, left, other, before)


def busy(microseconds):
    return pl.CostEstimate(
        flops=int(1.15e9 * microseconds), bytes_accessed=0, transcendentals=0
    )


def add_products(left, labels, vector, right, total, side, terms, capacity):
    blocks, rows, width = vector.shape[1:]
    parts = rows // PART
    moved, where = [], []
    for slot in range(terms * capacity):
        at = side * terms * capacity + slot
        block = vector[:, labels[0, at]].reshape(2 * rows, width)
        piece = left[at * parts : (at + 1) * parts].reshape(rows, width)
        product = jnp.dot(piece, block, preferred_element_type=jnp.float32)
        moved.append(product.astype(jnp.bfloat16))
        where.append(labels[1, at])
    for slot in range(terms * capacity):
        total[where[slot]] += jnp.dot(
            moved[slot], right[slot], preferred_element_type=jnp.float32
        )


def local_stats(total, wave_ref, device, stats_ref):
    blocks = wave_ref.shape[0]
    zero = jnp.zeros(wave_ref.shape[1:], jnp.float32)

    def sums(block, carry):
        cross, own = carry
        wave = wave_ref[block].astype(jnp.float32)
        return cross + wave * total[block], own + wave * wave

    cross, own = lax.fori_loop(0, blocks, sums, (zero, zero), unroll=4)
    cross, own = jnp.sum(cross, keepdims=True), jnp.sum(own, keepdims=True)
    local = jnp.where(own > 0, cross / own, 0.0)

    def squares(block, carry):
        rest = total[block] - local * wave_ref[block].astype(jnp.float32)
        return carry + rest * rest

    about = jnp.sum(lax.fori_loop(0, blocks, squares, zero, unroll=4), keepdims=True)
    lane = lax.broadcasted_iota(jnp.int32, stats_ref.shape, 1)
    row = lax.broadcasted_iota(jnp.int32, stats_ref.shape, 0)
    values = jnp.where(lane == 0, about, jnp.where(lane == 1, cross, jnp.where(lane == 2, own, local)))
    stats_ref[...] = jnp.where((row == device) & (lane < 4), values, 0.0)


def apply_kernel(sources, choices, chosen, first, end, terms, capacity, ids_ref, *refs):
    refs = list(refs)

    def take(count):
        taken, refs[:count] = refs[:count], []
        return taken

    lefts = take(choices or sources)
    rights = take(2)
    vectors = [take(2) for _ in range(sources)]
    (wave_in,) = take(1) if end == "stats" else (None,)
    (total_in,) = (None,) if first else take(1)
    (total_out,) = (None,) if end == "result" else take(1)
    (last_out,) = take(1)
    total, left, right, vector, raw, spread_labels, labels = take(7)
    left_sems, right_sems, vector_sems, raw_sems, label_sem, total_sem = take(6)
    wave, wave_sem = take(2) if end == "stats" else (None, None)
    half = ids_ref[0]
    blocks = vector.shape[2]
    parts = left.shape[1]

    def left_copies(source, piece):
        return [
            pltpu.make_async_copy(piece.at[parts], raw.at[source], raw_sems.at[source]),
            pltpu.make_async_copy(
                piece.at[pl.ds(0, parts)], left.at[source], left_sems.at[source]
            ),
        ]

    def vector_copies(source):
        return [
            pltpu.make_async_copy(
                vectors[source][part],
                vector.at[source, half if part == 0 else 1 - half],
                vector_sems.at[source, part],
            )
            for part in range(2)
        ]

    def load_right(source, side):
        for slot in range(terms * capacity):
            target = jnp.minimum(labels[source, 1, side * terms * capacity + slot], blocks - 1)
            pltpu.make_async_copy(
                rights[side].at[slot // capacity, target],
                right.at[source, side, slot],
                right_sems.at[source, side],
            ).start()

    def wait_right(source, side):
        whole = right.at[source, side]
        pltpu.make_async_copy(whole, whole, right_sems.at[source, side]).wait()

    for source in range(sources):
        if choices:
            for choice, piece in enumerate(lefts):

                @pl.when(ids_ref[chosen + source] == choice)
                def _():
                    for copy in left_copies(source, piece):
                        copy.start()

        else:
            for copy in left_copies(source, lefts[source]):
                copy.start()
    for source in range(sources):
        for copy in vector_copies(source):
            copy.start()
    if first:
        total[...] = jnp.zeros_like(total)
    else:
        load_total = pltpu.make_async_copy(total_in, total, total_sem)
        load_total.start()
    if end == "stats":
        load_wave = pltpu.make_async_copy(wave_in, wave, wave_sem)
        load_wave.start()
    if end == "go on":
        last_out[...] = jnp.zeros_like(last_out)

    for source in range(sources):
        left_copies(source, lefts[0])[0].wait()
    spread_labels[...] = raw[:, :8].astype(jnp.float32).astype(jnp.int32)
    move_labels = pltpu.make_async_copy(spread_labels, labels, label_sem)
    move_labels.start()
    move_labels.wait()
    for source in range(sources):
        for side in range(2):
            load_right(source, side)
    if not first:
        load_total.wait()
    for source in range(sources):
        for side in range(2):
            if side == 0:
                left_copies(source, lefts[0])[1].wait()
                for copy in vector_copies(source):
                    copy.wait()
            wait_right(source, side)
            add_products(
                left.at[source],
                labels.at[source],
                vector.at[source],
                right.at[source, side],
                total,
                side,
                terms,
                capacity,
            )
    if end == "result":
        last_out[...] = total[:blocks].astype(last_out.dtype)
    elif end == "stats":
        load_wave.wait()
        local_stats(total, wave, ids_ref[1], last_out)
        total_out[...] = total[:blocks]
    else:
        store_total = pltpu.make_async_copy(total, total_out, total_sem)
        store_total.start()
        store_total.wait()


def apply_group(ids, lefts, rights, vectors, total, end, wave=None, chosen=0):
    blocks, rows, width = vectors[0][0].shape
    terms = rights[0].shape[0]
    parts = lefts[0].shape[0] - 1
    capacity = parts * PART // (2 * terms * rows)
    sources, first = len(vectors), total is None
    arrays = [*lefts, *rights] + [unit for pair in vectors for unit in pair]
    arrays += [wave] if end == "stats" else []
    arrays += [] if first else [total]
    whole = pl.BlockSpec(memory_space=pltpu.VMEM)
    anywhere = pl.BlockSpec(memory_space=pl.ANY)
    total_shape = (blocks + 1, rows, width)
    scratch = [
        pltpu.VMEM(total_shape, jnp.float32),
        pltpu.VMEM((sources, parts, PART, width), jnp.bfloat16),
        pltpu.VMEM((sources, 2, terms * capacity, width, width), jnp.bfloat16),
        pltpu.VMEM((sources, 2, blocks, rows, width), jnp.bfloat16),
        pltpu.VMEM((sources, PART, width), jnp.bfloat16),
        pltpu.VMEM((sources, 8, width), jnp.int32),
        pltpu.SMEM((sources, 8, width), jnp.int32),
        pltpu.SemaphoreType.DMA((sources,)),
        pltpu.SemaphoreType.DMA((sources, 2)),
        pltpu.SemaphoreType.DMA((sources, 2)),
        pltpu.SemaphoreType.DMA((sources,)),
        pltpu.SemaphoreType.DMA,
        pltpu.SemaphoreType.DMA,
    ]
    if end == "stats":
        scratch += [pltpu.VMEM(wave.shape, wave.dtype), pltpu.SemaphoreType.DMA]
    devices = lax.axis_size("sec") * lax.axis_size("term")
    total_out = jax.ShapeDtypeStruct(total_shape, jnp.float32)
    out_shape, out_specs = {
        "go on": ((total_out, jax.ShapeDtypeStruct((8, width), jnp.float32)), (anywhere, whole)),
        "stats": (
            (
                jax.ShapeDtypeStruct((blocks, rows, width), jnp.float32),
                jax.ShapeDtypeStruct((devices, 128), jnp.float32),
            ),
            (whole, whole),
        ),
        "result": (jax.ShapeDtypeStruct((blocks, rows, width), jnp.bfloat16), whole),
    }[end]
    choices = len(lefts) if chosen else 0
    return pl.pallas_call(
        functools.partial(apply_kernel, sources, choices, chosen, first, end, terms, capacity),
        out_shape=out_shape,
        in_specs=[pl.BlockSpec(memory_space=pltpu.SMEM)] + [anywhere] * len(arrays),
        out_specs=out_specs,
        scratch_shapes=scratch,
        compiler_params=pltpu.CompilerParams(vmem_limit_bytes=VMEM_LIMIT),
        cost_estimate=busy(3.5 + 1.8 * sources),
    )(ids, *arrays)


def direction_kernel(entries, total_ref, wave_ref, stats_ref, out_ref, rayleigh_ref):
    blocks = wave_ref.shape[0]
    stats = stats_ref[...]
    about, cross, own, local = (stats[:, lane : lane + 1] for lane in range(4))
    rayleigh = jnp.sum(cross, keepdims=True) / jnp.sum(own, keepdims=True)
    offset = local - rayleigh
    residual_sq = jnp.sum(about + offset * offset * own, keepdims=True)
    factor = lax.rsqrt(residual_sq / entries + 1e-06)
    rayleigh_ref[...] = rayleigh

    @pl.loop(0, blocks, unroll=4)
    def _(block):
        rest = total_ref[block] - rayleigh * wave_ref[block].astype(jnp.float32)
        out_ref[block] = (rest * factor).astype(jnp.bfloat16)


def new_direction(total, wave, stats, entries):
    whole = pl.BlockSpec(memory_space=pltpu.VMEM)
    return pl.pallas_call(
        functools.partial(direction_kernel, entries),
        out_shape=(
            jax.ShapeDtypeStruct(wave.shape, jnp.bfloat16),
            jax.ShapeDtypeStruct((1, 1), jnp.float32),
        ),
        in_specs=[whole] * 3,
        out_specs=(whole, whole),
        compiler_params=pltpu.CompilerParams(vmem_limit_bytes=8 * 2**20),
        cost_estimate=busy(2.0),
    )(total, wave, stats)


def per_device_ring(wavefunction, left_operator, right_operator, target_owner, target_local):
    owners, halves = lax.axis_size("sec"), lax.axis_size("term")
    me, half = lax.axis_index("sec"), lax.axis_index("term")
    terms, blocks, height, width = left_operator.shape
    rows = height // halves
    capacity = 2 * blocks // owners
    place = ring_place(me, owners)
    ids = jnp.stack([me, half]).astype(jnp.int32)

    own_rows = lax.dynamic_slice_in_dim(wavefunction, half * rows, rows, 1)
    other_rows = lax.dynamic_slice_in_dim(wavefunction, (1 - half) * rows, rows, 1)
    plan = jnp.stack([target_owner[:, :, 0], target_local])
    other_left = swap(
        lax.dynamic_slice_in_dim(left_operator, (1 - half) * rows, rows, 2), owners, halves
    )
    order = [m for m in ORDER if m < owners] + list(range(len(ORDER), owners))
    rights = (right_operator, swap(right_operator, owners, halves))
    pieces = pack(
        ids,
        plan,
        swap(plan, owners, halves),
        left_operator,
        other_left,
        plan,
        order[1:] + order[:1],
        capacity,
    )
    lefts = [pieces[0]]
    for m in range(1, owners):
        piece = pieces[m]
        if m in PIECE_WAITS:
            piece = after(piece, lefts[PIECE_WAITS[m]])
        lefts.append(exchange(piece, owners, halves, m))
    near = mask_gather(own_rows, lefts, owners, halves)
    far = {m: swap(unit, owners, halves) if m else other_rows for m, unit in near.items()}

    reach = (owners - 1) // 2
    turn = 1 - 2 * half
    distances = [0] + [s for step in range(1, reach + 1) for s in (step, -step)] + [owners // 2]
    whose = [me ^ ring_owner(place - s * turn, owners) for s in distances]
    numbers = jnp.stack([half, me * halves + half, *whose]).astype(jnp.int32)
    total = None
    groups = [order[at : at + 2] for at in range(0, owners, 2)]
    for group in groups:
        total, stats = apply_group(
            numbers,
            [lefts[m] for m in group],
            rights,
            [(near[m], far[m]) for m in group],
            total,
            "go on" if group is not groups[-1] else "stats",
            own_rows,
        )

    entries = blocks * owners * height * width
    stats = spread(stats, owners * halves)
    direction, rayleigh = new_direction(total, own_rows, stats, entries)
    def add_group(total, units, end):
        vectors = [(unit, swap(units[-s], owners, halves)) for s, unit in units.items()]
        chosen = 2 + distances.index(next(iter(units)))
        return apply_group(numbers, lefts, rights, vectors, total, end, chosen=chosen)

    total, waiting = None, {0: direction}
    ahead = behind = direction
    for step in range(1, reach + 1):
        ahead = ring_send(ahead, owners, halves, (1, -1))
        behind = ring_send(behind, owners, halves, (-1, 1))
        if step > 1:
            total, token = add_group(total, waiting, "go on")
            ahead, waiting = after(ahead, token), {}
        waiting.update({step: ahead, -step: behind})
    last = ring_send(ahead, owners, halves, (1, -1))
    total, token = add_group(total, waiting, "go on")
    last = after(last, token)
    vectors = [(last, swap(last, owners, halves))]
    chosen = 2 + distances.index(owners // 2)
    total = apply_group(numbers, lefts, rights, vectors, total, "result", chosen=chosen)
    return (total, rayleigh[0])


def slot_codes(target_owner, target_local, owners, capacity):
    terms, blocks = target_local.shape
    owner = target_owner[:, :, 0]
    place = jnp.arange(blocks, dtype=jnp.int32)
    same = (owner[:, :, None] == owner[:, None, :]) & (place[None, :] < place[:, None])[None]
    position = jnp.sum(same.astype(jnp.int32), axis=2)
    hit = (
        owner[:, None, None, :] == jnp.arange(owners, dtype=jnp.int32)[None, :, None, None]
    ) & (position[:, None, None, :] == jnp.arange(capacity, dtype=jnp.int32)[None, None, :, None])
    code = place[None, :] * (2 * blocks) + target_local - blocks
    return blocks + jnp.sum(jnp.where(hit, code[:, None, None, :], 0), axis=3)


def stream_kernel(first, capacity, blocks, code_ref, left_ref, vector_ref, right_ref, *rest):
    total_in, total = (None, rest[0]) if first else rest
    step = pl.program_id(0)
    rows, width = left_ref.shape[2:]

    @pl.when(step == 0)
    def _():
        total[...] = jnp.zeros_like(total) if first else total_in[...]

    for term in range(2):
        moved, where = [], []
        for slot in range(capacity):
            code = code_ref[2 * step + term, slot]
            source, target = lax.div(code, 2 * blocks), lax.rem(code, 2 * blocks)
            block = vector_ref[0, :, source].reshape(2 * rows, width)
            product = jnp.dot(left_ref[term, slot], block, preferred_element_type=jnp.float32)
            moved.append(product.astype(jnp.bfloat16))
            where.append(target)
        for slot in range(capacity):
            target = where[slot]
            total[target] += jnp.dot(
                moved[slot],
                right_ref[term, jnp.minimum(target, blocks - 1)],
                preferred_element_type=jnp.float32,
            )


def stream_chunk(total, codes, left, vector, right):
    owners, _, blocks, rows, width = vector.shape
    capacity = left.shape[1]
    first = total is None
    spec_total = pl.BlockSpec((blocks + 1, rows, width), lambda s, c: (0, 0, 0))
    return pl.pallas_call(
        functools.partial(stream_kernel, first, capacity, blocks),
        out_shape=jax.ShapeDtypeStruct((blocks + 1, rows, width), jnp.float32),
        grid_spec=pltpu.PrefetchScalarGridSpec(
            num_scalar_prefetch=1,
            grid=(owners,),
            in_specs=[
                pl.BlockSpec((2, capacity, rows, width), lambda s, c: (s, 0, 0, 0)),
                pl.BlockSpec((1, 2, blocks, rows, width), lambda s, c: (s, 0, 0, 0, 0)),
                pl.BlockSpec((2, blocks, width, width), lambda s, c: (0, 0, 0, 0)),
            ]
            + ([] if first else [spec_total]),
            out_specs=spec_total,
        ),
        compiler_params=pltpu.CompilerParams(vmem_limit_bytes=32 * 2**20),
        cost_estimate=pl.CostEstimate(
            flops=owners * 2 * capacity * 2 * 2 * rows * width * width,
            bytes_accessed=left.size * 2 + vector.size * 2 + right.size * 2,
            transcendentals=0,
        ),
    )(codes, left, vector, right, *([] if first else [total]))


def per_device_streamed(wavefunction, left_operator, right_operator, target_owner, target_local):
    owners = lax.axis_size("sec")
    halves = lax.axis_size("term")
    me, half = lax.axis_index("sec"), lax.axis_index("term")
    terms, blocks, height, width = left_operator.shape
    rows = height // halves
    capacity = 2 * blocks // owners

    own_rows = lax.dynamic_slice_in_dim(wavefunction, half * rows, rows, 1)
    codes = slot_codes(target_owner, target_local, owners, capacity)
    sources = codes // (2 * blocks)

    moved_left = []
    for k in range(terms):
        pick = sources[k][:, None, :] * halves + jnp.arange(halves, dtype=jnp.int32)[None, :, None]
        pieces = left_operator[k].reshape(blocks * halves, rows, width)[pick.reshape(-1)]
        pieces = pieces.reshape(owners * halves, capacity, rows, width)
        moved_left.append(lax.all_to_all(pieces, BOTH, split_axis=0, concat_axis=0, tiled=True))
    all_codes = lax.all_gather(codes, BOTH, axis=0)
    my_codes = lax.dynamic_index_in_dim(all_codes, me, axis=3 - 1, keepdims=False)
    gathered = lax.all_gather(own_rows, BOTH, axis=0).reshape(owners, halves, blocks, rows, width)
    right = lax.all_gather(right_operator, "term", axis=1)

    def apply(vector):
        total = None
        for k in range(terms):
            total = stream_chunk(total, my_codes[:, k], moved_left[k], vector, right[k])
        return total[:blocks]

    sigma_rows = apply(gathered)
    wave = own_rows.astype(jnp.float32)
    cross, own = jnp.sum(wave * sigma_rows), jnp.sum(wave * wave)
    local = jnp.where(own > 0, cross / own, 0.0)
    about = jnp.sum(jnp.square(sigma_rows - local * wave))
    stats = lax.all_gather(jnp.stack([about, cross, own, local]), BOTH, axis=0)
    rayleigh = jnp.sum(stats[:, 1]) / jnp.sum(stats[:, 2])
    residual_sq = jnp.sum(stats[:, 0] + jnp.square(stats[:, 3] - rayleigh) * stats[:, 2])
    entries = blocks * owners * height * width
    factor = lax.rsqrt(residual_sq / entries + 1e-06)
    direction = ((sigma_rows - rayleigh * wave) * factor).astype(jnp.bfloat16)
    direction = lax.all_gather(direction, BOTH, axis=0).reshape(gathered.shape)
    sigma_two = apply(direction).astype(jnp.bfloat16)
    return (sigma_two, jnp.reshape(rayleigh, (1,)))


def per_device(wavefunction, *operands):
    owners = lax.axis_size("sec")
    gathered_bytes = owners * wavefunction.size * wavefunction.dtype.itemsize
    if owners < 8 or owners & (owners - 1) or 2 * gathered_bytes > RING_BYTES:
        return per_device_streamed(wavefunction, *operands)
    return per_device_ring(wavefunction, *operands)


def solution(mesh):
    placed = (
        P(("rep", "sec"), None, None),
        P("term", ("rep", "sec"), None, None),
        P("term", ("rep", "sec"), None, None),
        P("term", ("rep", "sec"), None),
        P("term", ("rep", "sec")),
    )
    return jax.shard_map(
        per_device,
        mesh=mesh,
        in_specs=placed,
        out_specs=(P(("rep", "sec"), "term", None), P("rep")),
        check_vma=False,
    )
```

```python
import functools

import jax
import jax.numpy as jnp
from jax import lax
from jax.experimental import pallas as pl
from jax.experimental.pallas import tpu as pltpu
from jax.sharding import PartitionSpec as P

BOTH = ("sec", "term")
VMEM_LIMIT = 64 * 2**20
PART = 16
ORDER = [0, 1, 4, 2, 5, 6, 3, 7]
WAITS = {4: 1, 2: 4, 6: 2}
PIECE_WAITS = {6: 4, 7: 5}
RING_BYTES = 24 * 2**20


def ring_order(owners):
    if owners % 2:
        return list(range(owners))
    return list(range(0, owners, 2)) + list(range(owners - 1, 0, -2))


def ring_place(owner, owners):
    if owners % 2:
        return owner
    return jnp.where(owner % 2 == 0, owner // 2, owners - 1 - owner // 2)


def ring_owner(place, owners):
    place = place % owners
    if owners % 2:
        return place
    return jnp.where(place < owners // 2, 2 * place, 2 * (owners - 1 - place) + 1)


def permute(value, owners, halves, target, flip=0):
    pairs = [
        (chip * halves + half, target(chip, half) * halves + (half ^ flip))
        for chip in range(owners)
        for half in range(halves)
    ]
    return lax.ppermute(value, BOTH, pairs)


def swap(value, owners, halves):
    return permute(value, owners, halves, lambda chip, half: chip, 1)


def exchange(value, owners, halves, mask):
    return permute(value, owners, halves, lambda chip, half: chip ^ mask)


def ring_send(value, owners, halves, shifts):
    ring = ring_order(owners)
    place = {chip: index for index, chip in enumerate(ring)}
    return permute(
        value, owners, halves, lambda chip, half: ring[(place[chip] + shifts[half]) % owners]
    )


def after_kernel(*refs):
    del refs


def after(value, *others):
    anywhere = pl.BlockSpec(memory_space=pl.ANY)
    return pl.pallas_call(
        after_kernel,
        out_shape=jax.ShapeDtypeStruct(value.shape, value.dtype),
        in_specs=[anywhere] * (1 + len(others)),
        out_specs=anywhere,
        input_output_aliases={0: 0},
        cost_estimate=busy(0.3),
    )(value, *others)


def mask_gather(unit, lefts, owners, halves):
    units = {0: unit}
    step = owners // 2
    masks = []
    while step:
        masks.append(step)
        units[step] = exchange(unit, owners, halves, step)
        step //= 2
    waits = dict(WAITS)
    for step in masks[1:]:
        for mask in [m for m in units if m >= 2 * step and m % (2 * step) == 0]:
            if mask in waits:
                units[mask] = after(units[mask], lefts[waits.pop(mask)])
            units[mask | step] = exchange(units[mask], owners, halves, step)
    return units


def spread(value, devices):
    step = 1
    while step < devices:
        masks = [step] if 2 * step == devices else [step, 2 * step, 3 * step]
        parts = [lax.ppermute(value, BOTH, [(d, d ^ m) for d in range(devices)]) for m in masks]
        for part in parts:
            value = value + part
        step *= 4
    return value


def pack_kernel(order, capacity, blocks, terms, ids_ref, plan_ref, other_plan_ref, *refs):
    left_ref, other_ref, _, *pieces, codes, seen, built, sems = refs
    owners = len(order)
    me, half = ids_ref[0], ids_ref[1]
    rows, width = other_ref.shape[2:]
    start = pl.multiple_of(half * rows, rows)
    parts = rows // PART

    @pl.loop(0, owners)
    def _(owner):
        for index in range(2 * terms * capacity):
            codes[0, owner, index] = 0
            codes[1, owner, index] = blocks

    for stream in range(2 * terms):
        plan = plan_ref if stream < terms else other_plan_ref

        @pl.loop(0, owners)
        def _(owner):
            seen[owner] = 0

        @pl.loop(0, blocks, unroll=4)
        def _(block):
            owner = plan[0, stream % terms, block]
            slot = seen[owner]
            seen[owner] = slot + 1
            codes[0, owner, stream * capacity + slot] = block
            codes[1, owner, stream * capacity + slot] = plan[1, stream % terms, block]

    lane = lax.broadcasted_iota(jnp.int32, (PART, width), 1)
    row = lax.broadcasted_iota(jnp.int32, (PART, width), 0)
    copies = []
    for mask in order:
        owner = me ^ mask
        labels = jnp.zeros((PART, width), jnp.int32)
        for stream in range(2 * terms):
            for slot in range(capacity):
                at = stream * capacity + slot
                block = codes[0, owner, at]
                if stream < terms:
                    value = left_ref[stream, block, pl.ds(start, rows), :]
                else:
                    value = other_ref[stream - terms, block]
                built[mask, at * parts : (at + 1) * parts] = value.reshape(parts, PART, width)
                label = jnp.where(row == 0, block, codes[1, owner, at])
                labels = jnp.where(lane == at, label, labels)
        built[mask, 2 * terms * capacity * parts] = labels.astype(jnp.float32).astype(jnp.bfloat16)
        copies.append(pltpu.make_async_copy(built.at[mask], pieces[mask], sems.at[mask]))
        copies[-1].start()
    for copy in copies:
        copy.wait()


def pack(ids, plan, other_plan, left, other, before, order, capacity):
    terms, blocks, rows, width = other.shape
    owners = len(order)
    scalars = pl.BlockSpec(memory_space=pltpu.SMEM)
    whole = pl.BlockSpec(memory_space=pltpu.VMEM)
    anywhere = pl.BlockSpec(memory_space=pl.ANY)
    shape = (2 * terms * capacity * rows // PART + 1, PART, width)
    return pl.pallas_call(
        functools.partial(pack_kernel, order, capacity, blocks, terms),
        out_shape=[jax.ShapeDtypeStruct(shape, jnp.bfloat16)] * owners,
        in_specs=[scalars] * 3 + [whole, whole, anywhere],
        out_specs=[anywhere] * owners,
        scratch_shapes=[
            pltpu.SMEM((2, owners, 2 * terms * capacity), jnp.int32),
            pltpu.SMEM((owners,), jnp.int32),
            pltpu.VMEM((owners,) + shape, jnp.bfloat16),
            pltpu.SemaphoreType.DMA((owners,)),
        ],
        compiler_params=pltpu.CompilerParams(vmem_limit_bytes=VMEM_LIMIT),
        cost_estimate=busy(5.0),
    )(ids, plan, other_plan, left, other, before)


def busy(microseconds):
    return pl.CostEstimate(
        flops=int(1.15e9 * microseconds), bytes_accessed=0, transcendentals=0
    )


def add_products(left, labels, vector, right, total, side, terms, capacity):
    blocks, rows, width = vector.shape[1:]
    parts = rows // PART
    moved, where = [], []
    for slot in range(terms * capacity):
        at = side * terms * capacity + slot
        block = vector[:, labels(0, at)].reshape(2 * rows, width)
        piece = left[at * parts : (at + 1) * parts].reshape(rows, width)
        product = jnp.dot(piece, block, preferred_element_type=jnp.float32)
        moved.append(product.astype(jnp.bfloat16))
        where.append(labels(1, at))
    for slot in range(terms * capacity):
        total[where[slot]] += jnp.dot(
            moved[slot], right[slot], preferred_element_type=jnp.float32
        )


def local_stats(total, wave_ref, device, stats_ref):
    blocks = wave_ref.shape[0]
    zero = jnp.zeros(wave_ref.shape[1:], jnp.float32)

    def sums(block, carry):
        cross, own = carry
        wave = wave_ref[block].astype(jnp.float32)
        return cross + wave * total[block], own + wave * wave

    cross, own = lax.fori_loop(0, blocks, sums, (zero, zero), unroll=4)
    cross, own = jnp.sum(cross, keepdims=True), jnp.sum(own, keepdims=True)
    local = jnp.where(own > 0, cross / own, 0.0)

    def squares(block, carry):
        rest = total[block] - local * wave_ref[block].astype(jnp.float32)
        return carry + rest * rest

    about = jnp.sum(lax.fori_loop(0, blocks, squares, zero, unroll=4), keepdims=True)
    lane = lax.broadcasted_iota(jnp.int32, stats_ref.shape, 1)
    row = lax.broadcasted_iota(jnp.int32, stats_ref.shape, 0)
    values = jnp.where(lane == 0, about, jnp.where(lane == 1, cross, jnp.where(lane == 2, own, local)))
    stats_ref[...] = jnp.where((row == device) & (lane < 4), values, 0.0)


def apply_kernel(sources, choices, chosen, first, end, terms, capacity, ids_ref, *refs):
    refs = list(refs)

    def take(count):
        taken, refs[:count] = refs[:count], []
        return taken

    (known,) = take(1) if choices else (None,)
    lefts = take(choices or sources)
    rights = take(2)
    vectors = [take(2) for _ in range(sources)]
    (wave_in,) = take(1) if end == "stats" else (None,)
    (total_in,) = (None,) if first else take(1)
    (total_out,) = (None,) if end == "result" else take(1)
    (last_out,) = take(1)
    total, left, right, vector, raw, spread_labels, labels = take(7)
    left_sems, right_sems, vector_sems, raw_sems, label_sem, total_sem = take(6)
    wave, wave_sem = take(2) if end == "stats" else (None, None)
    half = ids_ref[0]
    blocks = vector.shape[2]
    parts = left.shape[1]

    def labels_of(source):
        if choices:
            return lambda row, at: known[ids_ref[chosen + source], row, at]
        return lambda row, at: labels[source, row, at]

    def left_copies(source, piece):
        return [
            pltpu.make_async_copy(piece.at[parts], raw.at[source], raw_sems.at[source]),
            pltpu.make_async_copy(
                piece.at[pl.ds(0, parts)], left.at[source], left_sems.at[source]
            ),
        ]

    def vector_copies(source):
        return [
            pltpu.make_async_copy(
                vectors[source][part],
                vector.at[source, half if part == 0 else 1 - half],
                vector_sems.at[source, part],
            )
            for part in range(2)
        ]

    def load_right(source, side):
        for slot in range(terms * capacity):
            target = jnp.minimum(labels_of(source)(1, side * terms * capacity + slot), blocks - 1)
            pltpu.make_async_copy(
                rights[side].at[slot // capacity, target],
                right.at[source, side, slot],
                right_sems.at[source, side],
            ).start()

    def wait_right(source, side):
        whole = right.at[source, side]
        pltpu.make_async_copy(whole, whole, right_sems.at[source, side]).wait()

    for source in range(sources):
        if choices:
            for choice, piece in enumerate(lefts):

                @pl.when(ids_ref[chosen + source] == choice)
                def _():
                    left_copies(source, piece)[1].start()

        else:
            for copy in left_copies(source, lefts[source]):
                copy.start()
    for source in range(sources):
        for copy in vector_copies(source):
            copy.start()
    if first:
        total[...] = jnp.zeros_like(total)
    else:
        load_total = pltpu.make_async_copy(total_in, total, total_sem)
        load_total.start()
    if end == "stats":
        load_wave = pltpu.make_async_copy(wave_in, wave, wave_sem)
        load_wave.start()
    if end == "go on":
        last_out[...] = jnp.zeros_like(last_out)

    if not choices:
        for source in range(sources):
            left_copies(source, lefts[0])[0].wait()
        spread_labels[...] = raw[:, :8].astype(jnp.float32).astype(jnp.int32)
        move_labels = pltpu.make_async_copy(spread_labels, labels, label_sem)
        move_labels.start()
        move_labels.wait()
    for source in range(sources):
        for side in range(2):
            load_right(source, side)
    if not first:
        load_total.wait()
    for source in range(sources):
        for side in range(2):
            if side == 0:
                left_copies(source, lefts[0])[1].wait()
                for copy in vector_copies(source):
                    copy.wait()
            wait_right(source, side)
            add_products(
                left.at[source],
                labels_of(source),
                vector.at[source],
                right.at[source, side],
                total,
                side,
                terms,
                capacity,
            )
    if end == "result":
        last_out[...] = total[:blocks].astype(last_out.dtype)
    elif end == "stats":
        load_wave.wait()
        local_stats(total, wave, ids_ref[1], last_out)
        total_out[...] = total[:blocks]
    else:
        store_total = pltpu.make_async_copy(total, total_out, total_sem)
        store_total.start()
        store_total.wait()


def apply_group(ids, lefts, rights, vectors, total, end, wave=None, chosen=0, known=None):
    blocks, rows, width = vectors[0][0].shape
    terms = rights[0].shape[0]
    parts = lefts[0].shape[0] - 1
    capacity = parts * PART // (2 * terms * rows)
    sources, first = len(vectors), total is None
    arrays = [*lefts, *rights] + [unit for pair in vectors for unit in pair]
    arrays += [wave] if end == "stats" else []
    arrays += [] if first else [total]
    whole = pl.BlockSpec(memory_space=pltpu.VMEM)
    anywhere = pl.BlockSpec(memory_space=pl.ANY)
    total_shape = (blocks + 1, rows, width)
    scratch = [
        pltpu.VMEM(total_shape, jnp.float32),
        pltpu.VMEM((sources, parts, PART, width), jnp.bfloat16),
        pltpu.VMEM((sources, 2, terms * capacity, width, width), jnp.bfloat16),
        pltpu.VMEM((sources, 2, blocks, rows, width), jnp.bfloat16),
        pltpu.VMEM((sources, PART, width), jnp.bfloat16),
        pltpu.VMEM((sources, 8, width), jnp.int32),
        pltpu.SMEM((sources, 8, width), jnp.int32),
        pltpu.SemaphoreType.DMA((sources,)),
        pltpu.SemaphoreType.DMA((sources, 2)),
        pltpu.SemaphoreType.DMA((sources, 2)),
        pltpu.SemaphoreType.DMA((sources,)),
        pltpu.SemaphoreType.DMA,
        pltpu.SemaphoreType.DMA,
    ]
    if end == "stats":
        scratch += [pltpu.VMEM(wave.shape, wave.dtype), pltpu.SemaphoreType.DMA]
    devices = lax.axis_size("sec") * lax.axis_size("term")
    total_out = jax.ShapeDtypeStruct(total_shape, jnp.float32)
    out_shape, out_specs = {
        "go on": ((total_out, jax.ShapeDtypeStruct((8, width), jnp.float32)), (anywhere, whole)),
        "stats": (
            (
                jax.ShapeDtypeStruct((blocks, rows, width), jnp.float32),
                jax.ShapeDtypeStruct((devices, 128), jnp.float32),
            ),
            (whole, whole),
        ),
        "result": (jax.ShapeDtypeStruct((blocks, rows, width), jnp.bfloat16), whole),
    }[end]
    choices = len(lefts) if chosen else 0
    scalars = [ids, known] if chosen else [ids]
    return pl.pallas_call(
        functools.partial(apply_kernel, sources, choices, chosen, first, end, terms, capacity),
        out_shape=out_shape,
        in_specs=[pl.BlockSpec(memory_space=pltpu.SMEM)] * len(scalars)
        + [anywhere] * len(arrays),
        out_specs=out_specs,
        scratch_shapes=scratch,
        compiler_params=pltpu.CompilerParams(vmem_limit_bytes=VMEM_LIMIT),
        cost_estimate=busy(3.5 + 1.8 * sources),
    )(*scalars, *arrays)


def direction_kernel(entries, total_ref, wave_ref, stats_ref, out_ref, rayleigh_ref):
    blocks = wave_ref.shape[0]
    stats = stats_ref[...]
    about, cross, own, local = (stats[:, lane : lane + 1] for lane in range(4))
    rayleigh = jnp.sum(cross, keepdims=True) / jnp.sum(own, keepdims=True)
    offset = local - rayleigh
    residual_sq = jnp.sum(about + offset * offset * own, keepdims=True)
    factor = lax.rsqrt(residual_sq / entries + 1e-06)
    rayleigh_ref[...] = rayleigh

    @pl.loop(0, blocks, unroll=4)
    def _(block):
        rest = total_ref[block] - rayleigh * wave_ref[block].astype(jnp.float32)
        out_ref[block] = (rest * factor).astype(jnp.bfloat16)


def new_direction(total, wave, stats, entries):
    whole = pl.BlockSpec(memory_space=pltpu.VMEM)
    return pl.pallas_call(
        functools.partial(direction_kernel, entries),
        out_shape=(
            jax.ShapeDtypeStruct(wave.shape, jnp.bfloat16),
            jax.ShapeDtypeStruct((1, 1), jnp.float32),
        ),
        in_specs=[whole] * 3,
        out_specs=(whole, whole),
        compiler_params=pltpu.CompilerParams(vmem_limit_bytes=8 * 2**20),
        cost_estimate=busy(2.0),
    )(total, wave, stats)


def per_device_ring(wavefunction, left_operator, right_operator, target_owner, target_local):
    owners, halves = lax.axis_size("sec"), lax.axis_size("term")
    me, half = lax.axis_index("sec"), lax.axis_index("term")
    terms, blocks, height, width = left_operator.shape
    rows = height // halves
    capacity = 2 * blocks // owners
    place = ring_place(me, owners)
    ids = jnp.stack([me, half]).astype(jnp.int32)

    own_rows = lax.dynamic_slice_in_dim(wavefunction, half * rows, rows, 1)
    other_rows = lax.dynamic_slice_in_dim(wavefunction, (1 - half) * rows, rows, 1)
    plan = jnp.stack([target_owner[:, :, 0], target_local])
    other_left = swap(
        lax.dynamic_slice_in_dim(left_operator, (1 - half) * rows, rows, 2), owners, halves
    )
    order = [m for m in ORDER if m < owners] + list(range(len(ORDER), owners))
    rights = (right_operator, swap(right_operator, owners, halves))
    pieces = pack(
        ids,
        plan,
        swap(plan, owners, halves),
        left_operator,
        other_left,
        plan,
        order[1:] + order[:1],
        capacity,
    )
    lefts = [pieces[0]]
    for m in range(1, owners):
        piece = pieces[m]
        if m in PIECE_WAITS:
            piece = after(piece, lefts[PIECE_WAITS[m]])
        lefts.append(exchange(piece, owners, halves, m))
    near = mask_gather(own_rows, lefts, owners, halves)
    far = {m: swap(unit, owners, halves) if m else other_rows for m, unit in near.items()}

    reach = (owners - 1) // 2
    turn = 1 - 2 * half
    distances = [0] + [s for step in range(1, reach + 1) for s in (step, -step)] + [owners // 2]
    whose = [me ^ ring_owner(place - s * turn, owners) for s in distances]
    numbers = jnp.stack([half, me * halves + half, *whose]).astype(jnp.int32)
    total = None
    groups = [order[at : at + 2] for at in range(0, owners, 2)]
    for group in groups:
        total, stats = apply_group(
            numbers,
            [lefts[m] for m in group],
            rights,
            [(near[m], far[m]) for m in group],
            total,
            "go on" if group is not groups[-1] else "stats",
            own_rows,
        )

    entries = blocks * owners * height * width
    stats = spread(stats, owners * halves)
    direction, rayleigh = new_direction(total, own_rows, stats, entries)
    known = jnp.stack([left[-1, :2] for left in lefts]).astype(jnp.int32)

    def add_group(total, units, end):
        vectors = [(unit, swap(units[-s], owners, halves)) for s, unit in units.items()]
        chosen = 2 + distances.index(next(iter(units)))
        return apply_group(numbers, lefts, rights, vectors, total, end, chosen=chosen, known=known)

    total, waiting = None, {0: direction}
    ahead = behind = direction
    for step in range(1, reach + 1):
        ahead = ring_send(ahead, owners, halves, (1, -1))
        behind = ring_send(behind, owners, halves, (-1, 1))
        if step > 1:
            total, token = add_group(total, waiting, "go on")
            ahead, waiting = after(ahead, token), {}
        waiting.update({step: ahead, -step: behind})
    last = ring_send(ahead, owners, halves, (1, -1))
    total, token = add_group(total, waiting, "go on")
    last = after(last, token)
    vectors = [(last, swap(last, owners, halves))]
    chosen = 2 + distances.index(owners // 2)
    total = apply_group(
        numbers, lefts, rights, vectors, total, "result", chosen=chosen, known=known
    )
    return (total, rayleigh[0])


def slot_codes(target_owner, target_local, owners, capacity):
    terms, blocks = target_local.shape
    owner = target_owner[:, :, 0]
    place = jnp.arange(blocks, dtype=jnp.int32)
    same = (owner[:, :, None] == owner[:, None, :]) & (place[None, :] < place[:, None])[None]
    position = jnp.sum(same.astype(jnp.int32), axis=2)
    hit = (
        owner[:, None, None, :] == jnp.arange(owners, dtype=jnp.int32)[None, :, None, None]
    ) & (position[:, None, None, :] == jnp.arange(capacity, dtype=jnp.int32)[None, None, :, None])
    code = place[None, :] * (2 * blocks) + target_local - blocks
    return blocks + jnp.sum(jnp.where(hit, code[:, None, None, :], 0), axis=3)


def stream_kernel(first, capacity, blocks, code_ref, left_ref, vector_ref, right_ref, *rest):
    total_in, total = (None, rest[0]) if first else rest
    step = pl.program_id(0)
    rows, width = left_ref.shape[2:]

    @pl.when(step == 0)
    def _():
        total[...] = jnp.zeros_like(total) if first else total_in[...]

    for term in range(2):
        moved, where = [], []
        for slot in range(capacity):
            code = code_ref[2 * step + term, slot]
            source, target = lax.div(code, 2 * blocks), lax.rem(code, 2 * blocks)
            block = vector_ref[0, :, source].reshape(2 * rows, width)
            product = jnp.dot(left_ref[term, slot], block, preferred_element_type=jnp.float32)
            moved.append(product.astype(jnp.bfloat16))
            where.append(target)
        for slot in range(capacity):
            target = where[slot]
            total[target] += jnp.dot(
                moved[slot],
                right_ref[term, jnp.minimum(target, blocks - 1)],
                preferred_element_type=jnp.float32,
            )


def stream_chunk(total, codes, left, vector, right):
    owners, _, blocks, rows, width = vector.shape
    capacity = left.shape[1]
    first = total is None
    spec_total = pl.BlockSpec((blocks + 1, rows, width), lambda s, c: (0, 0, 0))
    return pl.pallas_call(
        functools.partial(stream_kernel, first, capacity, blocks),
        out_shape=jax.ShapeDtypeStruct((blocks + 1, rows, width), jnp.float32),
        grid_spec=pltpu.PrefetchScalarGridSpec(
            num_scalar_prefetch=1,
            grid=(owners,),
            in_specs=[
                pl.BlockSpec((2, capacity, rows, width), lambda s, c: (s, 0, 0, 0)),
                pl.BlockSpec((1, 2, blocks, rows, width), lambda s, c: (s, 0, 0, 0, 0)),
                pl.BlockSpec((2, blocks, width, width), lambda s, c: (0, 0, 0, 0)),
            ]
            + ([] if first else [spec_total]),
            out_specs=spec_total,
        ),
        compiler_params=pltpu.CompilerParams(vmem_limit_bytes=32 * 2**20),
        cost_estimate=pl.CostEstimate(
            flops=owners * 2 * capacity * 2 * 2 * rows * width * width,
            bytes_accessed=left.size * 2 + vector.size * 2 + right.size * 2,
            transcendentals=0,
        ),
    )(codes, left, vector, right, *([] if first else [total]))


def per_device_streamed(wavefunction, left_operator, right_operator, target_owner, target_local):
    owners = lax.axis_size("sec")
    halves = lax.axis_size("term")
    me, half = lax.axis_index("sec"), lax.axis_index("term")
    terms, blocks, height, width = left_operator.shape
    rows = height // halves
    capacity = 2 * blocks // owners

    own_rows = lax.dynamic_slice_in_dim(wavefunction, half * rows, rows, 1)
    codes = slot_codes(target_owner, target_local, owners, capacity)
    sources = codes // (2 * blocks)

    moved_left = []
    for k in range(terms):
        pick = sources[k][:, None, :] * halves + jnp.arange(halves, dtype=jnp.int32)[None, :, None]
        pieces = left_operator[k].reshape(blocks * halves, rows, width)[pick.reshape(-1)]
        pieces = pieces.reshape(owners * halves, capacity, rows, width)
        moved_left.append(lax.all_to_all(pieces, BOTH, split_axis=0, concat_axis=0, tiled=True))
    all_codes = lax.all_gather(codes, BOTH, axis=0)
    my_codes = lax.dynamic_index_in_dim(all_codes, me, axis=3 - 1, keepdims=False)
    gathered = lax.all_gather(own_rows, BOTH, axis=0).reshape(owners, halves, blocks, rows, width)
    right = lax.all_gather(right_operator, "term", axis=1)

    def apply(vector):
        total = None
        for k in range(terms):
            total = stream_chunk(total, my_codes[:, k], moved_left[k], vector, right[k])
        return total[:blocks]

    sigma_rows = apply(gathered)
    wave = own_rows.astype(jnp.float32)
    cross, own = jnp.sum(wave * sigma_rows), jnp.sum(wave * wave)
    local = jnp.where(own > 0, cross / own, 0.0)
    about = jnp.sum(jnp.square(sigma_rows - local * wave))
    stats = lax.all_gather(jnp.stack([about, cross, own, local]), BOTH, axis=0)
    rayleigh = jnp.sum(stats[:, 1]) / jnp.sum(stats[:, 2])
    residual_sq = jnp.sum(stats[:, 0] + jnp.square(stats[:, 3] - rayleigh) * stats[:, 2])
    entries = blocks * owners * height * width
    factor = lax.rsqrt(residual_sq / entries + 1e-06)
    direction = ((sigma_rows - rayleigh * wave) * factor).astype(jnp.bfloat16)
    direction = lax.all_gather(direction, BOTH, axis=0).reshape(gathered.shape)
    sigma_two = apply(direction).astype(jnp.bfloat16)
    return (sigma_two, jnp.reshape(rayleigh, (1,)))


def per_device(wavefunction, *operands):
    owners = lax.axis_size("sec")
    gathered_bytes = owners * wavefunction.size * wavefunction.dtype.itemsize
    if owners < 8 or owners & (owners - 1) or 2 * gathered_bytes > RING_BYTES:
        return per_device_streamed(wavefunction, *operands)
    return per_device_ring(wavefunction, *operands)


def solution(mesh):
    placed = (
        P(("rep", "sec"), None, None),
        P("term", ("rep", "sec"), None, None),
        P("term", ("rep", "sec"), None, None),
        P("term", ("rep", "sec"), None),
        P("term", ("rep", "sec")),
    )
    return jax.shard_map(
        per_device,
        mesh=mesh,
        in_specs=placed,
        out_specs=(P(("rep", "sec"), "term", None), P("rep")),
        check_vma=False,
    )
```

```python
import functools

import jax
import jax.numpy as jnp
from jax import lax
from jax.experimental import pallas as pl
from jax.experimental.pallas import tpu as pltpu
from jax.sharding import PartitionSpec as P

BOTH = ("sec", "term")
VMEM_LIMIT = 64 * 2**20
PART = 16
ORDER = [0, 4, 5, 1, 2, 6, 3, 7]
WAITS = {4: 1, 2: 5, 6: 2}
PIECE_WAITS = {6: 4, 7: 5}
RING_BYTES = 24 * 2**20


def ring_order(owners):
    if owners % 2:
        return list(range(owners))
    return list(range(0, owners, 2)) + list(range(owners - 1, 0, -2))


def ring_place(owner, owners):
    if owners % 2:
        return owner
    return jnp.where(owner % 2 == 0, owner // 2, owners - 1 - owner // 2)


def ring_owner(place, owners):
    place = place % owners
    if owners % 2:
        return place
    return jnp.where(place < owners // 2, 2 * place, 2 * (owners - 1 - place) + 1)


def permute(value, owners, halves, target, flip=0):
    pairs = [
        (chip * halves + half, target(chip, half) * halves + (half ^ flip))
        for chip in range(owners)
        for half in range(halves)
    ]
    return lax.ppermute(value, BOTH, pairs)


def swap(value, owners, halves):
    return permute(value, owners, halves, lambda chip, half: chip, 1)


def exchange(value, owners, halves, mask):
    return permute(value, owners, halves, lambda chip, half: chip ^ mask)


def ring_send(value, owners, halves, shifts):
    ring = ring_order(owners)
    place = {chip: index for index, chip in enumerate(ring)}
    return permute(
        value, owners, halves, lambda chip, half: ring[(place[chip] + shifts[half]) % owners]
    )


def after_kernel(*refs):
    del refs


def after(value, *others):
    anywhere = pl.BlockSpec(memory_space=pl.ANY)
    return pl.pallas_call(
        after_kernel,
        out_shape=jax.ShapeDtypeStruct(value.shape, value.dtype),
        in_specs=[anywhere] * (1 + len(others)),
        out_specs=anywhere,
        input_output_aliases={0: 0},
        cost_estimate=busy(0.3),
    )(value, *others)


def mask_gather(unit, lefts, owners, halves):
    units = {0: unit}
    step = owners // 2
    masks = []
    while step:
        masks.append(step)
        units[step] = exchange(unit, owners, halves, step)
        step //= 2
    waits = dict(WAITS)
    for step in masks[1:]:
        for mask in [m for m in units if m >= 2 * step and m % (2 * step) == 0]:
            if mask in waits:
                units[mask] = after(units[mask], lefts[waits.pop(mask)])
            units[mask | step] = exchange(units[mask], owners, halves, step)
    return units


def spread(value, devices):
    step = 1
    while step < devices:
        masks = [step] if 2 * step == devices else [step, 2 * step, 3 * step]
        parts = [lax.ppermute(value, BOTH, [(d, d ^ m) for d in range(devices)]) for m in masks]
        for part in parts:
            value = value + part
        step *= 4
    return value


def pack_kernel(order, capacity, blocks, terms, ids_ref, plan_ref, other_plan_ref, *refs):
    left_ref, other_ref, _, *pieces, codes, seen, built, sems = refs
    owners = len(order)
    me, half = ids_ref[0], ids_ref[1]
    rows, width = other_ref.shape[2:]
    start = pl.multiple_of(half * rows, rows)
    parts = rows // PART

    @pl.loop(0, owners)
    def _(owner):
        for index in range(2 * terms * capacity):
            codes[0, owner, index] = 0
            codes[1, owner, index] = blocks

    for stream in range(2 * terms):
        plan = plan_ref if stream < terms else other_plan_ref

        @pl.loop(0, owners)
        def _(owner):
            seen[owner] = 0

        @pl.loop(0, blocks, unroll=4)
        def _(block):
            owner = plan[0, stream % terms, block]
            slot = seen[owner]
            seen[owner] = slot + 1
            codes[0, owner, stream * capacity + slot] = block
            codes[1, owner, stream * capacity + slot] = plan[1, stream % terms, block]

    lane = lax.broadcasted_iota(jnp.int32, (PART, width), 1)
    row = lax.broadcasted_iota(jnp.int32, (PART, width), 0)
    copies = []
    for mask in order:
        owner = me ^ mask
        labels = jnp.zeros((PART, width), jnp.int32)
        for stream in range(2 * terms):
            for slot in range(capacity):
                at = stream * capacity + slot
                block = codes[0, owner, at]
                if stream < terms:
                    value = left_ref[stream, block, pl.ds(start, rows), :]
                else:
                    value = other_ref[stream - terms, block]
                built[mask, at * parts : (at + 1) * parts] = value.reshape(parts, PART, width)
                label = jnp.where(row == 0, block, codes[1, owner, at])
                labels = jnp.where(lane == at, label, labels)
        built[mask, 2 * terms * capacity * parts] = labels.astype(jnp.float32).astype(jnp.bfloat16)
        copies.append(pltpu.make_async_copy(built.at[mask], pieces[mask], sems.at[mask]))
        copies[-1].start()
    for copy in copies:
        copy.wait()


def pack(ids, plan, other_plan, left, other, before, order, capacity):
    terms, blocks, rows, width = other.shape
    owners = len(order)
    scalars = pl.BlockSpec(memory_space=pltpu.SMEM)
    whole = pl.BlockSpec(memory_space=pltpu.VMEM)
    anywhere = pl.BlockSpec(memory_space=pl.ANY)
    shape = (2 * terms * capacity * rows // PART + 1, PART, width)
    return pl.pallas_call(
        functools.partial(pack_kernel, order, capacity, blocks, terms),
        out_shape=[jax.ShapeDtypeStruct(shape, jnp.bfloat16)] * owners,
        in_specs=[scalars] * 3 + [whole, whole, anywhere],
        out_specs=[anywhere] * owners,
        scratch_shapes=[
            pltpu.SMEM((2, owners, 2 * terms * capacity), jnp.int32),
            pltpu.SMEM((owners,), jnp.int32),
            pltpu.VMEM((owners,) + shape, jnp.bfloat16),
            pltpu.SemaphoreType.DMA((owners,)),
        ],
        compiler_params=pltpu.CompilerParams(vmem_limit_bytes=VMEM_LIMIT),
        cost_estimate=busy(5.0),
    )(ids, plan, other_plan, left, other, before)


def busy(microseconds):
    return pl.CostEstimate(
        flops=int(1.15e9 * microseconds), bytes_accessed=0, transcendentals=0
    )


def add_products(left, labels, vector, right, total, side, terms, capacity):
    blocks, rows, width = vector.shape[1:]
    parts = rows // PART
    moved, where = [], []
    for slot in range(terms * capacity):
        at = side * terms * capacity + slot
        block = vector[:, labels[0, at]].reshape(2 * rows, width)
        piece = left[at * parts : (at + 1) * parts].reshape(rows, width)
        product = jnp.dot(piece, block, preferred_element_type=jnp.float32)
        moved.append(product.astype(jnp.bfloat16))
        where.append(labels[1, at])
    for slot in range(terms * capacity):
        total[where[slot]] += jnp.dot(
            moved[slot], right[slot], preferred_element_type=jnp.float32
        )


def local_stats(total, wave_ref, device, stats_ref):
    blocks = wave_ref.shape[0]
    zero = jnp.zeros(wave_ref.shape[1:], jnp.float32)

    def sums(block, carry):
        cross, own = carry
        wave = wave_ref[block].astype(jnp.float32)
        return cross + wave * total[block], own + wave * wave

    cross, own = lax.fori_loop(0, blocks, sums, (zero, zero), unroll=4)
    cross, own = jnp.sum(cross, keepdims=True), jnp.sum(own, keepdims=True)
    local = jnp.where(own > 0, cross / own, 0.0)

    def squares(block, carry):
        rest = total[block] - local * wave_ref[block].astype(jnp.float32)
        return carry + rest * rest

    about = jnp.sum(lax.fori_loop(0, blocks, squares, zero, unroll=4), keepdims=True)
    lane = lax.broadcasted_iota(jnp.int32, stats_ref.shape, 1)
    row = lax.broadcasted_iota(jnp.int32, stats_ref.shape, 0)
    values = jnp.where(lane == 0, about, jnp.where(lane == 1, cross, jnp.where(lane == 2, own, local)))
    stats_ref[...] = jnp.where((row == device) & (lane < 4), values, 0.0)


def apply_kernel(sources, choices, chosen, first, end, terms, capacity, ids_ref, *refs):
    refs = list(refs)

    def take(count):
        taken, refs[:count] = refs[:count], []
        return taken

    lefts = take(choices or sources)
    rights = take(2)
    vectors = [take(2) for _ in range(sources)]
    (wave_in,) = take(1) if end == "stats" else (None,)
    (total_in,) = (None,) if first else take(1)
    (total_out,) = (None,) if end == "result" else take(1)
    (last_out,) = take(1)
    total, left, right, vector, raw, spread_labels, labels = take(7)
    left_sems, right_sems, vector_sems, raw_sems, label_sem, total_sem = take(6)
    wave, wave_sem = take(2) if end == "stats" else (None, None)
    half = ids_ref[0]
    blocks = vector.shape[2]
    parts = left.shape[1]

    def left_copies(source, piece):
        return [
            pltpu.make_async_copy(piece.at[parts], raw.at[source], raw_sems.at[source]),
            pltpu.make_async_copy(
                piece.at[pl.ds(0, parts)], left.at[source], left_sems.at[source]
            ),
        ]

    def vector_copies(source):
        return [
            pltpu.make_async_copy(
                vectors[source][part],
                vector.at[source, half if part == 0 else 1 - half],
                vector_sems.at[source, part],
            )
            for part in range(2)
        ]

    def load_right(source, side):
        for slot in range(terms * capacity):
            target = jnp.minimum(labels[source, 1, side * terms * capacity + slot], blocks - 1)
            pltpu.make_async_copy(
                rights[side].at[slot // capacity, target],
                right.at[source, side, slot],
                right_sems.at[source, side],
            ).start()

    def wait_right(source, side):
        whole = right.at[source, side]
        pltpu.make_async_copy(whole, whole, right_sems.at[source, side]).wait()

    for source in range(sources):
        if choices:
            for choice, piece in enumerate(lefts):

                @pl.when(ids_ref[chosen + source] == choice)
                def _():
                    for copy in left_copies(source, piece):
                        copy.start()

        else:
            for copy in left_copies(source, lefts[source]):
                copy.start()
    for source in range(sources):
        for copy in vector_copies(source):
            copy.start()
    if first:
        total[...] = jnp.zeros_like(total)
    else:
        load_total = pltpu.make_async_copy(total_in, total, total_sem)
        load_total.start()
    if end == "stats":
        load_wave = pltpu.make_async_copy(wave_in, wave, wave_sem)
        load_wave.start()
    if end == "go on":
        last_out[...] = jnp.zeros_like(last_out)

    for source in range(sources):
        left_copies(source, lefts[0])[0].wait()
    spread_labels[...] = raw[:, :8].astype(jnp.float32).astype(jnp.int32)
    move_labels = pltpu.make_async_copy(spread_labels, labels, label_sem)
    move_labels.start()
    move_labels.wait()
    for source in range(sources):
        for side in range(2):
            load_right(source, side)
    if not first:
        load_total.wait()
    for source in range(sources):
        for side in range(2):
            if side == 0:
                left_copies(source, lefts[0])[1].wait()
                for copy in vector_copies(source):
                    copy.wait()
            wait_right(source, side)
            add_products(
                left.at[source],
                labels.at[source],
                vector.at[source],
                right.at[source, side],
                total,
                side,
                terms,
                capacity,
            )
    if end == "result":
        last_out[...] = total[:blocks].astype(last_out.dtype)
    elif end == "stats":
        load_wave.wait()
        local_stats(total, wave, ids_ref[1], last_out)
        total_out[...] = total[:blocks]
    else:
        store_total = pltpu.make_async_copy(total, total_out, total_sem)
        store_total.start()
        store_total.wait()


def apply_group(ids, lefts, rights, vectors, total, end, wave=None, chosen=0):
    blocks, rows, width = vectors[0][0].shape
    terms = rights[0].shape[0]
    parts = lefts[0].shape[0] - 1
    capacity = parts * PART // (2 * terms * rows)
    sources, first = len(vectors), total is None
    arrays = [*lefts, *rights] + [unit for pair in vectors for unit in pair]
    arrays += [wave] if end == "stats" else []
    arrays += [] if first else [total]
    whole = pl.BlockSpec(memory_space=pltpu.VMEM)
    anywhere = pl.BlockSpec(memory_space=pl.ANY)
    total_shape = (blocks + 1, rows, width)
    scratch = [
        pltpu.VMEM(total_shape, jnp.float32),
        pltpu.VMEM((sources, parts, PART, width), jnp.bfloat16),
        pltpu.VMEM((sources, 2, terms * capacity, width, width), jnp.bfloat16),
        pltpu.VMEM((sources, 2, blocks, rows, width), jnp.bfloat16),
        pltpu.VMEM((sources, PART, width), jnp.bfloat16),
        pltpu.VMEM((sources, 8, width), jnp.int32),
        pltpu.SMEM((sources, 8, width), jnp.int32),
        pltpu.SemaphoreType.DMA((sources,)),
        pltpu.SemaphoreType.DMA((sources, 2)),
        pltpu.SemaphoreType.DMA((sources, 2)),
        pltpu.SemaphoreType.DMA((sources,)),
        pltpu.SemaphoreType.DMA,
        pltpu.SemaphoreType.DMA,
    ]
    if end == "stats":
        scratch += [pltpu.VMEM(wave.shape, wave.dtype), pltpu.SemaphoreType.DMA]
    devices = lax.axis_size("sec") * lax.axis_size("term")
    total_out = jax.ShapeDtypeStruct(total_shape, jnp.float32)
    out_shape, out_specs = {
        "go on": ((total_out, jax.ShapeDtypeStruct((8, width), jnp.float32)), (anywhere, whole)),
        "stats": (
            (
                jax.ShapeDtypeStruct((blocks, rows, width), jnp.float32),
                jax.ShapeDtypeStruct((devices, 128), jnp.float32),
            ),
            (whole, whole),
        ),
        "result": (jax.ShapeDtypeStruct((blocks, rows, width), jnp.bfloat16), whole),
    }[end]
    choices = len(lefts) if chosen else 0
    return pl.pallas_call(
        functools.partial(apply_kernel, sources, choices, chosen, first, end, terms, capacity),
        out_shape=out_shape,
        in_specs=[pl.BlockSpec(memory_space=pltpu.SMEM)] + [anywhere] * len(arrays),
        out_specs=out_specs,
        scratch_shapes=scratch,
        compiler_params=pltpu.CompilerParams(vmem_limit_bytes=VMEM_LIMIT),
        cost_estimate=busy(3.5 + 1.8 * sources),
    )(ids, *arrays)


def direction_kernel(entries, total_ref, wave_ref, stats_ref, out_ref, rayleigh_ref):
    blocks = wave_ref.shape[0]
    stats = stats_ref[...]
    about, cross, own, local = (stats[:, lane : lane + 1] for lane in range(4))
    rayleigh = jnp.sum(cross, keepdims=True) / jnp.sum(own, keepdims=True)
    offset = local - rayleigh
    residual_sq = jnp.sum(about + offset * offset * own, keepdims=True)
    factor = lax.rsqrt(residual_sq / entries + 1e-06)
    rayleigh_ref[...] = rayleigh

    @pl.loop(0, blocks, unroll=4)
    def _(block):
        rest = total_ref[block] - rayleigh * wave_ref[block].astype(jnp.float32)
        out_ref[block] = (rest * factor).astype(jnp.bfloat16)


def new_direction(total, wave, stats, entries):
    whole = pl.BlockSpec(memory_space=pltpu.VMEM)
    return pl.pallas_call(
        functools.partial(direction_kernel, entries),
        out_shape=(
            jax.ShapeDtypeStruct(wave.shape, jnp.bfloat16),
            jax.ShapeDtypeStruct((1, 1), jnp.float32),
        ),
        in_specs=[whole] * 3,
        out_specs=(whole, whole),
        compiler_params=pltpu.CompilerParams(vmem_limit_bytes=8 * 2**20),
        cost_estimate=busy(2.0),
    )(total, wave, stats)


def per_device_ring(wavefunction, left_operator, right_operator, target_owner, target_local):
    owners, halves = lax.axis_size("sec"), lax.axis_size("term")
    me, half = lax.axis_index("sec"), lax.axis_index("term")
    terms, blocks, height, width = left_operator.shape
    rows = height // halves
    capacity = 2 * blocks // owners
    place = ring_place(me, owners)
    ids = jnp.stack([me, half]).astype(jnp.int32)

    own_rows = lax.dynamic_slice_in_dim(wavefunction, half * rows, rows, 1)
    other_rows = lax.dynamic_slice_in_dim(wavefunction, (1 - half) * rows, rows, 1)
    plan = jnp.stack([target_owner[:, :, 0], target_local])
    other_left = swap(
        lax.dynamic_slice_in_dim(left_operator, (1 - half) * rows, rows, 2), owners, halves
    )
    order = [m for m in ORDER if m < owners] + list(range(len(ORDER), owners))
    rights = (right_operator, swap(right_operator, owners, halves))
    pieces = pack(
        ids,
        plan,
        swap(plan, owners, halves),
        left_operator,
        other_left,
        plan,
        order[1:] + order[:1],
        capacity,
    )
    lefts = [pieces[0]]
    for m in range(1, owners):
        piece = pieces[m]
        if m in PIECE_WAITS:
            piece = after(piece, lefts[PIECE_WAITS[m]])
        lefts.append(exchange(piece, owners, halves, m))
    near = mask_gather(own_rows, lefts, owners, halves)
    far = {m: swap(unit, owners, halves) if m else other_rows for m, unit in near.items()}

    reach = (owners - 1) // 2
    turn = 1 - 2 * half
    distances = [0] + [s for step in range(1, reach + 1) for s in (step, -step)] + [owners // 2]
    whose = [me ^ ring_owner(place - s * turn, owners) for s in distances]
    numbers = jnp.stack([half, me * halves + half, *whose]).astype(jnp.int32)
    total = None
    groups = [order[at : at + 2] for at in range(0, owners, 2)]
    for group in groups:
        total, stats = apply_group(
            numbers,
            [lefts[m] for m in group],
            rights,
            [(near[m], far[m]) for m in group],
            total,
            "go on" if group is not groups[-1] else "stats",
            own_rows,
        )

    entries = blocks * owners * height * width
    stats = spread(stats, owners * halves)
    direction, rayleigh = new_direction(total, own_rows, stats, entries)
    def add_group(total, units, end):
        vectors = [(unit, swap(units[-s], owners, halves)) for s, unit in units.items()]
        chosen = 2 + distances.index(next(iter(units)))
        return apply_group(numbers, lefts, rights, vectors, total, end, chosen=chosen)

    total, waiting = None, {0: direction}
    ahead = behind = direction
    for step in range(1, reach + 1):
        ahead = ring_send(ahead, owners, halves, (1, -1))
        behind = ring_send(behind, owners, halves, (-1, 1))
        if step > 1:
            total, token = add_group(total, waiting, "go on")
            ahead, waiting = after(ahead, token), {}
        waiting.update({step: ahead, -step: behind})
    last = ring_send(ahead, owners, halves, (1, -1))
    total, token = add_group(total, waiting, "go on")
    last = after(last, token)
    vectors = [(last, swap(last, owners, halves))]
    chosen = 2 + distances.index(owners // 2)
    total = apply_group(numbers, lefts, rights, vectors, total, "result", chosen=chosen)
    return (total, rayleigh[0])


def slot_codes(target_owner, target_local, owners, capacity):
    terms, blocks = target_local.shape
    owner = target_owner[:, :, 0]
    place = jnp.arange(blocks, dtype=jnp.int32)
    same = (owner[:, :, None] == owner[:, None, :]) & (place[None, :] < place[:, None])[None]
    position = jnp.sum(same.astype(jnp.int32), axis=2)
    hit = (
        owner[:, None, None, :] == jnp.arange(owners, dtype=jnp.int32)[None, :, None, None]
    ) & (position[:, None, None, :] == jnp.arange(capacity, dtype=jnp.int32)[None, None, :, None])
    code = place[None, :] * (2 * blocks) + target_local - blocks
    return blocks + jnp.sum(jnp.where(hit, code[:, None, None, :], 0), axis=3)


def stream_kernel(first, capacity, blocks, code_ref, left_ref, vector_ref, right_ref, *rest):
    total_in, total = (None, rest[0]) if first else rest
    step = pl.program_id(0)
    rows, width = left_ref.shape[2:]

    @pl.when(step == 0)
    def _():
        total[...] = jnp.zeros_like(total) if first else total_in[...]

    for term in range(2):
        moved, where = [], []
        for slot in range(capacity):
            code = code_ref[2 * step + term, slot]
            source, target = lax.div(code, 2 * blocks), lax.rem(code, 2 * blocks)
            block = vector_ref[0, :, source].reshape(2 * rows, width)
            product = jnp.dot(left_ref[term, slot], block, preferred_element_type=jnp.float32)
            moved.append(product.astype(jnp.bfloat16))
            where.append(target)
        for slot in range(capacity):
            target = where[slot]
            total[target] += jnp.dot(
                moved[slot],
                right_ref[term, jnp.minimum(target, blocks - 1)],
                preferred_element_type=jnp.float32,
            )


def stream_chunk(total, codes, left, vector, right):
    owners, _, blocks, rows, width = vector.shape
    capacity = left.shape[1]
    first = total is None
    spec_total = pl.BlockSpec((blocks + 1, rows, width), lambda s, c: (0, 0, 0))
    return pl.pallas_call(
        functools.partial(stream_kernel, first, capacity, blocks),
        out_shape=jax.ShapeDtypeStruct((blocks + 1, rows, width), jnp.float32),
        grid_spec=pltpu.PrefetchScalarGridSpec(
            num_scalar_prefetch=1,
            grid=(owners,),
            in_specs=[
                pl.BlockSpec((2, capacity, rows, width), lambda s, c: (s, 0, 0, 0)),
                pl.BlockSpec((1, 2, blocks, rows, width), lambda s, c: (s, 0, 0, 0, 0)),
                pl.BlockSpec((2, blocks, width, width), lambda s, c: (0, 0, 0, 0)),
            ]
            + ([] if first else [spec_total]),
            out_specs=spec_total,
        ),
        compiler_params=pltpu.CompilerParams(vmem_limit_bytes=32 * 2**20),
        cost_estimate=pl.CostEstimate(
            flops=owners * 2 * capacity * 2 * 2 * rows * width * width,
            bytes_accessed=left.size * 2 + vector.size * 2 + right.size * 2,
            transcendentals=0,
        ),
    )(codes, left, vector, right, *([] if first else [total]))


def per_device_streamed(wavefunction, left_operator, right_operator, target_owner, target_local):
    owners = lax.axis_size("sec")
    halves = lax.axis_size("term")
    me, half = lax.axis_index("sec"), lax.axis_index("term")
    terms, blocks, height, width = left_operator.shape
    rows = height // halves
    capacity = 2 * blocks // owners

    own_rows = lax.dynamic_slice_in_dim(wavefunction, half * rows, rows, 1)
    codes = slot_codes(target_owner, target_local, owners, capacity)
    sources = codes // (2 * blocks)

    moved_left = []
    for k in range(terms):
        pick = sources[k][:, None, :] * halves + jnp.arange(halves, dtype=jnp.int32)[None, :, None]
        pieces = left_operator[k].reshape(blocks * halves, rows, width)[pick.reshape(-1)]
        pieces = pieces.reshape(owners * halves, capacity, rows, width)
        moved_left.append(lax.all_to_all(pieces, BOTH, split_axis=0, concat_axis=0, tiled=True))
    all_codes = lax.all_gather(codes, BOTH, axis=0)
    my_codes = lax.dynamic_index_in_dim(all_codes, me, axis=3 - 1, keepdims=False)
    gathered = lax.all_gather(own_rows, BOTH, axis=0).reshape(owners, halves, blocks, rows, width)
    right = lax.all_gather(right_operator, "term", axis=1)

    def apply(vector):
        total = None
        for k in range(terms):
            total = stream_chunk(total, my_codes[:, k], moved_left[k], vector, right[k])
        return total[:blocks]

    sigma_rows = apply(gathered)
    wave = own_rows.astype(jnp.float32)
    cross, own = jnp.sum(wave * sigma_rows), jnp.sum(wave * wave)
    local = jnp.where(own > 0, cross / own, 0.0)
    about = jnp.sum(jnp.square(sigma_rows - local * wave))
    stats = lax.all_gather(jnp.stack([about, cross, own, local]), BOTH, axis=0)
    rayleigh = jnp.sum(stats[:, 1]) / jnp.sum(stats[:, 2])
    residual_sq = jnp.sum(stats[:, 0] + jnp.square(stats[:, 3] - rayleigh) * stats[:, 2])
    entries = blocks * owners * height * width
    factor = lax.rsqrt(residual_sq / entries + 1e-06)
    direction = ((sigma_rows - rayleigh * wave) * factor).astype(jnp.bfloat16)
    direction = lax.all_gather(direction, BOTH, axis=0).reshape(gathered.shape)
    sigma_two = apply(direction).astype(jnp.bfloat16)
    return (sigma_two, jnp.reshape(rayleigh, (1,)))


def per_device(wavefunction, *operands):
    owners = lax.axis_size("sec")
    gathered_bytes = owners * wavefunction.size * wavefunction.dtype.itemsize
    if owners < 8 or owners & (owners - 1) or 2 * gathered_bytes > RING_BYTES:
        return per_device_streamed(wavefunction, *operands)
    return per_device_ring(wavefunction, *operands)


def solution(mesh):
    placed = (
        P(("rep", "sec"), None, None),
        P("term", ("rep", "sec"), None, None),
        P("term", ("rep", "sec"), None, None),
        P("term", ("rep", "sec"), None),
        P("term", ("rep", "sec")),
    )
    return jax.shard_map(
        per_device,
        mesh=mesh,
        in_specs=placed,
        out_specs=(P(("rep", "sec"), "term", None), P("rep")),
        check_vma=False,
    )
```

```python
import functools

import jax
import jax.numpy as jnp
from jax import lax
from jax.experimental import pallas as pl
from jax.experimental.pallas import tpu as pltpu
from jax.sharding import PartitionSpec as P

BOTH = ("sec", "term")
VMEM_LIMIT = 64 * 2**20
PART = 16
ORDER = [0, 4, 5, 1, 2, 6, 3, 7]
WAITS = {4: 1, 2: 5, 6: 2}
PIECE_WAITS = {6: 4, 7: 5}
RING_BYTES = 24 * 2**20


def ring_order(owners):
    if owners % 2:
        return list(range(owners))
    return list(range(0, owners, 2)) + list(range(owners - 1, 0, -2))


def ring_place(owner, owners):
    if owners % 2:
        return owner
    return jnp.where(owner % 2 == 0, owner // 2, owners - 1 - owner // 2)


def ring_owner(place, owners):
    place = place % owners
    if owners % 2:
        return place
    return jnp.where(place < owners // 2, 2 * place, 2 * (owners - 1 - place) + 1)


def permute(value, owners, halves, target, flip=0):
    pairs = [
        (chip * halves + half, target(chip, half) * halves + (half ^ flip))
        for chip in range(owners)
        for half in range(halves)
    ]
    return lax.ppermute(value, BOTH, pairs)


def swap(value, owners, halves):
    return permute(value, owners, halves, lambda chip, half: chip, 1)


def exchange(value, owners, halves, mask):
    return permute(value, owners, halves, lambda chip, half: chip ^ mask)


def ring_send(value, owners, halves, shifts):
    ring = ring_order(owners)
    place = {chip: index for index, chip in enumerate(ring)}
    return permute(
        value, owners, halves, lambda chip, half: ring[(place[chip] + shifts[half]) % owners]
    )


def after_kernel(*refs):
    del refs


def after(value, *others):
    anywhere = pl.BlockSpec(memory_space=pl.ANY)
    return pl.pallas_call(
        after_kernel,
        out_shape=jax.ShapeDtypeStruct(value.shape, value.dtype),
        in_specs=[anywhere] * (1 + len(others)),
        out_specs=anywhere,
        input_output_aliases={0: 0},
        cost_estimate=busy(0.3),
    )(value, *others)


def mask_gather(unit, lefts, owners, halves):
    units = {0: unit}
    step = owners // 2
    masks = []
    while step:
        masks.append(step)
        units[step] = exchange(unit, owners, halves, step)
        step //= 2
    waits = dict(WAITS)
    for step in masks[1:]:
        for mask in [m for m in units if m >= 2 * step and m % (2 * step) == 0]:
            if mask in waits:
                units[mask] = after(units[mask], lefts[waits.pop(mask)])
            units[mask | step] = exchange(units[mask], owners, halves, step)
    return units


def spread(value, devices):
    step = 1
    while step < devices:
        masks = [step] if 2 * step == devices else [step, 2 * step, 3 * step]
        parts = [lax.ppermute(value, BOTH, [(d, d ^ m) for d in range(devices)]) for m in masks]
        for part in parts:
            value = value + part
        step *= 4
    return value


def pack_kernel(order, capacity, blocks, terms, ids_ref, plan_ref, other_plan_ref, *refs):
    left_ref, other_ref, _, *pieces, codes, seen, built, sems = refs
    owners = len(order)
    me, half = ids_ref[0], ids_ref[1]
    rows, width = other_ref.shape[2:]
    start = pl.multiple_of(half * rows, rows)
    parts = rows // PART

    @pl.loop(0, owners)
    def _(owner):
        for index in range(2 * terms * capacity):
            codes[0, owner, index] = 0
            codes[1, owner, index] = blocks

    for stream in range(2 * terms):
        plan = plan_ref if stream < terms else other_plan_ref

        @pl.loop(0, owners)
        def _(owner):
            seen[owner] = 0

        @pl.loop(0, blocks, unroll=4)
        def _(block):
            owner = plan[0, stream % terms, block]
            slot = seen[owner]
            seen[owner] = slot + 1
            codes[0, owner, stream * capacity + slot] = block
            codes[1, owner, stream * capacity + slot] = plan[1, stream % terms, block]

    lane = lax.broadcasted_iota(jnp.int32, (PART, width), 1)
    row = lax.broadcasted_iota(jnp.int32, (PART, width), 0)
    copies = []
    for mask in order:
        owner = me ^ mask
        labels = jnp.zeros((PART, width), jnp.int32)
        for stream in range(2 * terms):
            for slot in range(capacity):
                at = stream * capacity + slot
                block = codes[0, owner, at]
                if stream < terms:
                    value = left_ref[stream, block, pl.ds(start, rows), :]
                else:
                    value = other_ref[stream - terms, block]
                built[mask, at * parts : (at + 1) * parts] = value.reshape(parts, PART, width)
                label = jnp.where(row == 0, block, codes[1, owner, at])
                labels = jnp.where(lane == at, label, labels)
        built[mask, 2 * terms * capacity * parts] = labels.astype(jnp.float32).astype(jnp.bfloat16)
        copies.append(pltpu.make_async_copy(built.at[mask], pieces[mask], sems.at[mask]))
        copies[-1].start()
    for copy in copies:
        copy.wait()


def pack(ids, plan, other_plan, left, other, before, order, capacity):
    terms, blocks, rows, width = other.shape
    owners = len(order)
    scalars = pl.BlockSpec(memory_space=pltpu.SMEM)
    whole = pl.BlockSpec(memory_space=pltpu.VMEM)
    anywhere = pl.BlockSpec(memory_space=pl.ANY)
    shape = (2 * terms * capacity * rows // PART + 1, PART, width)
    return pl.pallas_call(
        functools.partial(pack_kernel, order, capacity, blocks, terms),
        out_shape=[jax.ShapeDtypeStruct(shape, jnp.bfloat16)] * owners,
        in_specs=[scalars] * 3 + [whole, whole, anywhere],
        out_specs=[anywhere] * owners,
        scratch_shapes=[
            pltpu.SMEM((2, owners, 2 * terms * capacity), jnp.int32),
            pltpu.SMEM((owners,), jnp.int32),
            pltpu.VMEM((owners,) + shape, jnp.bfloat16),
            pltpu.SemaphoreType.DMA((owners,)),
        ],
        compiler_params=pltpu.CompilerParams(vmem_limit_bytes=VMEM_LIMIT),
        cost_estimate=busy(5.0),
    )(ids, plan, other_plan, left, other, before)


def busy(microseconds):
    return pl.CostEstimate(
        flops=int(1.15e9 * microseconds), bytes_accessed=0, transcendentals=0
    )


def add_products(left, labels, vector, right, total, side, terms, capacity):
    blocks, rows, width = vector.shape[1:]
    parts = rows // PART
    moved, where = [], []
    for slot in range(terms * capacity):
        at = side * terms * capacity + slot
        block = vector[:, labels[0, at]].reshape(2 * rows, width)
        piece = left[at * parts : (at + 1) * parts].reshape(rows, width)
        product = jnp.dot(piece, block, preferred_element_type=jnp.float32)
        moved.append(product.astype(jnp.bfloat16))
        where.append(labels[1, at])
    for slot in range(terms * capacity):
        total[where[slot]] += jnp.dot(
            moved[slot], right[slot], preferred_element_type=jnp.float32
        )


def local_stats(total, wave_ref, device, stats_ref):
    blocks = wave_ref.shape[0]
    zero = jnp.zeros(wave_ref.shape[1:], jnp.float32)

    def sums(block, carry):
        cross, own = carry
        wave = wave_ref[block].astype(jnp.float32)
        return cross + wave * total[block], own + wave * wave

    cross, own = lax.fori_loop(0, blocks, sums, (zero, zero), unroll=4)
    cross, own = jnp.sum(cross, keepdims=True), jnp.sum(own, keepdims=True)
    local = jnp.where(own > 0, cross / own, 0.0)

    def squares(block, carry):
        rest = total[block] - local * wave_ref[block].astype(jnp.float32)
        return carry + rest * rest

    about = jnp.sum(lax.fori_loop(0, blocks, squares, zero, unroll=4), keepdims=True)
    lane = lax.broadcasted_iota(jnp.int32, stats_ref.shape, 1)
    row = lax.broadcasted_iota(jnp.int32, stats_ref.shape, 0)
    values = jnp.where(lane == 0, about, jnp.where(lane == 1, cross, jnp.where(lane == 2, own, local)))
    stats_ref[...] = jnp.where((row == device) & (lane < 4), values, 0.0)


def apply_kernel(sources, choices, chosen, first, end, terms, capacity, ids_ref, *refs):
    refs = list(refs)

    def take(count):
        taken, refs[:count] = refs[:count], []
        return taken

    lefts = take(choices or sources)
    rights = take(2)
    vectors = [take(2) for _ in range(sources)]
    (wave_in,) = take(1) if end == "stats" else (None,)
    (total_in,) = (None,) if first else take(1)
    (total_out,) = (None,) if end == "result" else take(1)
    (last_out,) = take(1)
    total, left, right, vector, raw, spread_labels, labels = take(7)
    left_sems, right_sems, vector_sems, raw_sems, label_sem, total_sem = take(6)
    wave, wave_sem = take(2) if end == "stats" else (None, None)
    half = ids_ref[0]
    blocks = vector.shape[2]
    parts = left.shape[1]

    def left_copies(source, piece):
        return [
            pltpu.make_async_copy(piece.at[parts], raw.at[source], raw_sems.at[source]),
            pltpu.make_async_copy(
                piece.at[pl.ds(0, parts)], left.at[source], left_sems.at[source]
            ),
        ]

    def vector_copies(source):
        return [
            pltpu.make_async_copy(
                vectors[source][part],
                vector.at[source, half if part == 0 else 1 - half],
                vector_sems.at[source, part],
            )
            for part in range(2)
        ]

    def load_right(source, side):
        for slot in range(terms * capacity):
            target = jnp.minimum(labels[source, 1, side * terms * capacity + slot], blocks - 1)
            pltpu.make_async_copy(
                rights[side].at[slot // capacity, target],
                right.at[source, side, slot],
                right_sems.at[source, side],
            ).start()

    def wait_right(source, side):
        whole = right.at[source, side]
        pltpu.make_async_copy(whole, whole, right_sems.at[source, side]).wait()

    for which in range(2):
        for source in range(sources):
            if choices:
                for choice, piece in enumerate(lefts):

                    @pl.when(ids_ref[chosen + source] == choice)
                    def _():
                        left_copies(source, piece)[which].start()

            else:
                left_copies(source, lefts[source])[which].start()
    for source in range(sources):
        for copy in vector_copies(source):
            copy.start()
    if first:
        total[...] = jnp.zeros_like(total)
    else:
        load_total = pltpu.make_async_copy(total_in, total, total_sem)
        load_total.start()
    if end == "stats":
        load_wave = pltpu.make_async_copy(wave_in, wave, wave_sem)
        load_wave.start()
    if end == "go on":
        last_out[...] = jnp.zeros_like(last_out)

    for source in range(sources):
        left_copies(source, lefts[0])[0].wait()
    spread_labels[...] = raw[:, :8].astype(jnp.float32).astype(jnp.int32)
    move_labels = pltpu.make_async_copy(spread_labels, labels, label_sem)
    move_labels.start()
    move_labels.wait()
    for source in range(sources):
        for side in range(2):
            load_right(source, side)
    if not first:
        load_total.wait()
    for source in range(sources):
        for side in range(2):
            if side == 0:
                left_copies(source, lefts[0])[1].wait()
                for copy in vector_copies(source):
                    copy.wait()
            wait_right(source, side)
            add_products(
                left.at[source],
                labels.at[source],
                vector.at[source],
                right.at[source, side],
                total,
                side,
                terms,
                capacity,
            )
    if end == "result":
        last_out[...] = total[:blocks].astype(last_out.dtype)
    elif end == "stats":
        load_wave.wait()
        local_stats(total, wave, ids_ref[1], last_out)
        total_out[...] = total[:blocks]
    else:
        store_total = pltpu.make_async_copy(total, total_out, total_sem)
        store_total.start()
        store_total.wait()


def apply_group(ids, lefts, rights, vectors, total, end, wave=None, chosen=0):
    blocks, rows, width = vectors[0][0].shape
    terms = rights[0].shape[0]
    parts = lefts[0].shape[0] - 1
    capacity = parts * PART // (2 * terms * rows)
    sources, first = len(vectors), total is None
    arrays = [*lefts, *rights] + [unit for pair in vectors for unit in pair]
    arrays += [wave] if end == "stats" else []
    arrays += [] if first else [total]
    whole = pl.BlockSpec(memory_space=pltpu.VMEM)
    anywhere = pl.BlockSpec(memory_space=pl.ANY)
    total_shape = (blocks + 1, rows, width)
    scratch = [
        pltpu.VMEM(total_shape, jnp.float32),
        pltpu.VMEM((sources, parts, PART, width), jnp.bfloat16),
        pltpu.VMEM((sources, 2, terms * capacity, width, width), jnp.bfloat16),
        pltpu.VMEM((sources, 2, blocks, rows, width), jnp.bfloat16),
        pltpu.VMEM((sources, PART, width), jnp.bfloat16),
        pltpu.VMEM((sources, 8, width), jnp.int32),
        pltpu.SMEM((sources, 8, width), jnp.int32),
        pltpu.SemaphoreType.DMA((sources,)),
        pltpu.SemaphoreType.DMA((sources, 2)),
        pltpu.SemaphoreType.DMA((sources, 2)),
        pltpu.SemaphoreType.DMA((sources,)),
        pltpu.SemaphoreType.DMA,
        pltpu.SemaphoreType.DMA,
    ]
    if end == "stats":
        scratch += [pltpu.VMEM(wave.shape, wave.dtype), pltpu.SemaphoreType.DMA]
    devices = lax.axis_size("sec") * lax.axis_size("term")
    total_out = jax.ShapeDtypeStruct(total_shape, jnp.float32)
    out_shape, out_specs = {
        "go on": ((total_out, jax.ShapeDtypeStruct((8, width), jnp.float32)), (anywhere, whole)),
        "stats": (
            (
                jax.ShapeDtypeStruct((blocks, rows, width), jnp.float32),
                jax.ShapeDtypeStruct((devices, 128), jnp.float32),
            ),
            (whole, whole),
        ),
        "result": (jax.ShapeDtypeStruct((blocks, rows, width), jnp.bfloat16), whole),
    }[end]
    choices = len(lefts) if chosen else 0
    return pl.pallas_call(
        functools.partial(apply_kernel, sources, choices, chosen, first, end, terms, capacity),
        out_shape=out_shape,
        in_specs=[pl.BlockSpec(memory_space=pltpu.SMEM)] + [anywhere] * len(arrays),
        out_specs=out_specs,
        scratch_shapes=scratch,
        compiler_params=pltpu.CompilerParams(vmem_limit_bytes=VMEM_LIMIT),
        cost_estimate=busy(3.5 + 1.8 * sources),
    )(ids, *arrays)


def direction_kernel(entries, total_ref, wave_ref, stats_ref, out_ref, rayleigh_ref):
    blocks = wave_ref.shape[0]
    stats = stats_ref[...]
    about, cross, own, local = (stats[:, lane : lane + 1] for lane in range(4))
    rayleigh = jnp.sum(cross, keepdims=True) / jnp.sum(own, keepdims=True)
    offset = local - rayleigh
    residual_sq = jnp.sum(about + offset * offset * own, keepdims=True)
    factor = lax.rsqrt(residual_sq / entries + 1e-06)
    rayleigh_ref[...] = rayleigh

    @pl.loop(0, blocks, unroll=4)
    def _(block):
        rest = total_ref[block] - rayleigh * wave_ref[block].astype(jnp.float32)
        out_ref[block] = (rest * factor).astype(jnp.bfloat16)


def new_direction(total, wave, stats, entries):
    whole = pl.BlockSpec(memory_space=pltpu.VMEM)
    return pl.pallas_call(
        functools.partial(direction_kernel, entries),
        out_shape=(
            jax.ShapeDtypeStruct(wave.shape, jnp.bfloat16),
            jax.ShapeDtypeStruct((1, 1), jnp.float32),
        ),
        in_specs=[whole] * 3,
        out_specs=(whole, whole),
        compiler_params=pltpu.CompilerParams(vmem_limit_bytes=8 * 2**20),
        cost_estimate=busy(2.0),
    )(total, wave, stats)


def per_device_ring(wavefunction, left_operator, right_operator, target_owner, target_local):
    owners, halves = lax.axis_size("sec"), lax.axis_size("term")
    me, half = lax.axis_index("sec"), lax.axis_index("term")
    terms, blocks, height, width = left_operator.shape
    rows = height // halves
    capacity = 2 * blocks // owners
    place = ring_place(me, owners)
    ids = jnp.stack([me, half]).astype(jnp.int32)

    own_rows = lax.dynamic_slice_in_dim(wavefunction, half * rows, rows, 1)
    other_rows = lax.dynamic_slice_in_dim(wavefunction, (1 - half) * rows, rows, 1)
    plan = jnp.stack([target_owner[:, :, 0], target_local])
    other_left = swap(
        lax.dynamic_slice_in_dim(left_operator, (1 - half) * rows, rows, 2), owners, halves
    )
    order = [m for m in ORDER if m < owners] + list(range(len(ORDER), owners))
    rights = (right_operator, swap(right_operator, owners, halves))
    pieces = pack(
        ids,
        plan,
        swap(plan, owners, halves),
        left_operator,
        other_left,
        plan,
        order[1:] + order[:1],
        capacity,
    )
    lefts = [pieces[0]]
    for m in range(1, owners):
        piece = pieces[m]
        if m in PIECE_WAITS:
            piece = after(piece, lefts[PIECE_WAITS[m]])
        lefts.append(exchange(piece, owners, halves, m))
    near = mask_gather(own_rows, lefts, owners, halves)
    far = {m: swap(unit, owners, halves) if m else other_rows for m, unit in near.items()}

    reach = (owners - 1) // 2
    turn = 1 - 2 * half
    distances = [0] + [s for step in range(1, reach + 1) for s in (step, -step)] + [owners // 2]
    whose = [me ^ ring_owner(place - s * turn, owners) for s in distances]
    numbers = jnp.stack([half, me * halves + half, *whose]).astype(jnp.int32)
    total = None
    groups = [order[at : at + 2] for at in range(0, owners, 2)]
    for group in groups:
        total, stats = apply_group(
            numbers,
            [lefts[m] for m in group],
            rights,
            [(near[m], far[m]) for m in group],
            total,
            "go on" if group is not groups[-1] else "stats",
            own_rows,
        )

    entries = blocks * owners * height * width
    stats = spread(stats, owners * halves)
    direction, rayleigh = new_direction(total, own_rows, stats, entries)
    def add_group(total, units, end):
        vectors = [(unit, swap(units[-s], owners, halves)) for s, unit in units.items()]
        chosen = 2 + distances.index(next(iter(units)))
        return apply_group(numbers, lefts, rights, vectors, total, end, chosen=chosen)

    total, waiting = None, {0: direction}
    ahead = behind = direction
    for step in range(1, reach + 1):
        ahead = ring_send(ahead, owners, halves, (1, -1))
        behind = ring_send(behind, owners, halves, (-1, 1))
        if step > 1:
            total, token = add_group(total, waiting, "go on")
            ahead, waiting = after(ahead, token), {}
        waiting.update({step: ahead, -step: behind})
    last = ring_send(ahead, owners, halves, (1, -1))
    total, token = add_group(total, waiting, "go on")
    last = after(last, token)
    vectors = [(last, swap(last, owners, halves))]
    chosen = 2 + distances.index(owners // 2)
    total = apply_group(numbers, lefts, rights, vectors, total, "result", chosen=chosen)
    return (total, rayleigh[0])


def slot_codes(target_owner, target_local, owners, capacity):
    terms, blocks = target_local.shape
    owner = target_owner[:, :, 0]
    place = jnp.arange(blocks, dtype=jnp.int32)
    same = (owner[:, :, None] == owner[:, None, :]) & (place[None, :] < place[:, None])[None]
    position = jnp.sum(same.astype(jnp.int32), axis=2)
    hit = (
        owner[:, None, None, :] == jnp.arange(owners, dtype=jnp.int32)[None, :, None, None]
    ) & (position[:, None, None, :] == jnp.arange(capacity, dtype=jnp.int32)[None, None, :, None])
    code = place[None, :] * (2 * blocks) + target_local - blocks
    return blocks + jnp.sum(jnp.where(hit, code[:, None, None, :], 0), axis=3)


def stream_kernel(first, capacity, blocks, code_ref, left_ref, vector_ref, right_ref, *rest):
    total_in, total = (None, rest[0]) if first else rest
    step = pl.program_id(0)
    rows, width = left_ref.shape[2:]

    @pl.when(step == 0)
    def _():
        total[...] = jnp.zeros_like(total) if first else total_in[...]

    for term in range(2):
        moved, where = [], []
        for slot in range(capacity):
            code = code_ref[2 * step + term, slot]
            source, target = lax.div(code, 2 * blocks), lax.rem(code, 2 * blocks)
            block = vector_ref[0, :, source].reshape(2 * rows, width)
            product = jnp.dot(left_ref[term, slot], block, preferred_element_type=jnp.float32)
            moved.append(product.astype(jnp.bfloat16))
            where.append(target)
        for slot in range(capacity):
            target = where[slot]
            total[target] += jnp.dot(
                moved[slot],
                right_ref[term, jnp.minimum(target, blocks - 1)],
                preferred_element_type=jnp.float32,
            )


def stream_chunk(total, codes, left, vector, right):
    owners, _, blocks, rows, width = vector.shape
    capacity = left.shape[1]
    first = total is None
    spec_total = pl.BlockSpec((blocks + 1, rows, width), lambda s, c: (0, 0, 0))
    return pl.pallas_call(
        functools.partial(stream_kernel, first, capacity, blocks),
        out_shape=jax.ShapeDtypeStruct((blocks + 1, rows, width), jnp.float32),
        grid_spec=pltpu.PrefetchScalarGridSpec(
            num_scalar_prefetch=1,
            grid=(owners,),
            in_specs=[
                pl.BlockSpec((2, capacity, rows, width), lambda s, c: (s, 0, 0, 0)),
                pl.BlockSpec((1, 2, blocks, rows, width), lambda s, c: (s, 0, 0, 0, 0)),
                pl.BlockSpec((2, blocks, width, width), lambda s, c: (0, 0, 0, 0)),
            ]
            + ([] if first else [spec_total]),
            out_specs=spec_total,
        ),
        compiler_params=pltpu.CompilerParams(vmem_limit_bytes=32 * 2**20),
        cost_estimate=pl.CostEstimate(
            flops=owners * 2 * capacity * 2 * 2 * rows * width * width,
            bytes_accessed=left.size * 2 + vector.size * 2 + right.size * 2,
            transcendentals=0,
        ),
    )(codes, left, vector, right, *([] if first else [total]))


def per_device_streamed(wavefunction, left_operator, right_operator, target_owner, target_local):
    owners = lax.axis_size("sec")
    halves = lax.axis_size("term")
    me, half = lax.axis_index("sec"), lax.axis_index("term")
    terms, blocks, height, width = left_operator.shape
    rows = height // halves
    capacity = 2 * blocks // owners

    own_rows = lax.dynamic_slice_in_dim(wavefunction, half * rows, rows, 1)
    codes = slot_codes(target_owner, target_local, owners, capacity)
    sources = codes // (2 * blocks)

    moved_left = []
    for k in range(terms):
        pick = sources[k][:, None, :] * halves + jnp.arange(halves, dtype=jnp.int32)[None, :, None]
        pieces = left_operator[k].reshape(blocks * halves, rows, width)[pick.reshape(-1)]
        pieces = pieces.reshape(owners * halves, capacity, rows, width)
        moved_left.append(lax.all_to_all(pieces, BOTH, split_axis=0, concat_axis=0, tiled=True))
    all_codes = lax.all_gather(codes, BOTH, axis=0)
    my_codes = lax.dynamic_index_in_dim(all_codes, me, axis=3 - 1, keepdims=False)
    gathered = lax.all_gather(own_rows, BOTH, axis=0).reshape(owners, halves, blocks, rows, width)
    right = lax.all_gather(right_operator, "term", axis=1)

    def apply(vector):
        total = None
        for k in range(terms):
            total = stream_chunk(total, my_codes[:, k], moved_left[k], vector, right[k])
        return total[:blocks]

    sigma_rows = apply(gathered)
    wave = own_rows.astype(jnp.float32)
    cross, own = jnp.sum(wave * sigma_rows), jnp.sum(wave * wave)
    local = jnp.where(own > 0, cross / own, 0.0)
    about = jnp.sum(jnp.square(sigma_rows - local * wave))
    stats = lax.all_gather(jnp.stack([about, cross, own, local]), BOTH, axis=0)
    rayleigh = jnp.sum(stats[:, 1]) / jnp.sum(stats[:, 2])
    residual_sq = jnp.sum(stats[:, 0] + jnp.square(stats[:, 3] - rayleigh) * stats[:, 2])
    entries = blocks * owners * height * width
    factor = lax.rsqrt(residual_sq / entries + 1e-06)
    direction = ((sigma_rows - rayleigh * wave) * factor).astype(jnp.bfloat16)
    direction = lax.all_gather(direction, BOTH, axis=0).reshape(gathered.shape)
    sigma_two = apply(direction).astype(jnp.bfloat16)
    return (sigma_two, jnp.reshape(rayleigh, (1,)))


def per_device(wavefunction, *operands):
    owners = lax.axis_size("sec")
    gathered_bytes = owners * wavefunction.size * wavefunction.dtype.itemsize
    if owners < 8 or owners & (owners - 1) or 2 * gathered_bytes > RING_BYTES:
        return per_device_streamed(wavefunction, *operands)
    return per_device_ring(wavefunction, *operands)


def solution(mesh):
    placed = (
        P(("rep", "sec"), None, None),
        P("term", ("rep", "sec"), None, None),
        P("term", ("rep", "sec"), None, None),
        P("term", ("rep", "sec"), None),
        P("term", ("rep", "sec")),
    )
    return jax.shard_map(
        per_device,
        mesh=mesh,
        in_specs=placed,
        out_specs=(P(("rep", "sec"), "term", None), P("rep")),
        check_vma=False,
    )
```

```python
import functools

import jax
import jax.numpy as jnp
from jax import lax
from jax.experimental import pallas as pl
from jax.experimental.pallas import tpu as pltpu
from jax.sharding import PartitionSpec as P

BOTH = ("sec", "term")
VMEM_LIMIT = 64 * 2**20
PART = 16
ORDER = [0, 1, 4, 5, 2, 6, 3, 7]
WAITS = {4: 1, 2: 4}
PIECE_WAITS = {6: 4, 7: 5}
RING_BYTES = 24 * 2**20


def ring_order(owners):
    if owners % 2:
        return list(range(owners))
    return list(range(0, owners, 2)) + list(range(owners - 1, 0, -2))


def ring_place(owner, owners):
    if owners % 2:
        return owner
    return jnp.where(owner % 2 == 0, owner // 2, owners - 1 - owner // 2)


def ring_owner(place, owners):
    place = place % owners
    if owners % 2:
        return place
    return jnp.where(place < owners // 2, 2 * place, 2 * (owners - 1 - place) + 1)


def permute(value, owners, halves, target, flip=0):
    pairs = [
        (chip * halves + half, target(chip, half) * halves + (half ^ flip))
        for chip in range(owners)
        for half in range(halves)
    ]
    return lax.ppermute(value, BOTH, pairs)


def swap(value, owners, halves):
    return permute(value, owners, halves, lambda chip, half: chip, 1)


def exchange(value, owners, halves, mask):
    return permute(value, owners, halves, lambda chip, half: chip ^ mask)


def ring_send(value, owners, halves, shifts):
    ring = ring_order(owners)
    place = {chip: index for index, chip in enumerate(ring)}
    return permute(
        value, owners, halves, lambda chip, half: ring[(place[chip] + shifts[half]) % owners]
    )


def after_kernel(*refs):
    del refs


def after(value, *others):
    anywhere = pl.BlockSpec(memory_space=pl.ANY)
    return pl.pallas_call(
        after_kernel,
        out_shape=jax.ShapeDtypeStruct(value.shape, value.dtype),
        in_specs=[anywhere] * (1 + len(others)),
        out_specs=anywhere,
        input_output_aliases={0: 0},
        cost_estimate=busy(0.3),
    )(value, *others)


def mask_gather(unit, lefts, owners, halves):
    units = {0: unit}
    step = owners // 2
    masks = []
    while step:
        masks.append(step)
        units[step] = exchange(unit, owners, halves, step)
        step //= 2
    waits = dict(WAITS)
    for step in masks[1:]:
        for mask in [m for m in units if m >= 2 * step and m % (2 * step) == 0]:
            if mask in waits:
                units[mask] = after(units[mask], lefts[waits.pop(mask)])
            units[mask | step] = exchange(units[mask], owners, halves, step)
    return units


def spread(value, devices):
    step = 1
    while step < devices:
        masks = [step] if 2 * step == devices else [step, 2 * step, 3 * step]
        parts = [lax.ppermute(value, BOTH, [(d, d ^ m) for d in range(devices)]) for m in masks]
        for part in parts:
            value = value + part
        step *= 4
    return value


def pack_kernel(order, capacity, blocks, terms, ids_ref, plan_ref, other_plan_ref, *refs):
    left_ref, other_ref, _, *pieces, codes, seen, built, sems = refs
    owners = len(order)
    me, half = ids_ref[0], ids_ref[1]
    rows, width = other_ref.shape[2:]
    start = pl.multiple_of(half * rows, rows)
    parts = rows // PART

    @pl.loop(0, owners)
    def _(owner):
        for index in range(2 * terms * capacity):
            codes[0, owner, index] = 0
            codes[1, owner, index] = blocks

    for stream in range(2 * terms):
        plan = plan_ref if stream < terms else other_plan_ref

        @pl.loop(0, owners)
        def _(owner):
            seen[owner] = 0

        @pl.loop(0, blocks, unroll=4)
        def _(block):
            owner = plan[0, stream % terms, block]
            slot = seen[owner]
            seen[owner] = slot + 1
            codes[0, owner, stream * capacity + slot] = block
            codes[1, owner, stream * capacity + slot] = plan[1, stream % terms, block]

    lane = lax.broadcasted_iota(jnp.int32, (PART, width), 1)
    row = lax.broadcasted_iota(jnp.int32, (PART, width), 0)
    copies = []
    for mask in order:
        owner = me ^ mask
        labels = jnp.zeros((PART, width), jnp.int32)
        for stream in range(2 * terms):
            for slot in range(capacity):
                at = stream * capacity + slot
                block = codes[0, owner, at]
                if stream < terms:
                    value = left_ref[stream, block, pl.ds(start, rows), :]
                else:
                    value = other_ref[stream - terms, block]
                built[mask, at * parts : (at + 1) * parts] = value.reshape(parts, PART, width)
                label = jnp.where(row == 0, block, codes[1, owner, at])
                labels = jnp.where(lane == at, label, labels)
        built[mask, 2 * terms * capacity * parts] = labels.astype(jnp.float32).astype(jnp.bfloat16)
        copies.append(pltpu.make_async_copy(built.at[mask], pieces[mask], sems.at[mask]))
        copies[-1].start()
    for copy in copies:
        copy.wait()


def pack(ids, plan, other_plan, left, other, before, order, capacity):
    terms, blocks, rows, width = other.shape
    owners = len(order)
    scalars = pl.BlockSpec(memory_space=pltpu.SMEM)
    whole = pl.BlockSpec(memory_space=pltpu.VMEM)
    anywhere = pl.BlockSpec(memory_space=pl.ANY)
    shape = (2 * terms * capacity * rows // PART + 1, PART, width)
    return pl.pallas_call(
        functools.partial(pack_kernel, order, capacity, blocks, terms),
        out_shape=[jax.ShapeDtypeStruct(shape, jnp.bfloat16)] * owners,
        in_specs=[scalars] * 3 + [whole, whole, anywhere],
        out_specs=[anywhere] * owners,
        scratch_shapes=[
            pltpu.SMEM((2, owners, 2 * terms * capacity), jnp.int32),
            pltpu.SMEM((owners,), jnp.int32),
            pltpu.VMEM((owners,) + shape, jnp.bfloat16),
            pltpu.SemaphoreType.DMA((owners,)),
        ],
        compiler_params=pltpu.CompilerParams(vmem_limit_bytes=VMEM_LIMIT),
        cost_estimate=busy(5.0),
    )(ids, plan, other_plan, left, other, before)


def busy(microseconds):
    return pl.CostEstimate(
        flops=int(1.15e9 * microseconds), bytes_accessed=0, transcendentals=0
    )


def add_products(left, labels, vector, right, total, side, terms, capacity):
    blocks, rows, width = vector.shape[1:]
    parts = rows // PART
    moved, where = [], []
    for slot in range(terms * capacity):
        at = side * terms * capacity + slot
        block = vector[:, labels[0, at]].reshape(2 * rows, width)
        piece = left[at * parts : (at + 1) * parts].reshape(rows, width)
        product = jnp.dot(piece, block, preferred_element_type=jnp.float32)
        moved.append(product.astype(jnp.bfloat16))
        where.append(labels[1, at])
    for slot in range(terms * capacity):
        total[where[slot]] += jnp.dot(
            moved[slot], right[slot], preferred_element_type=jnp.float32
        )


def local_stats(total, wave_ref, device, stats_ref):
    blocks = wave_ref.shape[0]
    zero = jnp.zeros(wave_ref.shape[1:], jnp.float32)

    def sums(block, carry):
        cross, own = carry
        wave = wave_ref[block].astype(jnp.float32)
        return cross + wave * total[block], own + wave * wave

    cross, own = lax.fori_loop(0, blocks, sums, (zero, zero), unroll=4)
    cross, own = jnp.sum(cross, keepdims=True), jnp.sum(own, keepdims=True)
    local = jnp.where(own > 0, cross / own, 0.0)

    def squares(block, carry):
        rest = total[block] - local * wave_ref[block].astype(jnp.float32)
        return carry + rest * rest

    about = jnp.sum(lax.fori_loop(0, blocks, squares, zero, unroll=4), keepdims=True)
    lane = lax.broadcasted_iota(jnp.int32, stats_ref.shape, 1)
    row = lax.broadcasted_iota(jnp.int32, stats_ref.shape, 0)
    values = jnp.where(lane == 0, about, jnp.where(lane == 1, cross, jnp.where(lane == 2, own, local)))
    stats_ref[...] = jnp.where((row == device) & (lane < 4), values, 0.0)


def apply_kernel(sources, choices, chosen, first, end, terms, capacity, ids_ref, *refs):
    refs = list(refs)

    def take(count):
        taken, refs[:count] = refs[:count], []
        return taken

    lefts = take(choices or sources)
    rights = take(2)
    vectors = [take(2) for _ in range(sources)]
    (wave_in,) = take(1) if end == "stats" else (None,)
    (total_in,) = (None,) if first else take(1)
    (total_out,) = (None,) if end == "result" else take(1)
    (last_out,) = take(1)
    total, left, right, vector, raw, spread_labels, labels = take(7)
    left_sems, right_sems, vector_sems, raw_sems, label_sem, total_sem = take(6)
    wave, wave_sem = take(2) if end == "stats" else (None, None)
    half = ids_ref[0]
    blocks = vector.shape[2]
    parts = left.shape[1]

    def left_copies(source, piece):
        return [
            pltpu.make_async_copy(piece.at[parts], raw.at[source], raw_sems.at[source]),
            pltpu.make_async_copy(
                piece.at[pl.ds(0, parts)], left.at[source], left_sems.at[source]
            ),
        ]

    def vector_copies(source):
        return [
            pltpu.make_async_copy(
                vectors[source][part],
                vector.at[source, half if part == 0 else 1 - half],
                vector_sems.at[source, part],
            )
            for part in range(2)
        ]

    def load_right(source, side):
        for slot in range(terms * capacity):
            target = jnp.minimum(labels[source, 1, side * terms * capacity + slot], blocks - 1)
            pltpu.make_async_copy(
                rights[side].at[slot // capacity, target],
                right.at[source, side, slot],
                right_sems.at[source, side],
            ).start()

    def wait_right(source, side):
        whole = right.at[source, side]
        pltpu.make_async_copy(whole, whole, right_sems.at[source, side]).wait()

    for source in range(sources):
        if choices:
            for choice, piece in enumerate(lefts):

                @pl.when(ids_ref[chosen + source] == choice)
                def _():
                    for copy in left_copies(source, piece):
                        copy.start()

        else:
            for copy in left_copies(source, lefts[source]):
                copy.start()
    for source in range(sources):
        for copy in vector_copies(source):
            copy.start()
    if first:
        total[...] = jnp.zeros_like(total)
    else:
        load_total = pltpu.make_async_copy(total_in, total, total_sem)
        load_total.start()
    if end == "stats":
        load_wave = pltpu.make_async_copy(wave_in, wave, wave_sem)
        load_wave.start()
    if end == "go on":
        last_out[...] = jnp.zeros_like(last_out)

    for source in range(sources):
        left_copies(source, lefts[0])[0].wait()
    spread_labels[...] = raw[:, :8].astype(jnp.float32).astype(jnp.int32)
    move_labels = pltpu.make_async_copy(spread_labels, labels, label_sem)
    move_labels.start()
    move_labels.wait()
    for source in range(sources):
        for side in range(2):
            load_right(source, side)
    if not first:
        load_total.wait()
    for source in range(sources):
        for side in range(2):
            if side == 0:
                left_copies(source, lefts[0])[1].wait()
                for copy in vector_copies(source):
                    copy.wait()
            wait_right(source, side)
            add_products(
                left.at[source],
                labels.at[source],
                vector.at[source],
                right.at[source, side],
                total,
                side,
                terms,
                capacity,
            )
    if end == "result":
        last_out[...] = total[:blocks].astype(last_out.dtype)
    elif end == "stats":
        load_wave.wait()
        local_stats(total, wave, ids_ref[1], last_out)
        total_out[...] = total[:blocks]
    else:
        store_total = pltpu.make_async_copy(total, total_out, total_sem)
        store_total.start()
        store_total.wait()


def apply_group(ids, lefts, rights, vectors, total, end, wave=None, chosen=0):
    blocks, rows, width = vectors[0][0].shape
    terms = rights[0].shape[0]
    parts = lefts[0].shape[0] - 1
    capacity = parts * PART // (2 * terms * rows)
    sources, first = len(vectors), total is None
    arrays = [*lefts, *rights] + [unit for pair in vectors for unit in pair]
    arrays += [wave] if end == "stats" else []
    arrays += [] if first else [total]
    whole = pl.BlockSpec(memory_space=pltpu.VMEM)
    anywhere = pl.BlockSpec(memory_space=pl.ANY)
    total_shape = (blocks + 1, rows, width)
    scratch = [
        pltpu.VMEM(total_shape, jnp.float32),
        pltpu.VMEM((sources, parts, PART, width), jnp.bfloat16),
        pltpu.VMEM((sources, 2, terms * capacity, width, width), jnp.bfloat16),
        pltpu.VMEM((sources, 2, blocks, rows, width), jnp.bfloat16),
        pltpu.VMEM((sources, PART, width), jnp.bfloat16),
        pltpu.VMEM((sources, 8, width), jnp.int32),
        pltpu.SMEM((sources, 8, width), jnp.int32),
        pltpu.SemaphoreType.DMA((sources,)),
        pltpu.SemaphoreType.DMA((sources, 2)),
        pltpu.SemaphoreType.DMA((sources, 2)),
        pltpu.SemaphoreType.DMA((sources,)),
        pltpu.SemaphoreType.DMA,
        pltpu.SemaphoreType.DMA,
    ]
    if end == "stats":
        scratch += [pltpu.VMEM(wave.shape, wave.dtype), pltpu.SemaphoreType.DMA]
    devices = lax.axis_size("sec") * lax.axis_size("term")
    total_out = jax.ShapeDtypeStruct(total_shape, jnp.float32)
    out_shape, out_specs = {
        "go on": ((total_out, jax.ShapeDtypeStruct((8, width), jnp.float32)), (anywhere, whole)),
        "stats": (
            (
                jax.ShapeDtypeStruct((blocks, rows, width), jnp.float32),
                jax.ShapeDtypeStruct((devices, 128), jnp.float32),
            ),
            (whole, whole),
        ),
        "result": (jax.ShapeDtypeStruct((blocks, rows, width), jnp.bfloat16), whole),
    }[end]
    choices = len(lefts) if chosen else 0
    return pl.pallas_call(
        functools.partial(apply_kernel, sources, choices, chosen, first, end, terms, capacity),
        out_shape=out_shape,
        in_specs=[pl.BlockSpec(memory_space=pltpu.SMEM)] + [anywhere] * len(arrays),
        out_specs=out_specs,
        scratch_shapes=scratch,
        compiler_params=pltpu.CompilerParams(vmem_limit_bytes=VMEM_LIMIT),
        cost_estimate=busy(3.5 + 1.8 * sources),
    )(ids, *arrays)


def direction_kernel(entries, total_ref, wave_ref, stats_ref, out_ref, rayleigh_ref):
    blocks = wave_ref.shape[0]
    stats = stats_ref[...]
    about, cross, own, local = (stats[:, lane : lane + 1] for lane in range(4))
    rayleigh = jnp.sum(cross, keepdims=True) / jnp.sum(own, keepdims=True)
    offset = local - rayleigh
    residual_sq = jnp.sum(about + offset * offset * own, keepdims=True)
    factor = lax.rsqrt(residual_sq / entries + 1e-06)
    rayleigh_ref[...] = rayleigh

    @pl.loop(0, blocks, unroll=4)
    def _(block):
        rest = total_ref[block] - rayleigh * wave_ref[block].astype(jnp.float32)
        out_ref[block] = (rest * factor).astype(jnp.bfloat16)


def new_direction(total, wave, stats, entries):
    whole = pl.BlockSpec(memory_space=pltpu.VMEM)
    return pl.pallas_call(
        functools.partial(direction_kernel, entries),
        out_shape=(
            jax.ShapeDtypeStruct(wave.shape, jnp.bfloat16),
            jax.ShapeDtypeStruct((1, 1), jnp.float32),
        ),
        in_specs=[whole] * 3,
        out_specs=(whole, whole),
        compiler_params=pltpu.CompilerParams(vmem_limit_bytes=8 * 2**20),
        cost_estimate=busy(2.0),
    )(total, wave, stats)


def per_device_ring(wavefunction, left_operator, right_operator, target_owner, target_local):
    owners, halves = lax.axis_size("sec"), lax.axis_size("term")
    me, half = lax.axis_index("sec"), lax.axis_index("term")
    terms, blocks, height, width = left_operator.shape
    rows = height // halves
    capacity = 2 * blocks // owners
    place = ring_place(me, owners)
    ids = jnp.stack([me, half]).astype(jnp.int32)

    own_rows = lax.dynamic_slice_in_dim(wavefunction, half * rows, rows, 1)
    other_rows = lax.dynamic_slice_in_dim(wavefunction, (1 - half) * rows, rows, 1)
    plan = jnp.stack([target_owner[:, :, 0], target_local])
    other_left = swap(
        lax.dynamic_slice_in_dim(left_operator, (1 - half) * rows, rows, 2), owners, halves
    )
    order = [m for m in ORDER if m < owners] + list(range(len(ORDER), owners))
    rights = (right_operator, swap(right_operator, owners, halves))
    pieces = pack(
        ids,
        plan,
        swap(plan, owners, halves),
        left_operator,
        other_left,
        plan,
        order[1:] + order[:1],
        capacity,
    )
    lefts = [pieces[0]]
    for m in range(1, owners):
        piece = pieces[m]
        if m in PIECE_WAITS:
            piece = after(piece, lefts[PIECE_WAITS[m]])
        lefts.append(exchange(piece, owners, halves, m))
    near = mask_gather(own_rows, lefts, owners, halves)
    far = {m: swap(unit, owners, halves) if m else other_rows for m, unit in near.items()}

    reach = (owners - 1) // 2
    turn = 1 - 2 * half
    distances = [0] + [s for step in range(1, reach + 1) for s in (step, -step)] + [owners // 2]
    whose = [me ^ ring_owner(place - s * turn, owners) for s in distances]
    numbers = jnp.stack([half, me * halves + half, *whose]).astype(jnp.int32)
    total = None
    groups = [order[at : at + 2] for at in range(0, owners, 2)]
    for group in groups:
        total, stats = apply_group(
            numbers,
            [lefts[m] for m in group],
            rights,
            [(near[m], far[m]) for m in group],
            total,
            "go on" if group is not groups[-1] else "stats",
            own_rows,
        )

    entries = blocks * owners * height * width
    stats = spread(stats, owners * halves)
    direction, rayleigh = new_direction(total, own_rows, stats, entries)
    def add_group(total, units, end):
        vectors = [(unit, swap(units[-s], owners, halves)) for s, unit in units.items()]
        chosen = 2 + distances.index(next(iter(units)))
        return apply_group(numbers, lefts, rights, vectors, total, end, chosen=chosen)

    total, waiting = None, {0: direction}
    ahead = behind = direction
    for step in range(1, reach + 1):
        ahead = ring_send(ahead, owners, halves, (1, -1))
        behind = ring_send(behind, owners, halves, (-1, 1))
        if step > 1:
            total, token = add_group(total, waiting, "go on")
            ahead, waiting = after(ahead, token), {}
        waiting.update({step: ahead, -step: behind})
    last = ring_send(ahead, owners, halves, (1, -1))
    total, token = add_group(total, waiting, "go on")
    last = after(last, token)
    vectors = [(last, swap(last, owners, halves))]
    chosen = 2 + distances.index(owners // 2)
    total = apply_group(numbers, lefts, rights, vectors, total, "result", chosen=chosen)
    return (total, rayleigh[0])


def slot_codes(target_owner, target_local, owners, capacity):
    terms, blocks = target_local.shape
    owner = target_owner[:, :, 0]
    place = jnp.arange(blocks, dtype=jnp.int32)
    same = (owner[:, :, None] == owner[:, None, :]) & (place[None, :] < place[:, None])[None]
    position = jnp.sum(same.astype(jnp.int32), axis=2)
    hit = (
        owner[:, None, None, :] == jnp.arange(owners, dtype=jnp.int32)[None, :, None, None]
    ) & (position[:, None, None, :] == jnp.arange(capacity, dtype=jnp.int32)[None, None, :, None])
    code = place[None, :] * (2 * blocks) + target_local - blocks
    return blocks + jnp.sum(jnp.where(hit, code[:, None, None, :], 0), axis=3)


def stream_kernel(first, capacity, blocks, code_ref, left_ref, vector_ref, right_ref, *rest):
    total_in, total = (None, rest[0]) if first else rest
    step = pl.program_id(0)
    rows, width = left_ref.shape[2:]

    @pl.when(step == 0)
    def _():
        total[...] = jnp.zeros_like(total) if first else total_in[...]

    for term in range(2):
        moved, where = [], []
        for slot in range(capacity):
            code = code_ref[2 * step + term, slot]
            source, target = lax.div(code, 2 * blocks), lax.rem(code, 2 * blocks)
            block = vector_ref[0, :, source].reshape(2 * rows, width)
            product = jnp.dot(left_ref[term, slot], block, preferred_element_type=jnp.float32)
            moved.append(product.astype(jnp.bfloat16))
            where.append(target)
        for slot in range(capacity):
            target = where[slot]
            total[target] += jnp.dot(
                moved[slot],
                right_ref[term, jnp.minimum(target, blocks - 1)],
                preferred_element_type=jnp.float32,
            )


def stream_chunk(total, codes, left, vector, right):
    owners, _, blocks, rows, width = vector.shape
    capacity = left.shape[1]
    first = total is None
    spec_total = pl.BlockSpec((blocks + 1, rows, width), lambda s, c: (0, 0, 0))
    return pl.pallas_call(
        functools.partial(stream_kernel, first, capacity, blocks),
        out_shape=jax.ShapeDtypeStruct((blocks + 1, rows, width), jnp.float32),
        grid_spec=pltpu.PrefetchScalarGridSpec(
            num_scalar_prefetch=1,
            grid=(owners,),
            in_specs=[
                pl.BlockSpec((2, capacity, rows, width), lambda s, c: (s, 0, 0, 0)),
                pl.BlockSpec((1, 2, blocks, rows, width), lambda s, c: (s, 0, 0, 0, 0)),
                pl.BlockSpec((2, blocks, width, width), lambda s, c: (0, 0, 0, 0)),
            ]
            + ([] if first else [spec_total]),
            out_specs=spec_total,
        ),
        compiler_params=pltpu.CompilerParams(vmem_limit_bytes=32 * 2**20),
        cost_estimate=pl.CostEstimate(
            flops=owners * 2 * capacity * 2 * 2 * rows * width * width,
            bytes_accessed=left.size * 2 + vector.size * 2 + right.size * 2,
            transcendentals=0,
        ),
    )(codes, left, vector, right, *([] if first else [total]))


def per_device_streamed(wavefunction, left_operator, right_operator, target_owner, target_local):
    owners = lax.axis_size("sec")
    halves = lax.axis_size("term")
    me, half = lax.axis_index("sec"), lax.axis_index("term")
    terms, blocks, height, width = left_operator.shape
    rows = height // halves
    capacity = 2 * blocks // owners

    own_rows = lax.dynamic_slice_in_dim(wavefunction, half * rows, rows, 1)
    codes = slot_codes(target_owner, target_local, owners, capacity)
    sources = codes // (2 * blocks)

    moved_left = []
    for k in range(terms):
        pick = sources[k][:, None, :] * halves + jnp.arange(halves, dtype=jnp.int32)[None, :, None]
        pieces = left_operator[k].reshape(blocks * halves, rows, width)[pick.reshape(-1)]
        pieces = pieces.reshape(owners * halves, capacity, rows, width)
        moved_left.append(lax.all_to_all(pieces, BOTH, split_axis=0, concat_axis=0, tiled=True))
    all_codes = lax.all_gather(codes, BOTH, axis=0)
    my_codes = lax.dynamic_index_in_dim(all_codes, me, axis=3 - 1, keepdims=False)
    gathered = lax.all_gather(own_rows, BOTH, axis=0).reshape(owners, halves, blocks, rows, width)
    right = lax.all_gather(right_operator, "term", axis=1)

    def apply(vector):
        total = None
        for k in range(terms):
            total = stream_chunk(total, my_codes[:, k], moved_left[k], vector, right[k])
        return total[:blocks]

    sigma_rows = apply(gathered)
    wave = own_rows.astype(jnp.float32)
    cross, own = jnp.sum(wave * sigma_rows), jnp.sum(wave * wave)
    local = jnp.where(own > 0, cross / own, 0.0)
    about = jnp.sum(jnp.square(sigma_rows - local * wave))
    stats = lax.all_gather(jnp.stack([about, cross, own, local]), BOTH, axis=0)
    rayleigh = jnp.sum(stats[:, 1]) / jnp.sum(stats[:, 2])
    residual_sq = jnp.sum(stats[:, 0] + jnp.square(stats[:, 3] - rayleigh) * stats[:, 2])
    entries = blocks * owners * height * width
    factor = lax.rsqrt(residual_sq / entries + 1e-06)
    direction = ((sigma_rows - rayleigh * wave) * factor).astype(jnp.bfloat16)
    direction = lax.all_gather(direction, BOTH, axis=0).reshape(gathered.shape)
    sigma_two = apply(direction).astype(jnp.bfloat16)
    return (sigma_two, jnp.reshape(rayleigh, (1,)))


def per_device(wavefunction, *operands):
    owners = lax.axis_size("sec")
    gathered_bytes = owners * wavefunction.size * wavefunction.dtype.itemsize
    if owners < 8 or owners & (owners - 1) or 2 * gathered_bytes > RING_BYTES:
        return per_device_streamed(wavefunction, *operands)
    return per_device_ring(wavefunction, *operands)


def solution(mesh):
    placed = (
        P(("rep", "sec"), None, None),
        P("term", ("rep", "sec"), None, None),
        P("term", ("rep", "sec"), None, None),
        P("term", ("rep", "sec"), None),
        P("term", ("rep", "sec")),
    )
    return jax.shard_map(
        per_device,
        mesh=mesh,
        in_specs=placed,
        out_specs=(P(("rep", "sec"), "term", None), P("rep")),
        check_vma=False,
    )
```
